32 devices in a mesh: segment: 4 (over y, x), space: 8 (over z, core).
Axes of the slice: x: 2, y: 2, z: 4, core: 2. Of those that a mesh axis runs over, the one named last changes fastest.
Arguments:
- node_states: bfloat16 [2, 64, 29, 128], P(None, 'space'), may hold values from -6 to 6
- species: int32 [2, 64], P(None, 'space'), may hold values from 0 to 99
- species_table: bfloat16 [100, 128], replicated, may hold values from -6 to 6
- places: float32 [2, 3, 64], P(None, None, 'space'), may hold values from 0 to 2
- sources: int32 [2, 64, 8], P(None, 'space'), may hold values from 0 to 63, as said below
- radial_rate: float32 [4, 128], P('segment'), may hold values from 0.2 to 1.5
- zero_weight: bfloat16 [4, 896, 896], P('segment'), may hold values from -0.1875 to 0.1875
- one_weight: bfloat16 [4, 2, 768, 768], P('segment'), may hold values from -0.21875 to 0.21875
- two_weight: bfloat16 [4, 2, 640, 640], P('segment'), may hold values from -0.25 to 0.25
- read_weight: float32 [128], replicated, may hold values from -0.5 to 0.5
- energy_grad: float32 [2, 64], P(None, 'space'), may hold values from -6 to 6
Outputs:
- energies: float32 [2, 64], P(None, 'space')
- place_grads: float32 [2, 3, 64], P(None, None, 'space')
The draws below stay inside these ranges and needn't reach their ends.
Inputs may be any that keep to these rules, and one draw needn't show every extreme that they name: Each atom's 8 sources are distinct, differ from the atom, and lie in the atom's slab (index // 8) or in one of the two slabs beside it, the slabs forming a closed chain.
All inputs are finite; a program needn't handle non-finite values.
Results may differ from the reference program's by a relative error of at most 0.012.
The reference program's roundings to bfloat16 on the way (of `start` and `scaled`) count: a program that leaves them out, or rounds other values in their place, can miss the bound.
Values may be sent and summed in bfloat16 or wider, within the bound.
No kernel may reach another device: no remote copies, remote signals or barrier semaphores. Data moves between devices by JAX's collectives and lax.ppermute only.
A program may use at most 128 MiB of HBM per device.

```python
import math
import jax
import jax.numpy as jnp
from jax import lax

C = 128
COEFS = 29
SPECIES = 100
NEIGH = 8
A_DEV = 8
BATCHES = 2
LAYERS = 4
ATOMS = 64
N_SPACE = 8


def draw_sources(key, part):
    slab_count = ATOMS // A_DEV
    window = 3 * A_DEV
    scores = jax.random.randint(key, (BATCHES, ATOMS, window), 0, 1 << 20, dtype=jnp.int32)
    scores = scores * window + jnp.arange(window, dtype=jnp.int32)[None, None, :]
    own_column = A_DEV + jnp.arange(ATOMS, dtype=jnp.int32) % A_DEV
    scores = jnp.where(jnp.arange(window, dtype=jnp.int32)[None, None, :] == own_column[None, :, None], jnp.int32(1 << 30), scores)
    chosen = jnp.argsort(scores, axis=-1, stable=True)[..., :NEIGH].astype(jnp.int32)
    home = jnp.arange(ATOMS, dtype=jnp.int32) // A_DEV
    source_slab = jnp.mod(home[None, :, None] - 1 + chosen // A_DEV, slab_count)
    return (source_slab * A_DEV + chosen % A_DEV).astype(jnp.int32)


def plant(entries, key, smallest, top_value):
    shape = entries.shape
    index_at = [jax.random.randint(jax.random.fold_in(key, axis), (), 0, shape[axis]) for axis in range(len(shape))]
    entries = entries.at[tuple(index_at)].set(smallest)
    longest = shape.index(max(shape))
    index_at[longest] = (index_at[longest] + 1) % shape[longest]
    return entries.at[tuple(index_at)].set(top_value)


def steps_of(key, shape, shards, least, largest):
    level, own = 1.0, jax.random.fold_in(key, 6)
    for position, parts in shards:
        draws = jnp.exp(jax.random.uniform(jax.random.fold_in(own, position), (parts,), jnp.float32, least / len(shards), largest / len(shards)))
        level = level * jnp.repeat(draws, shape[position] // parts).reshape([-1 if axis == position else 1 for axis in range(len(shape))])
    return level


def scatter_about(own_key, shape, deviation, limit, cuts=(), kind=jnp.bfloat16):
    loudness = steps_of(own_key, shape, cuts, -0.22, 0.18) if cuts else 1.0
    drawn = jax.random.normal(own_key, shape, jnp.float32) * deviation * loudness
    return jnp.minimum(jnp.maximum(drawn, -limit), limit).astype(kind)


def setup_inputs(seed: int = 0) -> dict:
    streams_of = jax.random.split(jax.random.key(seed), 12)
    node_states = scatter_about(streams_of[0], (BATCHES, ATOMS, COEFS, C), 1.0, 6.0, ((1, 8),))
    species = plant(jax.random.randint(streams_of[1], (BATCHES, ATOMS), 0, SPECIES), jax.random.fold_in(streams_of[1], 1), 0, SPECIES - 1).astype(jnp.int32)
    species_table = scatter_about(streams_of[2], (SPECIES, C), 1.0, 6.0)
    places = jnp.clip(2.0 * jax.random.uniform(streams_of[3], (BATCHES, 3, ATOMS), jnp.float32) ** steps_of(streams_of[3], (BATCHES, 3, ATOMS), ((2, 8),), -0.2, 0.2), 0.0, 2.0)
    sources = draw_sources(jax.random.fold_in(streams_of[11], 71), 0)
    radial_rate = jnp.clip(jnp.exp(math.log(1.5) - 2.014903 * jax.random.uniform(streams_of[5], (LAYERS, C), jnp.float32) ** steps_of(streams_of[5], (LAYERS, C), ((0, 4),), -0.2, 0.2)), 0.2, 1.5)
    zero_weight = scatter_about(streams_of[6], (LAYERS, 7 * C, 7 * C), (7 * C) ** -0.5, 0.1875, ((0, 4),))
    one_weight = scatter_about(streams_of[7], (LAYERS, 2, 6 * C, 6 * C), (6 * C) ** -0.5, 0.21875, ((0, 4),))
    two_weight = scatter_about(streams_of[8], (LAYERS, 2, 5 * C, 5 * C), (5 * C) ** -0.5, 0.25, ((0, 4),))
    read_weight = scatter_about(streams_of[9], (C,), C ** -0.5, 0.5, (), jnp.float32)
    energy_grad = scatter_about(streams_of[10], (BATCHES, ATOMS), 1.0, 6.0, ((1, 8),), jnp.float32)
    return {"node_states": node_states, "species": species, "species_table": species_table, "places": places, "sources": sources, "radial_rate": radial_rate, "zero_weight": zero_weight, "one_weight": one_weight, "two_weight": two_weight, "read_weight": read_weight, "energy_grad": energy_grad}


slab_depth = 2.0

def layer_core(picked, offset, own_states, decay_rate, weight_zero, weight_one, weight_two):
    per_slab = own_states.shape[0]
    channels = own_states.shape[2]
    edge_count = picked.shape[0]
    neighbours = edge_count // per_slab
    length = jnp.sqrt(lax.optimization_barrier(jnp.sum(offset * offset, axis=0)) + 1.0)
    planar = jnp.sqrt(offset[0] * offset[0] + offset[1] * offset[1] + 1.0)
    cos_one = (offset[0] / planar)[:, None]
    sin_one = (offset[1] / planar)[:, None]
    cos_two = cos_one * cos_one - sin_one * sin_one
    sin_two = 2.0 * cos_one * sin_one
    radial = jnp.exp(-decay_rate[None, :] * length[:, None])
    scaled = (picked * radial[:, None, :]).astype(jnp.bfloat16)
    zero_in = scaled[:, 0:7].reshape(edge_count, 7 * channels)
    zero_out = jnp.dot(zero_in, weight_zero, preferred_element_type=jnp.float32)
    one_re = scaled[:, 7:13].reshape(edge_count, 6 * channels)
    one_im = scaled[:, 13:19].reshape(edge_count, 6 * channels)
    first_re = jnp.dot(one_re, weight_one[0], preferred_element_type=jnp.float32) - jnp.dot(one_im, weight_one[1], preferred_element_type=jnp.float32)
    first_im = jnp.dot(one_re, weight_one[1], preferred_element_type=jnp.float32) + jnp.dot(one_im, weight_one[0], preferred_element_type=jnp.float32)
    turn_one_re = cos_one * first_re - sin_one * first_im
    turn_one_im = sin_one * first_re + cos_one * first_im
    two_re = scaled[:, 19:24].reshape(edge_count, 5 * channels)
    two_im = scaled[:, 24:29].reshape(edge_count, 5 * channels)
    second_re = jnp.dot(two_re, weight_two[0], preferred_element_type=jnp.float32) - jnp.dot(two_im, weight_two[1], preferred_element_type=jnp.float32)
    second_im = jnp.dot(two_re, weight_two[1], preferred_element_type=jnp.float32) + jnp.dot(two_im, weight_two[0], preferred_element_type=jnp.float32)
    turn_two_re = cos_two * second_re - sin_two * second_im
    turn_two_im = sin_two * second_re + cos_two * second_im
    factor = neighbours ** (-0.5)

    def pool_edges(values, rows):
        return (lax.optimization_barrier(jnp.sum(values.reshape(per_slab, neighbours, -1), axis=1)) * factor).reshape(per_slab, rows, channels)
    pooled_zero = pool_edges(zero_out, 7)
    pooled_one_re = pool_edges(turn_one_re, 6)
    pooled_one_im = pool_edges(turn_one_im, 6)
    pooled_two_re = pool_edges(turn_two_re, 5)
    pooled_two_im = pool_edges(turn_two_im, 5)
    signal = pooled_zero[:, 0] + lax.optimization_barrier(jnp.sum(pooled_one_re * pooled_one_re + pooled_one_im * pooled_one_im, axis=1)) + lax.optimization_barrier(jnp.sum(pooled_two_re * pooled_two_re + pooled_two_im * pooled_two_im, axis=1))
    gate = jax.nn.sigmoid(signal)[:, None, :]
    head = own_states[:, 0:1] + jax.nn.silu(signal)[:, None, :]
    others = jnp.concatenate([pooled_zero[:, 1:], pooled_one_re, pooled_one_im, pooled_two_re, pooled_two_im], axis=1)
    remainder = own_states[:, 1:] + gate * others
    return jnp.concatenate([head, remainder], axis=1)

def readout(updated, read_weight):
    return lax.optimization_barrier(jnp.sum(read_weight[None, :] * jax.nn.silu(updated[:, 0, :]), axis=1))

def slab_layer(states, places, sources, decay_rate, weight_zero, weight_one, weight_two):

    def block_pass(slab_index):
        block_rows = lax.dynamic_slice_in_dim(sources, slab_index * A_DEV, A_DEV, 0)
        flat_sources = block_rows.reshape(-1)
        picked = jnp.take(states, flat_sources, axis=0)
        targets = slab_index * A_DEV + jnp.arange(A_DEV, dtype=jnp.int32)
        target_flat = jnp.repeat(targets, NEIGH)
        window = (jnp.mod(flat_sources // A_DEV - slab_index + 1, N_SPACE) - 1).astype(jnp.float32)
        source_places = jnp.take(places, flat_sources, axis=1)
        elevation = jnp.stack([jnp.zeros_like(window), jnp.zeros_like(window), slab_depth * window])
        offset = source_places + elevation - jnp.take(places, target_flat, axis=1)
        own_states = lax.dynamic_slice_in_dim(states, slab_index * A_DEV, A_DEV, 0)
        return layer_core(picked, offset, own_states, decay_rate, weight_zero, weight_one, weight_two)
    blocks = lax.map(jax.checkpoint(block_pass), jnp.arange(N_SPACE, dtype=jnp.int32))
    return blocks.reshape(ATOMS, COEFS, C)

def reference(node_states, species, species_table, places, sources, radial_rate, zero_weight, one_weight, two_weight, read_weight, energy_grad):
    onehot = (species[..., None] == jnp.arange(SPECIES, dtype=jnp.int32)[None, None, :]).astype(jnp.float32)
    embed = jnp.einsum('bak,kc->bac', onehot, species_table.astype(jnp.float32))
    start = jnp.concatenate([node_states[:, :, 0:1].astype(jnp.float32) + embed[:, :, None, :], node_states[:, :, 1:].astype(jnp.float32)], axis=2).astype(jnp.bfloat16)

    def weighted(all_places):
        energy_list = []
        for batch_now in range(BATCHES):
            state = start[batch_now]
            updated = None
            for layer in range(LAYERS):
                updated = slab_layer(state.astype(jnp.float32), all_places[batch_now], sources[batch_now], radial_rate[layer], zero_weight[layer], one_weight[layer], two_weight[layer])
                if layer + 1 < LAYERS:
                    state = updated.astype(jnp.bfloat16)
            energy_list.append(readout(updated, read_weight))
        stacked = jnp.stack(energy_list)
        return (jnp.sum(stacked * energy_grad), stacked)
    output, pullback, energies = jax.vjp(weighted, places, has_aux=True)
    gradient = pullback(jnp.ones_like(output))[0]
    return (energies, gradient)
```

```python
import functools

import jax
import jax.numpy as jnp
from jax import lax
from jax.experimental import pallas as pl
from jax.experimental.pallas import tpu as pltpu
from jax.sharding import PartitionSpec as P

SLAB_DEPTH = 2.0
F32 = jnp.float32
BF16 = jnp.bfloat16
LINK = F32
VMEM_LIMIT = 40 * 1024 * 1024


def split(value):
    high = value.astype(BF16)
    low = (value - high.astype(F32)).astype(BF16)
    return high, low


def dot(a, b):
    return lax.dot_general(a, b, (((1,), (0,)), ((), ())), preferred_element_type=F32)


def dot_t(a, b):
    return lax.dot_general(a, b, (((1,), (1,)), ((), ())), preferred_element_type=F32)


def fine_dot(value, weights, product):
    rows = value.shape[0]
    stacked = jnp.concatenate(split(value), axis=0)
    outs = []
    for weight in weights:
        out = product(stacked, weight)
        outs.append(out[:rows] + out[rows:])
    return outs


def silu_parts(value):
    gate = 1.0 / (1.0 + jnp.exp(-value))
    return gate, value * gate


class Sizes:
    def __init__(self, zero_shape, one_shape, two_shape, channels):
        self.c = channels
        self.zero = zero_shape[-1] // channels
        self.one = one_shape[-1] // channels
        self.two = two_shape[-1] // channels
        self.coefs = self.zero + 2 * (self.one + self.two)
        self.starts = (self.zero, self.zero + 2 * self.one)
        self.counts = (self.one, self.two)

    def cols(self, first, count=1):
        return slice(first * self.c, (first + count) * self.c)


def picked_group(refs, hot, sz, first, count):
    cols = sz.cols(first, count)
    window = jnp.concatenate([ref[:, cols] for ref in refs], axis=0)
    return dot(hot, window)


def pool(value, rows):
    total = value[:rows]
    for start in range(rows, value.shape[0], rows):
        total = total + value[start : start + rows]
    return total


def geo_at(geo_ref, which, edges):
    return geo_ref[which * edges : (which + 1) * edges, :]


def forward(refs, hot_ref, geo_ref, zero_ref, one_ref, two_ref, sz, rows, last):
    hot = hot_ref[...]
    edges = hot.shape[0]
    factor = (edges // rows) ** (-0.5)
    radial = geo_at(geo_ref, 0, edges)

    def scaled(block):
        return (block * radial).astype(BF16).astype(F32)

    pooled = [None] * sz.coefs
    group = picked_group(refs, hot, sz, 0, sz.zero)
    zin = jnp.concatenate(
        [pool(scaled(group[:, sz.cols(k)]), rows) for k in range(sz.zero)], axis=1
    )
    kept = 1 if last else sz.zero
    (zout,) = fine_dot(zin, [zero_ref[:, sz.cols(0, kept)]], dot)
    for k in range(kept):
        pooled[k] = zout[:, sz.cols(k)] * factor
    for order in range(2):
        first, count = sz.starts[order], sz.counts[order]
        weight_ref = (one_ref, two_ref)[order]
        cos = geo_at(geo_ref, 1 + 2 * order, edges)
        sin = geo_at(geo_ref, 2 + 2 * order, edges)
        group = picked_group(refs, hot, sz, first, 2 * count)
        res, ims = [], []
        for k in range(count):
            re = scaled(group[:, sz.cols(k)])
            im = scaled(group[:, sz.cols(count + k)])
            res.append(pool(cos * re - sin * im, rows))
            ims.append(pool(sin * re + cos * im, rows))
        both = jnp.concatenate(
            [jnp.concatenate(res, axis=1), jnp.concatenate(ims, axis=1)], axis=0
        )
        a, b = fine_dot(both, [weight_ref[0], weight_ref[1]], dot)
        out_re = (a[:rows] - b[rows:]) * factor
        out_im = (b[:rows] + a[rows:]) * factor
        for k in range(count):
            pooled[first + k] = out_re[:, sz.cols(k)]
            pooled[first + count + k] = out_im[:, sz.cols(k)]
    return pooled


def signal_of(pooled, sz):
    total = pooled[0]
    for k in range(sz.zero, sz.coefs):
        total = total + pooled[k] * pooled[k]
    return total


def backward(
    upstream, pooled, refs, hot_ref, hot_t_ref, geo_ref, zero_ref, one_ref, two_ref, sz, rows, last, outs, places_ref
):
    hot = hot_ref[...]
    edges = hot.shape[0]
    factor = (edges // rows) ** (-0.5)
    signal = signal_of(pooled, sz)
    gate, _ = silu_parts(signal)
    slope = gate * (1.0 - gate)
    d_signal = upstream[0] * (gate + signal * slope)
    if not last:
        inner = upstream[1] * pooled[1]
        for k in range(2, sz.coefs):
            inner = inner + upstream[k] * pooled[k]
        d_signal = d_signal + inner * slope
    d_pooled = [d_signal * factor]
    for k in range(1, sz.coefs):
        if last:
            d_pooled.append(2.0 * factor * d_signal * pooled[k] if k >= sz.zero else None)
        else:
            term = gate * upstream[k]
            if k >= sz.zero:
                term = term + 2.0 * d_signal * pooled[k]
            d_pooled.append(term * factor)

    radial = geo_at(geo_ref, 0, edges)
    kept = 1 if last else sz.zero
    (dz,) = fine_dot(jnp.concatenate(d_pooled[:kept], axis=1), [zero_ref[:, sz.cols(0, kept)]], dot_t)

    def spread(block):
        return jnp.concatenate([block] * (edges // rows), axis=0)

    hot_t = None if outs is None else hot_t_ref[...]

    def scatter(first, blocks):
        if outs is None:
            return
        value = jnp.concatenate(blocks, axis=1)
        high, low = split(value)
        back = dot(hot_t, high) + dot(hot_t, low)
        cols = sz.cols(first, len(blocks))
        for place in range(3):
            part = back[place * rows : (place + 1) * rows]
            if place == 1 and not last:
                part = part + jnp.concatenate(upstream[first : first + len(blocks)], axis=1)
            elif place == 1 and first == 0:
                part = jnp.concatenate([part[:, : sz.c] + upstream[0], part[:, sz.c :]], axis=1)
            outs[place][:, cols] = part.astype(outs[place].dtype)

    q_len = jnp.zeros((edges, sz.c), F32)
    group = picked_group(refs, hot, sz, 0, sz.zero)
    blocks = []
    for k in range(sz.zero):
        grad = spread(dz[:, sz.cols(k)])
        q_len = q_len + grad * group[:, sz.cols(k)]
        blocks.append(grad * radial)
    q_len = q_len * radial
    scatter(0, blocks)
    q_turn = []
    for order in range(2):
        first, count = sz.starts[order], sz.counts[order]
        weight_ref = (one_ref, two_ref)[order]
        cos = geo_at(geo_ref, 1 + 2 * order, edges)
        sin = geo_at(geo_ref, 2 + 2 * order, edges)
        both = jnp.concatenate(
            [
                jnp.concatenate(d_pooled[first : first + count], axis=1),
                jnp.concatenate(d_pooled[first + count : first + 2 * count], axis=1),
            ],
            axis=0,
        )
        a, b = fine_dot(both, [weight_ref[0], weight_ref[1]], dot_t)
        d_re = a[:rows] + b[rows:]
        d_im = a[rows:] - b[:rows]
        group = picked_group(refs, hot, sz, first, 2 * count)
        q_cos = jnp.zeros((edges, sz.c), F32)
        q_sin = jnp.zeros((edges, sz.c), F32)
        cos_r = cos * radial
        sin_r = sin * radial
        blocks_re, blocks_im = [], []
        for k in range(count):
            re = group[:, sz.cols(k)]
            im = group[:, sz.cols(count + k)]
            g_re = spread(d_re[:, sz.cols(k)])
            g_im = spread(d_im[:, sz.cols(k)])
            q_cos = q_cos + (re * g_re + im * g_im)
            q_sin = q_sin + (re * g_im - im * g_re)
            if outs is not None:
                blocks_re.append(cos_r * g_re + sin_r * g_im)
                blocks_im.append(cos_r * g_im - sin_r * g_re)
        scatter(first, blocks_re + blocks_im)
        q_cos = q_cos * radial
        q_sin = q_sin * radial
        q_len = q_len + cos * q_cos + sin * q_sin
        q_turn.append((q_cos, q_sin))

    rate = geo_at(geo_ref, 11, edges)

    def total(value):
        return jnp.sum(value, axis=1, keepdims=True)

    d_len = -total(q_len * rate)
    (dc1, ds1), (dc2, ds2) = [(total(a), total(b)) for a, b in q_turn]
    c1, s1 = geo_at(geo_ref, 1, edges), geo_at(geo_ref, 2, edges)
    ux, uy, uz = (geo_at(geo_ref, 5 + n, edges) for n in range(3))
    inv_planar = geo_at(geo_ref, 8, edges)
    dc1 = dc1 + 2.0 * (c1 * dc2 + s1 * ds2)
    ds1 = ds1 + 2.0 * (c1 * ds2 - s1 * dc2)
    along = c1 * dc1 + s1 * ds1
    dx = (dc1 - along * c1) * inv_planar + d_len * ux
    dy = (ds1 - along * s1) * inv_planar + d_len * uy
    dz_ = d_len * uz
    lane = lax.broadcasted_iota(jnp.int32, (edges, sz.c), 1)
    change = jnp.where(lane == 0, dx, jnp.where(lane == 1, dy, jnp.where(lane == 2, dz_, 0.0)))
    high, rest = change.astype(BF16), None
    rest = change - high.astype(F32)
    mid = rest.astype(BF16)
    low = (rest - mid.astype(F32)).astype(BF16)
    hot_t = hot_t_ref[...]
    moved = dot(hot_t, high) + dot(hot_t, mid) + dot(hot_t, low)
    places_ref[:rows, :] = moved[:rows]
    places_ref[rows : 2 * rows, :] = moved[rows : 2 * rows] - pool(change, rows)
    places_ref[2 * rows :, :] = moved[2 * rows :]


def geometry_kernel(index_ref, places_ref, rate_ref, hot_ref, geo_ref):
    edges = index_ref.shape[0]
    window = places_ref.shape[0]
    rows = window // 3
    c = rate_ref.shape[1]
    hot = (index_ref[...] == lax.broadcasted_iota(jnp.int32, (edges, window), 1)).astype(BF16)
    hot_ref[...] = hot
    repeats = edges // rows
    offset = []
    for n in range(3):
        column = jnp.broadcast_to(places_ref[:, n : n + 1], (window, c))
        high = column.astype(BF16)
        rest = column - high.astype(F32)
        mid = rest.astype(BF16)
        low = (rest - mid.astype(F32)).astype(BF16)
        there = dot(hot, high) + dot(hot, mid) + dot(hot, low)
        offset.append(there - jnp.concatenate([column[rows : 2 * rows]] * repeats, axis=0))
    flat = offset[0] * offset[0] + offset[1] * offset[1] + 1.0
    length = jnp.sqrt(flat + offset[2] * offset[2])
    planar = jnp.sqrt(flat)
    c1, s1 = offset[0] / planar, offset[1] / planar
    rate = jnp.broadcast_to(rate_ref[...], (edges, c))
    parts = [
        jnp.exp(-rate * length),
        c1,
        s1,
        c1 * c1 - s1 * s1,
        2.0 * c1 * s1,
        offset[0] / length,
        offset[1] / length,
        offset[2] / length,
        1.0 / planar,
        offset[0],
        offset[1],
        rate,
    ]
    for n, part in enumerate(parts):
        geo_ref[n * edges : (n + 1) * edges, :] = part


def forward_kernel(
    tick, sz, flag_ref, left_ref, own_ref, right_ref, hot_ref, geo_ref, zero_ref, one_ref, two_ref, out_ref, pooled_ref
):
    @pl.when(flag_ref[0] == tick)
    def _():
        rows = own_ref.shape[0]
        refs = (left_ref, own_ref, right_ref)
        pooled = forward(refs, hot_ref, geo_ref, zero_ref, one_ref, two_ref, sz, rows, False)
        for k in range(sz.coefs):
            pooled_ref[:, sz.cols(k)] = pooled[k]
        signal = signal_of(pooled, sz)
        gate, lifted = silu_parts(signal)
        for k in range(sz.coefs):
            added = lifted if k == 0 else gate * pooled[k]
            out_ref[:, sz.cols(k)] = (own_ref[:, sz.cols(k)].astype(F32) + added).astype(BF16)


def turn_kernel(
    tick, sz, flag_ref, left_ref, own_ref, right_ref, hot_ref, hot_t_ref, geo_ref, zero_ref, one_ref, two_ref,
    read_ref, seed_ref, *out_refs
):
    energy_ref, places_ref = out_refs[:2]
    outs = out_refs[2:] or None

    @pl.when(flag_ref[0] == tick)
    def _():
        rows = own_ref.shape[0]
        refs = (left_ref, own_ref, right_ref)
        pooled = forward(refs, hot_ref, geo_ref, zero_ref, one_ref, two_ref, sz, rows, True)
        signal = signal_of(pooled, sz)
        _, lifted = silu_parts(signal)
        updated = own_ref[:, sz.cols(0)].astype(F32) + lifted
        gate, active = silu_parts(updated)
        read = read_ref[...]
        energy_ref[...] = jnp.sum(read * active, axis=1, keepdims=True)
        upstream = [seed_ref[...] * read * (gate + updated * gate * (1.0 - gate))]
        backward(
            upstream, pooled, refs, hot_ref, hot_t_ref, geo_ref, zero_ref, one_ref, two_ref, sz, rows, True, outs, places_ref
        )


def backward_kernel(
    tick, sz, flag_ref, upstream_ref, pooled_ref, left_ref, own_ref, right_ref, hot_ref, hot_t_ref, geo_ref,
    zero_ref, one_ref, two_ref, *out_refs
):
    places_ref = out_refs[0]
    outs = out_refs[1:] or None

    @pl.when(flag_ref[0] == tick)
    def _():
        rows = own_ref.shape[0]
        refs = (left_ref, own_ref, right_ref)
        upstream = [upstream_ref[:, sz.cols(k)].astype(F32) for k in range(sz.coefs)]
        pooled = [pooled_ref[:, sz.cols(k)] for k in range(sz.coefs)]
        backward(
            upstream, pooled, refs, hot_ref, hot_t_ref, geo_ref, zero_ref, one_ref, two_ref, sz, rows, False, outs, places_ref
        )


def on_vmem(value):
    return pltpu.with_memory_space_constraint(value, pltpu.VMEM)


def call(body, operands, shapes, flagged, name):
    in_specs = [pl.BlockSpec(memory_space=pltpu.VMEM) for _ in operands]
    if flagged:
        in_specs[0] = pl.BlockSpec(memory_space=pltpu.SMEM)
    return pl.pallas_call(
        body,
        out_shape=shapes,
        in_specs=in_specs,
        out_specs=jax.tree.map(lambda _: pl.BlockSpec(memory_space=pltpu.VMEM), shapes),
        compiler_params=pltpu.CompilerParams(vmem_limit_bytes=VMEM_LIMIT),
        name=name,
    )(*operands)


def on_device(
    node_states,
    species,
    species_table,
    places,
    sources,
    radial_rate,
    zero_weight,
    one_weight,
    two_weight,
    read_weight,
    energy_grad,
):
    segments = lax.axis_size("segment")
    slabs = lax.axis_size("space")
    segment_now = lax.axis_index("segment")
    slab_now = lax.axis_index("space")
    batches, per_slab = species.shape
    coefs, channels = node_states.shape[2:]
    neighbours = sources.shape[2]
    rows = batches * per_slab
    edges = rows * neighbours
    width = coefs * channels
    sz = Sizes(zero_weight.shape, one_weight.shape, two_weight.shape, channels)
    axes = ("segment", "space")

    def to_right(value):
        return lax.ppermute(value, "space", [(i, (i + 1) % slabs) for i in range(slabs)])

    def to_left(value):
        return lax.ppermute(value, "space", [((i + 1) % slabs, i) for i in range(slabs)])

    def in_segment(value, segment, by):
        pairs = [(segment * slabs + i, segment * slabs + (i + by) % slabs) for i in range(slabs)]
        return lax.ppermute(value, axes, pairs)

    def hop(value, start, stop):
        return lax.ppermute(value, axes, [(start * slabs + i, stop * slabs + i) for i in range(slabs)])

    onehot = (species[..., None] == jnp.arange(species_table.shape[0], dtype=jnp.int32)).astype(BF16)
    embed = jnp.einsum("bak,kc->bac", onehot, species_table, preferred_element_type=F32)
    start = jnp.concatenate(
        [(node_states[:, :, 0].astype(F32) + embed).astype(BF16)[:, :, None], node_states[:, :, 1:]], axis=2
    ).reshape(rows, width)

    own_places = places.transpose(0, 2, 1).reshape(rows, 3)
    lift = jnp.array([0.0, 0.0, SLAB_DEPTH], F32)
    window_places = jnp.concatenate(
        [to_right(own_places) - lift, own_places, to_left(own_places) + lift], axis=0
    )
    window = jnp.mod(sources // per_slab - slab_now + 1, slabs)
    batch = jnp.arange(batches, dtype=jnp.int32)[:, None, None]
    index = window * rows + batch * per_slab + sources % per_slab
    index = index.transpose(2, 0, 1).reshape(1, edges)
    hot_t = (index == jnp.arange(3 * rows, dtype=jnp.int32)[:, None]).astype(BF16)
    hot, geo = call(
        geometry_kernel,
        [index.reshape(edges, 1), window_places, radial_rate],
        [jax.ShapeDtypeStruct((edges, 3 * rows), BF16), jax.ShapeDtypeStruct((12 * edges, channels), F32)],
        False,
        "geometry",
    )
    flag = jnp.reshape(segment_now, (1,)).astype(jnp.int32)
    weights = [on_vmem(zero_weight[0]), on_vmem(one_weight[0]), on_vmem(two_weight[0])]
    states = jax.ShapeDtypeStruct((rows, width), BF16)
    wide = jax.ShapeDtypeStruct((rows, width), F32)
    link = jax.ShapeDtypeStruct((rows, width), LINK)
    place_shape = jax.ShapeDtypeStruct((3 * rows, channels), F32)

    around = [(to_right(start), start, to_left(start))]
    pooled = []
    for tick in range(segments - 1):
        out, kept = call(
            functools.partial(forward_kernel, tick, sz),
            [flag, *around[tick], hot, geo, *weights],
            [states, wide],
            True,
            "forward",
        )
        pooled.append(kept)
        own = hop(out, tick, tick + 1)
        around.append((in_segment(own, tick + 1, 1), own, in_segment(own, tick + 1, -1)))
    final = segments - 1
    seeds = jnp.broadcast_to(energy_grad.reshape(rows, 1), (rows, channels))
    more = [link, wide, link]
    energy, moved, *parts = call(
        functools.partial(turn_kernel, final, sz),
        [flag, *around[final], hot, hot_t, geo, *weights, read_weight.reshape(1, channels), seeds],
        [jax.ShapeDtypeStruct((rows, 1), F32), place_shape] + (more if final else []),
        True,
        "turn",
    )
    moves = [moved]
    for tick in reversed(range(segments - 1)):
        low, own, high = parts
        back_low = in_segment(low, tick + 1, -1)
        back_high = in_segment(high, tick + 1, 1)
        total = (own + back_low.astype(F32) + back_high.astype(F32)).astype(BF16)
        upstream = hop(total, tick + 1, tick)
        moved, *parts = call(
            functools.partial(backward_kernel, tick, sz),
            [flag, upstream, pooled[tick], *around[tick], hot, hot_t, geo, *weights],
            [place_shape] + (more if tick else []),
            True,
            "backward",
        )
        moves.insert(0, moved)

    here = jnp.zeros((3 * rows, 3), F32)
    for tick in range(segments):
        here = jnp.where(segment_now == tick, moves[tick][:, :3], here)
    shares = here[rows : 2 * rows] + to_left(here[:rows]) + to_right(here[2 * rows :])
    energies = jnp.where(segment_now == final, energy, 0.0)
    whole = lax.psum(jnp.concatenate([shares, energies], axis=1), "segment")
    whole = whole.reshape(batches, per_slab, 4)
    return whole[..., 3], whole[..., :3].transpose(0, 2, 1)


def solution(mesh):
    in_specs = (
        P(None, "space", None, None),
        P(None, "space"),
        P(),
        P(None, None, "space"),
        P(None, "space", None),
        P("segment", None),
        P("segment", None, None),
        P("segment", None, None, None),
        P("segment", None, None, None),
        P(),
        P(None, "space"),
    )
    out_specs = (P(None, "space"), P(None, None, "space"))
    return jax.shard_map(
        on_device, mesh=mesh, in_specs=in_specs, out_specs=out_specs, check_vma=False
    )
```

```python
import functools

import jax
import jax.numpy as jnp
from jax import lax
from jax.experimental import pallas as pl
from jax.experimental.pallas import tpu as pltpu
from jax.sharding import PartitionSpec as P

SLAB_DEPTH = 2.0
F32 = jnp.float32
BF16 = jnp.bfloat16
VMEM_LIMIT = 16 * 1024 * 1024

MID, LOW, SOURCES = 32, 64, 96
BASE = 256


def split(value):
    high = value.astype(BF16)
    low = (value - high.astype(F32)).astype(BF16)
    return high, low


def split3(value):
    high = value.astype(BF16)
    rest = value - high.astype(F32)
    mid = rest.astype(BF16)
    return high, mid, (rest - mid.astype(F32)).astype(BF16)


def encode(value):
    high, mid, low = split3(value)
    return high.astype(F32) + pltpu.roll(mid.astype(F32), MID, 1) + pltpu.roll(low.astype(F32), LOW, 1)


def decode(value):
    lanes = value.shape[1]
    whole = value + pltpu.roll(value, lanes - MID, 1) + pltpu.roll(value, lanes - LOW, 1)
    lane = lax.broadcasted_iota(jnp.int32, value.shape, 1)
    return jnp.where(lane < 4, whole, 0.0)


def dot(a, b):
    return lax.dot_general(a, b, (((1,), (0,)), ((), ())), preferred_element_type=F32)


def dot_t(a, b):
    return lax.dot_general(a, b, (((1,), (1,)), ((), ())), preferred_element_type=F32)


def fine_dot(value, weights, product):
    rows = value.shape[0]
    stacked = jnp.concatenate(split(value), axis=0)
    outs = []
    for weight in weights:
        out = product(stacked, weight)
        outs.append(out[:rows] + out[rows:])
    return outs


def silu_parts(value):
    gate = 1.0 / (1.0 + jnp.exp(-value))
    return gate, value * gate


class Sizes:
    def __init__(self, zero_shape, one_shape, two_shape, channels):
        self.c = channels
        self.zero = zero_shape[-1] // channels
        self.one = one_shape[-1] // channels
        self.two = two_shape[-1] // channels
        self.coefs = self.zero + 2 * (self.one + self.two)
        self.starts = (self.zero, self.zero + 2 * self.one)
        self.counts = (self.one, self.two)

    def cols(self, first, count=1):
        return slice(first * self.c, (first + count) * self.c)


def picked_group(refs, hot, first, count):
    blocks = []
    for k in range(first, first + count):
        blocks.append(jnp.concatenate([ref[k].astype(F32) for ref in refs], axis=0).astype(BF16))
    return dot(hot, jnp.concatenate(blocks, axis=1))


def pool(value, rows):
    total = value[:rows]
    for start in range(rows, value.shape[0], rows):
        total = total + value[start : start + rows]
    return total


def geo_at(geo_ref, which, edges):
    return geo_ref[which * edges : (which + 1) * edges, :]


def forward(refs, hot_ref, geo_ref, zero_ref, one_ref, two_ref, sz, rows, last):
    hot = hot_ref[...]
    edges = hot.shape[0]
    factor = (edges // rows) ** (-0.5)
    radial = geo_at(geo_ref, 0, edges)

    def scaled(block):
        return (block * radial).astype(BF16).astype(F32)

    pooled = [None] * sz.coefs
    group = picked_group(refs, hot, 0, sz.zero)
    zin = jnp.concatenate(
        [pool(scaled(group[:, sz.cols(k)]), rows) for k in range(sz.zero)], axis=1
    )
    kept = 1 if last else sz.zero
    (zout,) = fine_dot(zin, [zero_ref[:, sz.cols(0, kept)]], dot)
    for k in range(kept):
        pooled[k] = zout[:, sz.cols(k)] * factor
    for order in range(2):
        first, count = sz.starts[order], sz.counts[order]
        weight_ref = (one_ref, two_ref)[order]
        cos = geo_at(geo_ref, 1 + 2 * order, edges)
        sin = geo_at(geo_ref, 2 + 2 * order, edges)
        group = picked_group(refs, hot, first, 2 * count)
        res, ims = [], []
        for k in range(count):
            re = scaled(group[:, sz.cols(k)])
            im = scaled(group[:, sz.cols(count + k)])
            res.append(pool(cos * re - sin * im, rows))
            ims.append(pool(sin * re + cos * im, rows))
        both = jnp.concatenate(
            [jnp.concatenate(res, axis=1), jnp.concatenate(ims, axis=1)], axis=0
        )
        a, b = fine_dot(both, [weight_ref[0], weight_ref[1]], dot)
        out_re = (a[:rows] - b[rows:]) * factor
        out_im = (b[:rows] + a[rows:]) * factor
        for k in range(count):
            pooled[first + k] = out_re[:, sz.cols(k)]
            pooled[first + count + k] = out_im[:, sz.cols(k)]
    return pooled


def signal_of(pooled, sz):
    total = pooled[0]
    for k in range(sz.zero, sz.coefs):
        total = total + pooled[k] * pooled[k]
    return total


def backward(
    upstream, carried, pooled, refs, hot_ref, hot_t_ref, geo_ref, zero_ref, one_ref, two_ref, sz, rows, last, outs
):
    hot = hot_ref[...]
    hot_t = hot_t_ref[...]
    edges = hot.shape[0]
    slab = rows // 2
    factor = (edges // rows) ** (-0.5)
    signal = signal_of(pooled, sz)
    gate, _ = silu_parts(signal)
    slope = gate * (1.0 - gate)
    d_signal = upstream[0] * (gate + signal * slope)
    if not last:
        inner = upstream[1] * pooled[1]
        for k in range(2, sz.coefs):
            inner = inner + upstream[k] * pooled[k]
        d_signal = d_signal + inner * slope
    d_pooled = [d_signal * factor]
    for k in range(1, sz.coefs):
        if last:
            d_pooled.append(2.0 * factor * d_signal * pooled[k] if k >= sz.zero else None)
        else:
            term = gate * upstream[k]
            if k >= sz.zero:
                term = term + 2.0 * d_signal * pooled[k]
            d_pooled.append(term * factor)

    radial = geo_at(geo_ref, 0, edges)
    kept = 1 if last else sz.zero
    (dz,) = fine_dot(jnp.concatenate(d_pooled[:kept], axis=1), [zero_ref[:, sz.cols(0, kept)]], dot_t)

    def spread(block):
        return jnp.concatenate([block] * (edges // rows), axis=0)

    def scatter(first, blocks):
        if outs is None:
            return
        high, low = split(jnp.concatenate(blocks, axis=1))
        back = dot(hot_t, high) + dot(hot_t, low)
        for n in range(len(blocks)):
            k = first + n
            part = back[:, sz.cols(n)]
            middle = part[slab : slab + rows]
            if not last or k == 0:
                middle = middle + upstream[k]
            outs[0][k] = part[:slab].astype(BF16)
            outs[1][k] = middle.astype(BF16)
            outs[2][k] = part[slab + rows :].astype(BF16)

    q_len = jnp.zeros((edges, sz.c), F32)
    group = picked_group(refs, hot, 0, sz.zero)
    blocks = []
    for k in range(sz.zero):
        grad = spread(dz[:, sz.cols(k)])
        q_len = q_len + grad * group[:, sz.cols(k)]
        blocks.append(grad * radial)
    q_len = q_len * radial
    scatter(0, blocks)
    q_turn = []
    for order in range(2):
        first, count = sz.starts[order], sz.counts[order]
        weight_ref = (one_ref, two_ref)[order]
        cos = geo_at(geo_ref, 1 + 2 * order, edges)
        sin = geo_at(geo_ref, 2 + 2 * order, edges)
        both = jnp.concatenate(
            [
                jnp.concatenate(d_pooled[first : first + count], axis=1),
                jnp.concatenate(d_pooled[first + count : first + 2 * count], axis=1),
            ],
            axis=0,
        )
        a, b = fine_dot(both, [weight_ref[0], weight_ref[1]], dot_t)
        d_re = a[:rows] + b[rows:]
        d_im = a[rows:] - b[:rows]
        group = picked_group(refs, hot, first, 2 * count)
        q_cos = jnp.zeros((edges, sz.c), F32)
        q_sin = jnp.zeros((edges, sz.c), F32)
        cos_r = cos * radial
        sin_r = sin * radial
        blocks_re, blocks_im = [], []
        for k in range(count):
            re = group[:, sz.cols(k)]
            im = group[:, sz.cols(count + k)]
            g_re = spread(d_re[:, sz.cols(k)])
            g_im = spread(d_im[:, sz.cols(k)])
            q_cos = q_cos + (re * g_re + im * g_im)
            q_sin = q_sin + (re * g_im - im * g_re)
            if outs is not None:
                blocks_re.append(cos_r * g_re + sin_r * g_im)
                blocks_im.append(cos_r * g_im - sin_r * g_re)
        scatter(first, blocks_re + blocks_im)
        q_cos = q_cos * radial
        q_sin = q_sin * radial
        q_len = q_len + cos * q_cos + sin * q_sin
        q_turn.append((q_cos, q_sin))

    rate = geo_at(geo_ref, 9, edges)

    def total(value):
        return jnp.sum(value, axis=1, keepdims=True)

    d_len = -total(q_len * rate)
    (dc1, ds1), (dc2, ds2) = [(total(a), total(b)) for a, b in q_turn]
    c1, s1 = geo_at(geo_ref, 1, edges), geo_at(geo_ref, 2, edges)
    ux, uy, uz = (geo_at(geo_ref, 5 + n, edges) for n in range(3))
    inv_planar = geo_at(geo_ref, 8, edges)
    dc1 = dc1 + 2.0 * (c1 * dc2 + s1 * ds2)
    ds1 = ds1 + 2.0 * (c1 * ds2 - s1 * dc2)
    along = c1 * dc1 + s1 * ds1
    dx = (dc1 - along * c1) * inv_planar + d_len * ux
    dy = (ds1 - along * s1) * inv_planar + d_len * uy
    dz_ = d_len * uz
    lane = lax.broadcasted_iota(jnp.int32, (edges, sz.c), 1)
    change = jnp.where(lane == 0, dx, jnp.where(lane == 1, dy, jnp.where(lane == 2, dz_, 0.0)))
    moved = sum(dot(hot_t, part) for part in split3(change))
    own = moved[slab : slab + rows] - pool(change, rows) + carried
    return moved[:slab], own, moved[slab + rows :]


def send_back(moved, outs, sz):
    for ref, value in zip(outs, moved):
        ref[sz.coefs] = encode(value).astype(BF16)


def pack_kernel(
    node_hbm, places_hbm, species_hbm, sources_hbm, grad_hbm, table_hbm, mine_ref, other_ref,
    states, places, species, sources, grads, table, sems
):
    slab_now = lax.axis_index("space")
    batch = lax.rem(slab_now, 2)
    copies = []
    pairs = (
        (node_hbm, states), (places_hbm, places), (species_hbm, species), (sources_hbm, sources),
        (grad_hbm, grads), (table_hbm, table),
    )
    for n, (source, target) in enumerate(pairs):
        copies.append(pltpu.make_async_copy(source, target, sems.at[n]))
        copies[-1].start()
    for copy in copies:
        copy.wait()
    coefs, per_slab, c = states.shape[1:]
    lane = lax.broadcasted_iota(jnp.int32, (per_slab, c), 1)
    eye = (
        lax.broadcasted_iota(jnp.int32, (per_slab, per_slab), 0)
        == lax.broadcasted_iota(jnp.int32, (per_slab, per_slab), 1)
    )

    def column(row):
        return jnp.sum(jnp.where(eye, jnp.broadcast_to(row, (per_slab, per_slab)), 0.0), axis=1, keepdims=True)

    both = []
    for b in range(2):
        names = column(species[b : b + 1, :].astype(F32)).astype(jnp.int32)
        kinds = table.shape[0]
        hot = (names == lax.broadcasted_iota(jnp.int32, (per_slab, kinds), 1)).astype(BF16)
        first = (states[b, 0].astype(F32) + dot(hot, table[...])).astype(BF16)
        extra = jnp.zeros((per_slab, c), F32)
        for n in range(3):
            extra = jnp.where(lane == n, column(places[n, b : b + 1, :]), extra)
        extra = encode(jnp.where(lane == 3, column(grads[b : b + 1, :]), extra))
        for j in range(sources.shape[2]):
            index = sources[b, :, j : j + 1]
            extra = jnp.where(lane == SOURCES + j, (index // BASE).astype(F32), extra)
            extra = jnp.where(lane == SOURCES + 8 + j, (index % BASE).astype(F32), extra)
        both.append((first, extra.astype(BF16)))
    for ref, chosen in ((mine_ref, batch), (other_ref, 1 - batch)):
        ref[pl.ds(0, coefs)] = states[chosen]
        ref[0] = jnp.where(chosen == 0, both[0][0].astype(F32), both[1][0].astype(F32)).astype(BF16)
        ref[coefs] = jnp.where(chosen == 0, both[0][1].astype(F32), both[1][1].astype(F32)).astype(BF16)


def open_kernel(
    slabs, neighbours, mine_ref, partner_ref, straight_ref, cross_ref, rate_ref,
    left_ref, own_ref, right_ref, hot_ref, hot_t_ref, geo_ref, seed_ref
):
    slab_now = lax.axis_index("space")
    batch = lax.rem(slab_now, 2)
    even = batch == 0
    coefs = own_ref.shape[0]
    rows, c = own_ref.shape[1:]
    per_slab = rows // 2
    window = 2 * rows
    edges = rows * neighbours

    def choose(a, b):
        return jnp.where(even, a, b)

    def parts(k):
        mine, partner = mine_ref[k].astype(F32), partner_ref[k].astype(F32)
        straight, cross = straight_ref[k].astype(F32), cross_ref[k].astype(F32)
        own = jnp.concatenate([choose(mine, partner), choose(partner, mine)], axis=0)
        return choose(cross, straight), own, choose(straight, cross)

    @pl.when(lax.axis_index("segment") == 0)
    def _():
        for k in range(coefs):
            left, own, right = parts(k)
            left_ref[k] = left.astype(BF16)
            own_ref[k] = own.astype(BF16)
            right_ref[k] = right.astype(BF16)

    extra = jnp.concatenate(parts(coefs), axis=0)
    numbers = decode(extra)
    seed_ref[...] = jnp.broadcast_to(numbers[per_slab : per_slab + rows, 3:4], (rows, c))
    own_extra = extra[per_slab : per_slab + rows]
    low = pltpu.roll(own_extra, c - 8, 1)
    index = own_extra.astype(jnp.int32) * BASE + low.astype(jnp.int32)
    first_slab = slab_now - batch
    place = lax.rem(index // per_slab - first_slab + (1 + slabs), slabs) * per_slab + index % per_slab
    columns = lax.broadcasted_iota(jnp.int32, (rows, c), 1)
    hot = jnp.concatenate(
        [
            (place[:, SOURCES + j : SOURCES + j + 1] == columns).astype(F32)
            for j in range(neighbours)
        ],
        axis=0,
    )
    hot_ref[...] = hot.astype(BF16)[:, :window]
    hot_t_ref[...] = jnp.transpose(hot).astype(BF16)[:window]
    hot = hot.astype(BF16)[:, :window]
    level = lax.broadcasted_iota(jnp.int32, (window, c), 0) // per_slab - 1
    offset = []
    for n in range(3):
        column = jnp.broadcast_to(numbers[:, n : n + 1], (window, c))
        if n == 2:
            column = column + SLAB_DEPTH * level.astype(F32)
        there = sum(dot(hot, part) for part in split3(column))
        offset.append(there - jnp.concatenate([column[per_slab : per_slab + rows]] * neighbours, axis=0))
    flat = offset[0] * offset[0] + offset[1] * offset[1] + 1.0
    length = jnp.sqrt(flat + offset[2] * offset[2])
    planar = jnp.sqrt(flat)
    c1, s1 = offset[0] / planar, offset[1] / planar
    rate = jnp.broadcast_to(rate_ref[...], (edges, c))
    values = [
        jnp.exp(-rate * length),
        c1,
        s1,
        c1 * c1 - s1 * s1,
        2.0 * c1 * s1,
        offset[0] / length,
        offset[1] / length,
        offset[2] / length,
        1.0 / planar,
        rate,
    ]
    for n, value in enumerate(values):
        geo_ref[n * edges : (n + 1) * edges, :] = value


def stage_kernel(zero_hbm, one_hbm, two_hbm, zero_ref, one_ref, two_ref, sems):
    copies = [
        pltpu.make_async_copy(source, target, sems.at[n])
        for n, (source, target) in enumerate(((zero_hbm, zero_ref), (one_hbm, one_ref), (two_hbm, two_ref)))
    ]
    for copy in copies:
        copy.start()
    for copy in copies:
        copy.wait()


def forward_kernel(
    tick, sz, left_ref, own_ref, right_ref, hot_ref, geo_ref, zero_ref, one_ref, two_ref,
    out_ref, low_ref, high_ref, pooled_ref
):
    @pl.when(lax.axis_index("segment") == tick)
    def _():
        rows = own_ref.shape[1]
        slab = rows // 2
        refs = (left_ref, own_ref, right_ref)
        pooled = forward(refs, hot_ref, geo_ref, zero_ref, one_ref, two_ref, sz, rows, False)
        signal = signal_of(pooled, sz)
        gate, lifted = silu_parts(signal)
        for k in range(sz.coefs):
            pooled_ref[k] = pooled[k]
            added = lifted if k == 0 else gate * pooled[k]
            updated = own_ref[k].astype(F32) + added
            out_ref[k] = updated.astype(BF16)
            low_ref[k] = updated[:slab].astype(BF16)
            high_ref[k] = updated[slab:].astype(BF16)


def turn_kernel(
    tick, sz, left_ref, own_ref, right_ref, hot_ref, hot_t_ref, geo_ref, zero_ref, one_ref, two_ref,
    read_ref, seed_ref, *outs
):
    @pl.when(lax.axis_index("segment") == tick)
    def _():
        rows = own_ref.shape[1]
        refs = (left_ref, own_ref, right_ref)
        pooled = forward(refs, hot_ref, geo_ref, zero_ref, one_ref, two_ref, sz, rows, True)
        signal = signal_of(pooled, sz)
        _, lifted = silu_parts(signal)
        updated = own_ref[0].astype(F32) + lifted
        gate, active = silu_parts(updated)
        read = read_ref[...]
        energy = jnp.sum(read * active, axis=1, keepdims=True)
        lane = lax.broadcasted_iota(jnp.int32, (rows, sz.c), 1)
        carried = jnp.where(lane == 3, energy, 0.0)
        upstream = [seed_ref[...] * read * (gate + updated * gate * (1.0 - gate))]
        moved = backward(
            upstream, carried, pooled, refs, hot_ref, hot_t_ref, geo_ref, zero_ref, one_ref, two_ref, sz, rows, True, outs
        )
        send_back(moved, outs, sz)


def backward_kernel(
    tick, sz, up_own_ref, up_low_ref, up_high_ref, pooled_ref, left_ref, own_ref, right_ref, hot_ref, hot_t_ref, geo_ref,
    zero_ref, one_ref, two_ref, *outs
):
    @pl.when(lax.axis_index("segment") == tick)
    def _():
        rows = own_ref.shape[1]
        refs = (left_ref, own_ref, right_ref)

        def arrived(k):
            halves = jnp.concatenate([up_low_ref[k].astype(F32), up_high_ref[k].astype(F32)], axis=0)
            return up_own_ref[k].astype(F32) + halves

        upstream = [arrived(k) for k in range(sz.coefs)]
        halves = jnp.concatenate(
            [decode(up_low_ref[sz.coefs].astype(F32)), decode(up_high_ref[sz.coefs].astype(F32))], axis=0
        )
        carried = decode(up_own_ref[sz.coefs].astype(F32)) + halves
        pooled = [pooled_ref[k] for k in range(sz.coefs)]
        moved = backward(
            upstream, carried, pooled, refs, hot_ref, hot_t_ref, geo_ref, zero_ref, one_ref, two_ref, sz, rows, False,
            outs if tick else None,
        )
        if tick:
            send_back(moved, outs, sz)
        else:
            share(moved, outs)


def share(moved, outs):
    left, own, right = moved
    slab = left.shape[0]
    even = lax.rem(lax.axis_index("space"), 2) == 0
    low, high = own[:slab], own[slab:]
    outs[0][...] = jnp.where(even, low, high)
    outs[1][...] = jnp.where(even, high, low)
    outs[2][...] = jnp.where(even, right, left)
    outs[3][...] = jnp.where(even, left, right)


def call(body, operands, shapes, name, spaces=None, scratch=()):
    spaces = spaces or [pltpu.VMEM] * len(operands)
    return pl.pallas_call(
        body,
        out_shape=shapes,
        in_specs=[pl.BlockSpec(memory_space=space) for space in spaces],
        out_specs=[pl.BlockSpec(memory_space=pltpu.VMEM) for _ in shapes],
        scratch_shapes=list(scratch),
        compiler_params=pltpu.CompilerParams(vmem_limit_bytes=VMEM_LIMIT),
        name=name,
    )(*operands)


def on_device(
    node_states,
    species,
    species_table,
    places,
    sources,
    radial_rate,
    zero_weight,
    one_weight,
    two_weight,
    read_weight,
    energy_grad,
):
    segments = lax.axis_size("segment")
    slabs = lax.axis_size("space")
    segment_now = lax.axis_index("segment")
    even = lax.rem(lax.axis_index("space"), 2) == 0
    batches, per_slab = species.shape
    coefs, channels = node_states.shape[2:]
    neighbours = sources.shape[2]
    rows = batches * per_slab
    edges = rows * neighbours
    sz = Sizes(zero_weight.shape, one_weight.shape, two_weight.shape, channels)
    axes = ("segment", "space")
    shape = jax.ShapeDtypeStruct

    def to_partner(i):
        return i + 1 - 2 * (i % 2)

    def outward(i):
        return (i + (2 if i % 2 else -2)) % slabs

    def inward(i):
        return (i + (-2 if i % 2 else 2)) % slabs

    def across(i):
        return (i + (1 if i % 2 else -1)) % slabs

    def within(value, target, only=None):
        chosen = range(segments) if only is None else [only]
        return lax.ppermute(value, axes, [(s * slabs + i, s * slabs + target(i)) for s in chosen for i in range(slabs)])

    def hop(value, start, stop, by):
        pairs = [(start * slabs + i, stop * slabs + (i + by) % slabs) for i in range(slabs)]
        return lax.ppermute(value, axes, pairs)

    raw = [
        node_states.transpose(0, 2, 1, 3), places.transpose(1, 0, 2), species, sources, energy_grad, species_table,
    ]
    packed = shape((coefs + 1, per_slab, channels), BF16)
    mine, other = call(
        pack_kernel, raw, [packed, packed], "pack", [pltpu.HBM] * len(raw),
        [pltpu.VMEM(v.shape, v.dtype) for v in raw] + [pltpu.SemaphoreType.DMA((len(raw),))],
    )
    partner = within(other, to_partner)
    straight = within(mine, outward)
    cross = within(other, across)
    weights = [zero_weight[0], one_weight[0], two_weight[0]]
    weights = call(
        stage_kernel, weights, [pltpu.VMEM(w.shape, w.dtype) for w in weights], "stage", [pltpu.HBM] * 3,
        [pltpu.SemaphoreType.DMA((3,))],
    )
    whole = shape((coefs, rows, channels), BF16)
    half = shape((coefs, per_slab, channels), BF16)
    left, own, right, hot, hot_t, geo, seeds = call(
        functools.partial(open_kernel, slabs, neighbours),
        [mine, partner, straight, cross, radial_rate],
        [
            half, whole, half, shape((edges, 2 * rows), BF16), shape((2 * rows, edges), BF16),
            shape((10 * edges, channels), F32), shape((rows, channels), F32),
        ],
        "open",
    )
    around = [(left, own, right)]
    kept = []
    for tick in range(segments - 1):
        out, low, high, pooled = call(
            functools.partial(forward_kernel, tick, sz),
            [*around[tick], hot, geo, *weights],
            [whole, half, half, shape((coefs, rows, channels), F32)],
            "forward",
        )
        kept.append(pooled)
        own = hop(out, tick, tick + 1, 0)
        right = hop(low, tick, tick + 1, -2)
        left = hop(high, tick, tick + 1, 2)
        around.append((left, own, right))
    final = segments - 1
    whole_more = shape((coefs + 1, rows, channels), BF16)
    last_shape = [shape((per_slab, channels), F32)] * 4
    parts = call(
        functools.partial(turn_kernel, final, sz),
        [*around[final], hot, hot_t, geo, *weights, read_weight.reshape(1, channels), seeds],
        [packed, whole_more, packed],
        "turn",
    )
    for tick in reversed(range(segments - 1)):
        left, own, right = parts
        up_own = hop(own, tick + 1, tick, 0)
        up_low = hop(right, tick + 1, tick, 2)
        up_high = hop(left, tick + 1, tick, -2)
        parts = call(
            functools.partial(backward_kernel, tick, sz),
            [up_own, up_low, up_high, kept[tick], *around[tick], hot, hot_t, geo, *weights],
            [packed, whole_more, packed] if tick else last_shape,
            "backward",
        )
    here, theirs, straight, cross = (value[:, :4] for value in parts)
    here = here + within(straight, inward, 0)
    there = within(theirs, to_partner, 0) + within(cross, across, 0)
    both = jnp.where(even, jnp.stack([here, there]), jnp.stack([there, here]))
    total = jnp.where(segment_now == 0, both, 0.0)
    for stop in range(1, segments):
        total = total + hop(both, 0, stop, 0)
    return total[..., 3], total[..., :3].transpose(0, 2, 1)


def solution(mesh):
    in_specs = (
        P(None, "space", None, None),
        P(None, "space"),
        P(),
        P(None, None, "space"),
        P(None, "space", None),
        P("segment", None),
        P("segment", None, None),
        P("segment", None, None, None),
        P("segment", None, None, None),
        P(),
        P(None, "space"),
    )
    out_specs = (P(None, "space"), P(None, None, "space"))
    return jax.shard_map(
        on_device, mesh=mesh, in_specs=in_specs, out_specs=out_specs, check_vma=False
    )
```

```python
import functools

import jax
import jax.numpy as jnp
from jax import lax
from jax.experimental import pallas as pl
from jax.experimental.pallas import tpu as pltpu
from jax.sharding import PartitionSpec as P

SLAB_DEPTH = 2.0
F32 = jnp.float32
BF16 = jnp.bfloat16
VMEM_LIMIT = 16 * 1024 * 1024

MID, LOW, SOURCES = 32, 64, 96
BASE = 256


def split(value):
    high = value.astype(BF16)
    low = (value - high.astype(F32)).astype(BF16)
    return high, low


def split3(value):
    high = value.astype(BF16)
    rest = value - high.astype(F32)
    mid = rest.astype(BF16)
    return high, mid, (rest - mid.astype(F32)).astype(BF16)


def encode(value):
    high, mid, low = split3(value)
    return high.astype(F32) + pltpu.roll(mid.astype(F32), MID, 1) + pltpu.roll(low.astype(F32), LOW, 1)


def decode(value):
    lanes = value.shape[1]
    whole = value + pltpu.roll(value, lanes - MID, 1) + pltpu.roll(value, lanes - LOW, 1)
    lane = lax.broadcasted_iota(jnp.int32, value.shape, 1)
    return jnp.where(lane < 4, whole, 0.0)


def dot(a, b):
    return lax.dot_general(a, b, (((1,), (0,)), ((), ())), preferred_element_type=F32)


def dot_t(a, b):
    return lax.dot_general(a, b, (((1,), (1,)), ((), ())), preferred_element_type=F32)


def fine_dot(value, weights, product):
    rows = value.shape[0]
    stacked = jnp.concatenate(split(value), axis=0)
    outs = []
    for weight in weights:
        out = product(stacked, weight)
        outs.append(out[:rows] + out[rows:])
    return outs


def silu_parts(value):
    gate = 1.0 / (1.0 + jnp.exp(-value))
    return gate, value * gate


class Sizes:
    def __init__(self, zero_shape, one_shape, two_shape, channels):
        self.c = channels
        self.zero = zero_shape[-1] // channels
        self.one = one_shape[-1] // channels
        self.two = two_shape[-1] // channels
        self.coefs = self.zero + 2 * (self.one + self.two)
        self.starts = (self.zero, self.zero + 2 * self.one)
        self.counts = (self.one, self.two)

    def cols(self, first, count=1):
        return slice(first * self.c, (first + count) * self.c)


def picked_group(refs, hot, first, count):
    blocks = [jnp.concatenate([ref[k] for ref in refs], axis=0) for k in range(first, first + count)]
    return dot(hot, jnp.concatenate(blocks, axis=1))


def own_rows(refs, k):
    low, high = (ref[k].astype(F32) for ref in refs)
    slab = low.shape[0] // 2
    return jnp.concatenate([low[slab:], high[:slab]], axis=0)


def pool(value, rows):
    total = value[:rows]
    for start in range(rows, value.shape[0], rows):
        total = total + value[start : start + rows]
    return total


def geo_at(geo_ref, which, edges):
    return geo_ref[which * edges : (which + 1) * edges, :]


def forward(refs, hot_ref, geo_ref, zero_ref, one_ref, two_ref, sz, rows, last):
    hot = hot_ref[...]
    edges = hot.shape[0]
    factor = (edges // rows) ** (-0.5)
    radial = geo_at(geo_ref, 0, edges)

    def scaled(block):
        return (block * radial).astype(BF16).astype(F32)

    pooled = [None] * sz.coefs
    group = picked_group(refs, hot, 0, sz.zero)
    zin = jnp.concatenate(
        [pool(scaled(group[:, sz.cols(k)]), rows) for k in range(sz.zero)], axis=1
    )
    kept = 1 if last else sz.zero
    (zout,) = fine_dot(zin, [zero_ref[:, sz.cols(0, kept)]], dot)
    for k in range(kept):
        pooled[k] = zout[:, sz.cols(k)] * factor
    for order in range(2):
        first, count = sz.starts[order], sz.counts[order]
        weight_ref = (one_ref, two_ref)[order]
        cos = geo_at(geo_ref, 1 + 2 * order, edges)
        sin = geo_at(geo_ref, 2 + 2 * order, edges)
        group = picked_group(refs, hot, first, 2 * count)
        res, ims = [], []
        for k in range(count):
            re = scaled(group[:, sz.cols(k)])
            im = scaled(group[:, sz.cols(count + k)])
            res.append(pool(cos * re - sin * im, rows))
            ims.append(pool(sin * re + cos * im, rows))
        both = jnp.concatenate(
            [jnp.concatenate(res, axis=1), jnp.concatenate(ims, axis=1)], axis=0
        )
        a, b = fine_dot(both, [weight_ref[0], weight_ref[1]], dot)
        out_re = (a[:rows] - b[rows:]) * factor
        out_im = (b[:rows] + a[rows:]) * factor
        for k in range(count):
            pooled[first + k] = out_re[:, sz.cols(k)]
            pooled[first + count + k] = out_im[:, sz.cols(k)]
    return pooled


def signal_of(pooled, sz):
    total = pooled[0]
    for k in range(sz.zero, sz.coefs):
        total = total + pooled[k] * pooled[k]
    return total


def backward(
    upstream, pooled, refs, hot_ref, hot_t_ref, geo_ref, zero_ref, one_ref, two_ref, sz, rows, last, outs
):
    hot = hot_ref[...]
    hot_t = hot_t_ref[...]
    edges = hot.shape[0]
    slab = rows // 2
    factor = (edges // rows) ** (-0.5)
    signal = signal_of(pooled, sz)
    gate, _ = silu_parts(signal)
    slope = gate * (1.0 - gate)
    d_signal = upstream[0] * (gate + signal * slope)
    if not last:
        inner = upstream[1] * pooled[1]
        for k in range(2, sz.coefs):
            inner = inner + upstream[k] * pooled[k]
        d_signal = d_signal + inner * slope
    d_pooled = [d_signal * factor]
    for k in range(1, sz.coefs):
        if last:
            d_pooled.append(2.0 * factor * d_signal * pooled[k] if k >= sz.zero else None)
        else:
            term = gate * upstream[k]
            if k >= sz.zero:
                term = term + 2.0 * d_signal * pooled[k]
            d_pooled.append(term * factor)

    radial = geo_at(geo_ref, 0, edges)
    kept = 1 if last else sz.zero
    (dz,) = fine_dot(jnp.concatenate(d_pooled[:kept], axis=1), [zero_ref[:, sz.cols(0, kept)]], dot_t)

    def spread(block):
        return jnp.concatenate([block] * (edges // rows), axis=0)

    def scatter(first, blocks):
        if outs is None:
            return
        high, low = split(jnp.concatenate(blocks, axis=1))
        back = dot(hot_t, high) + dot(hot_t, low)
        for n in range(len(blocks)):
            k = first + n
            part = back[:, sz.cols(n)]
            if not last or k == 0:
                part = part + around(upstream[k], slab)
            outs[0][k] = part[:rows].astype(BF16)
            outs[1][k] = part[rows:].astype(BF16)

    q_len = jnp.zeros((edges, sz.c), F32)
    group = picked_group(refs, hot, 0, sz.zero)
    blocks = []
    for k in range(sz.zero):
        grad = spread(dz[:, sz.cols(k)])
        q_len = q_len + grad * group[:, sz.cols(k)]
        blocks.append(grad * radial)
    q_len = q_len * radial
    scatter(0, blocks)
    q_turn = []
    for order in range(2):
        first, count = sz.starts[order], sz.counts[order]
        weight_ref = (one_ref, two_ref)[order]
        cos = geo_at(geo_ref, 1 + 2 * order, edges)
        sin = geo_at(geo_ref, 2 + 2 * order, edges)
        both = jnp.concatenate(
            [
                jnp.concatenate(d_pooled[first : first + count], axis=1),
                jnp.concatenate(d_pooled[first + count : first + 2 * count], axis=1),
            ],
            axis=0,
        )
        a, b = fine_dot(both, [weight_ref[0], weight_ref[1]], dot_t)
        d_re = a[:rows] + b[rows:]
        d_im = a[rows:] - b[:rows]
        group = picked_group(refs, hot, first, 2 * count)
        q_cos = jnp.zeros((edges, sz.c), F32)
        q_sin = jnp.zeros((edges, sz.c), F32)
        cos_r = cos * radial
        sin_r = sin * radial
        blocks_re, blocks_im = [], []
        for k in range(count):
            re = group[:, sz.cols(k)]
            im = group[:, sz.cols(count + k)]
            g_re = spread(d_re[:, sz.cols(k)])
            g_im = spread(d_im[:, sz.cols(k)])
            q_cos = q_cos + (re * g_re + im * g_im)
            q_sin = q_sin + (re * g_im - im * g_re)
            if outs is not None:
                blocks_re.append(cos_r * g_re + sin_r * g_im)
                blocks_im.append(cos_r * g_im - sin_r * g_re)
        scatter(first, blocks_re + blocks_im)
        q_cos = q_cos * radial
        q_sin = q_sin * radial
        q_len = q_len + cos * q_cos + sin * q_sin
        q_turn.append((q_cos, q_sin))

    rate = geo_at(geo_ref, 9, edges)

    def total(value):
        return jnp.sum(value, axis=1, keepdims=True)

    d_len = -total(q_len * rate)
    (dc1, ds1), (dc2, ds2) = [(total(a), total(b)) for a, b in q_turn]
    c1, s1 = geo_at(geo_ref, 1, edges), geo_at(geo_ref, 2, edges)
    ux, uy, uz = (geo_at(geo_ref, 5 + n, edges) for n in range(3))
    inv_planar = geo_at(geo_ref, 8, edges)
    dc1 = dc1 + 2.0 * (c1 * dc2 + s1 * ds2)
    ds1 = ds1 + 2.0 * (c1 * ds2 - s1 * dc2)
    along = c1 * dc1 + s1 * ds1
    dx = (dc1 - along * c1) * inv_planar + d_len * ux
    dy = (ds1 - along * s1) * inv_planar + d_len * uy
    dz_ = d_len * uz
    lane = lax.broadcasted_iota(jnp.int32, (edges, sz.c), 1)
    change = jnp.where(lane == 0, dx, jnp.where(lane == 1, dy, jnp.where(lane == 2, dz_, 0.0)))
    moved = sum(dot(hot_t, part) for part in split3(change))
    return moved - around(pool(change, rows), slab)


def around(own, slab):
    edge = jnp.zeros((slab, own.shape[1]), F32)
    return jnp.concatenate([edge, own, edge], axis=0)


def first_slab(slabs):
    slab_now = lax.axis_index("space")
    batch = lax.rem(slab_now, 2)
    shift = lax.rem(lax.axis_index("segment"), 2)
    return lax.rem(slab_now - batch + shift - 1 + slabs, slabs), batch


def publish(values, slabs, out_ref):
    window, c = values.shape
    count = out_ref.shape[1]
    start, batch = first_slab(slabs)
    row = lax.broadcasted_iota(jnp.int32, (window, count), 0)
    column = lax.broadcasted_iota(jnp.int32, (window, count), 1)
    target = lax.rem(start * (window // 4) + row, count // 2) + batch * (count // 2)
    hot = (column == target).astype(BF16)
    turned = jnp.transpose(jnp.concatenate([values, jnp.zeros((c - window, c), F32)], axis=0))
    turned = turned[: out_ref.shape[0], :window]
    out_ref[...] = sum(dot(part, hot) for part in split3(turned))


def pack_kernel(
    node_hbm, places_hbm, species_hbm, sources_hbm, grad_hbm, table_hbm, mine_ref, other_ref,
    states, places, species, sources, grads, table, sems
):
    slab_now = lax.axis_index("space")
    batch = lax.rem(slab_now, 2)
    copies = []
    pairs = (
        (node_hbm, states), (places_hbm, places), (species_hbm, species), (sources_hbm, sources),
        (grad_hbm, grads), (table_hbm, table),
    )
    for n, (source, target) in enumerate(pairs):
        copies.append(pltpu.make_async_copy(source, target, sems.at[n]))
        copies[-1].start()
    for copy in copies:
        copy.wait()
    coefs, per_slab, c = states.shape[1:]
    lane = lax.broadcasted_iota(jnp.int32, (per_slab, c), 1)
    eye = (
        lax.broadcasted_iota(jnp.int32, (per_slab, per_slab), 0)
        == lax.broadcasted_iota(jnp.int32, (per_slab, per_slab), 1)
    )

    def column(row):
        return jnp.sum(jnp.where(eye, jnp.broadcast_to(row, (per_slab, per_slab)), 0.0), axis=1, keepdims=True)

    both = []
    for b in range(2):
        names = column(species[b : b + 1, :].astype(F32)).astype(jnp.int32)
        kinds = table.shape[0]
        hot = (names == lax.broadcasted_iota(jnp.int32, (per_slab, kinds), 1)).astype(BF16)
        first = (states[b, 0].astype(F32) + dot(hot, table[...])).astype(BF16)
        extra = jnp.zeros((per_slab, c), F32)
        for n in range(3):
            extra = jnp.where(lane == n, column(places[n, b : b + 1, :]), extra)
        extra = encode(jnp.where(lane == 3, column(grads[b : b + 1, :]), extra))
        for j in range(sources.shape[2]):
            index = sources[b, :, j : j + 1]
            extra = jnp.where(lane == SOURCES + j, (index // BASE).astype(F32), extra)
            extra = jnp.where(lane == SOURCES + 8 + j, (index % BASE).astype(F32), extra)
        both.append((first, extra.astype(BF16)))
    for ref, chosen in ((mine_ref, batch), (other_ref, 1 - batch)):
        ref[pl.ds(0, coefs)] = states[chosen]
        ref[0] = jnp.where(chosen == 0, both[0][0].astype(F32), both[1][0].astype(F32)).astype(BF16)
        ref[coefs] = jnp.where(chosen == 0, both[0][1].astype(F32), both[1][1].astype(F32)).astype(BF16)


def open_kernel(
    slabs, neighbours, mine_ref, partner_ref, straight_ref, cross_ref, rate_ref,
    low_ref, high_ref, hot_ref, hot_t_ref, geo_ref, seed_ref
):
    start, batch = first_slab(slabs)
    even = batch == 0
    level = lax.rem(lax.axis_index("segment"), 2) == 0
    coefs = low_ref.shape[0]
    rows, c = low_ref.shape[1:]
    per_slab = rows // 2
    window = 2 * rows
    edges = rows * neighbours

    def choose(a, b):
        return jnp.where(even, a, b)

    def parts(k):
        mine, partner = mine_ref[k].astype(F32), partner_ref[k].astype(F32)
        straight, cross = straight_ref[k].astype(F32), cross_ref[k].astype(F32)
        low, high = choose(mine, partner), choose(partner, mine)
        after, last = choose(straight, cross), choose(cross, straight)
        return [
            jnp.where(level, last, low), jnp.where(level, low, high), jnp.where(level, high, after),
            jnp.where(level, after, last),
        ]

    @pl.when(lax.axis_index("segment") == 0)
    def _():
        for k in range(coefs):
            slab = parts(k)
            low_ref[k] = jnp.concatenate(slab[:2], axis=0).astype(BF16)
            high_ref[k] = jnp.concatenate(slab[2:], axis=0).astype(BF16)

    extra = jnp.concatenate(parts(coefs), axis=0)
    numbers = decode(extra)
    seed_ref[...] = jnp.broadcast_to(numbers[per_slab : per_slab + rows, 3:4], (rows, c))
    own_extra = extra[per_slab : per_slab + rows]
    low = pltpu.roll(own_extra, c - 8, 1)
    index = own_extra.astype(jnp.int32) * BASE + low.astype(jnp.int32)
    place = lax.rem(index // per_slab - start + slabs, slabs) * per_slab + index % per_slab
    columns = lax.broadcasted_iota(jnp.int32, (rows, c), 1)
    hot = jnp.concatenate(
        [
            (place[:, SOURCES + j : SOURCES + j + 1] == columns).astype(F32)
            for j in range(neighbours)
        ],
        axis=0,
    )
    hot_ref[...] = hot.astype(BF16)[:, :window]
    hot_t_ref[...] = jnp.transpose(hot).astype(BF16)[:window]
    hot = hot.astype(BF16)[:, :window]
    lift = lax.broadcasted_iota(jnp.int32, (window, c), 0) // per_slab - 1
    offset = []
    for n in range(3):
        column = jnp.broadcast_to(numbers[:, n : n + 1], (window, c))
        if n == 2:
            column = column + SLAB_DEPTH * lift.astype(F32)
        there = sum(dot(hot, part) for part in split3(column))
        offset.append(there - jnp.concatenate([column[per_slab : per_slab + rows]] * neighbours, axis=0))
    flat = offset[0] * offset[0] + offset[1] * offset[1] + 1.0
    length = jnp.sqrt(flat + offset[2] * offset[2])
    planar = jnp.sqrt(flat)
    c1, s1 = offset[0] / planar, offset[1] / planar
    rate = jnp.broadcast_to(rate_ref[...], (edges, c))
    values = [
        jnp.exp(-rate * length),
        c1,
        s1,
        c1 * c1 - s1 * s1,
        2.0 * c1 * s1,
        offset[0] / length,
        offset[1] / length,
        offset[2] / length,
        1.0 / planar,
        rate,
    ]
    for n, value in enumerate(values):
        geo_ref[n * edges : (n + 1) * edges, :] = value


def stage_kernel(zero_hbm, one_hbm, two_hbm, zero_ref, one_ref, two_ref, sems):
    copies = [
        pltpu.make_async_copy(source, target, sems.at[n])
        for n, (source, target) in enumerate(((zero_hbm, zero_ref), (one_hbm, one_ref), (two_hbm, two_ref)))
    ]
    for copy in copies:
        copy.start()
    for copy in copies:
        copy.wait()


def forward_kernel(
    tick, sz, low_ref, high_ref, hot_ref, geo_ref, zero_ref, one_ref, two_ref, out_ref, pooled_ref
):
    @pl.when(lax.axis_index("segment") == tick)
    def _():
        rows = low_ref.shape[1]
        refs = (low_ref, high_ref)
        pooled = forward(refs, hot_ref, geo_ref, zero_ref, one_ref, two_ref, sz, rows, False)
        signal = signal_of(pooled, sz)
        gate, lifted = silu_parts(signal)
        for k in range(sz.coefs):
            pooled_ref[k] = pooled[k]
            added = lifted if k == 0 else gate * pooled[k]
            out_ref[k] = (own_rows(refs, k) + added).astype(BF16)


def turn_kernel(
    tick, sz, slabs, low_ref, high_ref, hot_ref, hot_t_ref, geo_ref, zero_ref, one_ref, two_ref,
    read_ref, seed_ref, sums_ref, *outs
):
    @pl.when(lax.axis_index("segment") == tick)
    def _():
        rows = low_ref.shape[1]
        refs = (low_ref, high_ref)
        pooled = forward(refs, hot_ref, geo_ref, zero_ref, one_ref, two_ref, sz, rows, True)
        signal = signal_of(pooled, sz)
        _, lifted = silu_parts(signal)
        updated = own_rows(refs, 0) + lifted
        gate, active = silu_parts(updated)
        read = read_ref[...]
        energy = jnp.sum(read * active, axis=1, keepdims=True)
        lane = lax.broadcasted_iota(jnp.int32, (rows, sz.c), 1)
        energy = around(jnp.where(lane == 3, energy, 0.0), rows // 2)
        upstream = [seed_ref[...] * read * (gate + updated * gate * (1.0 - gate))]
        moved = backward(
            upstream, pooled, refs, hot_ref, hot_t_ref, geo_ref, zero_ref, one_ref, two_ref, sz, rows, True, outs
        )
        publish(moved + energy, slabs, sums_ref)


def backward_kernel(
    tick, sz, slabs, up_low_ref, up_high_ref, pooled_ref, low_ref, high_ref, hot_ref, hot_t_ref, geo_ref,
    zero_ref, one_ref, two_ref, *more
):
    earlier = () if tick else more[: lax.axis_size("segment") - 1]
    sums_ref, *outs = more[len(earlier) :]

    @pl.when(lax.axis_index("segment") == tick)
    def _():
        rows = low_ref.shape[1]
        refs = (low_ref, high_ref)
        upstream = [up_low_ref[k].astype(F32) + up_high_ref[k].astype(F32) for k in range(sz.coefs)]
        pooled = [pooled_ref[k] for k in range(sz.coefs)]
        moved = backward(
            upstream, pooled, refs, hot_ref, hot_t_ref, geo_ref, zero_ref, one_ref, two_ref, sz, rows, False,
            outs if tick else None,
        )
        publish(moved, slabs, sums_ref)

    for n, ref in enumerate(earlier):

        @pl.when(lax.axis_index("segment") == n + 1)
        def _(ref=ref):
            sums_ref[...] = ref[...]


def call(body, operands, shapes, name, spaces=None, scratch=()):
    spaces = spaces or [pltpu.VMEM] * len(operands)
    operands = [pltpu.with_memory_space_constraint(value, space) for value, space in zip(operands, spaces)]
    return pl.pallas_call(
        body,
        out_shape=shapes,
        in_specs=[pl.BlockSpec(memory_space=space) for space in spaces],
        out_specs=[pl.BlockSpec(memory_space=pltpu.VMEM) for _ in shapes],
        scratch_shapes=list(scratch),
        compiler_params=pltpu.CompilerParams(vmem_limit_bytes=VMEM_LIMIT),
        name=name,
    )(*operands)


def on_device(
    node_states,
    species,
    species_table,
    places,
    sources,
    radial_rate,
    zero_weight,
    one_weight,
    two_weight,
    read_weight,
    energy_grad,
):
    segments = lax.axis_size("segment")
    slabs = lax.axis_size("space")
    batches, per_slab = species.shape
    coefs, channels = node_states.shape[2:]
    neighbours = sources.shape[2]
    rows = batches * per_slab
    edges = rows * neighbours
    sz = Sizes(zero_weight.shape, one_weight.shape, two_weight.shape, channels)
    axes = ("segment", "space")
    shape = jax.ShapeDtypeStruct

    def within(value, target):
        pairs = [(s * slabs + i, s * slabs + target(s % 2, i) % slabs) for s in range(segments) for i in range(slabs)]
        return lax.ppermute(value, axes, pairs)

    def hop(value, start, stop, by):
        pairs = [(start * slabs + i, stop * slabs + (i + by) % slabs) for i in range(slabs)]
        return lax.ppermute(value, axes, pairs)

    raw = [
        node_states.transpose(0, 2, 1, 3), places.transpose(1, 0, 2), species, sources, energy_grad, species_table,
    ]
    packed = shape((coefs + 1, per_slab, channels), BF16)
    mine, other = call(
        pack_kernel, raw, [packed, packed], "pack", [pltpu.HBM] * len(raw),
        [pltpu.VMEM(v.shape, v.dtype) for v in raw] + [pltpu.SemaphoreType.DMA((len(raw),))],
    )
    partner = within(other, lambda odd, i: i + 1 - 2 * (i % 2))
    straight = within(mine, lambda odd, i: i - 2 if odd or i % 2 == 0 else i + 2)
    cross = within(other, lambda odd, i: i - 1 if i % 2 == 0 else i - 3 if odd else i + 1)
    weights = [zero_weight[0], one_weight[0], two_weight[0]]
    weights = call(
        stage_kernel, weights, [pltpu.VMEM(w.shape, w.dtype) for w in weights], "stage", [pltpu.HBM] * 3,
        [pltpu.SemaphoreType.DMA((3,))],
    )
    whole = shape((coefs, rows, channels), BF16)
    low, high, hot, hot_t, geo, seeds = call(
        functools.partial(open_kernel, slabs, neighbours),
        [mine, partner, straight, cross, radial_rate],
        [
            whole, whole, shape((edges, 2 * rows), BF16), shape((2 * rows, edges), BF16),
            shape((10 * edges, channels), F32), shape((rows, channels), F32),
        ],
        "open",
    )
    around_all = [(low, high)]
    kept = []
    for tick in range(segments - 1):
        out, pooled = call(
            functools.partial(forward_kernel, tick, sz),
            [*around_all[tick], hot, geo, *weights],
            [whole, shape((coefs, rows, channels), F32)],
            "forward",
        )
        kept.append(pooled)
        ways = (2, 0) if tick % 2 else (0, -2)
        around_all.append(tuple(hop(out, tick, tick + 1, by) for by in ways))
    final = segments - 1
    sums = shape((8, batches * slabs * per_slab), F32)
    sums_last, *parts = call(
        functools.partial(turn_kernel, final, sz, slabs),
        [*around_all[final], hot, hot_t, geo, *weights, read_weight.reshape(1, channels), seeds],
        [sums, whole, whole],
        "turn",
    )
    every = [sums_last]
    for tick in reversed(range(segments - 1)):
        ways = (2, 0) if tick % 2 else (0, -2)
        up = [hop(part, tick + 1, tick, -by) for part, by in zip(parts, ways)]
        sums_now, *parts = call(
            functools.partial(backward_kernel, tick, sz, slabs),
            [*up, kept[tick], *around_all[tick], hot, hot_t, geo, *weights] + ([] if tick else every),
            [sums, whole, whole] if tick else [sums],
            "backward",
        )
        every.insert(0, sums_now)
    total = lax.psum(every[0][:4], axes).reshape(4, batches, slabs * per_slab)
    mine = lax.dynamic_slice_in_dim(total, lax.axis_index("space") * per_slab, per_slab, 2)
    return mine[3], mine[:3].transpose(1, 0, 2)


def solution(mesh):
    in_specs = (
        P(None, "space", None, None),
        P(None, "space"),
        P(),
        P(None, None, "space"),
        P(None, "space", None),
        P("segment", None),
        P("segment", None, None),
        P("segment", None, None, None),
        P("segment", None, None, None),
        P(),
        P(None, "space"),
    )
    out_specs = (P(None, "space"), P(None, None, "space"))
    return jax.shard_map(
        on_device, mesh=mesh, in_specs=in_specs, out_specs=out_specs, check_vma=False
    )
```

```python
import functools

import jax
import jax.numpy as jnp
from jax import lax
from jax.experimental import pallas as pl
from jax.experimental.pallas import tpu as pltpu
from jax.sharding import PartitionSpec as P

SLAB_DEPTH = 2.0
F32 = jnp.float32
BF16 = jnp.bfloat16
VMEM_LIMIT = 16 * 1024 * 1024

MID, LOW, SOURCES = 32, 64, 96
BASE = 256


def split(value):
    high = value.astype(BF16)
    low = (value - high.astype(F32)).astype(BF16)
    return high, low


def split3(value):
    high = value.astype(BF16)
    rest = value - high.astype(F32)
    mid = rest.astype(BF16)
    return high, mid, (rest - mid.astype(F32)).astype(BF16)


def encode(value):
    high, mid, low = split3(value)
    return high.astype(F32) + pltpu.roll(mid.astype(F32), MID, 1) + pltpu.roll(low.astype(F32), LOW, 1)


def decode(value):
    lanes = value.shape[1]
    whole = value + pltpu.roll(value, lanes - MID, 1) + pltpu.roll(value, lanes - LOW, 1)
    lane = lax.broadcasted_iota(jnp.int32, value.shape, 1)
    return jnp.where(lane < 4, whole, 0.0)


def dot(a, b):
    return lax.dot_general(a, b, (((1,), (0,)), ((), ())), preferred_element_type=F32)


def dot_t(a, b):
    return lax.dot_general(a, b, (((1,), (1,)), ((), ())), preferred_element_type=F32)


def fine_dot(value, weights, product):
    rows = value.shape[0]
    stacked = jnp.concatenate(split(value), axis=0)
    outs = []
    for weight in weights:
        out = product(stacked, weight)
        outs.append(out[:rows] + out[rows:])
    return outs


def silu_parts(value):
    gate = 1.0 / (1.0 + jnp.exp(-value))
    return gate, value * gate


class Sizes:
    def __init__(self, zero_shape, one_shape, two_shape, channels):
        self.c = channels
        self.zero = zero_shape[-1] // channels
        self.one = one_shape[-1] // channels
        self.two = two_shape[-1] // channels
        self.coefs = self.zero + 2 * (self.one + self.two)
        self.starts = (self.zero, self.zero + 2 * self.one)
        self.counts = (self.one, self.two)

    def cols(self, first, count=1):
        return slice(first * self.c, (first + count) * self.c)


def picked_group(refs, hot, first, count):
    blocks = [jnp.concatenate([ref[k] for ref in refs], axis=0) for k in range(first, first + count)]
    return dot(hot, jnp.concatenate(blocks, axis=1))


def own_rows(refs, k):
    low, high = (ref[k].astype(F32) for ref in refs)
    slab = low.shape[0] // 2
    return jnp.concatenate([low[slab:], high[:slab]], axis=0)


def pool(value, rows):
    total = value[:rows]
    for start in range(rows, value.shape[0], rows):
        total = total + value[start : start + rows]
    return total


def geo_at(geo_ref, which, edges):
    return geo_ref[which * edges : (which + 1) * edges, :]


def forward(refs, hot_ref, geo_ref, zero_ref, one_ref, two_ref, sz, rows, last):
    hot = hot_ref[...]
    edges = hot.shape[0]
    factor = (edges // rows) ** (-0.5)
    radial = geo_at(geo_ref, 0, edges)

    def scaled(block):
        return (block * radial).astype(BF16).astype(F32)

    pooled = [None] * sz.coefs
    group = picked_group(refs, hot, 0, sz.zero)
    zin = jnp.concatenate(
        [pool(scaled(group[:, sz.cols(k)]), rows) for k in range(sz.zero)], axis=1
    )
    kept = 1 if last else sz.zero
    (zout,) = fine_dot(zin, [zero_ref[:, sz.cols(0, kept)]], dot)
    for k in range(kept):
        pooled[k] = zout[:, sz.cols(k)] * factor
    for order in range(2):
        first, count = sz.starts[order], sz.counts[order]
        weight_ref = (one_ref, two_ref)[order]
        cos = geo_at(geo_ref, 1 + 2 * order, edges)
        sin = geo_at(geo_ref, 2 + 2 * order, edges)
        group = picked_group(refs, hot, first, 2 * count)
        res, ims = [], []
        for k in range(count):
            re = scaled(group[:, sz.cols(k)])
            im = scaled(group[:, sz.cols(count + k)])
            res.append(pool(cos * re - sin * im, rows))
            ims.append(pool(sin * re + cos * im, rows))
        both = jnp.concatenate(
            [jnp.concatenate(res, axis=1), jnp.concatenate(ims, axis=1)], axis=0
        )
        a, b = fine_dot(both, [weight_ref[0], weight_ref[1]], dot)
        out_re = (a[:rows] - b[rows:]) * factor
        out_im = (b[:rows] + a[rows:]) * factor
        for k in range(count):
            pooled[first + k] = out_re[:, sz.cols(k)]
            pooled[first + count + k] = out_im[:, sz.cols(k)]
    return pooled


def signal_of(pooled, sz):
    total = pooled[0]
    for k in range(sz.zero, sz.coefs):
        total = total + pooled[k] * pooled[k]
    return total


def backward(
    upstream, pooled, refs, hot_ref, hot_t_ref, geo_ref, zero_ref, one_ref, two_ref, sz, rows, last, outs
):
    hot = hot_ref[...]
    hot_t = hot_t_ref[...]
    edges = hot.shape[0]
    slab = rows // 2
    factor = (edges // rows) ** (-0.5)
    signal = signal_of(pooled, sz)
    gate, _ = silu_parts(signal)
    slope = gate * (1.0 - gate)
    d_signal = upstream[0] * (gate + signal * slope)
    if not last:
        inner = upstream[1] * pooled[1]
        for k in range(2, sz.coefs):
            inner = inner + upstream[k] * pooled[k]
        d_signal = d_signal + inner * slope
    d_pooled = [d_signal * factor]
    for k in range(1, sz.coefs):
        if last:
            d_pooled.append(2.0 * factor * d_signal * pooled[k] if k >= sz.zero else None)
        else:
            term = gate * upstream[k]
            if k >= sz.zero:
                term = term + 2.0 * d_signal * pooled[k]
            d_pooled.append(term * factor)

    radial = geo_at(geo_ref, 0, edges)
    kept = 1 if last else sz.zero
    (dz,) = fine_dot(jnp.concatenate(d_pooled[:kept], axis=1), [zero_ref[:, sz.cols(0, kept)]], dot_t)

    def spread(block):
        return jnp.concatenate([block] * (edges // rows), axis=0)

    def scatter(first, blocks):
        if outs is None:
            return
        high, low = split(jnp.concatenate(blocks, axis=1))
        back = dot(hot_t, high) + dot(hot_t, low)
        for n in range(len(blocks)):
            k = first + n
            part = back[:, sz.cols(n)]
            if not last or k == 0:
                part = part + around(upstream[k], slab)
            outs[0][k] = part[:rows].astype(BF16)
            outs[1][k] = part[rows:].astype(BF16)

    q_len = jnp.zeros((edges, sz.c), F32)
    group = picked_group(refs, hot, 0, sz.zero)
    blocks = []
    for k in range(sz.zero):
        grad = spread(dz[:, sz.cols(k)])
        q_len = q_len + grad * group[:, sz.cols(k)]
        blocks.append(grad * radial)
    q_len = q_len * radial
    scatter(0, blocks)
    q_turn = []
    for order in range(2):
        first, count = sz.starts[order], sz.counts[order]
        weight_ref = (one_ref, two_ref)[order]
        cos = geo_at(geo_ref, 1 + 2 * order, edges)
        sin = geo_at(geo_ref, 2 + 2 * order, edges)
        both = jnp.concatenate(
            [
                jnp.concatenate(d_pooled[first : first + count], axis=1),
                jnp.concatenate(d_pooled[first + count : first + 2 * count], axis=1),
            ],
            axis=0,
        )
        a, b = fine_dot(both, [weight_ref[0], weight_ref[1]], dot_t)
        d_re = a[:rows] + b[rows:]
        d_im = a[rows:] - b[:rows]
        group = picked_group(refs, hot, first, 2 * count)
        q_cos = jnp.zeros((edges, sz.c), F32)
        q_sin = jnp.zeros((edges, sz.c), F32)
        cos_r = cos * radial
        sin_r = sin * radial
        blocks_re, blocks_im = [], []
        for k in range(count):
            re = group[:, sz.cols(k)]
            im = group[:, sz.cols(count + k)]
            g_re = spread(d_re[:, sz.cols(k)])
            g_im = spread(d_im[:, sz.cols(k)])
            q_cos = q_cos + (re * g_re + im * g_im)
            q_sin = q_sin + (re * g_im - im * g_re)
            if outs is not None:
                blocks_re.append(cos_r * g_re + sin_r * g_im)
                blocks_im.append(cos_r * g_im - sin_r * g_re)
        scatter(first, blocks_re + blocks_im)
        q_cos = q_cos * radial
        q_sin = q_sin * radial
        q_len = q_len + cos * q_cos + sin * q_sin
        q_turn.append((q_cos, q_sin))

    rate = geo_at(geo_ref, 9, edges)

    def total(value):
        return jnp.sum(value, axis=1, keepdims=True)

    d_len = -total(q_len * rate)
    (dc1, ds1), (dc2, ds2) = [(total(a), total(b)) for a, b in q_turn]
    c1, s1 = geo_at(geo_ref, 1, edges), geo_at(geo_ref, 2, edges)
    ux, uy, uz = (geo_at(geo_ref, 5 + n, edges) for n in range(3))
    inv_planar = geo_at(geo_ref, 8, edges)
    dc1 = dc1 + 2.0 * (c1 * dc2 + s1 * ds2)
    ds1 = ds1 + 2.0 * (c1 * ds2 - s1 * dc2)
    along = c1 * dc1 + s1 * ds1
    dx = (dc1 - along * c1) * inv_planar + d_len * ux
    dy = (ds1 - along * s1) * inv_planar + d_len * uy
    dz_ = d_len * uz
    lane = lax.broadcasted_iota(jnp.int32, (edges, sz.c), 1)
    change = jnp.where(lane == 0, dx, jnp.where(lane == 1, dy, jnp.where(lane == 2, dz_, 0.0)))
    moved = sum(dot(hot_t, part) for part in split3(change))
    return moved - around(pool(change, rows), slab)


def around(own, slab):
    edge = jnp.zeros((slab, own.shape[1]), F32)
    return jnp.concatenate([edge, own, edge], axis=0)


def first_slab(slabs):
    slab_now = lax.axis_index("space")
    batch = lax.rem(slab_now, 2)
    shift = lax.rem(lax.axis_index("segment"), 2)
    return lax.rem(slab_now - batch + shift - 1 + slabs, slabs), batch


def send_back(moved, outs, sz):
    rows = moved.shape[0] // 2
    coded = encode(moved).astype(BF16)
    outs[0][sz.coefs] = coded[:rows]
    outs[1][sz.coefs] = coded[rows:]


def share(moved, outs):
    slab = moved.shape[0] // 4
    left, low, high, right = (moved[n * slab : (n + 1) * slab] for n in range(4))
    even = lax.rem(lax.axis_index("space"), 2) == 0
    outs[0][...] = jnp.where(even, low, high)
    outs[1][...] = jnp.where(even, high, low)
    outs[2][...] = jnp.where(even, right, left)
    outs[3][...] = jnp.where(even, left, right)


def join_kernel(here_ref, theirs_ref, straight_ref, cross_ref, both_ref):
    slab = here_ref.shape[0]
    even = lax.rem(lax.axis_index("space"), 2) == 0
    here = here_ref[...] + straight_ref[...]
    there = theirs_ref[...] + cross_ref[...]
    both_ref[:slab, :] = jnp.where(even, here, there)
    both_ref[slab:, :] = jnp.where(even, there, here)


def close_kernel(*refs):
    *sums_refs, energies_ref, places_ref = refs
    slab = energies_ref.shape[1]
    for n, ref in enumerate(sums_refs):

        @pl.when(lax.axis_index("segment") == n)
        def _(ref=ref):
            sums = ref[...]
            rows, c = sums.shape
            turned = jnp.transpose(jnp.concatenate([sums, jnp.zeros((c - rows, c), F32)], axis=0))
            for b in range(2):
                energies_ref[b : b + 1, :] = turned[3:4, b * slab : (b + 1) * slab]
                for n in range(3):
                    places_ref[n, b : b + 1, :] = turned[n : n + 1, b * slab : (b + 1) * slab]


def pack_kernel(
    node_hbm, places_hbm, species_hbm, sources_hbm, grad_hbm, table_hbm, mine_ref, other_ref,
    states, places, species, sources, grads, table, sems
):
    slab_now = lax.axis_index("space")
    batch = lax.rem(slab_now, 2)
    copies = []
    pairs = (
        (node_hbm, states), (places_hbm, places), (species_hbm, species), (sources_hbm, sources),
        (grad_hbm, grads), (table_hbm, table),
    )
    for n, (source, target) in enumerate(pairs):
        copies.append(pltpu.make_async_copy(source, target, sems.at[n]))
        copies[-1].start()
    for copy in copies:
        copy.wait()
    coefs, per_slab, c = states.shape[1:]
    lane = lax.broadcasted_iota(jnp.int32, (per_slab, c), 1)
    eye = (
        lax.broadcasted_iota(jnp.int32, (per_slab, per_slab), 0)
        == lax.broadcasted_iota(jnp.int32, (per_slab, per_slab), 1)
    )

    def column(row):
        return jnp.sum(jnp.where(eye, jnp.broadcast_to(row, (per_slab, per_slab)), 0.0), axis=1, keepdims=True)

    both = []
    for b in range(2):
        names = column(species[b : b + 1, :].astype(F32)).astype(jnp.int32)
        kinds = table.shape[0]
        hot = (names == lax.broadcasted_iota(jnp.int32, (per_slab, kinds), 1)).astype(BF16)
        first = (states[b, 0].astype(F32) + dot(hot, table[...])).astype(BF16)
        extra = jnp.zeros((per_slab, c), F32)
        for n in range(3):
            extra = jnp.where(lane == n, column(places[n, b : b + 1, :]), extra)
        extra = encode(jnp.where(lane == 3, column(grads[b : b + 1, :]), extra))
        for j in range(sources.shape[2]):
            index = sources[b, :, j : j + 1]
            extra = jnp.where(lane == SOURCES + j, (index // BASE).astype(F32), extra)
            extra = jnp.where(lane == SOURCES + 8 + j, (index % BASE).astype(F32), extra)
        both.append((first, extra.astype(BF16)))
    for ref, chosen in ((mine_ref, batch), (other_ref, 1 - batch)):
        ref[pl.ds(0, coefs)] = states[chosen]
        ref[0] = jnp.where(chosen == 0, both[0][0].astype(F32), both[1][0].astype(F32)).astype(BF16)
        ref[coefs] = jnp.where(chosen == 0, both[0][1].astype(F32), both[1][1].astype(F32)).astype(BF16)


def open_kernel(
    slabs, neighbours, mine_ref, partner_ref, straight_ref, cross_ref, rate_ref,
    low_ref, high_ref, hot_ref, hot_t_ref, geo_ref, seed_ref
):
    start, batch = first_slab(slabs)
    even = batch == 0
    level = lax.rem(lax.axis_index("segment"), 2) == 0
    coefs = low_ref.shape[0]
    rows, c = low_ref.shape[1:]
    per_slab = rows // 2
    window = 2 * rows
    edges = rows * neighbours

    def choose(a, b):
        return jnp.where(even, a, b)

    def parts(k):
        mine, partner = mine_ref[k].astype(F32), partner_ref[k].astype(F32)
        straight, cross = straight_ref[k].astype(F32), cross_ref[k].astype(F32)
        low, high = choose(mine, partner), choose(partner, mine)
        after, last = choose(straight, cross), choose(cross, straight)
        return [
            jnp.where(level, last, low), jnp.where(level, low, high), jnp.where(level, high, after),
            jnp.where(level, after, last),
        ]

    @pl.when(lax.axis_index("segment") == 0)
    def _():
        for k in range(coefs):
            slab = parts(k)
            low_ref[k] = jnp.concatenate(slab[:2], axis=0).astype(BF16)
            high_ref[k] = jnp.concatenate(slab[2:], axis=0).astype(BF16)

    extra = jnp.concatenate(parts(coefs), axis=0)
    numbers = decode(extra)
    seed_ref[...] = jnp.broadcast_to(numbers[per_slab : per_slab + rows, 3:4], (rows, c))
    own_extra = extra[per_slab : per_slab + rows]
    low = pltpu.roll(own_extra, c - 8, 1)
    index = own_extra.astype(jnp.int32) * BASE + low.astype(jnp.int32)
    place = lax.rem(index // per_slab - start + slabs, slabs) * per_slab + index % per_slab
    columns = lax.broadcasted_iota(jnp.int32, (rows, c), 1)
    hot = jnp.concatenate(
        [
            (place[:, SOURCES + j : SOURCES + j + 1] == columns).astype(F32)
            for j in range(neighbours)
        ],
        axis=0,
    )
    hot_ref[...] = hot.astype(BF16)[:, :window]
    hot_t_ref[...] = jnp.transpose(hot).astype(BF16)[:window]
    hot = hot.astype(BF16)[:, :window]
    lift = lax.broadcasted_iota(jnp.int32, (window, c), 0) // per_slab - 1
    offset = []
    for n in range(3):
        column = jnp.broadcast_to(numbers[:, n : n + 1], (window, c))
        if n == 2:
            column = column + SLAB_DEPTH * lift.astype(F32)
        there = sum(dot(hot, part) for part in split3(column))
        offset.append(there - jnp.concatenate([column[per_slab : per_slab + rows]] * neighbours, axis=0))
    flat = offset[0] * offset[0] + offset[1] * offset[1] + 1.0
    length = jnp.sqrt(flat + offset[2] * offset[2])
    planar = jnp.sqrt(flat)
    c1, s1 = offset[0] / planar, offset[1] / planar
    rate = jnp.broadcast_to(rate_ref[...], (edges, c))
    values = [
        jnp.exp(-rate * length),
        c1,
        s1,
        c1 * c1 - s1 * s1,
        2.0 * c1 * s1,
        offset[0] / length,
        offset[1] / length,
        offset[2] / length,
        1.0 / planar,
        rate,
    ]
    for n, value in enumerate(values):
        geo_ref[n * edges : (n + 1) * edges, :] = value


def stage_kernel(zero_hbm, one_hbm, two_hbm, zero_ref, one_ref, two_ref, sems):
    copies = [
        pltpu.make_async_copy(source, target, sems.at[n])
        for n, (source, target) in enumerate(((zero_hbm, zero_ref), (one_hbm, one_ref), (two_hbm, two_ref)))
    ]
    for copy in copies:
        copy.start()
    for copy in copies:
        copy.wait()


def forward_kernel(
    tick, sz, low_ref, high_ref, hot_ref, geo_ref, zero_ref, one_ref, two_ref, out_ref, pooled_ref
):
    @pl.when(lax.axis_index("segment") == tick)
    def _():
        rows = low_ref.shape[1]
        refs = (low_ref, high_ref)
        pooled = forward(refs, hot_ref, geo_ref, zero_ref, one_ref, two_ref, sz, rows, False)
        signal = signal_of(pooled, sz)
        gate, lifted = silu_parts(signal)
        for k in range(sz.coefs):
            pooled_ref[k] = pooled[k]
            added = lifted if k == 0 else gate * pooled[k]
            out_ref[k] = (own_rows(refs, k) + added).astype(BF16)


def turn_kernel(
    tick, sz, low_ref, high_ref, hot_ref, hot_t_ref, geo_ref, zero_ref, one_ref, two_ref,
    read_ref, seed_ref, *outs
):
    @pl.when(lax.axis_index("segment") == tick)
    def _():
        rows = low_ref.shape[1]
        refs = (low_ref, high_ref)
        pooled = forward(refs, hot_ref, geo_ref, zero_ref, one_ref, two_ref, sz, rows, True)
        signal = signal_of(pooled, sz)
        _, lifted = silu_parts(signal)
        updated = own_rows(refs, 0) + lifted
        gate, active = silu_parts(updated)
        read = read_ref[...]
        energy = jnp.sum(read * active, axis=1, keepdims=True)
        lane = lax.broadcasted_iota(jnp.int32, (rows, sz.c), 1)
        energy = around(jnp.where(lane == 3, energy, 0.0), rows // 2)
        upstream = [seed_ref[...] * read * (gate + updated * gate * (1.0 - gate))]
        moved = backward(
            upstream, pooled, refs, hot_ref, hot_t_ref, geo_ref, zero_ref, one_ref, two_ref, sz, rows, True, outs
        )
        send_back(moved + energy, outs, sz)


def backward_kernel(
    tick, sz, up_low_ref, up_high_ref, pooled_ref, low_ref, high_ref, hot_ref, hot_t_ref, geo_ref,
    zero_ref, one_ref, two_ref, *outs
):
    @pl.when(lax.axis_index("segment") == tick)
    def _():
        rows = low_ref.shape[1]
        refs = (low_ref, high_ref)
        upstream = [up_low_ref[k].astype(F32) + up_high_ref[k].astype(F32) for k in range(sz.coefs)]
        pooled = [pooled_ref[k] for k in range(sz.coefs)]
        moved = backward(
            upstream, pooled, refs, hot_ref, hot_t_ref, geo_ref, zero_ref, one_ref, two_ref, sz, rows, False,
            outs if tick else None,
        )
        carried = decode(up_low_ref[sz.coefs].astype(F32)) + decode(up_high_ref[sz.coefs].astype(F32))
        moved = moved + around(carried, rows // 2)
        if tick:
            send_back(moved, outs, sz)
        else:
            share(moved, outs)


def call(body, operands, shapes, name, spaces=None, scratch=()):
    spaces = spaces or [pltpu.VMEM] * len(operands)
    operands = [pltpu.with_memory_space_constraint(value, space) for value, space in zip(operands, spaces)]
    return pl.pallas_call(
        body,
        out_shape=shapes,
        in_specs=[pl.BlockSpec(memory_space=space) for space in spaces],
        out_specs=[pl.BlockSpec(memory_space=pltpu.VMEM) for _ in shapes],
        scratch_shapes=list(scratch),
        compiler_params=pltpu.CompilerParams(vmem_limit_bytes=VMEM_LIMIT),
        name=name,
    )(*operands)


def on_device(
    node_states,
    species,
    species_table,
    places,
    sources,
    radial_rate,
    zero_weight,
    one_weight,
    two_weight,
    read_weight,
    energy_grad,
):
    segments = lax.axis_size("segment")
    slabs = lax.axis_size("space")
    batches, per_slab = species.shape
    coefs, channels = node_states.shape[2:]
    neighbours = sources.shape[2]
    rows = batches * per_slab
    edges = rows * neighbours
    sz = Sizes(zero_weight.shape, one_weight.shape, two_weight.shape, channels)
    axes = ("segment", "space")
    shape = jax.ShapeDtypeStruct

    def within(value, target, count):
        pairs = [(s * slabs + i, s * slabs + target(s % 2, i) % slabs) for s in range(count) for i in range(slabs)]
        return lax.ppermute(value, axes, pairs)

    def hop(value, start, stop, by):
        pairs = [(start * slabs + i, stop * slabs + (i + by) % slabs) for i in range(slabs)]
        return lax.ppermute(value, axes, pairs)

    raw = [
        node_states.transpose(0, 2, 1, 3), places.transpose(1, 0, 2), species, sources, energy_grad, species_table,
    ]
    packed = shape((coefs + 1, per_slab, channels), BF16)
    mine, other = call(
        pack_kernel, raw, [packed, packed], "pack", [pltpu.HBM] * len(raw),
        [pltpu.VMEM(v.shape, v.dtype) for v in raw] + [pltpu.SemaphoreType.DMA((len(raw),))],
    )
    partner = within(other, lambda odd, i: i + 1 - 2 * (i % 2), segments)
    straight = within(mine, lambda odd, i: i - 2 if odd or i % 2 == 0 else i + 2, segments)
    cross = within(other, lambda odd, i: i - 1 if i % 2 == 0 else i - 3 if odd else i + 1, segments)
    weights = [zero_weight[0], one_weight[0], two_weight[0]]
    weights = call(
        stage_kernel, weights, [pltpu.VMEM(w.shape, w.dtype) for w in weights], "stage", [pltpu.HBM] * 3,
        [pltpu.SemaphoreType.DMA((3,))],
    )
    whole = shape((coefs, rows, channels), BF16)
    low, high, hot, hot_t, geo, seeds = call(
        functools.partial(open_kernel, slabs, neighbours),
        [mine, partner, straight, cross, radial_rate],
        [
            whole, whole, shape((edges, 2 * rows), BF16), shape((2 * rows, edges), BF16),
            shape((10 * edges, channels), F32), shape((rows, channels), F32),
        ],
        "open",
    )
    around_all = [(low, high)]
    kept = []
    for tick in range(segments - 1):
        out, pooled = call(
            functools.partial(forward_kernel, tick, sz),
            [*around_all[tick], hot, geo, *weights],
            [whole, shape((coefs, rows, channels), F32)],
            "forward",
        )
        kept.append(pooled)
        ways = (2, 0) if tick % 2 else (0, -2)
        around_all.append(tuple(hop(out, tick, tick + 1, by) for by in ways))
    final = segments - 1
    whole_more = shape((coefs + 1, rows, channels), BF16)
    slab_sums = shape((per_slab, channels), F32)
    parts = call(
        functools.partial(turn_kernel, final, sz),
        [*around_all[final], hot, hot_t, geo, *weights, read_weight.reshape(1, channels), seeds],
        [whole_more, whole_more],
        "turn",
    )
    for tick in reversed(range(segments - 1)):
        ways = (2, 0) if tick % 2 else (0, -2)
        up = [hop(part, tick + 1, tick, -by) for part, by in zip(parts, ways)]
        parts = call(
            functools.partial(backward_kernel, tick, sz),
            [*up, kept[tick], *around_all[tick], hot, hot_t, geo, *weights],
            [whole_more, whole_more] if tick else [slab_sums] * 4,
            "backward",
        )
    here, theirs, straight, cross = parts
    theirs = within(theirs, lambda odd, i: i + 1 - 2 * (i % 2), 1)
    straight = within(straight, lambda odd, i: i - 2 if i % 2 else i + 2, 1)
    cross = within(cross, lambda odd, i: i + 1 if i % 2 else i - 1, 1)
    (both,) = call(join_kernel, [here, theirs, straight, cross], [shape((rows, channels), F32)], "join")
    copies = [both] + [hop(both, 0, stop, 0) for stop in range(1, segments)]
    energies, gradients = call(
        close_kernel, copies, [shape((batches, per_slab), F32), shape((3, batches, per_slab), F32)], "close"
    )
    return energies, gradients.transpose(1, 0, 2)


def solution(mesh):
    in_specs = (
        P(None, "space", None, None),
        P(None, "space"),
        P(),
        P(None, None, "space"),
        P(None, "space", None),
        P("segment", None),
        P("segment", None, None),
        P("segment", None, None, None),
        P("segment", None, None, None),
        P(),
        P(None, "space"),
    )
    out_specs = (P(None, "space"), P(None, None, "space"))
    return jax.shard_map(
        on_device, mesh=mesh, in_specs=in_specs, out_specs=out_specs, check_vma=False
    )
```

```python
import functools

import jax
import jax.numpy as jnp
from jax import lax
from jax.experimental import pallas as pl
from jax.experimental.pallas import tpu as pltpu
from jax.sharding import PartitionSpec as P

SLAB_DEPTH = 2.0
F32 = jnp.float32
BF16 = jnp.bfloat16
VMEM_LIMIT = 16 * 1024 * 1024

MID, LOW, SOURCES = 32, 64, 96
BASE = 256


def split(value):
    high = value.astype(BF16)
    low = (value - high.astype(F32)).astype(BF16)
    return high, low


def split3(value):
    high = value.astype(BF16)
    rest = value - high.astype(F32)
    mid = rest.astype(BF16)
    return high, mid, (rest - mid.astype(F32)).astype(BF16)


def encode(value):
    high, mid, low = split3(value)
    return high.astype(F32) + pltpu.roll(mid.astype(F32), MID, 1) + pltpu.roll(low.astype(F32), LOW, 1)


def decode(value):
    lanes = value.shape[1]
    whole = value + pltpu.roll(value, lanes - MID, 1) + pltpu.roll(value, lanes - LOW, 1)
    lane = lax.broadcasted_iota(jnp.int32, value.shape, 1)
    return jnp.where(lane < 4, whole, 0.0)


def dot(a, b):
    return lax.dot_general(a, b, (((1,), (0,)), ((), ())), preferred_element_type=F32)


def dot_t(a, b):
    return lax.dot_general(a, b, (((1,), (1,)), ((), ())), preferred_element_type=F32)


def fine_dot(value, weights, product):
    rows = value.shape[0]
    stacked = jnp.concatenate(split(value), axis=0)
    outs = []
    for weight in weights:
        out = product(stacked, weight)
        outs.append(out[:rows] + out[rows:])
    return outs


def silu_parts(value):
    gate = 1.0 / (1.0 + jnp.exp(-value))
    return gate, value * gate


class Sizes:
    def __init__(self, zero_shape, one_shape, two_shape, channels):
        self.c = channels
        self.zero = zero_shape[-1] // channels
        self.one = one_shape[-1] // channels
        self.two = two_shape[-1] // channels
        self.coefs = self.zero + 2 * (self.one + self.two)
        self.starts = (self.zero, self.zero + 2 * self.one)
        self.counts = (self.one, self.two)

    def cols(self, first, count=1):
        return slice(first * self.c, (first + count) * self.c)


def picked_group(refs, hot, first, count):
    blocks = [jnp.concatenate([ref[k] for ref in refs], axis=0) for k in range(first, first + count)]
    return dot(hot, jnp.concatenate(blocks, axis=1))


def own_rows(refs, k):
    low, high = (ref[k].astype(F32) for ref in refs)
    slab = low.shape[0] // 2
    return jnp.concatenate([low[slab:], high[:slab]], axis=0)


def pool(value, rows):
    total = value[:rows]
    for start in range(rows, value.shape[0], rows):
        total = total + value[start : start + rows]
    return total


def geo_at(geo_ref, which, edges):
    return geo_ref[which * edges : (which + 1) * edges, :]


def forward(refs, hot_ref, geo_ref, zero_ref, one_ref, two_ref, sz, rows, last):
    hot = hot_ref[...]
    edges = hot.shape[0]
    factor = (edges // rows) ** (-0.5)
    radial = geo_at(geo_ref, 0, edges)

    def scaled(block):
        return (block * radial).astype(BF16).astype(F32)

    pooled = [None] * sz.coefs
    group = picked_group(refs, hot, 0, sz.zero)
    zin = jnp.concatenate(
        [pool(scaled(group[:, sz.cols(k)]), rows) for k in range(sz.zero)], axis=1
    )
    kept = 1 if last else sz.zero
    (zout,) = fine_dot(zin, [zero_ref[:, sz.cols(0, kept)]], dot)
    for k in range(kept):
        pooled[k] = zout[:, sz.cols(k)] * factor
    for order in range(2):
        first, count = sz.starts[order], sz.counts[order]
        weight_ref = (one_ref, two_ref)[order]
        cos = geo_at(geo_ref, 1 + 2 * order, edges)
        sin = geo_at(geo_ref, 2 + 2 * order, edges)
        group = picked_group(refs, hot, first, 2 * count)
        res, ims = [], []
        for k in range(count):
            re = scaled(group[:, sz.cols(k)])
            im = scaled(group[:, sz.cols(count + k)])
            res.append(pool(cos * re - sin * im, rows))
            ims.append(pool(sin * re + cos * im, rows))
        both = jnp.concatenate(
            [jnp.concatenate(res, axis=1), jnp.concatenate(ims, axis=1)], axis=0
        )
        a, b = fine_dot(both, [weight_ref[0], weight_ref[1]], dot)
        out_re = (a[:rows] - b[rows:]) * factor
        out_im = (b[:rows] + a[rows:]) * factor
        for k in range(count):
            pooled[first + k] = out_re[:, sz.cols(k)]
            pooled[first + count + k] = out_im[:, sz.cols(k)]
    return pooled


def signal_of(pooled, sz):
    total = pooled[0]
    for k in range(sz.zero, sz.coefs):
        total = total + pooled[k] * pooled[k]
    return total


def backward(
    upstream, pooled, refs, hot_ref, hot_t_ref, geo_ref, zero_ref, one_ref, two_ref, sz, rows, last, outs
):
    hot = hot_ref[...]
    hot_t = hot_t_ref[...]
    edges = hot.shape[0]
    slab = rows // 2
    factor = (edges // rows) ** (-0.5)
    signal = signal_of(pooled, sz)
    gate, _ = silu_parts(signal)
    slope = gate * (1.0 - gate)
    d_signal = upstream[0] * (gate + signal * slope)
    if not last:
        inner = upstream[1] * pooled[1]
        for k in range(2, sz.coefs):
            inner = inner + upstream[k] * pooled[k]
        d_signal = d_signal + inner * slope
    d_pooled = [d_signal * factor]
    for k in range(1, sz.coefs):
        if last:
            d_pooled.append(2.0 * factor * d_signal * pooled[k] if k >= sz.zero else None)
        else:
            term = gate * upstream[k]
            if k >= sz.zero:
                term = term + 2.0 * d_signal * pooled[k]
            d_pooled.append(term * factor)

    radial = geo_at(geo_ref, 0, edges)
    kept = 1 if last else sz.zero
    (dz,) = fine_dot(jnp.concatenate(d_pooled[:kept], axis=1), [zero_ref[:, sz.cols(0, kept)]], dot_t)

    def spread(block):
        return jnp.concatenate([block] * (edges // rows), axis=0)

    def scatter(first, blocks):
        if outs is None:
            return
        high, low = split(jnp.concatenate(blocks, axis=1))
        back = dot(hot_t, high) + dot(hot_t, low)
        for n in range(len(blocks)):
            k = first + n
            part = back[:, sz.cols(n)]
            if not last or k == 0:
                part = part + around(upstream[k], slab)
            outs[0][k] = part[:rows].astype(BF16)
            outs[1][k] = part[rows:].astype(BF16)

    q_len = jnp.zeros((edges, sz.c), F32)
    group = picked_group(refs, hot, 0, sz.zero)
    blocks = []
    for k in range(sz.zero):
        grad = spread(dz[:, sz.cols(k)])
        q_len = q_len + grad * group[:, sz.cols(k)]
        blocks.append(grad * radial)
    q_len = q_len * radial
    scatter(0, blocks)
    q_turn = []
    for order in range(2):
        first, count = sz.starts[order], sz.counts[order]
        weight_ref = (one_ref, two_ref)[order]
        cos = geo_at(geo_ref, 1 + 2 * order, edges)
        sin = geo_at(geo_ref, 2 + 2 * order, edges)
        both = jnp.concatenate(
            [
                jnp.concatenate(d_pooled[first : first + count], axis=1),
                jnp.concatenate(d_pooled[first + count : first + 2 * count], axis=1),
            ],
            axis=0,
        )
        a, b = fine_dot(both, [weight_ref[0], weight_ref[1]], dot_t)
        d_re = a[:rows] + b[rows:]
        d_im = a[rows:] - b[:rows]
        group = picked_group(refs, hot, first, 2 * count)
        q_cos = jnp.zeros((edges, sz.c), F32)
        q_sin = jnp.zeros((edges, sz.c), F32)
        cos_r = cos * radial
        sin_r = sin * radial
        blocks_re, blocks_im = [], []
        for k in range(count):
            re = group[:, sz.cols(k)]
            im = group[:, sz.cols(count + k)]
            g_re = spread(d_re[:, sz.cols(k)])
            g_im = spread(d_im[:, sz.cols(k)])
            q_cos = q_cos + (re * g_re + im * g_im)
            q_sin = q_sin + (re * g_im - im * g_re)
            if outs is not None:
                blocks_re.append(cos_r * g_re + sin_r * g_im)
                blocks_im.append(cos_r * g_im - sin_r * g_re)
        scatter(first, blocks_re + blocks_im)
        q_cos = q_cos * radial
        q_sin = q_sin * radial
        q_len = q_len + cos * q_cos + sin * q_sin
        q_turn.append((q_cos, q_sin))

    rate = geo_at(geo_ref, 9, edges)

    def total(value):
        return jnp.sum(value, axis=1, keepdims=True)

    d_len = -total(q_len * rate)
    (dc1, ds1), (dc2, ds2) = [(total(a), total(b)) for a, b in q_turn]
    c1, s1 = geo_at(geo_ref, 1, edges), geo_at(geo_ref, 2, edges)
    ux, uy, uz = (geo_at(geo_ref, 5 + n, edges) for n in range(3))
    inv_planar = geo_at(geo_ref, 8, edges)
    dc1 = dc1 + 2.0 * (c1 * dc2 + s1 * ds2)
    ds1 = ds1 + 2.0 * (c1 * ds2 - s1 * dc2)
    along = c1 * dc1 + s1 * ds1
    dx = (dc1 - along * c1) * inv_planar + d_len * ux
    dy = (ds1 - along * s1) * inv_planar + d_len * uy
    dz_ = d_len * uz
    lane = lax.broadcasted_iota(jnp.int32, (edges, sz.c), 1)
    change = jnp.where(lane == 0, dx, jnp.where(lane == 1, dy, jnp.where(lane == 2, dz_, 0.0)))
    moved = sum(dot(hot_t, part) for part in split3(change))
    return moved - around(pool(change, rows), slab)


def around(own, slab):
    edge = jnp.zeros((slab, own.shape[1]), F32)
    return jnp.concatenate([edge, own, edge], axis=0)


def first_slab(slabs):
    slab_now = lax.axis_index("space")
    batch = lax.rem(slab_now, 2)
    shift = lax.rem(lax.axis_index("segment"), 2)
    return lax.rem(slab_now - batch + shift - 1 + slabs, slabs), batch


def send_back(moved, outs, sz):
    rows = moved.shape[0] // 2
    coded = encode(moved).astype(BF16)
    outs[0][sz.coefs] = coded[:rows]
    outs[1][sz.coefs] = coded[rows:]


def share(moved, outs):
    slab = moved.shape[0] // 4
    left, low, high, right = (moved[n * slab : (n + 1) * slab] for n in range(4))
    even = lax.rem(lax.axis_index("space"), 2) == 0
    outs[0][...] = jnp.where(even, low, high)
    outs[1][...] = jnp.where(even, high, low)
    outs[2][...] = jnp.where(even, right, left)
    outs[3][...] = jnp.where(even, left, right)


def join_kernel(here_ref, theirs_ref, straight_ref, cross_ref, both_ref):
    slab = here_ref.shape[0]
    even = lax.rem(lax.axis_index("space"), 2) == 0
    here = here_ref[...] + straight_ref[...]
    there = theirs_ref[...] + cross_ref[...]
    both_ref[:slab, :] = jnp.where(even, here, there)
    both_ref[slab:, :] = jnp.where(even, there, here)


def close_kernel(*refs):
    *sums_refs, energies_ref, places_ref = refs
    slab = energies_ref.shape[1]
    for n, ref in enumerate(sums_refs):

        @pl.when(lax.axis_index("segment") == n)
        def _(ref=ref):
            sums = ref[...]
            rows, c = sums.shape
            turned = jnp.transpose(jnp.concatenate([sums, jnp.zeros((c - rows, c), F32)], axis=0))
            for b in range(2):
                energies_ref[b : b + 1, :] = turned[3:4, b * slab : (b + 1) * slab]
                for n in range(3):
                    places_ref[n, b : b + 1, :] = turned[n : n + 1, b * slab : (b + 1) * slab]


def pack_kernel(
    node_hbm, places_hbm, species_hbm, sources_hbm, grad_hbm, table_hbm, mine_ref, other_ref,
    states, places, species, sources, grads, table, sems
):
    slab_now = lax.axis_index("space")
    batch = lax.rem(slab_now, 2)
    copies = []
    pairs = (
        (node_hbm, states), (places_hbm, places), (species_hbm, species), (sources_hbm, sources),
        (grad_hbm, grads), (table_hbm, table),
    )
    for n, (source, target) in enumerate(pairs):
        copies.append(pltpu.make_async_copy(source, target, sems.at[n]))
        copies[-1].start()
    for copy in copies:
        copy.wait()
    coefs, per_slab, c = states.shape[1:]
    lane = lax.broadcasted_iota(jnp.int32, (per_slab, c), 1)
    eye = (
        lax.broadcasted_iota(jnp.int32, (per_slab, per_slab), 0)
        == lax.broadcasted_iota(jnp.int32, (per_slab, per_slab), 1)
    )

    def column(row):
        return jnp.sum(jnp.where(eye, jnp.broadcast_to(row, (per_slab, per_slab)), 0.0), axis=1, keepdims=True)

    both = []
    for b in range(2):
        names = column(species[b : b + 1, :].astype(F32)).astype(jnp.int32)
        kinds = table.shape[0]
        hot = (names == lax.broadcasted_iota(jnp.int32, (per_slab, kinds), 1)).astype(BF16)
        first = (states[b, 0].astype(F32) + dot(hot, table[...])).astype(BF16)
        extra = jnp.zeros((per_slab, c), F32)
        for n in range(3):
            extra = jnp.where(lane == n, column(places[n, b : b + 1, :]), extra)
        extra = encode(jnp.where(lane == 3, column(grads[b : b + 1, :]), extra))
        for j in range(sources.shape[2]):
            index = sources[b, :, j : j + 1]
            extra = jnp.where(lane == SOURCES + j, (index // BASE).astype(F32), extra)
            extra = jnp.where(lane == SOURCES + 8 + j, (index % BASE).astype(F32), extra)
        both.append((first, extra.astype(BF16)))
    for ref, chosen in ((mine_ref, batch), (other_ref, 1 - batch)):
        ref[pl.ds(0, coefs)] = states[chosen]
        ref[0] = jnp.where(chosen == 0, both[0][0].astype(F32), both[1][0].astype(F32)).astype(BF16)
        ref[coefs] = jnp.where(chosen == 0, both[0][1].astype(F32), both[1][1].astype(F32)).astype(BF16)


def open_kernel(
    slabs, neighbours, mine_ref, partner_ref, straight_ref, cross_ref, rate_ref,
    low_ref, high_ref, hot_ref, hot_t_ref, geo_ref, seed_ref
):
    start, batch = first_slab(slabs)
    even = batch == 0
    level = lax.rem(lax.axis_index("segment"), 2) == 0
    coefs = low_ref.shape[0]
    rows, c = low_ref.shape[1:]
    per_slab = rows // 2
    window = 2 * rows
    edges = rows * neighbours

    def choose(a, b):
        return jnp.where(even, a, b)

    def parts(k):
        mine, partner = mine_ref[k].astype(F32), partner_ref[k].astype(F32)
        straight, cross = straight_ref[k].astype(F32), cross_ref[k].astype(F32)
        low, high = choose(mine, partner), choose(partner, mine)
        after, last = choose(straight, cross), choose(cross, straight)
        return [
            jnp.where(level, last, low), jnp.where(level, low, high), jnp.where(level, high, after),
            jnp.where(level, after, last),
        ]

    @pl.when(lax.axis_index("segment") == 0)
    def _():
        for k in range(coefs):
            slab = parts(k)
            low_ref[k] = jnp.concatenate(slab[:2], axis=0).astype(BF16)
            high_ref[k] = jnp.concatenate(slab[2:], axis=0).astype(BF16)

    extra = jnp.concatenate(parts(coefs), axis=0)
    numbers = decode(extra)
    seed_ref[...] = jnp.broadcast_to(numbers[per_slab : per_slab + rows, 3:4], (rows, c))
    own_extra = extra[per_slab : per_slab + rows]
    low = pltpu.roll(own_extra, c - 8, 1)
    index = own_extra.astype(jnp.int32) * BASE + low.astype(jnp.int32)
    place = lax.rem(index // per_slab - start + slabs, slabs) * per_slab + index % per_slab
    columns = lax.broadcasted_iota(jnp.int32, (rows, c), 1)
    hot = jnp.concatenate(
        [
            (place[:, SOURCES + j : SOURCES + j + 1] == columns).astype(F32)
            for j in range(neighbours)
        ],
        axis=0,
    )
    hot_ref[...] = hot.astype(BF16)[:, :window]
    hot_t_ref[...] = jnp.transpose(hot).astype(BF16)[:window]
    hot = hot.astype(BF16)[:, :window]
    lift = lax.broadcasted_iota(jnp.int32, (window, c), 0) // per_slab - 1
    offset = []
    for n in range(3):
        column = jnp.broadcast_to(numbers[:, n : n + 1], (window, c))
        if n == 2:
            column = column + SLAB_DEPTH * lift.astype(F32)
        there = sum(dot(hot, part) for part in split3(column))
        offset.append(there - jnp.concatenate([column[per_slab : per_slab + rows]] * neighbours, axis=0))
    flat = offset[0] * offset[0] + offset[1] * offset[1] + 1.0
    length = jnp.sqrt(flat + offset[2] * offset[2])
    planar = jnp.sqrt(flat)
    c1, s1 = offset[0] / planar, offset[1] / planar
    rate = jnp.broadcast_to(rate_ref[...], (edges, c))
    values = [
        jnp.exp(-rate * length),
        c1,
        s1,
        c1 * c1 - s1 * s1,
        2.0 * c1 * s1,
        offset[0] / length,
        offset[1] / length,
        offset[2] / length,
        1.0 / planar,
        rate,
    ]
    for n, value in enumerate(values):
        geo_ref[n * edges : (n + 1) * edges, :] = value


def works_late():
    return (lax.axis_index("segment") == 0) & (lax.rem(lax.axis_index("space"), 2) == 1)


def stage_kernel(late, zero_hbm, one_hbm, two_hbm, *more):
    zero_ref, one_ref, two_ref, sems = more[-4:]

    @pl.when(works_late() == late)
    def _():
        pairs = [(zero_hbm, zero_ref)]
        for source, target in ((one_hbm, one_ref), (two_hbm, two_ref)):
            pairs += [(source.at[n], target.at[n]) for n in range(2)]
        copies = [pltpu.make_async_copy(source, target, sems.at[n]) for n, (source, target) in enumerate(pairs)]
        for copy in copies:
            copy.start()
        for copy in copies:
            copy.wait()


def forward_kernel(
    tick, sz, low_ref, high_ref, hot_ref, geo_ref, zero_ref, one_ref, two_ref, out_ref, pooled_ref
):
    @pl.when(lax.axis_index("segment") == tick)
    def _():
        rows = low_ref.shape[1]
        refs = (low_ref, high_ref)
        pooled = forward(refs, hot_ref, geo_ref, zero_ref, one_ref, two_ref, sz, rows, False)
        signal = signal_of(pooled, sz)
        gate, lifted = silu_parts(signal)
        for k in range(sz.coefs):
            pooled_ref[k] = pooled[k]
            added = lifted if k == 0 else gate * pooled[k]
            out_ref[k] = (own_rows(refs, k) + added).astype(BF16)


def turn_kernel(
    tick, sz, low_ref, high_ref, hot_ref, hot_t_ref, geo_ref, zero_ref, one_ref, two_ref,
    read_ref, seed_ref, *outs
):
    @pl.when(lax.axis_index("segment") == tick)
    def _():
        rows = low_ref.shape[1]
        refs = (low_ref, high_ref)
        pooled = forward(refs, hot_ref, geo_ref, zero_ref, one_ref, two_ref, sz, rows, True)
        signal = signal_of(pooled, sz)
        _, lifted = silu_parts(signal)
        updated = own_rows(refs, 0) + lifted
        gate, active = silu_parts(updated)
        read = read_ref[...]
        energy = jnp.sum(read * active, axis=1, keepdims=True)
        lane = lax.broadcasted_iota(jnp.int32, (rows, sz.c), 1)
        energy = around(jnp.where(lane == 3, energy, 0.0), rows // 2)
        upstream = [seed_ref[...] * read * (gate + updated * gate * (1.0 - gate))]
        moved = backward(
            upstream, pooled, refs, hot_ref, hot_t_ref, geo_ref, zero_ref, one_ref, two_ref, sz, rows, True, outs
        )
        send_back(moved + energy, outs, sz)


def backward_kernel(
    tick, sz, up_low_ref, up_high_ref, pooled_ref, low_ref, high_ref, hot_ref, hot_t_ref, geo_ref,
    zero_ref, one_ref, two_ref, *outs
):
    @pl.when(lax.axis_index("segment") == tick)
    def _():
        rows = low_ref.shape[1]
        refs = (low_ref, high_ref)
        upstream = [up_low_ref[k].astype(F32) + up_high_ref[k].astype(F32) for k in range(sz.coefs)]
        pooled = [pooled_ref[k] for k in range(sz.coefs)]
        moved = backward(
            upstream, pooled, refs, hot_ref, hot_t_ref, geo_ref, zero_ref, one_ref, two_ref, sz, rows, False,
            outs if tick else None,
        )
        carried = decode(up_low_ref[sz.coefs].astype(F32)) + decode(up_high_ref[sz.coefs].astype(F32))
        moved = moved + around(carried, rows // 2)
        if tick:
            send_back(moved, outs, sz)
        else:
            share(moved, outs)


def call(body, operands, shapes, name, spaces=None, scratch=(), aliases=None):
    spaces = spaces or [pltpu.VMEM] * len(operands)
    operands = [pltpu.with_memory_space_constraint(value, space) for value, space in zip(operands, spaces)]
    return pl.pallas_call(
        body,
        out_shape=shapes,
        in_specs=[pl.BlockSpec(memory_space=space) for space in spaces],
        out_specs=[pl.BlockSpec(memory_space=pltpu.VMEM) for _ in shapes],
        scratch_shapes=list(scratch),
        input_output_aliases=aliases or {},
        compiler_params=pltpu.CompilerParams(vmem_limit_bytes=VMEM_LIMIT),
        name=name,
    )(*operands)


def on_device(
    node_states,
    species,
    species_table,
    places,
    sources,
    radial_rate,
    zero_weight,
    one_weight,
    two_weight,
    read_weight,
    energy_grad,
):
    segments = lax.axis_size("segment")
    slabs = lax.axis_size("space")
    batches, per_slab = species.shape
    coefs, channels = node_states.shape[2:]
    neighbours = sources.shape[2]
    rows = batches * per_slab
    edges = rows * neighbours
    sz = Sizes(zero_weight.shape, one_weight.shape, two_weight.shape, channels)
    axes = ("segment", "space")
    shape = jax.ShapeDtypeStruct

    def within(value, target, count):
        pairs = [(s * slabs + i, s * slabs + target(s % 2, i) % slabs) for s in range(count) for i in range(slabs)]
        return lax.ppermute(value, axes, pairs)

    def hop(value, start, stop, by):
        pairs = [(start * slabs + i, stop * slabs + (i + by) % slabs) for i in range(slabs)]
        return lax.ppermute(value, axes, pairs)

    raw = [
        node_states.transpose(0, 2, 1, 3), places.transpose(1, 0, 2), species, sources, energy_grad, species_table,
    ]
    packed = shape((coefs + 1, per_slab, channels), BF16)
    mine, other = call(
        pack_kernel, raw, [packed, packed], "pack", [pltpu.HBM] * len(raw),
        [pltpu.VMEM(v.shape, v.dtype) for v in raw] + [pltpu.SemaphoreType.DMA((len(raw),))],
    )
    partner = within(other, lambda odd, i: i + 1 - 2 * (i % 2), segments)
    straight = within(mine, lambda odd, i: i - 2 if odd or i % 2 == 0 else i + 2, segments)
    cross = within(other, lambda odd, i: i - 1 if i % 2 == 0 else i - 3 if odd else i + 1, segments)
    stored = [zero_weight[0], one_weight[0], two_weight[0]]
    spaces = [pltpu.HBM] * 3
    on_chip = [pltpu.VMEM(w.shape, w.dtype) for w in stored]
    sems = [pltpu.SemaphoreType.DMA((5,))]
    weights = call(functools.partial(stage_kernel, False), stored, on_chip, "stage", spaces, sems)
    whole = shape((coefs, rows, channels), BF16)
    low, high, hot, hot_t, geo, seeds = call(
        functools.partial(open_kernel, slabs, neighbours),
        [mine, partner, straight, cross, radial_rate],
        [
            whole, whole, shape((edges, 2 * rows), BF16), shape((2 * rows, edges), BF16),
            shape((10 * edges, channels), F32), shape((rows, channels), F32),
        ],
        "open",
    )
    weights = call(
        functools.partial(stage_kernel, True), [*stored, *weights, seeds], on_chip, "stage_late",
        spaces + [pltpu.VMEM] * 4, sems, {3: 0, 4: 1, 5: 2},
    )
    around_all = [(low, high)]
    kept = []
    for tick in range(segments - 1):
        out, pooled = call(
            functools.partial(forward_kernel, tick, sz),
            [*around_all[tick], hot, geo, *weights],
            [whole, shape((coefs, rows, channels), F32)],
            "forward",
        )
        kept.append(pooled)
        ways = (2, 0) if tick % 2 else (0, -2)
        around_all.append(tuple(hop(out, tick, tick + 1, by) for by in ways))
    final = segments - 1
    whole_more = shape((coefs + 1, rows, channels), BF16)
    slab_sums = shape((per_slab, channels), F32)
    parts = call(
        functools.partial(turn_kernel, final, sz),
        [*around_all[final], hot, hot_t, geo, *weights, read_weight.reshape(1, channels), seeds],
        [whole_more, whole_more],
        "turn",
    )
    for tick in reversed(range(segments - 1)):
        ways = (2, 0) if tick % 2 else (0, -2)
        up = [hop(part, tick + 1, tick, -by) for part, by in zip(parts, ways)]
        parts = call(
            functools.partial(backward_kernel, tick, sz),
            [*up, kept[tick], *around_all[tick], hot, hot_t, geo, *weights],
            [whole_more, whole_more] if tick else [slab_sums] * 4,
            "backward",
        )
    here, theirs, straight, cross = parts
    theirs = within(theirs, lambda odd, i: i + 1 - 2 * (i % 2), 1)
    straight = within(straight, lambda odd, i: i - 2 if i % 2 else i + 2, 1)
    cross = within(cross, lambda odd, i: i + 1 if i % 2 else i - 1, 1)
    (both,) = call(join_kernel, [here, theirs, straight, cross], [shape((rows, channels), F32)], "join")
    copies = [both] + [hop(both, 0, stop, 0) for stop in range(1, segments)]
    energies, gradients = call(
        close_kernel, copies, [shape((batches, per_slab), F32), shape((3, batches, per_slab), F32)], "close"
    )
    return energies, gradients.transpose(1, 0, 2)


def solution(mesh):
    in_specs = (
        P(None, "space", None, None),
        P(None, "space"),
        P(),
        P(None, None, "space"),
        P(None, "space", None),
        P("segment", None),
        P("segment", None, None),
        P("segment", None, None, None),
        P("segment", None, None, None),
        P(),
        P(None, "space"),
    )
    out_specs = (P(None, "space"), P(None, None, "space"))
    return jax.shard_map(
        on_device, mesh=mesh, in_specs=in_specs, out_specs=out_specs, check_vma=False
    )
```

```python
import functools

import jax
import jax.numpy as jnp
from jax import lax
from jax.experimental import pallas as pl
from jax.experimental.pallas import tpu as pltpu
from jax.sharding import PartitionSpec as P

SLAB_DEPTH = 2.0
F32 = jnp.float32
BF16 = jnp.bfloat16
VMEM_LIMIT = 16 * 1024 * 1024

MID, LOW, SOURCES = 32, 64, 96
BASE = 256


def split(value):
    high = value.astype(BF16)
    low = (value - high.astype(F32)).astype(BF16)
    return high, low


def split3(value):
    high = value.astype(BF16)
    rest = value - high.astype(F32)
    mid = rest.astype(BF16)
    return high, mid, (rest - mid.astype(F32)).astype(BF16)


def encode(value):
    high, mid, low = split3(value)
    return high.astype(F32) + pltpu.roll(mid.astype(F32), MID, 1) + pltpu.roll(low.astype(F32), LOW, 1)


def decode(value):
    lanes = value.shape[1]
    whole = value + pltpu.roll(value, lanes - MID, 1) + pltpu.roll(value, lanes - LOW, 1)
    lane = lax.broadcasted_iota(jnp.int32, value.shape, 1)
    return jnp.where(lane < 4, whole, 0.0)


def dot(a, b):
    return lax.dot_general(a, b, (((1,), (0,)), ((), ())), preferred_element_type=F32)


def dot_t(a, b):
    return lax.dot_general(a, b, (((1,), (1,)), ((), ())), preferred_element_type=F32)


def fine_dot(value, weights, product):
    rows = value.shape[0]
    stacked = jnp.concatenate(split(value), axis=0)
    outs = []
    for weight in weights:
        out = product(stacked, weight)
        outs.append(out[:rows] + out[rows:])
    return outs


def silu_parts(value):
    gate = 1.0 / (1.0 + jnp.exp(-value))
    return gate, value * gate


class Sizes:
    def __init__(self, zero_shape, one_shape, two_shape, channels):
        self.c = channels
        self.zero = zero_shape[-1] // channels
        self.one = one_shape[-1] // channels
        self.two = two_shape[-1] // channels
        self.coefs = self.zero + 2 * (self.one + self.two)
        self.starts = (self.zero, self.zero + 2 * self.one)
        self.counts = (self.one, self.two)

    def cols(self, first, count=1):
        return slice(first * self.c, (first + count) * self.c)


def picked_group(refs, hot, first, count):
    blocks = [jnp.concatenate([ref[k] for ref in refs], axis=0) for k in range(first, first + count)]
    return dot(hot, jnp.concatenate(blocks, axis=1))


def own_rows(refs, k):
    low, high = (ref[k].astype(F32) for ref in refs)
    slab = low.shape[0] // 2
    return jnp.concatenate([low[slab:], high[:slab]], axis=0)


def pool(value, rows):
    total = value[:rows]
    for start in range(rows, value.shape[0], rows):
        total = total + value[start : start + rows]
    return total


def geo_at(geo_ref, which, edges):
    return geo_ref[which * edges : (which + 1) * edges, :]


def forward(refs, hot_ref, geo_ref, zero_ref, one_ref, two_ref, sz, rows, last):
    hot = hot_ref[...]
    edges = hot.shape[0]
    factor = (edges // rows) ** (-0.5)
    radial = geo_at(geo_ref, 0, edges)

    def scaled(block):
        return (block * radial).astype(BF16).astype(F32)

    pooled = [None] * sz.coefs
    group = picked_group(refs, hot, 0, sz.zero)
    zin = jnp.concatenate(
        [pool(scaled(group[:, sz.cols(k)]), rows) for k in range(sz.zero)], axis=1
    )
    kept = 1 if last else sz.zero
    (zout,) = fine_dot(zin, [zero_ref[:, sz.cols(0, kept)]], dot)
    for k in range(kept):
        pooled[k] = zout[:, sz.cols(k)] * factor
    for order in range(2):
        first, count = sz.starts[order], sz.counts[order]
        weight_ref = (one_ref, two_ref)[order]
        cos = geo_at(geo_ref, 1 + 2 * order, edges)
        sin = geo_at(geo_ref, 2 + 2 * order, edges)
        group = picked_group(refs, hot, first, 2 * count)
        res, ims = [], []
        for k in range(count):
            re = scaled(group[:, sz.cols(k)])
            im = scaled(group[:, sz.cols(count + k)])
            res.append(pool(cos * re - sin * im, rows))
            ims.append(pool(sin * re + cos * im, rows))
        both = jnp.concatenate(
            [jnp.concatenate(res, axis=1), jnp.concatenate(ims, axis=1)], axis=0
        )
        a, b = fine_dot(both, [weight_ref[0], weight_ref[1]], dot)
        out_re = (a[:rows] - b[rows:]) * factor
        out_im = (b[:rows] + a[rows:]) * factor
        for k in range(count):
            pooled[first + k] = out_re[:, sz.cols(k)]
            pooled[first + count + k] = out_im[:, sz.cols(k)]
    return pooled


def signal_of(pooled, sz):
    total = pooled[0]
    for k in range(sz.zero, sz.coefs):
        total = total + pooled[k] * pooled[k]
    return total


def backward(
    upstream, pooled, refs, hot_ref, hot_t_ref, geo_ref, zero_ref, one_ref, two_ref, sz, rows, last, outs
):
    hot = hot_ref[...]
    hot_t = hot_t_ref[...]
    edges = hot.shape[0]
    slab = rows // 2
    factor = (edges // rows) ** (-0.5)
    signal = signal_of(pooled, sz)
    gate, _ = silu_parts(signal)
    slope = gate * (1.0 - gate)
    d_signal = upstream[0] * (gate + signal * slope)
    if not last:
        inner = upstream[1] * pooled[1]
        for k in range(2, sz.coefs):
            inner = inner + upstream[k] * pooled[k]
        d_signal = d_signal + inner * slope
    d_pooled = [d_signal * factor]
    for k in range(1, sz.coefs):
        if last:
            d_pooled.append(2.0 * factor * d_signal * pooled[k] if k >= sz.zero else None)
        else:
            term = gate * upstream[k]
            if k >= sz.zero:
                term = term + 2.0 * d_signal * pooled[k]
            d_pooled.append(term * factor)

    radial = geo_at(geo_ref, 0, edges)
    kept = 1 if last else sz.zero
    (dz,) = fine_dot(jnp.concatenate(d_pooled[:kept], axis=1), [zero_ref[:, sz.cols(0, kept)]], dot_t)

    def spread(block):
        return jnp.concatenate([block] * (edges // rows), axis=0)

    def scatter(first, blocks):
        if outs is None:
            return
        high, low = split(jnp.concatenate(blocks, axis=1))
        back = dot(hot_t, high) + dot(hot_t, low)
        for n in range(len(blocks)):
            k = first + n
            part = back[:, sz.cols(n)]
            if not last or k == 0:
                part = part + around(upstream[k], slab)
            outs[0][k] = part[:rows].astype(BF16)
            outs[1][k] = part[rows:].astype(BF16)

    q_len = jnp.zeros((edges, sz.c), F32)
    group = picked_group(refs, hot, 0, sz.zero)
    blocks = []
    for k in range(sz.zero):
        grad = spread(dz[:, sz.cols(k)])
        q_len = q_len + grad * group[:, sz.cols(k)]
        blocks.append(grad * radial)
    q_len = q_len * radial
    scatter(0, blocks)
    q_turn = []
    for order in range(2):
        first, count = sz.starts[order], sz.counts[order]
        weight_ref = (one_ref, two_ref)[order]
        cos = geo_at(geo_ref, 1 + 2 * order, edges)
        sin = geo_at(geo_ref, 2 + 2 * order, edges)
        both = jnp.concatenate(
            [
                jnp.concatenate(d_pooled[first : first + count], axis=1),
                jnp.concatenate(d_pooled[first + count : first + 2 * count], axis=1),
            ],
            axis=0,
        )
        a, b = fine_dot(both, [weight_ref[0], weight_ref[1]], dot_t)
        d_re = a[:rows] + b[rows:]
        d_im = a[rows:] - b[:rows]
        group = picked_group(refs, hot, first, 2 * count)
        q_cos = jnp.zeros((edges, sz.c), F32)
        q_sin = jnp.zeros((edges, sz.c), F32)
        cos_r = cos * radial
        sin_r = sin * radial
        blocks_re, blocks_im = [], []
        for k in range(count):
            re = group[:, sz.cols(k)]
            im = group[:, sz.cols(count + k)]
            g_re = spread(d_re[:, sz.cols(k)])
            g_im = spread(d_im[:, sz.cols(k)])
            q_cos = q_cos + (re * g_re + im * g_im)
            q_sin = q_sin + (re * g_im - im * g_re)
            if outs is not None:
                blocks_re.append(cos_r * g_re + sin_r * g_im)
                blocks_im.append(cos_r * g_im - sin_r * g_re)
        scatter(first, blocks_re + blocks_im)
        q_cos = q_cos * radial
        q_sin = q_sin * radial
        q_len = q_len + cos * q_cos + sin * q_sin
        q_turn.append((q_cos, q_sin))

    rate = geo_at(geo_ref, 9, edges)

    def total(value):
        return jnp.sum(value, axis=1, keepdims=True)

    d_len = -total(q_len * rate)
    (dc1, ds1), (dc2, ds2) = [(total(a), total(b)) for a, b in q_turn]
    c1, s1 = geo_at(geo_ref, 1, edges), geo_at(geo_ref, 2, edges)
    ux, uy, uz = (geo_at(geo_ref, 5 + n, edges) for n in range(3))
    inv_planar = geo_at(geo_ref, 8, edges)
    dc1 = dc1 + 2.0 * (c1 * dc2 + s1 * ds2)
    ds1 = ds1 + 2.0 * (c1 * ds2 - s1 * dc2)
    along = c1 * dc1 + s1 * ds1
    dx = (dc1 - along * c1) * inv_planar + d_len * ux
    dy = (ds1 - along * s1) * inv_planar + d_len * uy
    dz_ = d_len * uz
    lane = lax.broadcasted_iota(jnp.int32, (edges, sz.c), 1)
    change = jnp.where(lane == 0, dx, jnp.where(lane == 1, dy, jnp.where(lane == 2, dz_, 0.0)))
    moved = sum(dot(hot_t, part) for part in split3(change))
    return moved - around(pool(change, rows), slab)


def around(own, slab):
    edge = jnp.zeros((slab, own.shape[1]), F32)
    return jnp.concatenate([edge, own, edge], axis=0)


def first_slab(slabs):
    slab_now = lax.axis_index("space")
    batch = lax.rem(slab_now, 2)
    shift = lax.rem(lax.axis_index("segment"), 2)
    return lax.rem(slab_now - batch + shift - 1 + slabs, slabs), batch


def send_back(moved, outs, sz):
    rows = moved.shape[0] // 2
    coded = encode(moved).astype(BF16)
    outs[0][sz.coefs] = coded[:rows]
    outs[1][sz.coefs] = coded[rows:]


def share(moved, outs):
    slab = moved.shape[0] // 4
    left, low, high, right = (moved[n * slab : (n + 1) * slab] for n in range(4))
    even = lax.rem(lax.axis_index("space"), 2) == 0
    outs[0][...] = jnp.where(even, low, high)
    outs[1][...] = jnp.where(even, high, low)
    outs[2][...] = jnp.where(even, right, left)
    outs[3][...] = jnp.where(even, left, right)


def join_kernel(here_ref, theirs_ref, straight_ref, cross_ref, both_ref):
    slab = here_ref.shape[0]
    even = lax.rem(lax.axis_index("space"), 2) == 0
    here = here_ref[...] + straight_ref[...]
    there = theirs_ref[...] + cross_ref[...]
    both_ref[:slab, :] = jnp.where(even, here, there)
    both_ref[slab:, :] = jnp.where(even, there, here)


def close_kernel(*refs):
    *sums_refs, energies_ref, places_ref = refs
    slab = energies_ref.shape[1]
    for n, ref in enumerate(sums_refs):

        @pl.when(lax.axis_index("segment") == n)
        def _(ref=ref):
            sums = ref[...]
            rows, c = sums.shape
            turned = jnp.transpose(jnp.concatenate([sums, jnp.zeros((c - rows, c), F32)], axis=0))
            for b in range(2):
                energies_ref[b : b + 1, :] = turned[3:4, b * slab : (b + 1) * slab]
                for n in range(3):
                    places_ref[n, b : b + 1, :] = turned[n : n + 1, b * slab : (b + 1) * slab]


def pack_kernel(
    node_hbm, places_hbm, species_hbm, sources_hbm, grad_hbm, table_hbm, mine_ref, other_ref,
    states, places, species, sources, grads, table, sems
):
    slab_now = lax.axis_index("space")
    batch = lax.rem(slab_now, 2)
    copies = []
    pairs = (
        (node_hbm, states), (places_hbm, places), (species_hbm, species), (sources_hbm, sources),
        (grad_hbm, grads), (table_hbm, table),
    )
    for n, (source, target) in enumerate(pairs):
        copies.append(pltpu.make_async_copy(source, target, sems.at[n]))
        copies[-1].start()
    for copy in copies:
        copy.wait()
    coefs, per_slab, c = states.shape[1:]
    lane = lax.broadcasted_iota(jnp.int32, (per_slab, c), 1)
    eye = (
        lax.broadcasted_iota(jnp.int32, (per_slab, per_slab), 0)
        == lax.broadcasted_iota(jnp.int32, (per_slab, per_slab), 1)
    )

    def column(row):
        return jnp.sum(jnp.where(eye, jnp.broadcast_to(row, (per_slab, per_slab)), 0.0), axis=1, keepdims=True)

    both = []
    for b in range(2):
        names = column(species[b : b + 1, :].astype(F32)).astype(jnp.int32)
        kinds = table.shape[0]
        hot = (names == lax.broadcasted_iota(jnp.int32, (per_slab, kinds), 1)).astype(BF16)
        first = (states[b, 0].astype(F32) + dot(hot, table[...])).astype(BF16)
        extra = jnp.zeros((per_slab, c), F32)
        for n in range(3):
            extra = jnp.where(lane == n, column(places[n, b : b + 1, :]), extra)
        extra = encode(jnp.where(lane == 3, column(grads[b : b + 1, :]), extra))
        for j in range(sources.shape[2]):
            index = sources[b, :, j : j + 1]
            extra = jnp.where(lane == SOURCES + j, (index // BASE).astype(F32), extra)
            extra = jnp.where(lane == SOURCES + 8 + j, (index % BASE).astype(F32), extra)
        both.append((first, extra.astype(BF16)))
    for ref, chosen in ((mine_ref, batch), (other_ref, 1 - batch)):
        ref[pl.ds(0, coefs)] = states[chosen]
        ref[0] = jnp.where(chosen == 0, both[0][0].astype(F32), both[1][0].astype(F32)).astype(BF16)
        ref[coefs] = jnp.where(chosen == 0, both[0][1].astype(F32), both[1][1].astype(F32)).astype(BF16)


def open_kernel(
    slabs, neighbours, mine_ref, partner_ref, straight_ref, cross_ref, rate_ref,
    low_ref, high_ref, hot_ref, hot_t_ref, geo_ref, seed_ref
):
    start, batch = first_slab(slabs)
    even = batch == 0
    level = lax.rem(lax.axis_index("segment"), 2) == 0
    coefs = low_ref.shape[0]
    rows, c = low_ref.shape[1:]
    per_slab = rows // 2
    window = 2 * rows
    edges = rows * neighbours

    def choose(a, b):
        return jnp.where(even, a, b)

    def parts(k):
        mine, partner = mine_ref[k].astype(F32), partner_ref[k].astype(F32)
        straight, cross = straight_ref[k].astype(F32), cross_ref[k].astype(F32)
        low, high = choose(mine, partner), choose(partner, mine)
        after, last = choose(straight, cross), choose(cross, straight)
        return [
            jnp.where(level, last, low), jnp.where(level, low, high), jnp.where(level, high, after),
            jnp.where(level, after, last),
        ]

    @pl.when(lax.axis_index("segment") == 0)
    def _():
        for k in range(coefs):
            slab = parts(k)
            low_ref[k] = jnp.concatenate(slab[:2], axis=0).astype(BF16)
            high_ref[k] = jnp.concatenate(slab[2:], axis=0).astype(BF16)

    extra = jnp.concatenate(parts(coefs), axis=0)
    numbers = decode(extra)
    seed_ref[...] = jnp.broadcast_to(numbers[per_slab : per_slab + rows, 3:4], (rows, c))
    own_extra = extra[per_slab : per_slab + rows]
    low = pltpu.roll(own_extra, c - 8, 1)
    index = own_extra.astype(jnp.int32) * BASE + low.astype(jnp.int32)
    place = lax.rem(index // per_slab - start + slabs, slabs) * per_slab + index % per_slab
    columns = lax.broadcasted_iota(jnp.int32, (rows, c), 1)
    hot = jnp.concatenate(
        [
            (place[:, SOURCES + j : SOURCES + j + 1] == columns).astype(F32)
            for j in range(neighbours)
        ],
        axis=0,
    )
    hot_ref[...] = hot.astype(BF16)[:, :window]
    hot_t_ref[...] = jnp.transpose(hot).astype(BF16)[:window]
    hot = hot.astype(BF16)[:, :window]
    lift = lax.broadcasted_iota(jnp.int32, (window, c), 0) // per_slab - 1
    offset = []
    for n in range(3):
        column = jnp.broadcast_to(numbers[:, n : n + 1], (window, c))
        if n == 2:
            column = column + SLAB_DEPTH * lift.astype(F32)
        there = sum(dot(hot, part) for part in split3(column))
        offset.append(there - jnp.concatenate([column[per_slab : per_slab + rows]] * neighbours, axis=0))
    flat = offset[0] * offset[0] + offset[1] * offset[1] + 1.0
    length = jnp.sqrt(flat + offset[2] * offset[2])
    planar = jnp.sqrt(flat)
    c1, s1 = offset[0] / planar, offset[1] / planar
    rate = jnp.broadcast_to(rate_ref[...], (edges, c))
    values = [
        jnp.exp(-rate * length),
        c1,
        s1,
        c1 * c1 - s1 * s1,
        2.0 * c1 * s1,
        offset[0] / length,
        offset[1] / length,
        offset[2] / length,
        1.0 / planar,
        rate,
    ]
    for n, value in enumerate(values):
        geo_ref[n * edges : (n + 1) * edges, :] = value


def turn_to_stage():
    odd = lax.rem(lax.axis_index("space"), 2)
    return jnp.where(lax.axis_index("segment") == 0, odd, 2)


def stage_kernel(moment, zero_hbm, one_hbm, two_hbm, *more):
    zero_ref, one_ref, two_ref, sems = more[-4:]

    @pl.when(turn_to_stage() == moment)
    def _():
        pairs = [(zero_hbm, zero_ref)]
        for source, target in ((one_hbm, one_ref), (two_hbm, two_ref)):
            pairs += [(source.at[n], target.at[n]) for n in range(2)]
        copies = [pltpu.make_async_copy(source, target, sems.at[n]) for n, (source, target) in enumerate(pairs)]
        for copy in copies:
            copy.start()
        for copy in copies:
            copy.wait()


def forward_kernel(
    tick, sz, low_ref, high_ref, hot_ref, geo_ref, zero_ref, one_ref, two_ref, out_ref, pooled_ref
):
    @pl.when(lax.axis_index("segment") == tick)
    def _():
        rows = low_ref.shape[1]
        refs = (low_ref, high_ref)
        pooled = forward(refs, hot_ref, geo_ref, zero_ref, one_ref, two_ref, sz, rows, False)
        signal = signal_of(pooled, sz)
        gate, lifted = silu_parts(signal)
        for k in range(sz.coefs):
            pooled_ref[k] = pooled[k]
            added = lifted if k == 0 else gate * pooled[k]
            out_ref[k] = (own_rows(refs, k) + added).astype(BF16)


def turn_kernel(
    tick, sz, low_ref, high_ref, hot_ref, hot_t_ref, geo_ref, zero_ref, one_ref, two_ref,
    read_ref, seed_ref, *outs
):
    @pl.when(lax.axis_index("segment") == tick)
    def _():
        rows = low_ref.shape[1]
        refs = (low_ref, high_ref)
        pooled = forward(refs, hot_ref, geo_ref, zero_ref, one_ref, two_ref, sz, rows, True)
        signal = signal_of(pooled, sz)
        _, lifted = silu_parts(signal)
        updated = own_rows(refs, 0) + lifted
        gate, active = silu_parts(updated)
        read = read_ref[...]
        energy = jnp.sum(read * active, axis=1, keepdims=True)
        lane = lax.broadcasted_iota(jnp.int32, (rows, sz.c), 1)
        energy = around(jnp.where(lane == 3, energy, 0.0), rows // 2)
        upstream = [seed_ref[...] * read * (gate + updated * gate * (1.0 - gate))]
        moved = backward(
            upstream, pooled, refs, hot_ref, hot_t_ref, geo_ref, zero_ref, one_ref, two_ref, sz, rows, True, outs
        )
        send_back(moved + energy, outs, sz)


def backward_kernel(
    tick, sz, up_low_ref, up_high_ref, pooled_ref, low_ref, high_ref, hot_ref, hot_t_ref, geo_ref,
    zero_ref, one_ref, two_ref, *outs
):
    @pl.when(lax.axis_index("segment") == tick)
    def _():
        rows = low_ref.shape[1]
        refs = (low_ref, high_ref)
        upstream = [up_low_ref[k].astype(F32) + up_high_ref[k].astype(F32) for k in range(sz.coefs)]
        pooled = [pooled_ref[k] for k in range(sz.coefs)]
        moved = backward(
            upstream, pooled, refs, hot_ref, hot_t_ref, geo_ref, zero_ref, one_ref, two_ref, sz, rows, False,
            outs if tick else None,
        )
        carried = decode(up_low_ref[sz.coefs].astype(F32)) + decode(up_high_ref[sz.coefs].astype(F32))
        moved = moved + around(carried, rows // 2)
        if tick:
            send_back(moved, outs, sz)
        else:
            share(moved, outs)


def call(body, operands, shapes, name, spaces=None, scratch=(), aliases=None):
    spaces = spaces or [pltpu.VMEM] * len(operands)
    operands = [pltpu.with_memory_space_constraint(value, space) for value, space in zip(operands, spaces)]
    return pl.pallas_call(
        body,
        out_shape=shapes,
        in_specs=[pl.BlockSpec(memory_space=space) for space in spaces],
        out_specs=[pl.BlockSpec(memory_space=pltpu.VMEM) for _ in shapes],
        scratch_shapes=list(scratch),
        input_output_aliases=aliases or {},
        compiler_params=pltpu.CompilerParams(vmem_limit_bytes=VMEM_LIMIT),
        name=name,
    )(*operands)


def on_device(
    node_states,
    species,
    species_table,
    places,
    sources,
    radial_rate,
    zero_weight,
    one_weight,
    two_weight,
    read_weight,
    energy_grad,
):
    segments = lax.axis_size("segment")
    slabs = lax.axis_size("space")
    batches, per_slab = species.shape
    coefs, channels = node_states.shape[2:]
    neighbours = sources.shape[2]
    rows = batches * per_slab
    edges = rows * neighbours
    sz = Sizes(zero_weight.shape, one_weight.shape, two_weight.shape, channels)
    axes = ("segment", "space")
    shape = jax.ShapeDtypeStruct

    def within(value, target, count):
        pairs = [(s * slabs + i, s * slabs + target(s % 2, i) % slabs) for s in range(count) for i in range(slabs)]
        return lax.ppermute(value, axes, pairs)

    def hop(value, start, stop, by):
        pairs = [(start * slabs + i, stop * slabs + (i + by) % slabs) for i in range(slabs)]
        return lax.ppermute(value, axes, pairs)

    raw = [
        node_states.transpose(0, 2, 1, 3), places.transpose(1, 0, 2), species, sources, energy_grad, species_table,
    ]
    packed = shape((coefs + 1, per_slab, channels), BF16)
    mine, other = call(
        pack_kernel, raw, [packed, packed], "pack", [pltpu.HBM] * len(raw),
        [pltpu.VMEM(v.shape, v.dtype) for v in raw] + [pltpu.SemaphoreType.DMA((len(raw),))],
    )
    partner = within(other, lambda odd, i: i + 1 - 2 * (i % 2), segments)
    straight = within(mine, lambda odd, i: i - 2 if odd or i % 2 == 0 else i + 2, segments)
    cross = within(other, lambda odd, i: i - 1 if i % 2 == 0 else i - 3 if odd else i + 1, segments)
    stored = [zero_weight[0], one_weight[0], two_weight[0]]
    spaces = [pltpu.HBM] * 3
    on_chip = [pltpu.VMEM(w.shape, w.dtype) for w in stored]
    sems = [pltpu.SemaphoreType.DMA((5,))]
    weights = call(functools.partial(stage_kernel, 0), stored, on_chip, "stage", spaces, sems)
    whole = shape((coefs, rows, channels), BF16)
    low, high, hot, hot_t, geo, seeds = call(
        functools.partial(open_kernel, slabs, neighbours),
        [mine, partner, straight, cross, radial_rate],
        [
            whole, whole, shape((edges, 2 * rows), BF16), shape((2 * rows, edges), BF16),
            shape((10 * edges, channels), F32), shape((rows, channels), F32),
        ],
        "open",
    )

    def stage_more(moment, weights, after):
        return call(
            functools.partial(stage_kernel, moment), [*stored, *weights, after], on_chip, "stage",
            spaces + [pltpu.VMEM] * 4, sems, {3: 0, 4: 1, 5: 2},
        )

    weights = stage_more(1, weights, seeds)
    around_all = [(low, high)]
    kept = []
    for tick in range(segments - 1):
        out, pooled = call(
            functools.partial(forward_kernel, tick, sz),
            [*around_all[tick], hot, geo, *weights],
            [whole, shape((coefs, rows, channels), F32)],
            "forward",
        )
        kept.append(pooled)
        if tick == 0:
            weights = stage_more(2, weights, out)
        ways = (2, 0) if tick % 2 else (0, -2)
        around_all.append(tuple(hop(out, tick, tick + 1, by) for by in ways))
    final = segments - 1
    whole_more = shape((coefs + 1, rows, channels), BF16)
    slab_sums = shape((per_slab, channels), F32)
    parts = call(
        functools.partial(turn_kernel, final, sz),
        [*around_all[final], hot, hot_t, geo, *weights, read_weight.reshape(1, channels), seeds],
        [whole_more, whole_more],
        "turn",
    )
    for tick in reversed(range(segments - 1)):
        ways = (2, 0) if tick % 2 else (0, -2)
        up = [hop(part, tick + 1, tick, -by) for part, by in zip(parts, ways)]
        parts = call(
            functools.partial(backward_kernel, tick, sz),
            [*up, kept[tick], *around_all[tick], hot, hot_t, geo, *weights],
            [whole_more, whole_more] if tick else [slab_sums] * 4,
            "backward",
        )
    here, theirs, straight, cross = parts
    theirs = within(theirs, lambda odd, i: i + 1 - 2 * (i % 2), 1)
    straight = within(straight, lambda odd, i: i - 2 if i % 2 else i + 2, 1)
    cross = within(cross, lambda odd, i: i + 1 if i % 2 else i - 1, 1)
    (both,) = call(join_kernel, [here, theirs, straight, cross], [shape((rows, channels), F32)], "join")
    copies = [both] + [hop(both, 0, stop, 0) for stop in range(1, segments)]
    energies, gradients = call(
        close_kernel, copies, [shape((batches, per_slab), F32), shape((3, batches, per_slab), F32)], "close"
    )
    return energies, gradients.transpose(1, 0, 2)


def solution(mesh):
    in_specs = (
        P(None, "space", None, None),
        P(None, "space"),
        P(),
        P(None, None, "space"),
        P(None, "space", None),
        P("segment", None),
        P("segment", None, None),
        P("segment", None, None, None),
        P("segment", None, None, None),
        P(),
        P(None, "space"),
    )
    out_specs = (P(None, "space"), P(None, None, "space"))
    return jax.shard_map(
        on_device, mesh=mesh, in_specs=in_specs, out_specs=out_specs, check_vma=False
    )
```

```python
import functools

import jax
import jax.numpy as jnp
from jax import lax
from jax.experimental import pallas as pl
from jax.experimental.pallas import tpu as pltpu
from jax.sharding import PartitionSpec as P

SLAB_DEPTH = 2.0
F32 = jnp.float32
BF16 = jnp.bfloat16
VMEM_LIMIT = 16 * 1024 * 1024

MID, LOW, SOURCES = 32, 64, 96
BASE = 256


def split(value):
    high = value.astype(BF16)
    low = (value - high.astype(F32)).astype(BF16)
    return high, low


def split3(value):
    high = value.astype(BF16)
    rest = value - high.astype(F32)
    mid = rest.astype(BF16)
    return high, mid, (rest - mid.astype(F32)).astype(BF16)


def encode(value):
    high, mid, low = split3(value)
    return high.astype(F32) + pltpu.roll(mid.astype(F32), MID, 1) + pltpu.roll(low.astype(F32), LOW, 1)


def decode(value):
    lanes = value.shape[1]
    whole = value + pltpu.roll(value, lanes - MID, 1) + pltpu.roll(value, lanes - LOW, 1)
    lane = lax.broadcasted_iota(jnp.int32, value.shape, 1)
    return jnp.where(lane < 4, whole, 0.0)


def dot(a, b):
    return lax.dot_general(a, b, (((1,), (0,)), ((), ())), preferred_element_type=F32)


def dot_t(a, b):
    return lax.dot_general(a, b, (((1,), (1,)), ((), ())), preferred_element_type=F32)


def fine_dot(value, weights, product):
    rows = value.shape[0]
    stacked = jnp.concatenate(split(value), axis=0)
    outs = []
    for weight in weights:
        out = product(stacked, weight)
        outs.append(out[:rows] + out[rows:])
    return outs


def silu_parts(value):
    gate = 1.0 / (1.0 + jnp.exp(-value))
    return gate, value * gate


class Sizes:
    def __init__(self, zero_shape, one_shape, two_shape, channels):
        self.c = channels
        self.zero = zero_shape[-1] // channels
        self.one = one_shape[-1] // channels
        self.two = two_shape[-1] // channels
        self.coefs = self.zero + 2 * (self.one + self.two)
        self.starts = (self.zero, self.zero + 2 * self.one)
        self.counts = (self.one, self.two)

    def cols(self, first, count=1):
        return slice(first * self.c, (first + count) * self.c)


def picked_group(refs, hot, first, count):
    blocks = [jnp.concatenate([ref[k] for ref in refs], axis=0) for k in range(first, first + count)]
    return dot(hot, jnp.concatenate(blocks, axis=1))


def own_rows(refs, k):
    low, high = (ref[k].astype(F32) for ref in refs)
    slab = low.shape[0] // 2
    return jnp.concatenate([low[slab:], high[:slab]], axis=0)


def pool(value, rows):
    total = value[:rows]
    for start in range(rows, value.shape[0], rows):
        total = total + value[start : start + rows]
    return total


def geo_at(geo_ref, which, edges):
    return geo_ref[which * edges : (which + 1) * edges, :]


def forward(refs, hot_ref, geo_ref, zero_ref, one_ref, two_ref, sz, rows, last):
    hot = hot_ref[...]
    edges = hot.shape[0]
    factor = (edges // rows) ** (-0.5)
    radial = geo_at(geo_ref, 0, edges)

    def scaled(block):
        return (block * radial).astype(BF16).astype(F32)

    pooled = [None] * sz.coefs
    group = picked_group(refs, hot, 0, sz.zero)
    zin = jnp.concatenate(
        [pool(scaled(group[:, sz.cols(k)]), rows) for k in range(sz.zero)], axis=1
    )
    kept = 1 if last else sz.zero
    (zout,) = fine_dot(zin, [zero_ref[:, sz.cols(0, kept)]], dot)
    for k in range(kept):
        pooled[k] = zout[:, sz.cols(k)] * factor
    for order in range(2):
        first, count = sz.starts[order], sz.counts[order]
        weight_ref = (one_ref, two_ref)[order]
        cos = geo_at(geo_ref, 1 + 2 * order, edges)
        sin = geo_at(geo_ref, 2 + 2 * order, edges)
        group = picked_group(refs, hot, first, 2 * count)
        res, ims = [], []
        for k in range(count):
            re = scaled(group[:, sz.cols(k)])
            im = scaled(group[:, sz.cols(count + k)])
            res.append(pool(cos * re - sin * im, rows))
            ims.append(pool(sin * re + cos * im, rows))
        both = jnp.concatenate(
            [jnp.concatenate(res, axis=1), jnp.concatenate(ims, axis=1)], axis=0
        )
        a, b = fine_dot(both, [weight_ref[0], weight_ref[1]], dot)
        out_re = (a[:rows] - b[rows:]) * factor
        out_im = (b[:rows] + a[rows:]) * factor
        for k in range(count):
            pooled[first + k] = out_re[:, sz.cols(k)]
            pooled[first + count + k] = out_im[:, sz.cols(k)]
    return pooled


def signal_of(pooled, sz):
    total = pooled[0]
    for k in range(sz.zero, sz.coefs):
        total = total + pooled[k] * pooled[k]
    return total


def backward(
    upstream, pooled, refs, hot_ref, hot_t_ref, geo_ref, zero_ref, one_ref, two_ref, sz, rows, last, outs
):
    hot = hot_ref[...]
    hot_t = hot_t_ref[...]
    edges = hot.shape[0]
    slab = rows // 2
    factor = (edges // rows) ** (-0.5)
    signal = signal_of(pooled, sz)
    gate, _ = silu_parts(signal)
    slope = gate * (1.0 - gate)
    d_signal = upstream[0] * (gate + signal * slope)
    if not last:
        inner = upstream[1] * pooled[1]
        for k in range(2, sz.coefs):
            inner = inner + upstream[k] * pooled[k]
        d_signal = d_signal + inner * slope
    d_pooled = [d_signal * factor]
    for k in range(1, sz.coefs):
        if last:
            d_pooled.append(2.0 * factor * d_signal * pooled[k] if k >= sz.zero else None)
        else:
            term = gate * upstream[k]
            if k >= sz.zero:
                term = term + 2.0 * d_signal * pooled[k]
            d_pooled.append(term * factor)

    radial = geo_at(geo_ref, 0, edges)
    kept = 1 if last else sz.zero
    (dz,) = fine_dot(jnp.concatenate(d_pooled[:kept], axis=1), [zero_ref[:, sz.cols(0, kept)]], dot_t)

    def spread(block):
        return jnp.concatenate([block] * (edges // rows), axis=0)

    def scatter(first, blocks):
        if outs is None:
            return
        high, low = split(jnp.concatenate(blocks, axis=1))
        back = dot(hot_t, high) + dot(hot_t, low)
        for n in range(len(blocks)):
            k = first + n
            part = back[:, sz.cols(n)]
            if not last or k == 0:
                part = part + around(upstream[k], slab)
            outs[0][k] = part[:rows].astype(BF16)
            outs[1][k] = part[rows:].astype(BF16)

    q_len = jnp.zeros((edges, sz.c), F32)
    group = picked_group(refs, hot, 0, sz.zero)
    blocks = []
    for k in range(sz.zero):
        grad = spread(dz[:, sz.cols(k)])
        q_len = q_len + grad * group[:, sz.cols(k)]
        blocks.append(grad * radial)
    q_len = q_len * radial
    scatter(0, blocks)
    q_turn = []
    for order in range(2):
        first, count = sz.starts[order], sz.counts[order]
        weight_ref = (one_ref, two_ref)[order]
        cos = geo_at(geo_ref, 1 + 2 * order, edges)
        sin = geo_at(geo_ref, 2 + 2 * order, edges)
        both = jnp.concatenate(
            [
                jnp.concatenate(d_pooled[first : first + count], axis=1),
                jnp.concatenate(d_pooled[first + count : first + 2 * count], axis=1),
            ],
            axis=0,
        )
        a, b = fine_dot(both, [weight_ref[0], weight_ref[1]], dot_t)
        d_re = a[:rows] + b[rows:]
        d_im = a[rows:] - b[:rows]
        group = picked_group(refs, hot, first, 2 * count)
        q_cos = jnp.zeros((edges, sz.c), F32)
        q_sin = jnp.zeros((edges, sz.c), F32)
        cos_r = cos * radial
        sin_r = sin * radial
        blocks_re, blocks_im = [], []
        for k in range(count):
            re = group[:, sz.cols(k)]
            im = group[:, sz.cols(count + k)]
            g_re = spread(d_re[:, sz.cols(k)])
            g_im = spread(d_im[:, sz.cols(k)])
            q_cos = q_cos + (re * g_re + im * g_im)
            q_sin = q_sin + (re * g_im - im * g_re)
            if outs is not None:
                blocks_re.append(cos_r * g_re + sin_r * g_im)
                blocks_im.append(cos_r * g_im - sin_r * g_re)
        scatter(first, blocks_re + blocks_im)
        q_cos = q_cos * radial
        q_sin = q_sin * radial
        q_len = q_len + cos * q_cos + sin * q_sin
        q_turn.append((q_cos, q_sin))

    rate = geo_at(geo_ref, 9, edges)

    def total(value):
        return jnp.sum(value, axis=1, keepdims=True)

    d_len = -total(q_len * rate)
    (dc1, ds1), (dc2, ds2) = [(total(a), total(b)) for a, b in q_turn]
    c1, s1 = geo_at(geo_ref, 1, edges), geo_at(geo_ref, 2, edges)
    ux, uy, uz = (geo_at(geo_ref, 5 + n, edges) for n in range(3))
    inv_planar = geo_at(geo_ref, 8, edges)
    dc1 = dc1 + 2.0 * (c1 * dc2 + s1 * ds2)
    ds1 = ds1 + 2.0 * (c1 * ds2 - s1 * dc2)
    along = c1 * dc1 + s1 * ds1
    dx = (dc1 - along * c1) * inv_planar + d_len * ux
    dy = (ds1 - along * s1) * inv_planar + d_len * uy
    dz_ = d_len * uz
    lane = lax.broadcasted_iota(jnp.int32, (edges, sz.c), 1)
    change = jnp.where(lane == 0, dx, jnp.where(lane == 1, dy, jnp.where(lane == 2, dz_, 0.0)))
    moved = sum(dot(hot_t, part) for part in split3(change))
    return moved - around(pool(change, rows), slab)


def around(own, slab):
    edge = jnp.zeros((slab, own.shape[1]), F32)
    return jnp.concatenate([edge, own, edge], axis=0)


def first_slab(slabs):
    slab_now = lax.axis_index("space")
    batch = lax.rem(slab_now, 2)
    shift = lax.rem(lax.axis_index("segment"), 2)
    return lax.rem(slab_now - batch + shift - 1 + slabs, slabs), batch


def send_back(moved, outs, sz):
    rows = moved.shape[0] // 2
    coded = encode(moved).astype(BF16)
    outs[0][sz.coefs] = coded[:rows]
    outs[1][sz.coefs] = coded[rows:]


def share(moved, outs):
    slab = moved.shape[0] // 4
    left, low, high, right = (moved[n * slab : (n + 1) * slab] for n in range(4))
    even = lax.rem(lax.axis_index("space"), 2) == 0
    outs[0][...] = jnp.where(even, low, high)
    outs[1][...] = jnp.where(even, high, low)
    outs[2][...] = jnp.where(even, right, left)
    outs[3][...] = jnp.where(even, left, right)


def join_kernel(here_ref, theirs_ref, straight_ref, cross_ref, both_ref):
    slab = here_ref.shape[0]
    even = lax.rem(lax.axis_index("space"), 2) == 0
    here = here_ref[...] + straight_ref[...]
    there = theirs_ref[...] + cross_ref[...]
    both_ref[:slab, :] = jnp.where(even, here, there)
    both_ref[slab:, :] = jnp.where(even, there, here)


def close_kernel(*refs):
    *sums_refs, energies_ref, places_ref = refs
    slab = energies_ref.shape[1]
    for n, ref in enumerate(sums_refs):

        @pl.when(lax.axis_index("segment") == n)
        def _(ref=ref):
            sums = ref[...]
            rows, c = sums.shape
            turned = jnp.transpose(jnp.concatenate([sums, jnp.zeros((c - rows, c), F32)], axis=0))
            for b in range(2):
                energies_ref[b : b + 1, :] = turned[3:4, b * slab : (b + 1) * slab]
                for n in range(3):
                    places_ref[n, b : b + 1, :] = turned[n : n + 1, b * slab : (b + 1) * slab]


def pack_kernel(
    node_hbm, places_hbm, species_hbm, sources_hbm, grad_hbm, table_hbm, mine_ref, other_ref,
    states, places, species, sources, grads, table, sems
):
    slab_now = lax.axis_index("space")
    batch = lax.rem(slab_now, 2)
    copies = []
    pairs = (
        (node_hbm, states), (places_hbm, places), (species_hbm, species), (sources_hbm, sources),
        (grad_hbm, grads), (table_hbm, table),
    )
    for n, (source, target) in enumerate(pairs):
        copies.append(pltpu.make_async_copy(source, target, sems.at[n]))
        copies[-1].start()
    for copy in copies:
        copy.wait()
    coefs, per_slab, c = states.shape[1:]
    lane = lax.broadcasted_iota(jnp.int32, (per_slab, c), 1)
    eye = (
        lax.broadcasted_iota(jnp.int32, (per_slab, per_slab), 0)
        == lax.broadcasted_iota(jnp.int32, (per_slab, per_slab), 1)
    )

    def column(row):
        return jnp.sum(jnp.where(eye, jnp.broadcast_to(row, (per_slab, per_slab)), 0.0), axis=1, keepdims=True)

    both = []
    for b in range(2):
        names = column(species[b : b + 1, :].astype(F32)).astype(jnp.int32)
        kinds = table.shape[0]
        hot = (names == lax.broadcasted_iota(jnp.int32, (per_slab, kinds), 1)).astype(BF16)
        first = (states[b, 0].astype(F32) + dot(hot, table[...])).astype(BF16)
        extra = jnp.zeros((per_slab, c), F32)
        for n in range(3):
            extra = jnp.where(lane == n, column(places[n, b : b + 1, :]), extra)
        extra = encode(jnp.where(lane == 3, column(grads[b : b + 1, :]), extra))
        for j in range(sources.shape[2]):
            index = sources[b, :, j : j + 1]
            extra = jnp.where(lane == SOURCES + j, (index // BASE).astype(F32), extra)
            extra = jnp.where(lane == SOURCES + 8 + j, (index % BASE).astype(F32), extra)
        both.append((first, extra.astype(BF16)))
    for ref, chosen in ((mine_ref, batch), (other_ref, 1 - batch)):
        ref[pl.ds(0, coefs)] = states[chosen]
        ref[0] = jnp.where(chosen == 0, both[0][0].astype(F32), both[1][0].astype(F32)).astype(BF16)
        ref[coefs] = jnp.where(chosen == 0, both[0][1].astype(F32), both[1][1].astype(F32)).astype(BF16)


def open_kernel(
    slabs, neighbours, mine_ref, partner_ref, straight_ref, cross_ref, rate_ref,
    low_ref, high_ref, hot_ref, hot_t_ref, geo_ref, seed_ref
):
    start, batch = first_slab(slabs)
    even = batch == 0
    level = lax.rem(lax.axis_index("segment"), 2) == 0
    coefs = low_ref.shape[0]
    rows, c = low_ref.shape[1:]
    per_slab = rows // 2
    window = 2 * rows
    edges = rows * neighbours

    def choose(a, b):
        return jnp.where(even, a, b)

    def parts(k):
        mine, partner = mine_ref[k].astype(F32), partner_ref[k].astype(F32)
        straight, cross = straight_ref[k].astype(F32), cross_ref[k].astype(F32)
        low, high = choose(mine, partner), choose(partner, mine)
        after, last = choose(straight, cross), choose(cross, straight)
        return [
            jnp.where(level, last, low), jnp.where(level, low, high), jnp.where(level, high, after),
            jnp.where(level, after, last),
        ]

    @pl.when(lax.axis_index("segment") == 0)
    def _():
        for k in range(coefs):
            slab = parts(k)
            low_ref[k] = jnp.concatenate(slab[:2], axis=0).astype(BF16)
            high_ref[k] = jnp.concatenate(slab[2:], axis=0).astype(BF16)

    extra = jnp.concatenate(parts(coefs), axis=0)
    numbers = decode(extra)
    seed_ref[...] = jnp.broadcast_to(numbers[per_slab : per_slab + rows, 3:4], (rows, c))
    own_extra = extra[per_slab : per_slab + rows]
    low = pltpu.roll(own_extra, c - 8, 1)
    index = own_extra.astype(jnp.int32) * BASE + low.astype(jnp.int32)
    place = lax.rem(index // per_slab - start + slabs, slabs) * per_slab + index % per_slab
    columns = lax.broadcasted_iota(jnp.int32, (rows, c), 1)
    hot = jnp.concatenate(
        [
            (place[:, SOURCES + j : SOURCES + j + 1] == columns).astype(F32)
            for j in range(neighbours)
        ],
        axis=0,
    )
    hot_ref[...] = hot.astype(BF16)[:, :window]
    hot_t_ref[...] = jnp.transpose(hot).astype(BF16)[:window]
    hot = hot.astype(BF16)[:, :window]
    lift = lax.broadcasted_iota(jnp.int32, (window, c), 0) // per_slab - 1
    offset = []
    for n in range(3):
        column = jnp.broadcast_to(numbers[:, n : n + 1], (window, c))
        if n == 2:
            column = column + SLAB_DEPTH * lift.astype(F32)
        there = sum(dot(hot, part) for part in split3(column))
        offset.append(there - jnp.concatenate([column[per_slab : per_slab + rows]] * neighbours, axis=0))
    flat = offset[0] * offset[0] + offset[1] * offset[1] + 1.0
    length = jnp.sqrt(flat + offset[2] * offset[2])
    planar = jnp.sqrt(flat)
    c1, s1 = offset[0] / planar, offset[1] / planar
    rate = jnp.broadcast_to(rate_ref[...], (edges, c))
    values = [
        jnp.exp(-rate * length),
        c1,
        s1,
        c1 * c1 - s1 * s1,
        2.0 * c1 * s1,
        offset[0] / length,
        offset[1] / length,
        offset[2] / length,
        1.0 / planar,
        rate,
    ]
    for n, value in enumerate(values):
        geo_ref[n * edges : (n + 1) * edges, :] = value


def turn_to_stage():
    segment = lax.axis_index("segment")
    odd = lax.rem(lax.axis_index("space"), 2)
    return jnp.where(segment == 0, odd, jnp.where(segment == 1, 2 + odd, 2))


def stage_kernel(moment, zero_hbm, one_hbm, two_hbm, *more):
    zero_ref, one_ref, two_ref, sems = more[-4:]

    @pl.when(turn_to_stage() == moment)
    def _():
        pairs = [(zero_hbm, zero_ref)]
        for source, target in ((one_hbm, one_ref), (two_hbm, two_ref)):
            pairs += [(source.at[n], target.at[n]) for n in range(2)]
        copies = [pltpu.make_async_copy(source, target, sems.at[n]) for n, (source, target) in enumerate(pairs)]
        for copy in copies:
            copy.start()
        for copy in copies:
            copy.wait()


def forward_kernel(
    tick, sz, low_ref, high_ref, hot_ref, geo_ref, zero_ref, one_ref, two_ref, out_ref, pooled_ref
):
    @pl.when(lax.axis_index("segment") == tick)
    def _():
        rows = low_ref.shape[1]
        refs = (low_ref, high_ref)
        pooled = forward(refs, hot_ref, geo_ref, zero_ref, one_ref, two_ref, sz, rows, False)
        signal = signal_of(pooled, sz)
        gate, lifted = silu_parts(signal)
        for k in range(sz.coefs):
            pooled_ref[k] = pooled[k]
            added = lifted if k == 0 else gate * pooled[k]
            out_ref[k] = (own_rows(refs, k) + added).astype(BF16)


def turn_kernel(
    tick, sz, low_ref, high_ref, hot_ref, hot_t_ref, geo_ref, zero_ref, one_ref, two_ref,
    read_ref, seed_ref, *outs
):
    @pl.when(lax.axis_index("segment") == tick)
    def _():
        rows = low_ref.shape[1]
        refs = (low_ref, high_ref)
        pooled = forward(refs, hot_ref, geo_ref, zero_ref, one_ref, two_ref, sz, rows, True)
        signal = signal_of(pooled, sz)
        _, lifted = silu_parts(signal)
        updated = own_rows(refs, 0) + lifted
        gate, active = silu_parts(updated)
        read = read_ref[...]
        energy = jnp.sum(read * active, axis=1, keepdims=True)
        lane = lax.broadcasted_iota(jnp.int32, (rows, sz.c), 1)
        energy = around(jnp.where(lane == 3, energy, 0.0), rows // 2)
        upstream = [seed_ref[...] * read * (gate + updated * gate * (1.0 - gate))]
        moved = backward(
            upstream, pooled, refs, hot_ref, hot_t_ref, geo_ref, zero_ref, one_ref, two_ref, sz, rows, True, outs
        )
        send_back(moved + energy, outs, sz)


def backward_kernel(
    tick, sz, up_low_ref, up_high_ref, pooled_ref, low_ref, high_ref, hot_ref, hot_t_ref, geo_ref,
    zero_ref, one_ref, two_ref, *outs
):
    @pl.when(lax.axis_index("segment") == tick)
    def _():
        rows = low_ref.shape[1]
        refs = (low_ref, high_ref)
        upstream = [up_low_ref[k].astype(F32) + up_high_ref[k].astype(F32) for k in range(sz.coefs)]
        pooled = [pooled_ref[k] for k in range(sz.coefs)]
        moved = backward(
            upstream, pooled, refs, hot_ref, hot_t_ref, geo_ref, zero_ref, one_ref, two_ref, sz, rows, False,
            outs if tick else None,
        )
        carried = decode(up_low_ref[sz.coefs].astype(F32)) + decode(up_high_ref[sz.coefs].astype(F32))
        moved = moved + around(carried, rows // 2)
        if tick:
            send_back(moved, outs, sz)
        else:
            share(moved, outs)


def call(body, operands, shapes, name, spaces=None, scratch=(), aliases=None):
    spaces = spaces or [pltpu.VMEM] * len(operands)
    operands = [pltpu.with_memory_space_constraint(value, space) for value, space in zip(operands, spaces)]
    return pl.pallas_call(
        body,
        out_shape=shapes,
        in_specs=[pl.BlockSpec(memory_space=space) for space in spaces],
        out_specs=[pl.BlockSpec(memory_space=pltpu.VMEM) for _ in shapes],
        scratch_shapes=list(scratch),
        input_output_aliases=aliases or {},
        compiler_params=pltpu.CompilerParams(vmem_limit_bytes=VMEM_LIMIT),
        name=name,
    )(*operands)


def on_device(
    node_states,
    species,
    species_table,
    places,
    sources,
    radial_rate,
    zero_weight,
    one_weight,
    two_weight,
    read_weight,
    energy_grad,
):
    segments = lax.axis_size("segment")
    slabs = lax.axis_size("space")
    batches, per_slab = species.shape
    coefs, channels = node_states.shape[2:]
    neighbours = sources.shape[2]
    rows = batches * per_slab
    edges = rows * neighbours
    sz = Sizes(zero_weight.shape, one_weight.shape, two_weight.shape, channels)
    axes = ("segment", "space")
    shape = jax.ShapeDtypeStruct

    def within(value, target, count):
        pairs = [(s * slabs + i, s * slabs + target(s % 2, i) % slabs) for s in range(count) for i in range(slabs)]
        return lax.ppermute(value, axes, pairs)

    def hop(value, start, stop, by):
        pairs = [(start * slabs + i, stop * slabs + (i + by) % slabs) for i in range(slabs)]
        return lax.ppermute(value, axes, pairs)

    raw = [
        node_states.transpose(0, 2, 1, 3), places.transpose(1, 0, 2), species, sources, energy_grad, species_table,
    ]
    packed = shape((coefs + 1, per_slab, channels), BF16)
    mine, other = call(
        pack_kernel, raw, [packed, packed], "pack", [pltpu.HBM] * len(raw),
        [pltpu.VMEM(v.shape, v.dtype) for v in raw] + [pltpu.SemaphoreType.DMA((len(raw),))],
    )
    partner = within(other, lambda odd, i: i + 1 - 2 * (i % 2), segments)
    straight = within(mine, lambda odd, i: i - 2 if odd or i % 2 == 0 else i + 2, segments)
    cross = within(other, lambda odd, i: i - 1 if i % 2 == 0 else i - 3 if odd else i + 1, segments)
    stored = [zero_weight[0], one_weight[0], two_weight[0]]
    spaces = [pltpu.HBM] * 3
    on_chip = [pltpu.VMEM(w.shape, w.dtype) for w in stored]
    sems = [pltpu.SemaphoreType.DMA((5,))]
    weights = call(functools.partial(stage_kernel, 0), stored, on_chip, "stage", spaces, sems)
    whole = shape((coefs, rows, channels), BF16)
    low, high, hot, hot_t, geo, seeds = call(
        functools.partial(open_kernel, slabs, neighbours),
        [mine, partner, straight, cross, radial_rate],
        [
            whole, whole, shape((edges, 2 * rows), BF16), shape((2 * rows, edges), BF16),
            shape((10 * edges, channels), F32), shape((rows, channels), F32),
        ],
        "open",
    )

    def stage_more(moment, weights, after):
        return call(
            functools.partial(stage_kernel, moment), [*stored, *weights, after], on_chip, "stage",
            spaces + [pltpu.VMEM] * 4, sems, {3: 0, 4: 1, 5: 2},
        )

    weights = stage_more(1, weights, seeds)
    around_all = [(low, high)]
    kept = []
    for tick in range(segments - 1):
        out, pooled = call(
            functools.partial(forward_kernel, tick, sz),
            [*around_all[tick], hot, geo, *weights],
            [whole, shape((coefs, rows, channels), F32)],
            "forward",
        )
        kept.append(pooled)
        if tick == 0:
            weights = stage_more(2, weights, out)
        ways = (2, 0) if tick % 2 else (0, -2)
        around_all.append(tuple(hop(out, tick, tick + 1, by) for by in ways))
        if tick == 0:
            weights = stage_more(3, weights, around_all[1][0])
    final = segments - 1
    whole_more = shape((coefs + 1, rows, channels), BF16)
    slab_sums = shape((per_slab, channels), F32)
    parts = call(
        functools.partial(turn_kernel, final, sz),
        [*around_all[final], hot, hot_t, geo, *weights, read_weight.reshape(1, channels), seeds],
        [whole_more, whole_more],
        "turn",
    )
    for tick in reversed(range(segments - 1)):
        ways = (2, 0) if tick % 2 else (0, -2)
        up = [hop(part, tick + 1, tick, -by) for part, by in zip(parts, ways)]
        parts = call(
            functools.partial(backward_kernel, tick, sz),
            [*up, kept[tick], *around_all[tick], hot, hot_t, geo, *weights],
            [whole_more, whole_more] if tick else [slab_sums] * 4,
            "backward",
        )
    here, theirs, straight, cross = parts
    theirs = within(theirs, lambda odd, i: i + 1 - 2 * (i % 2), 1)
    straight = within(straight, lambda odd, i: i - 2 if i % 2 else i + 2, 1)
    cross = within(cross, lambda odd, i: i + 1 if i % 2 else i - 1, 1)
    (both,) = call(join_kernel, [here, theirs, straight, cross], [shape((rows, channels), F32)], "join")
    copies = [both] + [hop(both, 0, stop, 0) for stop in range(1, segments)]
    energies, gradients = call(
        close_kernel, copies, [shape((batches, per_slab), F32), shape((3, batches, per_slab), F32)], "close"
    )
    return energies, gradients.transpose(1, 0, 2)


def solution(mesh):
    in_specs = (
        P(None, "space", None, None),
        P(None, "space"),
        P(),
        P(None, None, "space"),
        P(None, "space", None),
        P("segment", None),
        P("segment", None, None),
        P("segment", None, None, None),
        P("segment", None, None, None),
        P(),
        P(None, "space"),
    )
    out_specs = (P(None, "space"), P(None, None, "space"))
    return jax.shard_map(
        on_device, mesh=mesh, in_specs=in_specs, out_specs=out_specs, check_vma=False
    )
```

```python
import functools

import jax
import jax.numpy as jnp
from jax import lax
from jax.experimental import pallas as pl
from jax.experimental.pallas import tpu as pltpu
from jax.sharding import PartitionSpec as P

SLAB_DEPTH = 2.0
F32 = jnp.float32
BF16 = jnp.bfloat16
VMEM_LIMIT = 16 * 1024 * 1024

MID, LOW, SOURCES = 32, 64, 96
BASE = 256


def split(value):
    high = value.astype(BF16)
    low = (value - high.astype(F32)).astype(BF16)
    return high, low


def split3(value):
    high = value.astype(BF16)
    rest = value - high.astype(F32)
    mid = rest.astype(BF16)
    return high, mid, (rest - mid.astype(F32)).astype(BF16)


def encode(value):
    high, mid, low = split3(value)
    return high.astype(F32) + pltpu.roll(mid.astype(F32), MID, 1) + pltpu.roll(low.astype(F32), LOW, 1)


def decode(value):
    lanes = value.shape[1]
    whole = value + pltpu.roll(value, lanes - MID, 1) + pltpu.roll(value, lanes - LOW, 1)
    lane = lax.broadcasted_iota(jnp.int32, value.shape, 1)
    return jnp.where(lane < 4, whole, 0.0)


def dot(a, b):
    return lax.dot_general(a, b, (((1,), (0,)), ((), ())), preferred_element_type=F32)


def dot_t(a, b):
    return lax.dot_general(a, b, (((1,), (1,)), ((), ())), preferred_element_type=F32)


def fine_dot(value, weights, product):
    rows = value.shape[0]
    stacked = jnp.concatenate(split(value), axis=0)
    outs = []
    for weight in weights:
        out = product(stacked, weight)
        outs.append(out[:rows] + out[rows:])
    return outs


def silu_parts(value):
    gate = 1.0 / (1.0 + jnp.exp(-value))
    return gate, value * gate


class Sizes:
    def __init__(self, zero_shape, one_shape, two_shape, channels):
        self.c = channels
        self.zero = zero_shape[-1] // channels
        self.one = one_shape[-1] // channels
        self.two = two_shape[-1] // channels
        self.coefs = self.zero + 2 * (self.one + self.two)
        self.starts = (self.zero, self.zero + 2 * self.one)
        self.counts = (self.one, self.two)

    def cols(self, first, count=1):
        return slice(first * self.c, (first + count) * self.c)


def picked_group(refs, hot, first, count):
    blocks = [jnp.concatenate([ref[k] for ref in refs], axis=0) for k in range(first, first + count)]
    return dot(hot, jnp.concatenate(blocks, axis=1))


def own_rows(refs, k):
    low, high = (ref[k].astype(F32) for ref in refs)
    slab = low.shape[0] // 2
    return jnp.concatenate([low[slab:], high[:slab]], axis=0)


def pool(value, rows):
    total = value[:rows]
    for start in range(rows, value.shape[0], rows):
        total = total + value[start : start + rows]
    return total


def geo_at(geo_ref, which, edges):
    return geo_ref[which * edges : (which + 1) * edges, :]


def forward(refs, hot_ref, geo_ref, zero_ref, one_ref, two_ref, sz, rows, last):
    hot = hot_ref[...]
    edges = hot.shape[0]
    factor = (edges // rows) ** (-0.5)
    radial = geo_at(geo_ref, 0, edges)

    def scaled(block):
        return (block * radial).astype(BF16).astype(F32)

    pooled = [None] * sz.coefs
    group = picked_group(refs, hot, 0, sz.zero)
    zin = jnp.concatenate(
        [pool(scaled(group[:, sz.cols(k)]), rows) for k in range(sz.zero)], axis=1
    )
    kept = 1 if last else sz.zero
    (zout,) = fine_dot(zin, [zero_ref[:, sz.cols(0, kept)]], dot)
    for k in range(kept):
        pooled[k] = zout[:, sz.cols(k)] * factor
    for order in range(2):
        first, count = sz.starts[order], sz.counts[order]
        weight_ref = (one_ref, two_ref)[order]
        cos = geo_at(geo_ref, 1 + 2 * order, edges)
        sin = geo_at(geo_ref, 2 + 2 * order, edges)
        group = picked_group(refs, hot, first, 2 * count)
        res, ims = [], []
        for k in range(count):
            re = scaled(group[:, sz.cols(k)])
            im = scaled(group[:, sz.cols(count + k)])
            res.append(pool(cos * re - sin * im, rows))
            ims.append(pool(sin * re + cos * im, rows))
        both = jnp.concatenate(
            [jnp.concatenate(res, axis=1), jnp.concatenate(ims, axis=1)], axis=0
        )
        a, b = fine_dot(both, [weight_ref[0], weight_ref[1]], dot)
        out_re = (a[:rows] - b[rows:]) * factor
        out_im = (b[:rows] + a[rows:]) * factor
        for k in range(count):
            pooled[first + k] = out_re[:, sz.cols(k)]
            pooled[first + count + k] = out_im[:, sz.cols(k)]
    return pooled


def signal_of(pooled, sz):
    total = pooled[0]
    for k in range(sz.zero, sz.coefs):
        total = total + pooled[k] * pooled[k]
    return total


def backward(
    upstream, pooled, refs, hot_ref, hot_t_ref, geo_ref, zero_ref, one_ref, two_ref, sz, rows, last, outs
):
    hot = hot_ref[...]
    hot_t = hot_t_ref[...]
    edges = hot.shape[0]
    slab = rows // 2
    factor = (edges // rows) ** (-0.5)
    signal = signal_of(pooled, sz)
    gate, _ = silu_parts(signal)
    slope = gate * (1.0 - gate)
    d_signal = upstream[0] * (gate + signal * slope)
    if not last:
        inner = upstream[1] * pooled[1]
        for k in range(2, sz.coefs):
            inner = inner + upstream[k] * pooled[k]
        d_signal = d_signal + inner * slope
    d_pooled = [d_signal * factor]
    for k in range(1, sz.coefs):
        if last:
            d_pooled.append(2.0 * factor * d_signal * pooled[k] if k >= sz.zero else None)
        else:
            term = gate * upstream[k]
            if k >= sz.zero:
                term = term + 2.0 * d_signal * pooled[k]
            d_pooled.append(term * factor)

    radial = geo_at(geo_ref, 0, edges)
    kept = 1 if last else sz.zero
    (dz,) = fine_dot(jnp.concatenate(d_pooled[:kept], axis=1), [zero_ref[:, sz.cols(0, kept)]], dot_t)

    def spread(block):
        return jnp.concatenate([block] * (edges // rows), axis=0)

    def scatter(first, blocks):
        if outs is None:
            return
        high, low = split(jnp.concatenate(blocks, axis=1))
        back = dot(hot_t, high) + dot(hot_t, low)
        for n in range(len(blocks)):
            k = first + n
            part = back[:, sz.cols(n)]
            if not last or k == 0:
                part = part + around(upstream[k], slab)
            outs[0][k] = part[:rows].astype(BF16)
            outs[1][k] = part[rows:].astype(BF16)

    q_len = jnp.zeros((edges, sz.c), F32)
    group = picked_group(refs, hot, 0, sz.zero)
    blocks = []
    for k in range(sz.zero):
        grad = spread(dz[:, sz.cols(k)])
        q_len = q_len + grad * group[:, sz.cols(k)]
        blocks.append(grad * radial)
    q_len = q_len * radial
    scatter(0, blocks)
    q_turn = []
    for order in range(2):
        first, count = sz.starts[order], sz.counts[order]
        weight_ref = (one_ref, two_ref)[order]
        cos = geo_at(geo_ref, 1 + 2 * order, edges)
        sin = geo_at(geo_ref, 2 + 2 * order, edges)
        both = jnp.concatenate(
            [
                jnp.concatenate(d_pooled[first : first + count], axis=1),
                jnp.concatenate(d_pooled[first + count : first + 2 * count], axis=1),
            ],
            axis=0,
        )
        a, b = fine_dot(both, [weight_ref[0], weight_ref[1]], dot_t)
        d_re = a[:rows] + b[rows:]
        d_im = a[rows:] - b[:rows]
        group = picked_group(refs, hot, first, 2 * count)
        q_cos = jnp.zeros((edges, sz.c), F32)
        q_sin = jnp.zeros((edges, sz.c), F32)
        cos_r = cos * radial
        sin_r = sin * radial
        blocks_re, blocks_im = [], []
        for k in range(count):
            re = group[:, sz.cols(k)]
            im = group[:, sz.cols(count + k)]
            g_re = spread(d_re[:, sz.cols(k)])
            g_im = spread(d_im[:, sz.cols(k)])
            q_cos = q_cos + (re * g_re + im * g_im)
            q_sin = q_sin + (re * g_im - im * g_re)
            if outs is not None:
                blocks_re.append(cos_r * g_re + sin_r * g_im)
                blocks_im.append(cos_r * g_im - sin_r * g_re)
        scatter(first, blocks_re + blocks_im)
        q_cos = q_cos * radial
        q_sin = q_sin * radial
        q_len = q_len + cos * q_cos + sin * q_sin
        q_turn.append((q_cos, q_sin))

    rate = geo_at(geo_ref, 9, edges)

    def total(value):
        return jnp.sum(value, axis=1, keepdims=True)

    d_len = -total(q_len * rate)
    (dc1, ds1), (dc2, ds2) = [(total(a), total(b)) for a, b in q_turn]
    c1, s1 = geo_at(geo_ref, 1, edges), geo_at(geo_ref, 2, edges)
    ux, uy, uz = (geo_at(geo_ref, 5 + n, edges) for n in range(3))
    inv_planar = geo_at(geo_ref, 8, edges)
    dc1 = dc1 + 2.0 * (c1 * dc2 + s1 * ds2)
    ds1 = ds1 + 2.0 * (c1 * ds2 - s1 * dc2)
    along = c1 * dc1 + s1 * ds1
    dx = (dc1 - along * c1) * inv_planar + d_len * ux
    dy = (ds1 - along * s1) * inv_planar + d_len * uy
    dz_ = d_len * uz
    lane = lax.broadcasted_iota(jnp.int32, (edges, sz.c), 1)
    change = jnp.where(lane == 0, dx, jnp.where(lane == 1, dy, jnp.where(lane == 2, dz_, 0.0)))
    moved = sum(dot(hot_t, part) for part in split3(change))
    return moved - around(pool(change, rows), slab)


def around(own, slab):
    edge = jnp.zeros((slab, own.shape[1]), F32)
    return jnp.concatenate([edge, own, edge], axis=0)


def place_of(pair, pairs, segment):
    if segment == 0:
        return pair
    return 2 * pair if pair < pairs // 2 else 2 * (pairs - 1 - pair) + 1


def first_slab(slabs):
    slab_now = lax.axis_index("space")
    segment = lax.axis_index("segment")
    chip = slab_now // 2
    folded = jnp.where(lax.rem(chip, 2) == 0, chip // 2, slabs // 2 - 1 - chip // 2)
    pair = jnp.where(segment == 0, chip, folded)
    return lax.rem(2 * pair + lax.rem(segment, 2) - 1 + slabs, slabs), lax.rem(slab_now, 2)


def send_back(moved, outs, sz):
    rows = moved.shape[0] // 2
    coded = encode(moved).astype(BF16)
    outs[0][sz.coefs] = coded[:rows]
    outs[1][sz.coefs] = coded[rows:]


def share(moved, outs):
    slab = moved.shape[0] // 4
    left, low, high, right = (moved[n * slab : (n + 1) * slab] for n in range(4))
    even = lax.rem(lax.axis_index("space"), 2) == 0
    outs[0][...] = jnp.where(even, low, high)
    outs[1][...] = jnp.where(even, high, low)
    outs[2][...] = jnp.where(even, right, left)
    outs[3][...] = jnp.where(even, left, right)


def join_kernel(here_ref, theirs_ref, straight_ref, cross_ref, both_ref):
    slab = here_ref.shape[0]
    even = lax.rem(lax.axis_index("space"), 2) == 0
    here = here_ref[...] + straight_ref[...]
    there = theirs_ref[...] + cross_ref[...]
    both_ref[:slab, :] = jnp.where(even, here, there)
    both_ref[slab:, :] = jnp.where(even, there, here)


def close_kernel(*refs):
    *sums_refs, energies_ref, places_ref = refs
    slab = energies_ref.shape[1]
    for n, ref in enumerate(sums_refs):

        @pl.when(lax.axis_index("segment") == n)
        def _(ref=ref):
            sums = ref[...]
            rows, c = sums.shape
            turned = jnp.transpose(jnp.concatenate([sums, jnp.zeros((c - rows, c), F32)], axis=0))
            for b in range(2):
                energies_ref[b : b + 1, :] = turned[3:4, b * slab : (b + 1) * slab]
                for n in range(3):
                    places_ref[n, b : b + 1, :] = turned[n : n + 1, b * slab : (b + 1) * slab]


def pack_kernel(
    node_hbm, places_hbm, species_hbm, sources_hbm, grad_hbm, table_hbm, mine_ref, other_ref,
    states, places, species, sources, grads, table, sems
):
    @pl.when(lax.axis_index("segment") == 0)
    def _():
        pack(
            (node_hbm, places_hbm, species_hbm, sources_hbm, grad_hbm, table_hbm), mine_ref, other_ref,
            states, places, species, sources, grads, table, sems,
        )


def pack(given, mine_ref, other_ref, states, places, species, sources, grads, table, sems):
    batch = lax.rem(lax.axis_index("space"), 2)
    copies = []
    for n, (source, target) in enumerate(zip(given, (states, places, species, sources, grads, table))):
        copies.append(pltpu.make_async_copy(source, target, sems.at[n]))
        copies[-1].start()
    for copy in copies:
        copy.wait()
    coefs, per_slab, c = states.shape[1:]
    lane = lax.broadcasted_iota(jnp.int32, (per_slab, c), 1)
    eye = (
        lax.broadcasted_iota(jnp.int32, (per_slab, per_slab), 0)
        == lax.broadcasted_iota(jnp.int32, (per_slab, per_slab), 1)
    )

    def column(row):
        return jnp.sum(jnp.where(eye, jnp.broadcast_to(row, (per_slab, per_slab)), 0.0), axis=1, keepdims=True)

    both = []
    for b in range(2):
        names = column(species[b : b + 1, :].astype(F32)).astype(jnp.int32)
        kinds = table.shape[0]
        hot = (names == lax.broadcasted_iota(jnp.int32, (per_slab, kinds), 1)).astype(BF16)
        first = (states[b, 0].astype(F32) + dot(hot, table[...])).astype(BF16)
        extra = jnp.zeros((per_slab, c), F32)
        for n in range(3):
            extra = jnp.where(lane == n, column(places[n, b : b + 1, :]), extra)
        extra = encode(jnp.where(lane == 3, column(grads[b : b + 1, :]), extra))
        for j in range(sources.shape[2]):
            index = sources[b, :, j : j + 1]
            extra = jnp.where(lane == SOURCES + j, (index // BASE).astype(F32), extra)
            extra = jnp.where(lane == SOURCES + 8 + j, (index % BASE).astype(F32), extra)
        both.append((first, extra.astype(BF16)))
    for ref, chosen in ((mine_ref, batch), (other_ref, 1 - batch)):
        ref[pl.ds(0, coefs)] = states[chosen]
        ref[0] = jnp.where(chosen == 0, both[0][0].astype(F32), both[1][0].astype(F32)).astype(BF16)
        ref[coefs] = jnp.where(chosen == 0, both[0][1].astype(F32), both[1][1].astype(F32)).astype(BF16)


def open_kernel(mine_ref, partner_ref, straight_ref, cross_ref, low_ref, high_ref):
    @pl.when(lax.axis_index("segment") == 0)
    def _():
        even = lax.rem(lax.axis_index("space"), 2) == 0

        def choose(a, b):
            return jnp.where(even, a, b)

        for k in range(low_ref.shape[0]):
            mine, partner = mine_ref[k].astype(F32), partner_ref[k].astype(F32)
            straight, cross = straight_ref[k].astype(F32), cross_ref[k].astype(F32)
            low_ref[k] = jnp.concatenate([choose(cross, straight), choose(mine, partner)], axis=0).astype(BF16)
            high_ref[k] = jnp.concatenate([choose(partner, mine), choose(straight, cross)], axis=0).astype(BF16)


def edges_of(refs, coefs, slabs, neighbours, rate_ref, hot_ref, hot_t_ref, geo_ref):
    start, _ = first_slab(slabs)
    extra = jnp.concatenate([ref[coefs].astype(F32) for ref in refs], axis=0)
    window, c = extra.shape
    rows = window // 2
    per_slab = rows // 2
    edges = rows * neighbours
    numbers = decode(extra)
    own_extra = extra[per_slab : per_slab + rows]
    low = pltpu.roll(own_extra, c - 8, 1)
    index = own_extra.astype(jnp.int32) * BASE + low.astype(jnp.int32)
    place = lax.rem(index // per_slab - start + slabs, slabs) * per_slab + index % per_slab
    columns = lax.broadcasted_iota(jnp.int32, (rows, c), 1)
    hot = jnp.concatenate(
        [
            (place[:, SOURCES + j : SOURCES + j + 1] == columns).astype(F32)
            for j in range(neighbours)
        ],
        axis=0,
    )
    hot_t_ref[...] = jnp.transpose(hot).astype(BF16)[:window]
    hot = hot.astype(BF16)[:, :window]
    hot_ref[...] = hot
    lift = lax.broadcasted_iota(jnp.int32, (window, c), 0) // per_slab - 1
    offset = []
    for n in range(3):
        column = jnp.broadcast_to(numbers[:, n : n + 1], (window, c))
        if n == 2:
            column = column + SLAB_DEPTH * lift.astype(F32)
        there = sum(dot(hot, part) for part in split3(column))
        offset.append(there - jnp.concatenate([column[per_slab : per_slab + rows]] * neighbours, axis=0))
    flat = offset[0] * offset[0] + offset[1] * offset[1] + 1.0
    length = jnp.sqrt(flat + offset[2] * offset[2])
    planar = jnp.sqrt(flat)
    c1, s1 = offset[0] / planar, offset[1] / planar
    rate = jnp.broadcast_to(rate_ref[...], (edges, c))
    values = [
        jnp.exp(-rate * length),
        c1,
        s1,
        c1 * c1 - s1 * s1,
        2.0 * c1 * s1,
        offset[0] / length,
        offset[1] / length,
        offset[2] / length,
        1.0 / planar,
        rate,
    ]
    for n, value in enumerate(values):
        geo_ref[n * edges : (n + 1) * edges, :] = value
    return numbers[per_slab : per_slab + rows]


def turn_to_stage():
    odd = lax.rem(lax.axis_index("space"), 2)
    return jnp.where(lax.axis_index("segment") == 0, odd, 0)


def stage_kernel(moment, zero_hbm, one_hbm, two_hbm, *more):
    zero_ref, one_ref, two_ref, sems = more[-4:]

    @pl.when(turn_to_stage() == moment)
    def _():
        pairs = [(zero_hbm, zero_ref)]
        for source, target in ((one_hbm, one_ref), (two_hbm, two_ref)):
            pairs += [(source.at[n], target.at[n]) for n in range(2)]
        copies = [pltpu.make_async_copy(source, target, sems.at[n]) for n, (source, target) in enumerate(pairs)]
        for copy in copies:
            copy.start()
        for copy in copies:
            copy.wait()


def forward_kernel(
    tick, sz, slabs, neighbours, low_ref, high_ref, rate_ref, zero_ref, one_ref, two_ref,
    out_ref, pooled_ref, hot_ref, hot_t_ref, geo_ref
):
    @pl.when(lax.axis_index("segment") == tick)
    def _():
        rows = low_ref.shape[1]
        refs = (low_ref, high_ref)
        edges_of(refs, sz.coefs, slabs, neighbours, rate_ref, hot_ref, hot_t_ref, geo_ref)
        pooled = forward(refs, hot_ref, geo_ref, zero_ref, one_ref, two_ref, sz, rows, False)
        signal = signal_of(pooled, sz)
        gate, lifted = silu_parts(signal)
        for k in range(sz.coefs):
            pooled_ref[k] = pooled[k]
            added = lifted if k == 0 else gate * pooled[k]
            out_ref[k] = (own_rows(refs, k) + added).astype(BF16)
        out_ref[sz.coefs] = own_rows(refs, sz.coefs).astype(BF16)


def turn_kernel(
    tick, sz, slabs, neighbours, low_ref, high_ref, rate_ref, zero_ref, one_ref, two_ref, read_ref,
    back_low_ref, back_high_ref, hot_ref, hot_t_ref, geo_ref
):
    @pl.when(lax.axis_index("segment") == tick)
    def _():
        rows = low_ref.shape[1]
        refs = (low_ref, high_ref)
        outs = (back_low_ref, back_high_ref)
        own = edges_of(refs, sz.coefs, slabs, neighbours, rate_ref, hot_ref, hot_t_ref, geo_ref)
        pooled = forward(refs, hot_ref, geo_ref, zero_ref, one_ref, two_ref, sz, rows, True)
        signal = signal_of(pooled, sz)
        _, lifted = silu_parts(signal)
        updated = own_rows(refs, 0) + lifted
        gate, active = silu_parts(updated)
        read = read_ref[...]
        energy = jnp.sum(read * active, axis=1, keepdims=True)
        lane = lax.broadcasted_iota(jnp.int32, (rows, sz.c), 1)
        energy = around(jnp.where(lane == 3, energy, 0.0), rows // 2)
        upstream = [own[:, 3:4] * read * (gate + updated * gate * (1.0 - gate))]
        moved = backward(
            upstream, pooled, refs, hot_ref, hot_t_ref, geo_ref, zero_ref, one_ref, two_ref, sz, rows, True, outs
        )
        send_back(moved + energy, outs, sz)


def backward_kernel(
    tick, sz, up_low_ref, up_high_ref, pooled_ref, low_ref, high_ref, hot_ref, hot_t_ref, geo_ref,
    zero_ref, one_ref, two_ref, *outs
):
    @pl.when(lax.axis_index("segment") == tick)
    def _():
        rows = low_ref.shape[1]
        refs = (low_ref, high_ref)
        upstream = [up_low_ref[k].astype(F32) + up_high_ref[k].astype(F32) for k in range(sz.coefs)]
        pooled = [pooled_ref[k] for k in range(sz.coefs)]
        moved = backward(
            upstream, pooled, refs, hot_ref, hot_t_ref, geo_ref, zero_ref, one_ref, two_ref, sz, rows, False,
            outs if tick else None,
        )
        carried = decode(up_low_ref[sz.coefs].astype(F32)) + decode(up_high_ref[sz.coefs].astype(F32))
        moved = moved + around(carried, rows // 2)
        if tick:
            send_back(moved, outs, sz)
        else:
            share(moved, outs)


def call(body, operands, shapes, name, spaces=None, scratch=(), aliases=None):
    spaces = spaces or [pltpu.VMEM] * len(operands)
    operands = [pltpu.with_memory_space_constraint(value, space) for value, space in zip(operands, spaces)]
    return pl.pallas_call(
        body,
        out_shape=shapes,
        in_specs=[pl.BlockSpec(memory_space=space) for space in spaces],
        out_specs=[pl.BlockSpec(memory_space=pltpu.VMEM) for _ in shapes],
        scratch_shapes=list(scratch),
        input_output_aliases=aliases or {},
        compiler_params=pltpu.CompilerParams(vmem_limit_bytes=VMEM_LIMIT),
        name=name,
    )(*operands)


def on_device(
    node_states,
    species,
    species_table,
    places,
    sources,
    radial_rate,
    zero_weight,
    one_weight,
    two_weight,
    read_weight,
    energy_grad,
):
    segments = lax.axis_size("segment")
    slabs = lax.axis_size("space")
    batches, per_slab = species.shape
    coefs, channels = node_states.shape[2:]
    neighbours = sources.shape[2]
    rows = batches * per_slab
    edges = rows * neighbours
    sz = Sizes(zero_weight.shape, one_weight.shape, two_weight.shape, channels)
    axes = ("segment", "space")
    shape = jax.ShapeDtypeStruct

    pairs = slabs // 2

    def within(value, target):
        return lax.ppermute(value, axes, [(i, target(i) % slabs) for i in range(slabs)])

    def hop(value, start, stop, by):
        ways = [(place_of(q, pairs, start), place_of((q + by) % pairs, pairs, stop)) for q in range(pairs)]
        return lax.ppermute(
            value, axes, [(start * slabs + 2 * a + c, stop * slabs + 2 * b + c) for a, b in ways for c in range(2)]
        )

    raw = [
        node_states.transpose(0, 2, 1, 3), places.transpose(1, 0, 2), species, sources, energy_grad, species_table,
    ]
    packed = shape((coefs + 1, per_slab, channels), BF16)
    mine, other = call(
        pack_kernel, raw, [packed, packed], "pack", [pltpu.HBM] * len(raw),
        [pltpu.VMEM(v.shape, v.dtype) for v in raw] + [pltpu.SemaphoreType.DMA((len(raw),))],
    )
    partner = within(other, lambda i: i + 1 - 2 * (i % 2))
    straight = within(mine, lambda i: i + 2 if i % 2 else i - 2)
    cross = within(other, lambda i: i + 1 if i % 2 else i - 1)
    stored = [zero_weight[0], one_weight[0], two_weight[0]]
    spaces = [pltpu.HBM] * 3
    on_chip = [pltpu.VMEM(w.shape, w.dtype) for w in stored]
    sems = [pltpu.SemaphoreType.DMA((5,))]
    weights = call(functools.partial(stage_kernel, 0), stored, on_chip, "stage", spaces, sems)
    whole = shape((coefs + 1, rows, channels), BF16)
    around_all = [call(open_kernel, [mine, partner, straight, cross], [whole, whole], "open")]
    weights = call(
        functools.partial(stage_kernel, 1), [*stored, *weights, around_all[0][0]], on_chip, "stage",
        spaces + [pltpu.VMEM] * 4, sems, {3: 0, 4: 1, 5: 2},
    )
    edge_shapes = [
        shape((edges, 2 * rows), BF16), shape((2 * rows, edges), BF16), shape((10 * edges, channels), F32),
    ]
    kept = []
    for tick in range(segments - 1):
        out, *residuals = call(
            functools.partial(forward_kernel, tick, sz, slabs, neighbours),
            [*around_all[tick], radial_rate, *weights],
            [whole, shape((coefs, rows, channels), F32), *edge_shapes],
            "forward",
        )
        kept.append(residuals)
        ways = (1, 0) if tick % 2 else (0, -1)
        around_all.append([hop(out, tick, tick + 1, by) for by in ways])
    final = segments - 1
    slab_sums = shape((per_slab, channels), F32)
    parts = call(
        functools.partial(turn_kernel, final, sz, slabs, neighbours),
        [*around_all[final], radial_rate, *weights, read_weight.reshape(1, channels)],
        [whole, whole, *edge_shapes],
        "turn",
    )[:2]
    for tick in reversed(range(segments - 1)):
        ways = (1, 0) if tick % 2 else (0, -1)
        up = [hop(part, tick + 1, tick, -by) for part, by in zip(parts, ways)]
        pooled, *residuals = kept[tick]
        parts = call(
            functools.partial(backward_kernel, tick, sz),
            [*up, pooled, *around_all[tick], *residuals, *weights],
            [whole, whole] if tick else [slab_sums] * 4,
            "backward",
        )
    here, theirs, straight, cross = parts
    theirs = within(theirs, lambda i: i + 1 - 2 * (i % 2))
    straight = within(straight, lambda i: i - 2 if i % 2 else i + 2)
    cross = within(cross, lambda i: i + 1 if i % 2 else i - 1)
    (both,) = call(join_kernel, [here, theirs, straight, cross], [shape((rows, channels), F32)], "join")
    copies = [both] + [
        lax.ppermute(both, axes, [(i, stop * slabs + i) for i in range(slabs)]) for stop in range(1, segments)
    ]
    energies, gradients = call(
        close_kernel, copies, [shape((batches, per_slab), F32), shape((3, batches, per_slab), F32)], "close"
    )
    return energies, gradients.transpose(1, 0, 2)


def solution(mesh):
    in_specs = (
        P(None, "space", None, None),
        P(None, "space"),
        P(),
        P(None, None, "space"),
        P(None, "space", None),
        P("segment", None),
        P("segment", None, None),
        P("segment", None, None, None),
        P("segment", None, None, None),
        P(),
        P(None, "space"),
    )
    out_specs = (P(None, "space"), P(None, None, "space"))
    return jax.shard_map(
        on_device, mesh=mesh, in_specs=in_specs, out_specs=out_specs, check_vma=False
    )
```

```python
import functools

import jax
import jax.numpy as jnp
from jax import lax
from jax.experimental import pallas as pl
from jax.experimental.pallas import tpu as pltpu
from jax.sharding import PartitionSpec as P

SLAB_DEPTH = 2.0
F32 = jnp.float32
BF16 = jnp.bfloat16
VMEM_LIMIT = 16 * 1024 * 1024

MID, LOW, SOURCES = 32, 64, 96
BASE = 256


def split(value):
    high = value.astype(BF16)
    low = (value - high.astype(F32)).astype(BF16)
    return high, low


def split3(value):
    high = value.astype(BF16)
    rest = value - high.astype(F32)
    mid = rest.astype(BF16)
    return high, mid, (rest - mid.astype(F32)).astype(BF16)


def encode(value):
    high, mid, low = split3(value)
    return high.astype(F32) + pltpu.roll(mid.astype(F32), MID, 1) + pltpu.roll(low.astype(F32), LOW, 1)


def decode(value):
    lanes = value.shape[1]
    whole = value + pltpu.roll(value, lanes - MID, 1) + pltpu.roll(value, lanes - LOW, 1)
    lane = lax.broadcasted_iota(jnp.int32, value.shape, 1)
    return jnp.where(lane < 4, whole, 0.0)


def dot(a, b):
    return lax.dot_general(a, b, (((1,), (0,)), ((), ())), preferred_element_type=F32)


def dot_t(a, b):
    return lax.dot_general(a, b, (((1,), (1,)), ((), ())), preferred_element_type=F32)


def fine_dot(value, weights, product):
    rows = value.shape[0]
    stacked = jnp.concatenate(split(value), axis=0)
    outs = []
    for weight in weights:
        out = product(stacked, weight)
        outs.append(out[:rows] + out[rows:])
    return outs


def silu_parts(value):
    gate = 1.0 / (1.0 + jnp.exp(-value))
    return gate, value * gate


class Sizes:
    def __init__(self, zero_shape, one_shape, two_shape, channels):
        self.c = channels
        self.zero = zero_shape[-1] // channels
        self.one = one_shape[-1] // channels
        self.two = two_shape[-1] // channels
        self.coefs = self.zero + 2 * (self.one + self.two)
        self.starts = (self.zero, self.zero + 2 * self.one)
        self.counts = (self.one, self.two)

    def cols(self, first, count=1):
        return slice(first * self.c, (first + count) * self.c)


def picked_group(refs, hot, first, count):
    blocks = [jnp.concatenate([ref[k] for ref in refs], axis=0) for k in range(first, first + count)]
    return dot(hot, jnp.concatenate(blocks, axis=1))


def own_rows(refs, k):
    low, high = (ref[k].astype(F32) for ref in refs)
    slab = low.shape[0] // 2
    return jnp.concatenate([low[slab:], high[:slab]], axis=0)


def pool(value, rows):
    total = value[:rows]
    for start in range(rows, value.shape[0], rows):
        total = total + value[start : start + rows]
    return total


def geo_at(geo_ref, which, edges):
    return geo_ref[which * edges : (which + 1) * edges, :]


def forward(refs, hot_ref, geo_ref, zero_ref, one_ref, two_ref, sz, rows, last):
    hot = hot_ref[...]
    edges = hot.shape[0]
    factor = (edges // rows) ** (-0.5)
    radial = geo_at(geo_ref, 0, edges)

    def scaled(block):
        return (block * radial).astype(BF16).astype(F32)

    pooled = [None] * sz.coefs
    group = picked_group(refs, hot, 0, sz.zero)
    zin = jnp.concatenate(
        [pool(scaled(group[:, sz.cols(k)]), rows) for k in range(sz.zero)], axis=1
    )
    kept = 1 if last else sz.zero
    (zout,) = fine_dot(zin, [zero_ref[:, sz.cols(0, kept)]], dot)
    for k in range(kept):
        pooled[k] = zout[:, sz.cols(k)] * factor
    for order in range(2):
        first, count = sz.starts[order], sz.counts[order]
        weight_ref = (one_ref, two_ref)[order]
        cos = geo_at(geo_ref, 1 + 2 * order, edges)
        sin = geo_at(geo_ref, 2 + 2 * order, edges)
        group = picked_group(refs, hot, first, 2 * count)
        res, ims = [], []
        for k in range(count):
            re = scaled(group[:, sz.cols(k)])
            im = scaled(group[:, sz.cols(count + k)])
            res.append(pool(cos * re - sin * im, rows))
            ims.append(pool(sin * re + cos * im, rows))
        both = jnp.concatenate(
            [jnp.concatenate(res, axis=1), jnp.concatenate(ims, axis=1)], axis=0
        )
        a, b = fine_dot(both, [weight_ref[0], weight_ref[1]], dot)
        out_re = (a[:rows] - b[rows:]) * factor
        out_im = (b[:rows] + a[rows:]) * factor
        for k in range(count):
            pooled[first + k] = out_re[:, sz.cols(k)]
            pooled[first + count + k] = out_im[:, sz.cols(k)]
    return pooled


def signal_of(pooled, sz):
    total = pooled[0]
    for k in range(sz.zero, sz.coefs):
        total = total + pooled[k] * pooled[k]
    return total


def backward(
    upstream, pooled, refs, hot_ref, hot_t_ref, geo_ref, zero_ref, one_ref, two_ref, sz, rows, last, outs
):
    hot = hot_ref[...]
    hot_t = hot_t_ref[...]
    edges = hot.shape[0]
    slab = rows // 2
    factor = (edges // rows) ** (-0.5)
    signal = signal_of(pooled, sz)
    gate, _ = silu_parts(signal)
    slope = gate * (1.0 - gate)
    d_signal = upstream[0] * (gate + signal * slope)
    if not last:
        inner = upstream[1] * pooled[1]
        for k in range(2, sz.coefs):
            inner = inner + upstream[k] * pooled[k]
        d_signal = d_signal + inner * slope
    d_pooled = [d_signal * factor]
    for k in range(1, sz.coefs):
        if last:
            d_pooled.append(2.0 * factor * d_signal * pooled[k] if k >= sz.zero else None)
        else:
            term = gate * upstream[k]
            if k >= sz.zero:
                term = term + 2.0 * d_signal * pooled[k]
            d_pooled.append(term * factor)

    radial = geo_at(geo_ref, 0, edges)
    kept = 1 if last else sz.zero
    (dz,) = fine_dot(jnp.concatenate(d_pooled[:kept], axis=1), [zero_ref[:, sz.cols(0, kept)]], dot_t)

    def spread(block):
        return jnp.concatenate([block] * (edges // rows), axis=0)

    def scatter(first, blocks):
        if outs is None:
            return
        high, low = split(jnp.concatenate(blocks, axis=1))
        back = dot(hot_t, high) + dot(hot_t, low)
        for n in range(len(blocks)):
            k = first + n
            part = back[:, sz.cols(n)]
            if not last or k == 0:
                part = part + around(upstream[k], slab)
            outs[0][k] = part[:rows].astype(BF16)
            outs[1][k] = part[rows:].astype(BF16)

    q_len = jnp.zeros((edges, sz.c), F32)
    group = picked_group(refs, hot, 0, sz.zero)
    blocks = []
    for k in range(sz.zero):
        grad = spread(dz[:, sz.cols(k)])
        q_len = q_len + grad * group[:, sz.cols(k)]
        blocks.append(grad * radial)
    q_len = q_len * radial
    scatter(0, blocks)
    q_turn = []
    for order in range(2):
        first, count = sz.starts[order], sz.counts[order]
        weight_ref = (one_ref, two_ref)[order]
        cos = geo_at(geo_ref, 1 + 2 * order, edges)
        sin = geo_at(geo_ref, 2 + 2 * order, edges)
        both = jnp.concatenate(
            [
                jnp.concatenate(d_pooled[first : first + count], axis=1),
                jnp.concatenate(d_pooled[first + count : first + 2 * count], axis=1),
            ],
            axis=0,
        )
        a, b = fine_dot(both, [weight_ref[0], weight_ref[1]], dot_t)
        d_re = a[:rows] + b[rows:]
        d_im = a[rows:] - b[:rows]
        group = picked_group(refs, hot, first, 2 * count)
        q_cos = jnp.zeros((edges, sz.c), F32)
        q_sin = jnp.zeros((edges, sz.c), F32)
        cos_r = cos * radial
        sin_r = sin * radial
        blocks_re, blocks_im = [], []
        for k in range(count):
            re = group[:, sz.cols(k)]
            im = group[:, sz.cols(count + k)]
            g_re = spread(d_re[:, sz.cols(k)])
            g_im = spread(d_im[:, sz.cols(k)])
            q_cos = q_cos + (re * g_re + im * g_im)
            q_sin = q_sin + (re * g_im - im * g_re)
            if outs is not None:
                blocks_re.append(cos_r * g_re + sin_r * g_im)
                blocks_im.append(cos_r * g_im - sin_r * g_re)
        scatter(first, blocks_re + blocks_im)
        q_cos = q_cos * radial
        q_sin = q_sin * radial
        q_len = q_len + cos * q_cos + sin * q_sin
        q_turn.append((q_cos, q_sin))

    rate = geo_at(geo_ref, 9, edges)

    def total(value):
        return jnp.sum(value, axis=1, keepdims=True)

    d_len = -total(q_len * rate)
    (dc1, ds1), (dc2, ds2) = [(total(a), total(b)) for a, b in q_turn]
    c1, s1 = geo_at(geo_ref, 1, edges), geo_at(geo_ref, 2, edges)
    ux, uy, uz = (geo_at(geo_ref, 5 + n, edges) for n in range(3))
    inv_planar = geo_at(geo_ref, 8, edges)
    dc1 = dc1 + 2.0 * (c1 * dc2 + s1 * ds2)
    ds1 = ds1 + 2.0 * (c1 * ds2 - s1 * dc2)
    along = c1 * dc1 + s1 * ds1
    dx = (dc1 - along * c1) * inv_planar + d_len * ux
    dy = (ds1 - along * s1) * inv_planar + d_len * uy
    dz_ = d_len * uz
    lane = lax.broadcasted_iota(jnp.int32, (edges, sz.c), 1)
    change = jnp.where(lane == 0, dx, jnp.where(lane == 1, dy, jnp.where(lane == 2, dz_, 0.0)))
    moved = sum(dot(hot_t, part) for part in split3(change))
    return moved - around(pool(change, rows), slab)


def around(own, slab):
    edge = jnp.zeros((slab, own.shape[1]), F32)
    return jnp.concatenate([edge, own, edge], axis=0)


def place_of(pair, pairs, segment):
    if segment == 0:
        return pair
    return 2 * pair if pair < pairs // 2 else 2 * (pairs - 1 - pair) + 1


def first_slab(slabs):
    slab_now = lax.axis_index("space")
    segment = lax.axis_index("segment")
    chip = slab_now // 2
    folded = jnp.where(lax.rem(chip, 2) == 0, chip // 2, slabs // 2 - 1 - chip // 2)
    pair = jnp.where(segment == 0, chip, folded)
    return lax.rem(2 * pair + lax.rem(segment, 2) - 1 + slabs, slabs), lax.rem(slab_now, 2)


def send_back(moved, outs, sz):
    rows = moved.shape[0] // 2
    coded = encode(moved).astype(BF16)
    outs[0][sz.coefs] = coded[:rows]
    outs[1][sz.coefs] = coded[rows:]


def share(moved, outs):
    slab = moved.shape[0] // 4
    left, low, high, right = (moved[n * slab : (n + 1) * slab] for n in range(4))
    even = lax.rem(lax.axis_index("space"), 2) == 0
    outs[0][...] = jnp.where(even, low, high)
    outs[1][...] = jnp.where(even, high, low)
    outs[2][...] = jnp.where(even, right, left)
    outs[3][...] = jnp.where(even, left, right)


def join_kernel(here_ref, theirs_ref, straight_ref, cross_ref, both_ref):
    slab = here_ref.shape[0]
    even = lax.rem(lax.axis_index("space"), 2) == 0
    here = here_ref[...] + straight_ref[...]
    there = theirs_ref[...] + cross_ref[...]
    both_ref[:slab, :] = jnp.where(even, here, there)
    both_ref[slab:, :] = jnp.where(even, there, here)


def close_kernel(*refs):
    *sums_refs, energies_ref, places_ref = refs
    slab = energies_ref.shape[1]
    for n, ref in enumerate(sums_refs):

        @pl.when(lax.axis_index("segment") == n)
        def _(ref=ref):
            sums = ref[...]
            rows, c = sums.shape
            turned = jnp.transpose(jnp.concatenate([sums, jnp.zeros((c - rows, c), F32)], axis=0))
            for b in range(2):
                energies_ref[b : b + 1, :] = turned[3:4, b * slab : (b + 1) * slab]
                for n in range(3):
                    places_ref[n, b : b + 1, :] = turned[n : n + 1, b * slab : (b + 1) * slab]


def pack_kernel(
    node_hbm, places_hbm, species_hbm, sources_hbm, grad_hbm, table_hbm, mine_ref, other_ref,
    states, places, species, sources, grads, table, sems
):
    @pl.when(lax.axis_index("segment") == 0)
    def _():
        pack(
            (node_hbm, places_hbm, species_hbm, sources_hbm, grad_hbm, table_hbm), mine_ref, other_ref,
            states, places, species, sources, grads, table, sems,
        )


def pack(given, mine_ref, other_ref, states, places, species, sources, grads, table, sems):
    batch = lax.rem(lax.axis_index("space"), 2)
    copies = []
    for n, (source, target) in enumerate(zip(given, (states, places, species, sources, grads, table))):
        copies.append(pltpu.make_async_copy(source, target, sems.at[n]))
        copies[-1].start()
    for copy in copies:
        copy.wait()
    coefs, per_slab, c = states.shape[1:]
    lane = lax.broadcasted_iota(jnp.int32, (per_slab, c), 1)
    eye = (
        lax.broadcasted_iota(jnp.int32, (per_slab, per_slab), 0)
        == lax.broadcasted_iota(jnp.int32, (per_slab, per_slab), 1)
    )

    def column(row):
        return jnp.sum(jnp.where(eye, jnp.broadcast_to(row, (per_slab, per_slab)), 0.0), axis=1, keepdims=True)

    both = []
    for b in range(2):
        names = column(species[b : b + 1, :].astype(F32)).astype(jnp.int32)
        kinds = table.shape[0]
        hot = (names == lax.broadcasted_iota(jnp.int32, (per_slab, kinds), 1)).astype(BF16)
        first = (states[b, 0].astype(F32) + dot(hot, table[...])).astype(BF16)
        extra = jnp.zeros((per_slab, c), F32)
        for n in range(3):
            extra = jnp.where(lane == n, column(places[n, b : b + 1, :]), extra)
        extra = encode(jnp.where(lane == 3, column(grads[b : b + 1, :]), extra))
        for j in range(sources.shape[2]):
            index = sources[b, :, j : j + 1]
            extra = jnp.where(lane == SOURCES + j, (index // BASE).astype(F32), extra)
            extra = jnp.where(lane == SOURCES + 8 + j, (index % BASE).astype(F32), extra)
        both.append((first, extra.astype(BF16)))
    for ref, chosen in ((mine_ref, batch), (other_ref, 1 - batch)):
        ref[pl.ds(0, coefs)] = states[chosen]
        ref[0] = jnp.where(chosen == 0, both[0][0].astype(F32), both[1][0].astype(F32)).astype(BF16)
        ref[coefs] = jnp.where(chosen == 0, both[0][1].astype(F32), both[1][1].astype(F32)).astype(BF16)


def open_kernel(mine_ref, partner_ref, straight_ref, cross_ref, low_ref, high_ref):
    @pl.when(lax.axis_index("segment") == 0)
    def _():
        even = lax.rem(lax.axis_index("space"), 2) == 0

        def choose(a, b):
            return jnp.where(even, a, b)

        for k in range(low_ref.shape[0]):
            mine, partner = mine_ref[k].astype(F32), partner_ref[k].astype(F32)
            straight, cross = straight_ref[k].astype(F32), cross_ref[k].astype(F32)
            low_ref[k] = jnp.concatenate([choose(cross, straight), choose(mine, partner)], axis=0).astype(BF16)
            high_ref[k] = jnp.concatenate([choose(partner, mine), choose(straight, cross)], axis=0).astype(BF16)


def edges_of(refs, coefs, slabs, neighbours, rate_ref, hot_ref, hot_t_ref, geo_ref):
    start, _ = first_slab(slabs)
    extra = jnp.concatenate([ref[coefs].astype(F32) for ref in refs], axis=0)
    window, c = extra.shape
    rows = window // 2
    per_slab = rows // 2
    edges = rows * neighbours
    numbers = decode(extra)
    own_extra = extra[per_slab : per_slab + rows]
    low = pltpu.roll(own_extra, c - 8, 1)
    index = own_extra.astype(jnp.int32) * BASE + low.astype(jnp.int32)
    place = lax.rem(index // per_slab - start + slabs, slabs) * per_slab + index % per_slab
    columns = lax.broadcasted_iota(jnp.int32, (rows, c), 1)
    hot = jnp.concatenate(
        [
            (place[:, SOURCES + j : SOURCES + j + 1] == columns).astype(F32)
            for j in range(neighbours)
        ],
        axis=0,
    )
    hot_t_ref[...] = jnp.transpose(hot).astype(BF16)[:window]
    hot = hot.astype(BF16)[:, :window]
    hot_ref[...] = hot
    lift = lax.broadcasted_iota(jnp.int32, (window, c), 0) // per_slab - 1
    offset = []
    for n in range(3):
        column = jnp.broadcast_to(numbers[:, n : n + 1], (window, c))
        if n == 2:
            column = column + SLAB_DEPTH * lift.astype(F32)
        there = sum(dot(hot, part) for part in split3(column))
        offset.append(there - jnp.concatenate([column[per_slab : per_slab + rows]] * neighbours, axis=0))
    flat = offset[0] * offset[0] + offset[1] * offset[1] + 1.0
    length = jnp.sqrt(flat + offset[2] * offset[2])
    planar = jnp.sqrt(flat)
    c1, s1 = offset[0] / planar, offset[1] / planar
    rate = jnp.broadcast_to(rate_ref[...], (edges, c))
    values = [
        jnp.exp(-rate * length),
        c1,
        s1,
        c1 * c1 - s1 * s1,
        2.0 * c1 * s1,
        offset[0] / length,
        offset[1] / length,
        offset[2] / length,
        1.0 / planar,
        rate,
    ]
    for n, value in enumerate(values):
        geo_ref[n * edges : (n + 1) * edges, :] = value
    return numbers[per_slab : per_slab + rows]


def turn_to_stage():
    odd = lax.rem(lax.axis_index("space"), 2)
    return jnp.where(lax.axis_index("segment") == 0, odd, 0)


def stage_kernel(moment, zero_hbm, one_hbm, two_hbm, *more):
    zero_ref, one_ref, two_ref, sems = more[-4:]

    @pl.when(turn_to_stage() == moment)
    def _():
        pairs = [(zero_hbm, zero_ref)]
        for source, target in ((one_hbm, one_ref), (two_hbm, two_ref)):
            pairs += [(source.at[n], target.at[n]) for n in range(2)]
        copies = [pltpu.make_async_copy(source, target, sems.at[n]) for n, (source, target) in enumerate(pairs)]
        for copy in copies:
            copy.start()
        for copy in copies:
            copy.wait()


def forward_kernel(
    tick, sz, slabs, neighbours, low_ref, high_ref, rate_ref, zero_ref, one_ref, two_ref,
    out_ref, pooled_ref, hot_ref, hot_t_ref, geo_ref
):
    @pl.when(lax.axis_index("segment") == tick)
    def _():
        rows = low_ref.shape[1]
        refs = (low_ref, high_ref)
        edges_of(refs, sz.coefs, slabs, neighbours, rate_ref, hot_ref, hot_t_ref, geo_ref)
        pooled = forward(refs, hot_ref, geo_ref, zero_ref, one_ref, two_ref, sz, rows, False)
        signal = signal_of(pooled, sz)
        gate, lifted = silu_parts(signal)
        for k in range(sz.coefs):
            pooled_ref[k] = pooled[k]
            added = lifted if k == 0 else gate * pooled[k]
            out_ref[k] = (own_rows(refs, k) + added).astype(BF16)
        out_ref[sz.coefs] = own_rows(refs, sz.coefs).astype(BF16)


def turn_kernel(
    tick, sz, slabs, neighbours, low_ref, high_ref, rate_ref, zero_ref, one_ref, two_ref, read_ref,
    back_low_ref, back_high_ref, hot_ref, hot_t_ref, geo_ref
):
    @pl.when(lax.axis_index("segment") == tick)
    def _():
        rows = low_ref.shape[1]
        refs = (low_ref, high_ref)
        outs = (back_low_ref, back_high_ref)
        own = edges_of(refs, sz.coefs, slabs, neighbours, rate_ref, hot_ref, hot_t_ref, geo_ref)
        pooled = forward(refs, hot_ref, geo_ref, zero_ref, one_ref, two_ref, sz, rows, True)
        signal = signal_of(pooled, sz)
        _, lifted = silu_parts(signal)
        updated = own_rows(refs, 0) + lifted
        gate, active = silu_parts(updated)
        read = read_ref[...]
        energy = jnp.sum(read * active, axis=1, keepdims=True)
        lane = lax.broadcasted_iota(jnp.int32, (rows, sz.c), 1)
        energy = around(jnp.where(lane == 3, energy, 0.0), rows // 2)
        upstream = [own[:, 3:4] * read * (gate + updated * gate * (1.0 - gate))]
        moved = backward(
            upstream, pooled, refs, hot_ref, hot_t_ref, geo_ref, zero_ref, one_ref, two_ref, sz, rows, True, outs
        )
        send_back(moved + energy, outs, sz)


def backward_kernel(
    tick, sz, up_low_ref, up_high_ref, pooled_ref, low_ref, high_ref, hot_ref, hot_t_ref, geo_ref,
    zero_ref, one_ref, two_ref, *outs
):
    @pl.when(lax.axis_index("segment") == tick)
    def _():
        rows = low_ref.shape[1]
        refs = (low_ref, high_ref)
        upstream = [up_low_ref[k].astype(F32) + up_high_ref[k].astype(F32) for k in range(sz.coefs)]
        pooled = [pooled_ref[k] for k in range(sz.coefs)]
        moved = backward(
            upstream, pooled, refs, hot_ref, hot_t_ref, geo_ref, zero_ref, one_ref, two_ref, sz, rows, False,
            outs if tick else None,
        )
        carried = decode(up_low_ref[sz.coefs].astype(F32)) + decode(up_high_ref[sz.coefs].astype(F32))
        moved = moved + around(carried, rows // 2)
        if tick:
            send_back(moved, outs, sz)
        else:
            share(moved, outs)


def call(body, operands, shapes, name, spaces=None, scratch=(), aliases=None):
    spaces = spaces or [pltpu.VMEM] * len(operands)
    operands = [pltpu.with_memory_space_constraint(value, space) for value, space in zip(operands, spaces)]
    return pl.pallas_call(
        body,
        out_shape=shapes,
        in_specs=[pl.BlockSpec(memory_space=space) for space in spaces],
        out_specs=[pl.BlockSpec(memory_space=pltpu.VMEM) for _ in shapes],
        scratch_shapes=list(scratch),
        input_output_aliases=aliases or {},
        compiler_params=pltpu.CompilerParams(vmem_limit_bytes=VMEM_LIMIT),
        name=name,
    )(*operands)


def on_device(
    node_states,
    species,
    species_table,
    places,
    sources,
    radial_rate,
    zero_weight,
    one_weight,
    two_weight,
    read_weight,
    energy_grad,
):
    segments = lax.axis_size("segment")
    slabs = lax.axis_size("space")
    batches, per_slab = species.shape
    coefs, channels = node_states.shape[2:]
    neighbours = sources.shape[2]
    rows = batches * per_slab
    edges = rows * neighbours
    sz = Sizes(zero_weight.shape, one_weight.shape, two_weight.shape, channels)
    axes = ("segment", "space")
    shape = jax.ShapeDtypeStruct

    pairs = slabs // 2

    def within(value, target):
        ways = [(s * slabs + i, s * slabs + target(i) % slabs) for s in range(segments) for i in range(slabs)]
        return lax.ppermute(value, axes, ways)

    def hop(value, start, stop, by):
        ways = [(place_of(q, pairs, start), place_of((q + by) % pairs, pairs, stop)) for q in range(pairs)]
        ways = [(start * slabs + 2 * a + c, stop * slabs + 2 * b + c) for a, b in ways for c in range(2)]
        ways += [(b, a) for a, b in ways]
        moving = {a for a, _ in ways}
        ways += [(i, i) for i in range(segments * slabs) if i not in moving]
        return lax.ppermute(value, axes, ways)

    raw = [
        node_states.transpose(0, 2, 1, 3), places.transpose(1, 0, 2), species, sources, energy_grad, species_table,
    ]
    packed = shape((coefs + 1, per_slab, channels), BF16)
    mine, other = call(
        pack_kernel, raw, [packed, packed], "pack", [pltpu.HBM] * len(raw),
        [pltpu.VMEM(v.shape, v.dtype) for v in raw] + [pltpu.SemaphoreType.DMA((len(raw),))],
    )
    partner = within(other, lambda i: i + 1 - 2 * (i % 2))
    straight = within(mine, lambda i: i + 2 if i % 2 else i - 2)
    cross = within(other, lambda i: i + 1 if i % 2 else i - 1)
    stored = [zero_weight[0], one_weight[0], two_weight[0]]
    spaces = [pltpu.HBM] * 3
    on_chip = [pltpu.VMEM(w.shape, w.dtype) for w in stored]
    sems = [pltpu.SemaphoreType.DMA((5,))]
    weights = call(functools.partial(stage_kernel, 0), stored, on_chip, "stage", spaces, sems)
    whole = shape((coefs + 1, rows, channels), BF16)
    around_all = [call(open_kernel, [mine, partner, straight, cross], [whole, whole], "open")]
    weights = call(
        functools.partial(stage_kernel, 1), [*stored, *weights, around_all[0][0]], on_chip, "stage",
        spaces + [pltpu.VMEM] * 4, sems, {3: 0, 4: 1, 5: 2},
    )
    edge_shapes = [
        shape((edges, 2 * rows), BF16), shape((2 * rows, edges), BF16), shape((10 * edges, channels), F32),
    ]
    kept = []
    for tick in range(segments - 1):
        out, *residuals = call(
            functools.partial(forward_kernel, tick, sz, slabs, neighbours),
            [*around_all[tick], radial_rate, *weights],
            [whole, shape((coefs, rows, channels), F32), *edge_shapes],
            "forward",
        )
        kept.append(residuals)
        ways = (1, 0) if tick % 2 else (0, -1)
        around_all.append([hop(out, tick, tick + 1, by) for by in ways])
    final = segments - 1
    slab_sums = shape((per_slab, channels), F32)
    parts = call(
        functools.partial(turn_kernel, final, sz, slabs, neighbours),
        [*around_all[final], radial_rate, *weights, read_weight.reshape(1, channels)],
        [whole, whole],
        "turn",
        scratch=[pltpu.VMEM(v.shape, v.dtype) for v in edge_shapes],
    )
    for tick in reversed(range(segments - 1)):
        ways = (1, 0) if tick % 2 else (0, -1)
        up = [hop(part, tick + 1, tick, -by) for part, by in zip(parts, ways)]
        pooled, *residuals = kept[tick]
        parts = call(
            functools.partial(backward_kernel, tick, sz),
            [*up, pooled, *around_all[tick], *residuals, *weights],
            [whole, whole] if tick else [slab_sums] * 4,
            "backward",
        )
    here, theirs, straight, cross = parts
    theirs = within(theirs, lambda i: i + 1 - 2 * (i % 2))
    straight = within(straight, lambda i: i - 2 if i % 2 else i + 2)
    cross = within(cross, lambda i: i + 1 if i % 2 else i - 1)
    (both,) = call(join_kernel, [here, theirs, straight, cross], [shape((rows, channels), F32)], "join")
    copies = [both] + [
        lax.ppermute(both, "segment", [(s, (s + stop) % segments) for s in range(segments)])
        for stop in range(1, segments)
    ]
    energies, gradients = call(
        close_kernel, copies, [shape((batches, per_slab), F32), shape((3, batches, per_slab), F32)], "close"
    )
    return energies, gradients.transpose(1, 0, 2)


def solution(mesh):
    in_specs = (
        P(None, "space", None, None),
        P(None, "space"),
        P(),
        P(None, None, "space"),
        P(None, "space", None),
        P("segment", None),
        P("segment", None, None),
        P("segment", None, None, None),
        P("segment", None, None, None),
        P(),
        P(None, "space"),
    )
    out_specs = (P(None, "space"), P(None, None, "space"))
    return jax.shard_map(
        on_device, mesh=mesh, in_specs=in_specs, out_specs=out_specs, check_vma=False
    )
```

```python
import functools

import jax
import jax.numpy as jnp
from jax import lax
from jax.experimental import pallas as pl
from jax.experimental.pallas import tpu as pltpu
from jax.sharding import PartitionSpec as P

SLAB_DEPTH = 2.0
F32 = jnp.float32
BF16 = jnp.bfloat16
VMEM_LIMIT = 16 * 1024 * 1024

MID, LOW, SOURCES = 32, 64, 96
BASE = 256


def split(value):
    high = value.astype(BF16)
    low = (value - high.astype(F32)).astype(BF16)
    return high, low


def split3(value):
    high = value.astype(BF16)
    rest = value - high.astype(F32)
    mid = rest.astype(BF16)
    return high, mid, (rest - mid.astype(F32)).astype(BF16)


def encode(value):
    high, mid, low = split3(value)
    return high.astype(F32) + pltpu.roll(mid.astype(F32), MID, 1) + pltpu.roll(low.astype(F32), LOW, 1)


def decode(value):
    lanes = value.shape[1]
    whole = value + pltpu.roll(value, lanes - MID, 1) + pltpu.roll(value, lanes - LOW, 1)
    lane = lax.broadcasted_iota(jnp.int32, value.shape, 1)
    return jnp.where(lane < 4, whole, 0.0)


def dot(a, b):
    return lax.dot_general(a, b, (((1,), (0,)), ((), ())), preferred_element_type=F32)


def dot_t(a, b):
    return lax.dot_general(a, b, (((1,), (1,)), ((), ())), preferred_element_type=F32)


def fine_dot(value, weights, product):
    rows = value.shape[0]
    stacked = jnp.concatenate(split(value), axis=0)
    outs = []
    for weight in weights:
        out = product(stacked, weight)
        outs.append(out[:rows] + out[rows:])
    return outs


def silu_parts(value):
    gate = 1.0 / (1.0 + jnp.exp(-value))
    return gate, value * gate


class Sizes:
    def __init__(self, zero_shape, one_shape, two_shape, channels):
        self.c = channels
        self.zero = zero_shape[-1] // channels
        self.one = one_shape[-1] // channels
        self.two = two_shape[-1] // channels
        self.coefs = self.zero + 2 * (self.one + self.two)
        self.starts = (self.zero, self.zero + 2 * self.one)
        self.counts = (self.one, self.two)

    def cols(self, first, count=1):
        return slice(first * self.c, (first + count) * self.c)


def picked_group(refs, hot, first, count):
    blocks = [jnp.concatenate([ref[k] for ref in refs], axis=0) for k in range(first, first + count)]
    return dot(hot, jnp.concatenate(blocks, axis=1))


def own_rows(refs, k):
    low, high = (ref[k].astype(F32) for ref in refs)
    slab = low.shape[0] // 2
    return jnp.concatenate([low[slab:], high[:slab]], axis=0)


def pool(value, rows):
    total = value[:rows]
    for start in range(rows, value.shape[0], rows):
        total = total + value[start : start + rows]
    return total


def geo_at(geo_ref, which, edges):
    return geo_ref[which * edges : (which + 1) * edges, :]


def forward(refs, hot_ref, geo_ref, zero_ref, one_ref, two_ref, sz, rows, last):
    hot = hot_ref[...]
    edges = hot.shape[0]
    factor = (edges // rows) ** (-0.5)
    radial = geo_at(geo_ref, 0, edges)

    def scaled(block):
        return (block * radial).astype(BF16).astype(F32)

    pooled = [None] * sz.coefs
    group = picked_group(refs, hot, 0, sz.zero)
    zin = jnp.concatenate(
        [pool(scaled(group[:, sz.cols(k)]), rows) for k in range(sz.zero)], axis=1
    )
    kept = 1 if last else sz.zero
    (zout,) = fine_dot(zin, [zero_ref[:, sz.cols(0, kept)]], dot)
    for k in range(kept):
        pooled[k] = zout[:, sz.cols(k)] * factor
    for order in range(2):
        first, count = sz.starts[order], sz.counts[order]
        weight_ref = (one_ref, two_ref)[order]
        cos = geo_at(geo_ref, 1 + 2 * order, edges)
        sin = geo_at(geo_ref, 2 + 2 * order, edges)
        group = picked_group(refs, hot, first, 2 * count)
        res, ims = [], []
        for k in range(count):
            re = scaled(group[:, sz.cols(k)])
            im = scaled(group[:, sz.cols(count + k)])
            res.append(pool(cos * re - sin * im, rows))
            ims.append(pool(sin * re + cos * im, rows))
        both = jnp.concatenate(
            [jnp.concatenate(res, axis=1), jnp.concatenate(ims, axis=1)], axis=0
        )
        a, b = fine_dot(both, [weight_ref[0], weight_ref[1]], dot)
        out_re = (a[:rows] - b[rows:]) * factor
        out_im = (b[:rows] + a[rows:]) * factor
        for k in range(count):
            pooled[first + k] = out_re[:, sz.cols(k)]
            pooled[first + count + k] = out_im[:, sz.cols(k)]
    return pooled


def signal_of(pooled, sz):
    total = pooled[0]
    for k in range(sz.zero, sz.coefs):
        total = total + pooled[k] * pooled[k]
    return total


def backward(
    upstream, pooled, refs, hot_ref, hot_t_ref, geo_ref, zero_ref, one_ref, two_ref, sz, rows, last, outs
):
    hot = hot_ref[...]
    hot_t = hot_t_ref[...]
    edges = hot.shape[0]
    slab = rows // 2
    factor = (edges // rows) ** (-0.5)
    signal = signal_of(pooled, sz)
    gate, _ = silu_parts(signal)
    slope = gate * (1.0 - gate)
    d_signal = upstream[0] * (gate + signal * slope)
    if not last:
        inner = upstream[1] * pooled[1]
        for k in range(2, sz.coefs):
            inner = inner + upstream[k] * pooled[k]
        d_signal = d_signal + inner * slope
    d_pooled = [d_signal * factor]
    for k in range(1, sz.coefs):
        if last:
            d_pooled.append(2.0 * factor * d_signal * pooled[k] if k >= sz.zero else None)
        else:
            term = gate * upstream[k]
            if k >= sz.zero:
                term = term + 2.0 * d_signal * pooled[k]
            d_pooled.append(term * factor)

    radial = geo_at(geo_ref, 0, edges)
    kept = 1 if last else sz.zero
    (dz,) = fine_dot(jnp.concatenate(d_pooled[:kept], axis=1), [zero_ref[:, sz.cols(0, kept)]], dot_t)

    def spread(block):
        return jnp.concatenate([block] * (edges // rows), axis=0)

    def scatter(first, blocks):
        if outs is None:
            return
        high, low = split(jnp.concatenate(blocks, axis=1))
        back = dot(hot_t, high) + dot(hot_t, low)
        for n in range(len(blocks)):
            k = first + n
            part = back[:, sz.cols(n)]
            if not last or k == 0:
                part = part + around(upstream[k], slab)
            outs[0][k] = part[:rows].astype(BF16)
            outs[1][k] = part[rows:].astype(BF16)

    q_len = jnp.zeros((edges, sz.c), F32)
    group = picked_group(refs, hot, 0, sz.zero)
    blocks = []
    for k in range(sz.zero):
        grad = spread(dz[:, sz.cols(k)])
        q_len = q_len + grad * group[:, sz.cols(k)]
        blocks.append(grad * radial)
    q_len = q_len * radial
    scatter(0, blocks)
    q_turn = []
    for order in range(2):
        first, count = sz.starts[order], sz.counts[order]
        weight_ref = (one_ref, two_ref)[order]
        cos = geo_at(geo_ref, 1 + 2 * order, edges)
        sin = geo_at(geo_ref, 2 + 2 * order, edges)
        both = jnp.concatenate(
            [
                jnp.concatenate(d_pooled[first : first + count], axis=1),
                jnp.concatenate(d_pooled[first + count : first + 2 * count], axis=1),
            ],
            axis=0,
        )
        a, b = fine_dot(both, [weight_ref[0], weight_ref[1]], dot_t)
        d_re = a[:rows] + b[rows:]
        d_im = a[rows:] - b[:rows]
        group = picked_group(refs, hot, first, 2 * count)
        q_cos = jnp.zeros((edges, sz.c), F32)
        q_sin = jnp.zeros((edges, sz.c), F32)
        cos_r = cos * radial
        sin_r = sin * radial
        blocks_re, blocks_im = [], []
        for k in range(count):
            re = group[:, sz.cols(k)]
            im = group[:, sz.cols(count + k)]
            g_re = spread(d_re[:, sz.cols(k)])
            g_im = spread(d_im[:, sz.cols(k)])
            q_cos = q_cos + (re * g_re + im * g_im)
            q_sin = q_sin + (re * g_im - im * g_re)
            if outs is not None:
                blocks_re.append(cos_r * g_re + sin_r * g_im)
                blocks_im.append(cos_r * g_im - sin_r * g_re)
        scatter(first, blocks_re + blocks_im)
        q_cos = q_cos * radial
        q_sin = q_sin * radial
        q_len = q_len + cos * q_cos + sin * q_sin
        q_turn.append((q_cos, q_sin))

    rate = geo_at(geo_ref, 9, edges)

    def total(value):
        return jnp.sum(value, axis=1, keepdims=True)

    d_len = -total(q_len * rate)
    (dc1, ds1), (dc2, ds2) = [(total(a), total(b)) for a, b in q_turn]
    c1, s1 = geo_at(geo_ref, 1, edges), geo_at(geo_ref, 2, edges)
    ux, uy, uz = (geo_at(geo_ref, 5 + n, edges) for n in range(3))
    inv_planar = geo_at(geo_ref, 8, edges)
    dc1 = dc1 + 2.0 * (c1 * dc2 + s1 * ds2)
    ds1 = ds1 + 2.0 * (c1 * ds2 - s1 * dc2)
    along = c1 * dc1 + s1 * ds1
    dx = (dc1 - along * c1) * inv_planar + d_len * ux
    dy = (ds1 - along * s1) * inv_planar + d_len * uy
    dz_ = d_len * uz
    lane = lax.broadcasted_iota(jnp.int32, (edges, sz.c), 1)
    change = jnp.where(lane == 0, dx, jnp.where(lane == 1, dy, jnp.where(lane == 2, dz_, 0.0)))
    moved = sum(dot(hot_t, part) for part in split3(change))
    return moved - around(pool(change, rows), slab)


def around(own, slab):
    edge = jnp.zeros((slab, own.shape[1]), F32)
    return jnp.concatenate([edge, own, edge], axis=0)


def place_of(pair, pairs, segment):
    if segment == 0:
        return pair
    return 2 * pair if pair < pairs // 2 else 2 * (pairs - 1 - pair) + 1


def first_slab(slabs):
    slab_now = lax.axis_index("space")
    segment = lax.axis_index("segment")
    chip = slab_now // 2
    folded = jnp.where(lax.rem(chip, 2) == 0, chip // 2, slabs // 2 - 1 - chip // 2)
    pair = jnp.where(segment == 0, chip, folded)
    return lax.rem(2 * pair + lax.rem(segment, 2) - 1 + slabs, slabs), lax.rem(slab_now, 2)


def send_back(moved, outs, sz):
    rows = moved.shape[0] // 2
    coded = encode(moved).astype(BF16)
    outs[0][sz.coefs] = coded[:rows]
    outs[1][sz.coefs] = coded[rows:]


def share(moved, outs):
    slab = moved.shape[0] // 4
    left, low, high, right = (moved[n * slab : (n + 1) * slab] for n in range(4))
    even = lax.rem(lax.axis_index("space"), 2) == 0
    outs[0][...] = jnp.where(even, low, high)
    outs[1][...] = jnp.where(even, high, low)
    outs[2][...] = jnp.where(even, right, left)
    outs[3][...] = jnp.where(even, left, right)


def join_kernel(here_ref, theirs_ref, straight_ref, cross_ref, both_ref):
    slab = here_ref.shape[0]
    even = lax.rem(lax.axis_index("space"), 2) == 0
    here = here_ref[...] + straight_ref[...]
    there = theirs_ref[...] + cross_ref[...]
    both_ref[:slab, :] = jnp.where(even, here, there)
    both_ref[slab:, :] = jnp.where(even, there, here)


def close_kernel(*refs):
    *sums_refs, energies_ref, places_ref = refs
    slab = energies_ref.shape[1]
    for n, ref in enumerate(sums_refs):

        @pl.when(lax.axis_index("segment") == n)
        def _(ref=ref):
            sums = ref[...]
            rows, c = sums.shape
            turned = jnp.transpose(jnp.concatenate([sums, jnp.zeros((c - rows, c), F32)], axis=0))
            for b in range(2):
                energies_ref[b : b + 1, :] = turned[3:4, b * slab : (b + 1) * slab]
                for n in range(3):
                    places_ref[n, b : b + 1, :] = turned[n : n + 1, b * slab : (b + 1) * slab]


def pack_kernel(
    node_hbm, places_hbm, species_hbm, sources_hbm, grad_hbm, table_hbm, mine_ref, other_ref,
    states, places, species, sources, grads, table, sems
):
    @pl.when(lax.axis_index("segment") == 0)
    def _():
        pack(
            (node_hbm, places_hbm, species_hbm, sources_hbm, grad_hbm, table_hbm), mine_ref, other_ref,
            states, places, species, sources, grads, table, sems,
        )


def pack(given, mine_ref, other_ref, states, places, species, sources, grads, table, sems):
    batch = lax.rem(lax.axis_index("space"), 2)
    copies = []
    for n, (source, target) in enumerate(zip(given, (states, places, species, sources, grads, table))):
        copies.append(pltpu.make_async_copy(source, target, sems.at[n]))
        copies[-1].start()
    for copy in copies:
        copy.wait()
    coefs, per_slab, c = states.shape[1:]
    lane = lax.broadcasted_iota(jnp.int32, (per_slab, c), 1)
    eye = (
        lax.broadcasted_iota(jnp.int32, (per_slab, per_slab), 0)
        == lax.broadcasted_iota(jnp.int32, (per_slab, per_slab), 1)
    )

    def column(row):
        return jnp.sum(jnp.where(eye, jnp.broadcast_to(row, (per_slab, per_slab)), 0.0), axis=1, keepdims=True)

    both = []
    for b in range(2):
        names = column(species[b : b + 1, :].astype(F32)).astype(jnp.int32)
        kinds = table.shape[0]
        hot = (names == lax.broadcasted_iota(jnp.int32, (per_slab, kinds), 1)).astype(BF16)
        first = (states[b, 0].astype(F32) + dot(hot, table[...])).astype(BF16)
        extra = jnp.zeros((per_slab, c), F32)
        for n in range(3):
            extra = jnp.where(lane == n, column(places[n, b : b + 1, :]), extra)
        extra = encode(jnp.where(lane == 3, column(grads[b : b + 1, :]), extra))
        for j in range(sources.shape[2]):
            index = sources[b, :, j : j + 1]
            extra = jnp.where(lane == SOURCES + j, (index // BASE).astype(F32), extra)
            extra = jnp.where(lane == SOURCES + 8 + j, (index % BASE).astype(F32), extra)
        both.append((first, extra.astype(BF16)))
    for ref, chosen in ((mine_ref, batch), (other_ref, 1 - batch)):
        ref[pl.ds(0, coefs)] = states[chosen]
        ref[0] = jnp.where(chosen == 0, both[0][0].astype(F32), both[1][0].astype(F32)).astype(BF16)
        ref[coefs] = jnp.where(chosen == 0, both[0][1].astype(F32), both[1][1].astype(F32)).astype(BF16)


def open_kernel(mine_ref, partner_ref, straight_ref, cross_ref, low_ref, high_ref):
    @pl.when(lax.axis_index("segment") == 0)
    def _():
        even = lax.rem(lax.axis_index("space"), 2) == 0

        def choose(a, b):
            return jnp.where(even, a, b)

        for k in range(low_ref.shape[0]):
            mine, partner = mine_ref[k].astype(F32), partner_ref[k].astype(F32)
            straight, cross = straight_ref[k].astype(F32), cross_ref[k].astype(F32)
            low_ref[k] = jnp.concatenate([choose(cross, straight), choose(mine, partner)], axis=0).astype(BF16)
            high_ref[k] = jnp.concatenate([choose(partner, mine), choose(straight, cross)], axis=0).astype(BF16)


def edges_of(refs, coefs, slabs, neighbours, rate_ref, hot_ref, hot_t_ref, geo_ref):
    start, _ = first_slab(slabs)
    extra = jnp.concatenate([ref[coefs].astype(F32) for ref in refs], axis=0)
    window, c = extra.shape
    rows = window // 2
    per_slab = rows // 2
    edges = rows * neighbours
    numbers = decode(extra)
    own_extra = extra[per_slab : per_slab + rows]
    low = pltpu.roll(own_extra, c - 8, 1)
    index = own_extra.astype(jnp.int32) * BASE + low.astype(jnp.int32)
    place = lax.rem(index // per_slab - start + slabs, slabs) * per_slab + index % per_slab
    columns = lax.broadcasted_iota(jnp.int32, (rows, c), 1)
    hot = jnp.concatenate(
        [
            (place[:, SOURCES + j : SOURCES + j + 1] == columns).astype(F32)
            for j in range(neighbours)
        ],
        axis=0,
    )
    hot_t_ref[...] = jnp.transpose(hot).astype(BF16)[:window]
    hot = hot.astype(BF16)[:, :window]
    hot_ref[...] = hot
    lift = lax.broadcasted_iota(jnp.int32, (window, c), 0) // per_slab - 1
    offset = []
    for n in range(3):
        column = jnp.broadcast_to(numbers[:, n : n + 1], (window, c))
        if n == 2:
            column = column + SLAB_DEPTH * lift.astype(F32)
        there = sum(dot(hot, part) for part in split3(column))
        offset.append(there - jnp.concatenate([column[per_slab : per_slab + rows]] * neighbours, axis=0))
    flat = offset[0] * offset[0] + offset[1] * offset[1] + 1.0
    length = jnp.sqrt(flat + offset[2] * offset[2])
    planar = jnp.sqrt(flat)
    c1, s1 = offset[0] / planar, offset[1] / planar
    rate = jnp.broadcast_to(rate_ref[...], (edges, c))
    values = [
        jnp.exp(-rate * length),
        c1,
        s1,
        c1 * c1 - s1 * s1,
        2.0 * c1 * s1,
        offset[0] / length,
        offset[1] / length,
        offset[2] / length,
        1.0 / planar,
        rate,
    ]
    for n, value in enumerate(values):
        geo_ref[n * edges : (n + 1) * edges, :] = value
    return numbers[per_slab : per_slab + rows]


def turn_to_stage():
    odd = lax.rem(lax.axis_index("space"), 2)
    return jnp.where(lax.axis_index("segment") == 0, odd, 0)


def stage_kernel(moment, zero_hbm, one_hbm, two_hbm, *more):
    zero_ref, one_ref, two_ref, sems = more[-4:]

    @pl.when(turn_to_stage() == moment)
    def _():
        pairs = [(zero_hbm, zero_ref)]
        for source, target in ((one_hbm, one_ref), (two_hbm, two_ref)):
            pairs += [(source.at[n], target.at[n]) for n in range(2)]
        copies = [pltpu.make_async_copy(source, target, sems.at[n]) for n, (source, target) in enumerate(pairs)]
        for copy in copies:
            copy.start()
        for copy in copies:
            copy.wait()


def forward_kernel(
    tick, sz, slabs, neighbours, low_ref, high_ref, rate_ref, zero_ref, one_ref, two_ref,
    out_ref, pooled_ref, hot_ref, hot_t_ref, geo_ref
):
    @pl.when(lax.axis_index("segment") == tick)
    def _():
        rows = low_ref.shape[1]
        refs = (low_ref, high_ref)
        edges_of(refs, sz.coefs, slabs, neighbours, rate_ref, hot_ref, hot_t_ref, geo_ref)
        pooled = forward(refs, hot_ref, geo_ref, zero_ref, one_ref, two_ref, sz, rows, False)
        signal = signal_of(pooled, sz)
        gate, lifted = silu_parts(signal)
        for k in range(sz.coefs):
            pooled_ref[k] = pooled[k]
            added = lifted if k == 0 else gate * pooled[k]
            out_ref[k] = (own_rows(refs, k) + added).astype(BF16)
        out_ref[sz.coefs] = own_rows(refs, sz.coefs).astype(BF16)


def turn_kernel(
    tick, sz, slabs, neighbours, low_ref, high_ref, rate_ref, zero_ref, one_ref, two_ref, read_ref,
    back_low_ref, back_high_ref, hot_ref, hot_t_ref, geo_ref
):
    @pl.when(lax.axis_index("segment") == tick)
    def _():
        rows = low_ref.shape[1]
        refs = (low_ref, high_ref)
        outs = (back_low_ref, back_high_ref)
        own = edges_of(refs, sz.coefs, slabs, neighbours, rate_ref, hot_ref, hot_t_ref, geo_ref)
        pooled = forward(refs, hot_ref, geo_ref, zero_ref, one_ref, two_ref, sz, rows, True)
        signal = signal_of(pooled, sz)
        _, lifted = silu_parts(signal)
        updated = own_rows(refs, 0) + lifted
        gate, active = silu_parts(updated)
        read = read_ref[...]
        energy = jnp.sum(read * active, axis=1, keepdims=True)
        lane = lax.broadcasted_iota(jnp.int32, (rows, sz.c), 1)
        energy = around(jnp.where(lane == 3, energy, 0.0), rows // 2)
        upstream = [own[:, 3:4] * read * (gate + updated * gate * (1.0 - gate))]
        moved = backward(
            upstream, pooled, refs, hot_ref, hot_t_ref, geo_ref, zero_ref, one_ref, two_ref, sz, rows, True, outs
        )
        send_back(moved + energy, outs, sz)


def backward_kernel(
    tick, sz, up_low_ref, up_high_ref, pooled_ref, low_ref, high_ref, hot_ref, hot_t_ref, geo_ref,
    zero_ref, one_ref, two_ref, *outs
):
    @pl.when(lax.axis_index("segment") == tick)
    def _():
        rows = low_ref.shape[1]
        refs = (low_ref, high_ref)
        upstream = [up_low_ref[k].astype(F32) + up_high_ref[k].astype(F32) for k in range(sz.coefs)]
        pooled = [pooled_ref[k] for k in range(sz.coefs)]
        moved = backward(
            upstream, pooled, refs, hot_ref, hot_t_ref, geo_ref, zero_ref, one_ref, two_ref, sz, rows, False,
            outs if tick else None,
        )
        carried = decode(up_low_ref[sz.coefs].astype(F32)) + decode(up_high_ref[sz.coefs].astype(F32))
        moved = moved + around(carried, rows // 2)
        if tick:
            send_back(moved, outs, sz)
        else:
            share(moved, outs)


def call(body, operands, shapes, name, spaces=None, scratch=(), aliases=None):
    spaces = spaces or [pltpu.VMEM] * len(operands)
    operands = [pltpu.with_memory_space_constraint(value, space) for value, space in zip(operands, spaces)]
    return pl.pallas_call(
        body,
        out_shape=shapes,
        in_specs=[pl.BlockSpec(memory_space=space) for space in spaces],
        out_specs=[pl.BlockSpec(memory_space=pltpu.VMEM) for _ in shapes],
        scratch_shapes=list(scratch),
        input_output_aliases=aliases or {},
        compiler_params=pltpu.CompilerParams(vmem_limit_bytes=VMEM_LIMIT),
        name=name,
    )(*operands)


def on_device(
    node_states,
    species,
    species_table,
    places,
    sources,
    radial_rate,
    zero_weight,
    one_weight,
    two_weight,
    read_weight,
    energy_grad,
):
    segments = lax.axis_size("segment")
    slabs = lax.axis_size("space")
    batches, per_slab = species.shape
    coefs, channels = node_states.shape[2:]
    neighbours = sources.shape[2]
    rows = batches * per_slab
    edges = rows * neighbours
    sz = Sizes(zero_weight.shape, one_weight.shape, two_weight.shape, channels)
    axes = ("segment", "space")
    shape = jax.ShapeDtypeStruct

    pairs = slabs // 2

    def within(value, target):
        ways = [(s * slabs + i, s * slabs + target(i) % slabs) for s in range(segments) for i in range(slabs)]
        return lax.ppermute(value, axes, ways)

    def hop(value, step, by):
        ways = []
        for start in range(segments):
            stop = (start + step) % segments
            for q in range(pairs):
                a, b = place_of(q, pairs, start), place_of((q + by) % pairs, pairs, stop)
                ways += [(start * slabs + 2 * a + c, stop * slabs + 2 * b + c) for c in range(2)]
        return lax.ppermute(value, axes, ways)

    raw = [
        node_states.transpose(0, 2, 1, 3), places.transpose(1, 0, 2), species, sources, energy_grad, species_table,
    ]
    packed = shape((coefs + 1, per_slab, channels), BF16)
    mine, other = call(
        pack_kernel, raw, [packed, packed], "pack", [pltpu.HBM] * len(raw),
        [pltpu.VMEM(v.shape, v.dtype) for v in raw] + [pltpu.SemaphoreType.DMA((len(raw),))],
    )
    partner = within(other, lambda i: i + 1 - 2 * (i % 2))
    straight = within(mine, lambda i: i + 2 if i % 2 else i - 2)
    cross = within(other, lambda i: i + 1 if i % 2 else i - 1)
    stored = [zero_weight[0], one_weight[0], two_weight[0]]
    spaces = [pltpu.HBM] * 3
    on_chip = [pltpu.VMEM(w.shape, w.dtype) for w in stored]
    sems = [pltpu.SemaphoreType.DMA((5,))]
    weights = call(functools.partial(stage_kernel, 0), stored, on_chip, "stage", spaces, sems)
    whole = shape((coefs + 1, rows, channels), BF16)
    around_all = [call(open_kernel, [mine, partner, straight, cross], [whole, whole], "open")]
    weights = call(
        functools.partial(stage_kernel, 1), [*stored, *weights, around_all[0][0]], on_chip, "stage",
        spaces + [pltpu.VMEM] * 4, sems, {3: 0, 4: 1, 5: 2},
    )
    edge_shapes = [
        shape((edges, 2 * rows), BF16), shape((2 * rows, edges), BF16), shape((10 * edges, channels), F32),
    ]
    kept = []
    for tick in range(segments - 1):
        out, *residuals = call(
            functools.partial(forward_kernel, tick, sz, slabs, neighbours),
            [*around_all[tick], radial_rate, *weights],
            [whole, shape((coefs, rows, channels), F32), *edge_shapes],
            "forward",
        )
        kept.append(residuals)
        ways = (1, 0) if tick % 2 else (0, -1)
        around_all.append([hop(out, 1, by) for by in ways])
    final = segments - 1
    slab_sums = shape((per_slab, channels), F32)
    parts = call(
        functools.partial(turn_kernel, final, sz, slabs, neighbours),
        [*around_all[final], radial_rate, *weights, read_weight.reshape(1, channels)],
        [whole, whole],
        "turn",
        scratch=[pltpu.VMEM(v.shape, v.dtype) for v in edge_shapes],
    )
    for tick in reversed(range(segments - 1)):
        ways = (1, 0) if tick % 2 else (0, -1)
        up = [hop(part, -1, -by) for part, by in zip(parts, ways)]
        pooled, *residuals = kept[tick]
        parts = call(
            functools.partial(backward_kernel, tick, sz),
            [*up, pooled, *around_all[tick], *residuals, *weights],
            [whole, whole] if tick else [slab_sums] * 4,
            "backward",
        )
    here, theirs, straight, cross = parts
    theirs = within(theirs, lambda i: i + 1 - 2 * (i % 2))
    straight = within(straight, lambda i: i - 2 if i % 2 else i + 2)
    cross = within(cross, lambda i: i + 1 if i % 2 else i - 1)
    (both,) = call(join_kernel, [here, theirs, straight, cross], [shape((rows, channels), F32)], "join")
    copies = [both] + [
        lax.ppermute(both, "segment", [(s, (s + stop) % segments) for s in range(segments)])
        for stop in range(1, segments)
    ]
    energies, gradients = call(
        close_kernel, copies, [shape((batches, per_slab), F32), shape((3, batches, per_slab), F32)], "close"
    )
    return energies, gradients.transpose(1, 0, 2)


def solution(mesh):
    in_specs = (
        P(None, "space", None, None),
        P(None, "space"),
        P(),
        P(None, None, "space"),
        P(None, "space", None),
        P("segment", None),
        P("segment", None, None),
        P("segment", None, None, None),
        P("segment", None, None, None),
        P(),
        P(None, "space"),
    )
    out_specs = (P(None, "space"), P(None, None, "space"))
    return jax.shard_map(
        on_device, mesh=mesh, in_specs=in_specs, out_specs=out_specs, check_vma=False
    )
```

```python
import functools

import jax
import jax.numpy as jnp
from jax import lax
from jax.experimental import pallas as pl
from jax.experimental.pallas import tpu as pltpu
from jax.sharding import PartitionSpec as P

SLAB_DEPTH = 2.0
F32 = jnp.float32
BF16 = jnp.bfloat16
VMEM_LIMIT = 16 * 1024 * 1024

MID, LOW, SOURCES = 32, 64, 96
BASE = 256


def split(value):
    high = value.astype(BF16)
    low = (value - high.astype(F32)).astype(BF16)
    return high, low


def split3(value):
    high = value.astype(BF16)
    rest = value - high.astype(F32)
    mid = rest.astype(BF16)
    return high, mid, (rest - mid.astype(F32)).astype(BF16)


def encode(value):
    high, mid, low = split3(value)
    return high.astype(F32) + pltpu.roll(mid.astype(F32), MID, 1) + pltpu.roll(low.astype(F32), LOW, 1)


def decode(value):
    lanes = value.shape[1]
    whole = value + pltpu.roll(value, lanes - MID, 1) + pltpu.roll(value, lanes - LOW, 1)
    lane = lax.broadcasted_iota(jnp.int32, value.shape, 1)
    return jnp.where(lane < 4, whole, 0.0)


def dot(a, b):
    return lax.dot_general(a, b, (((1,), (0,)), ((), ())), preferred_element_type=F32)


def dot_t(a, b):
    return lax.dot_general(a, b, (((1,), (1,)), ((), ())), preferred_element_type=F32)


def fine_dot(value, weights, product):
    rows = value.shape[0]
    stacked = jnp.concatenate(split(value), axis=0)
    outs = []
    for weight in weights:
        out = product(stacked, weight)
        outs.append(out[:rows] + out[rows:])
    return outs


def silu_parts(value):
    gate = 1.0 / (1.0 + jnp.exp(-value))
    return gate, value * gate


class Sizes:
    def __init__(self, zero_shape, one_shape, two_shape, channels):
        self.c = channels
        self.zero = zero_shape[-1] // channels
        self.one = one_shape[-1] // channels
        self.two = two_shape[-1] // channels
        self.coefs = self.zero + 2 * (self.one + self.two)
        self.starts = (self.zero, self.zero + 2 * self.one)
        self.counts = (self.one, self.two)

    def cols(self, first, count=1):
        return slice(first * self.c, (first + count) * self.c)


def picked_group(refs, hot, first, count):
    blocks = [jnp.concatenate([ref[k] for ref in refs], axis=0) for k in range(first, first + count)]
    return dot(hot, jnp.concatenate(blocks, axis=1))


def own_rows(refs, k):
    low, high = (ref[k].astype(F32) for ref in refs)
    slab = low.shape[0] // 2
    return jnp.concatenate([low[slab:], high[:slab]], axis=0)


def pool(value, rows):
    total = value[:rows]
    for start in range(rows, value.shape[0], rows):
        total = total + value[start : start + rows]
    return total


def geo_at(geo_ref, which, edges):
    return geo_ref[which * edges : (which + 1) * edges, :]


def forward(refs, hot_ref, geo_ref, zero_ref, one_ref, two_ref, sz, rows, last):
    hot = hot_ref[...]
    edges = hot.shape[0]
    factor = (edges // rows) ** (-0.5)
    radial = geo_at(geo_ref, 0, edges)

    def scaled(block):
        return (block * radial).astype(BF16).astype(F32)

    pooled = [None] * sz.coefs
    group = picked_group(refs, hot, 0, sz.zero)
    zin = jnp.concatenate(
        [pool(scaled(group[:, sz.cols(k)]), rows) for k in range(sz.zero)], axis=1
    )
    kept = 1 if last else sz.zero
    (zout,) = fine_dot(zin, [zero_ref[:, sz.cols(0, kept)]], dot)
    for k in range(kept):
        pooled[k] = zout[:, sz.cols(k)] * factor
    for order in range(2):
        first, count = sz.starts[order], sz.counts[order]
        weight_ref = (one_ref, two_ref)[order]
        cos = geo_at(geo_ref, 1 + 2 * order, edges)
        sin = geo_at(geo_ref, 2 + 2 * order, edges)
        group = picked_group(refs, hot, first, 2 * count)
        res, ims = [], []
        for k in range(count):
            re = scaled(group[:, sz.cols(k)])
            im = scaled(group[:, sz.cols(count + k)])
            res.append(pool(cos * re - sin * im, rows))
            ims.append(pool(sin * re + cos * im, rows))
        both = jnp.concatenate(
            [jnp.concatenate(res, axis=1), jnp.concatenate(ims, axis=1)], axis=0
        )
        a, b = fine_dot(both, [weight_ref[0], weight_ref[1]], dot)
        out_re = (a[:rows] - b[rows:]) * factor
        out_im = (b[:rows] + a[rows:]) * factor
        for k in range(count):
            pooled[first + k] = out_re[:, sz.cols(k)]
            pooled[first + count + k] = out_im[:, sz.cols(k)]
    return pooled


def signal_of(pooled, sz):
    total = pooled[0]
    for k in range(sz.zero, sz.coefs):
        total = total + pooled[k] * pooled[k]
    return total


def backward(
    upstream, pooled, refs, hot_ref, hot_t_ref, geo_ref, zero_ref, one_ref, two_ref, sz, rows, last, outs
):
    hot = hot_ref[...]
    hot_t = hot_t_ref[...]
    edges = hot.shape[0]
    slab = rows // 2
    factor = (edges // rows) ** (-0.5)
    signal = signal_of(pooled, sz)
    gate, _ = silu_parts(signal)
    slope = gate * (1.0 - gate)
    d_signal = upstream[0] * (gate + signal * slope)
    if not last:
        inner = upstream[1] * pooled[1]
        for k in range(2, sz.coefs):
            inner = inner + upstream[k] * pooled[k]
        d_signal = d_signal + inner * slope
    d_pooled = [d_signal * factor]
    for k in range(1, sz.coefs):
        if last:
            d_pooled.append(2.0 * factor * d_signal * pooled[k] if k >= sz.zero else None)
        else:
            term = gate * upstream[k]
            if k >= sz.zero:
                term = term + 2.0 * d_signal * pooled[k]
            d_pooled.append(term * factor)

    radial = geo_at(geo_ref, 0, edges)
    kept = 1 if last else sz.zero
    (dz,) = fine_dot(jnp.concatenate(d_pooled[:kept], axis=1), [zero_ref[:, sz.cols(0, kept)]], dot_t)

    def spread(block):
        return jnp.concatenate([block] * (edges // rows), axis=0)

    def scatter(first, blocks):
        if outs is None:
            return
        high, low = split(jnp.concatenate(blocks, axis=1))
        back = dot(hot_t, high) + dot(hot_t, low)
        for n in range(len(blocks)):
            k = first + n
            part = back[:, sz.cols(n)]
            if not last or k == 0:
                part = part + around(upstream[k], slab)
            outs[0][k] = part[:rows].astype(BF16)
            outs[1][k] = part[rows:].astype(BF16)

    q_len = jnp.zeros((edges, sz.c), F32)
    group = picked_group(refs, hot, 0, sz.zero)
    blocks = []
    for k in range(sz.zero):
        grad = spread(dz[:, sz.cols(k)])
        q_len = q_len + grad * group[:, sz.cols(k)]
        blocks.append(grad * radial)
    q_len = q_len * radial
    scatter(0, blocks)
    q_turn = []
    for order in range(2):
        first, count = sz.starts[order], sz.counts[order]
        weight_ref = (one_ref, two_ref)[order]
        cos = geo_at(geo_ref, 1 + 2 * order, edges)
        sin = geo_at(geo_ref, 2 + 2 * order, edges)
        both = jnp.concatenate(
            [
                jnp.concatenate(d_pooled[first : first + count], axis=1),
                jnp.concatenate(d_pooled[first + count : first + 2 * count], axis=1),
            ],
            axis=0,
        )
        a, b = fine_dot(both, [weight_ref[0], weight_ref[1]], dot_t)
        d_re = a[:rows] + b[rows:]
        d_im = a[rows:] - b[:rows]
        group = picked_group(refs, hot, first, 2 * count)
        q_cos = jnp.zeros((edges, sz.c), F32)
        q_sin = jnp.zeros((edges, sz.c), F32)
        cos_r = cos * radial
        sin_r = sin * radial
        blocks_re, blocks_im = [], []
        for k in range(count):
            re = group[:, sz.cols(k)]
            im = group[:, sz.cols(count + k)]
            g_re = spread(d_re[:, sz.cols(k)])
            g_im = spread(d_im[:, sz.cols(k)])
            q_cos = q_cos + (re * g_re + im * g_im)
            q_sin = q_sin + (re * g_im - im * g_re)
            if outs is not None:
                blocks_re.append(cos_r * g_re + sin_r * g_im)
                blocks_im.append(cos_r * g_im - sin_r * g_re)
        scatter(first, blocks_re + blocks_im)
        q_cos = q_cos * radial
        q_sin = q_sin * radial
        q_len = q_len + cos * q_cos + sin * q_sin
        q_turn.append((q_cos, q_sin))

    rate = geo_at(geo_ref, 9, edges)

    def total(value):
        return jnp.sum(value, axis=1, keepdims=True)

    d_len = -total(q_len * rate)
    (dc1, ds1), (dc2, ds2) = [(total(a), total(b)) for a, b in q_turn]
    c1, s1 = geo_at(geo_ref, 1, edges), geo_at(geo_ref, 2, edges)
    ux, uy, uz = (geo_at(geo_ref, 5 + n, edges) for n in range(3))
    inv_planar = geo_at(geo_ref, 8, edges)
    dc1 = dc1 + 2.0 * (c1 * dc2 + s1 * ds2)
    ds1 = ds1 + 2.0 * (c1 * ds2 - s1 * dc2)
    along = c1 * dc1 + s1 * ds1
    dx = (dc1 - along * c1) * inv_planar + d_len * ux
    dy = (ds1 - along * s1) * inv_planar + d_len * uy
    dz_ = d_len * uz
    lane = lax.broadcasted_iota(jnp.int32, (edges, sz.c), 1)
    change = jnp.where(lane == 0, dx, jnp.where(lane == 1, dy, jnp.where(lane == 2, dz_, 0.0)))
    moved = sum(dot(hot_t, part) for part in split3(change))
    return moved - around(pool(change, rows), slab)


def around(own, slab):
    edge = jnp.zeros((slab, own.shape[1]), F32)
    return jnp.concatenate([edge, own, edge], axis=0)


def place_of(pair, pairs, segment):
    if segment == 0:
        return pair
    return 2 * pair if pair < pairs // 2 else 2 * (pairs - 1 - pair) + 1


def first_slab(slabs):
    slab_now = lax.axis_index("space")
    segment = lax.axis_index("segment")
    chip = slab_now // 2
    folded = jnp.where(lax.rem(chip, 2) == 0, chip // 2, slabs // 2 - 1 - chip // 2)
    pair = jnp.where(segment == 0, chip, folded)
    return lax.rem(2 * pair + lax.rem(segment, 2) - 1 + slabs, slabs), lax.rem(slab_now, 2)


def send_back(moved, outs, sz):
    rows = moved.shape[0] // 2
    coded = encode(moved).astype(BF16)
    outs[0][sz.coefs] = coded[:rows]
    outs[1][sz.coefs] = coded[rows:]


def share(moved, outs):
    slab = moved.shape[0] // 4
    left, low, high, right = (moved[n * slab : (n + 1) * slab] for n in range(4))
    even = lax.rem(lax.axis_index("space"), 2) == 0
    outs[0][...] = jnp.where(even, low, high)
    outs[1][...] = jnp.where(even, high, low)
    outs[2][...] = jnp.where(even, right, left)
    outs[3][...] = jnp.where(even, left, right)


def join_kernel(here_ref, theirs_ref, straight_ref, cross_ref, both_ref):
    slab = here_ref.shape[0]
    even = lax.rem(lax.axis_index("space"), 2) == 0
    here = here_ref[...] + straight_ref[...]
    there = theirs_ref[...] + cross_ref[...]
    both_ref[:slab, :] = jnp.where(even, here, there)
    both_ref[slab:, :] = jnp.where(even, there, here)


def close_kernel(*refs):
    *sums_refs, energies_ref, places_ref = refs
    slab = energies_ref.shape[1]
    for n, ref in enumerate(sums_refs):

        @pl.when(lax.axis_index("segment") == n)
        def _(ref=ref):
            sums = ref[...]
            rows, c = sums.shape
            turned = jnp.transpose(jnp.concatenate([sums, jnp.zeros((c - rows, c), F32)], axis=0))
            for b in range(2):
                energies_ref[b : b + 1, :] = turned[3:4, b * slab : (b + 1) * slab]
                for n in range(3):
                    places_ref[n, b : b + 1, :] = turned[n : n + 1, b * slab : (b + 1) * slab]


def pack_kernel(
    node_hbm, places_hbm, species_hbm, sources_hbm, grad_hbm, table_hbm, mine_ref, other_ref,
    states, places, species, sources, grads, table, sems
):
    @pl.when(lax.axis_index("segment") == 0)
    def _():
        pack(
            (node_hbm, places_hbm, species_hbm, sources_hbm, grad_hbm, table_hbm), mine_ref, other_ref,
            states, places, species, sources, grads, table, sems,
        )


def pack(given, mine_ref, other_ref, states, places, species, sources, grads, table, sems):
    batch = lax.rem(lax.axis_index("space"), 2)
    copies = []
    for n, (source, target) in enumerate(zip(given, (states, places, species, sources, grads, table))):
        copies.append(pltpu.make_async_copy(source, target, sems.at[n]))
        copies[-1].start()
    for copy in copies:
        copy.wait()
    coefs, per_slab, c = states.shape[1:]
    lane = lax.broadcasted_iota(jnp.int32, (per_slab, c), 1)
    eye = (
        lax.broadcasted_iota(jnp.int32, (per_slab, per_slab), 0)
        == lax.broadcasted_iota(jnp.int32, (per_slab, per_slab), 1)
    )

    def column(row):
        return jnp.sum(jnp.where(eye, jnp.broadcast_to(row, (per_slab, per_slab)), 0.0), axis=1, keepdims=True)

    both = []
    for b in range(2):
        names = column(species[b : b + 1, :].astype(F32)).astype(jnp.int32)
        kinds = table.shape[0]
        hot = (names == lax.broadcasted_iota(jnp.int32, (per_slab, kinds), 1)).astype(BF16)
        first = (states[b, 0].astype(F32) + dot(hot, table[...])).astype(BF16)
        extra = jnp.zeros((per_slab, c), F32)
        for n in range(3):
            extra = jnp.where(lane == n, column(places[n, b : b + 1, :]), extra)
        extra = encode(jnp.where(lane == 3, column(grads[b : b + 1, :]), extra))
        for j in range(sources.shape[2]):
            index = sources[b, :, j : j + 1]
            extra = jnp.where(lane == SOURCES + j, (index // BASE).astype(F32), extra)
            extra = jnp.where(lane == SOURCES + 8 + j, (index % BASE).astype(F32), extra)
        both.append((first, extra.astype(BF16)))
    for ref, chosen in ((mine_ref, batch), (other_ref, 1 - batch)):
        ref[pl.ds(0, coefs)] = states[chosen]
        ref[0] = jnp.where(chosen == 0, both[0][0].astype(F32), both[1][0].astype(F32)).astype(BF16)
        ref[coefs] = jnp.where(chosen == 0, both[0][1].astype(F32), both[1][1].astype(F32)).astype(BF16)


def open_kernel(mine_ref, partner_ref, straight_ref, cross_ref, low_ref, high_ref):
    @pl.when(lax.axis_index("segment") == 0)
    def _():
        even = lax.rem(lax.axis_index("space"), 2) == 0

        def choose(a, b):
            return jnp.where(even, a, b)

        for k in range(low_ref.shape[0]):
            mine, partner = mine_ref[k].astype(F32), partner_ref[k].astype(F32)
            straight, cross = straight_ref[k].astype(F32), cross_ref[k].astype(F32)
            low_ref[k] = jnp.concatenate([choose(cross, straight), choose(mine, partner)], axis=0).astype(BF16)
            high_ref[k] = jnp.concatenate([choose(partner, mine), choose(straight, cross)], axis=0).astype(BF16)


def edges_of(refs, coefs, slabs, neighbours, rate_ref, hot_ref, hot_t_ref, geo_ref):
    start, _ = first_slab(slabs)
    extra = jnp.concatenate([ref[coefs].astype(F32) for ref in refs], axis=0)
    window, c = extra.shape
    rows = window // 2
    per_slab = rows // 2
    edges = rows * neighbours
    numbers = decode(extra)
    own_extra = extra[per_slab : per_slab + rows]
    low = pltpu.roll(own_extra, c - 8, 1)
    index = own_extra.astype(jnp.int32) * BASE + low.astype(jnp.int32)
    place = lax.rem(index // per_slab - start + slabs, slabs) * per_slab + index % per_slab
    columns = lax.broadcasted_iota(jnp.int32, (rows, c), 1)
    hot = jnp.concatenate(
        [
            (place[:, SOURCES + j : SOURCES + j + 1] == columns).astype(F32)
            for j in range(neighbours)
        ],
        axis=0,
    )
    hot_t_ref[...] = jnp.transpose(hot).astype(BF16)[:window]
    hot = hot.astype(BF16)[:, :window]
    hot_ref[...] = hot
    lift = lax.broadcasted_iota(jnp.int32, (window, c), 0) // per_slab - 1
    offset = []
    for n in range(3):
        column = jnp.broadcast_to(numbers[:, n : n + 1], (window, c))
        if n == 2:
            column = column + SLAB_DEPTH * lift.astype(F32)
        there = sum(dot(hot, part) for part in split3(column))
        offset.append(there - jnp.concatenate([column[per_slab : per_slab + rows]] * neighbours, axis=0))
    flat = offset[0] * offset[0] + offset[1] * offset[1] + 1.0
    length = jnp.sqrt(flat + offset[2] * offset[2])
    planar = jnp.sqrt(flat)
    c1, s1 = offset[0] / planar, offset[1] / planar
    rate = jnp.broadcast_to(rate_ref[...], (edges, c))
    values = [
        jnp.exp(-rate * length),
        c1,
        s1,
        c1 * c1 - s1 * s1,
        2.0 * c1 * s1,
        offset[0] / length,
        offset[1] / length,
        offset[2] / length,
        1.0 / planar,
        rate,
    ]
    for n, value in enumerate(values):
        geo_ref[n * edges : (n + 1) * edges, :] = value
    return numbers[per_slab : per_slab + rows]


def turn_to_stage():
    odd = lax.rem(lax.axis_index("space"), 2)
    segment = lax.axis_index("segment")
    return jnp.where(segment < 2, odd * (1 + segment), 0)


def stage_kernel(moment, zero_hbm, one_hbm, two_hbm, *more):
    zero_ref, one_ref, two_ref, sems = more[-4:]

    @pl.when(turn_to_stage() == moment)
    def _():
        pairs = [(zero_hbm, zero_ref)]
        for source, target in ((one_hbm, one_ref), (two_hbm, two_ref)):
            pairs += [(source.at[n], target.at[n]) for n in range(2)]
        copies = [pltpu.make_async_copy(source, target, sems.at[n]) for n, (source, target) in enumerate(pairs)]
        for copy in copies:
            copy.start()
        for copy in copies:
            copy.wait()


def forward_kernel(
    tick, sz, slabs, neighbours, low_ref, high_ref, rate_ref, zero_ref, one_ref, two_ref,
    out_ref, pooled_ref, hot_ref, hot_t_ref, geo_ref
):
    @pl.when(lax.axis_index("segment") == tick)
    def _():
        rows = low_ref.shape[1]
        refs = (low_ref, high_ref)
        edges_of(refs, sz.coefs, slabs, neighbours, rate_ref, hot_ref, hot_t_ref, geo_ref)
        pooled = forward(refs, hot_ref, geo_ref, zero_ref, one_ref, two_ref, sz, rows, False)
        signal = signal_of(pooled, sz)
        gate, lifted = silu_parts(signal)
        for k in range(sz.coefs):
            pooled_ref[k] = pooled[k]
            added = lifted if k == 0 else gate * pooled[k]
            out_ref[k] = (own_rows(refs, k) + added).astype(BF16)
        out_ref[sz.coefs] = own_rows(refs, sz.coefs).astype(BF16)


def turn_kernel(
    tick, sz, slabs, neighbours, low_ref, high_ref, rate_ref, zero_ref, one_ref, two_ref, read_ref,
    back_low_ref, back_high_ref, hot_ref, hot_t_ref, geo_ref
):
    @pl.when(lax.axis_index("segment") == tick)
    def _():
        rows = low_ref.shape[1]
        refs = (low_ref, high_ref)
        outs = (back_low_ref, back_high_ref)
        own = edges_of(refs, sz.coefs, slabs, neighbours, rate_ref, hot_ref, hot_t_ref, geo_ref)
        pooled = forward(refs, hot_ref, geo_ref, zero_ref, one_ref, two_ref, sz, rows, True)
        signal = signal_of(pooled, sz)
        _, lifted = silu_parts(signal)
        updated = own_rows(refs, 0) + lifted
        gate, active = silu_parts(updated)
        read = read_ref[...]
        energy = jnp.sum(read * active, axis=1, keepdims=True)
        lane = lax.broadcasted_iota(jnp.int32, (rows, sz.c), 1)
        energy = around(jnp.where(lane == 3, energy, 0.0), rows // 2)
        upstream = [own[:, 3:4] * read * (gate + updated * gate * (1.0 - gate))]
        moved = backward(
            upstream, pooled, refs, hot_ref, hot_t_ref, geo_ref, zero_ref, one_ref, two_ref, sz, rows, True, outs
        )
        send_back(moved + energy, outs, sz)


def backward_kernel(
    tick, sz, up_low_ref, up_high_ref, pooled_ref, low_ref, high_ref, hot_ref, hot_t_ref, geo_ref,
    zero_ref, one_ref, two_ref, *outs
):
    @pl.when(lax.axis_index("segment") == tick)
    def _():
        rows = low_ref.shape[1]
        refs = (low_ref, high_ref)
        upstream = [up_low_ref[k].astype(F32) + up_high_ref[k].astype(F32) for k in range(sz.coefs)]
        pooled = [pooled_ref[k] for k in range(sz.coefs)]
        moved = backward(
            upstream, pooled, refs, hot_ref, hot_t_ref, geo_ref, zero_ref, one_ref, two_ref, sz, rows, False,
            outs if tick else None,
        )
        carried = decode(up_low_ref[sz.coefs].astype(F32)) + decode(up_high_ref[sz.coefs].astype(F32))
        moved = moved + around(carried, rows // 2)
        if tick:
            send_back(moved, outs, sz)
        else:
            share(moved, outs)


def call(body, operands, shapes, name, spaces=None, scratch=(), aliases=None):
    spaces = spaces or [pltpu.VMEM] * len(operands)
    operands = [pltpu.with_memory_space_constraint(value, space) for value, space in zip(operands, spaces)]
    return pl.pallas_call(
        body,
        out_shape=shapes,
        in_specs=[pl.BlockSpec(memory_space=space) for space in spaces],
        out_specs=[pl.BlockSpec(memory_space=pltpu.VMEM) for _ in shapes],
        scratch_shapes=list(scratch),
        input_output_aliases=aliases or {},
        compiler_params=pltpu.CompilerParams(vmem_limit_bytes=VMEM_LIMIT),
        name=name,
    )(*operands)


def on_device(
    node_states,
    species,
    species_table,
    places,
    sources,
    radial_rate,
    zero_weight,
    one_weight,
    two_weight,
    read_weight,
    energy_grad,
):
    segments = lax.axis_size("segment")
    slabs = lax.axis_size("space")
    batches, per_slab = species.shape
    coefs, channels = node_states.shape[2:]
    neighbours = sources.shape[2]
    rows = batches * per_slab
    edges = rows * neighbours
    sz = Sizes(zero_weight.shape, one_weight.shape, two_weight.shape, channels)
    axes = ("segment", "space")
    shape = jax.ShapeDtypeStruct

    pairs = slabs // 2

    def within(value, target):
        ways = [(s * slabs + i, s * slabs + target(i) % slabs) for s in range(segments) for i in range(slabs)]
        return lax.ppermute(value, axes, ways)

    def hop(value, step, by):
        ways = []
        for start in range(segments):
            stop = (start + step) % segments
            for q in range(pairs):
                a, b = place_of(q, pairs, start), place_of((q + by) % pairs, pairs, stop)
                ways += [(start * slabs + 2 * a + c, stop * slabs + 2 * b + c) for c in range(2)]
        return lax.ppermute(value, axes, ways)

    raw = [
        node_states.transpose(0, 2, 1, 3), places.transpose(1, 0, 2), species, sources, energy_grad, species_table,
    ]
    packed = shape((coefs + 1, per_slab, channels), BF16)
    mine, other = call(
        pack_kernel, raw, [packed, packed], "pack", [pltpu.HBM] * len(raw),
        [pltpu.VMEM(v.shape, v.dtype) for v in raw] + [pltpu.SemaphoreType.DMA((len(raw),))],
    )
    partner = within(other, lambda i: i + 1 - 2 * (i % 2))
    straight = within(mine, lambda i: i + 2 if i % 2 else i - 2)
    cross = within(other, lambda i: i + 1 if i % 2 else i - 1)
    stored = [zero_weight[0], one_weight[0], two_weight[0]]
    spaces = [pltpu.HBM] * 3
    on_chip = [pltpu.VMEM(w.shape, w.dtype) for w in stored]
    sems = [pltpu.SemaphoreType.DMA((5,))]
    weights = call(functools.partial(stage_kernel, 0), stored, on_chip, "stage", spaces, sems)
    whole = shape((coefs + 1, rows, channels), BF16)
    around_all = [call(open_kernel, [mine, partner, straight, cross], [whole, whole], "open")]

    def stage_more(moment, weights, after):
        return call(
            functools.partial(stage_kernel, moment), [*stored, *weights, after], on_chip, "stage",
            spaces + [pltpu.VMEM] * 4, sems, {3: 0, 4: 1, 5: 2},
        )

    weights = stage_more(1, weights, around_all[0][0])
    edge_shapes = [
        shape((edges, 2 * rows), BF16), shape((2 * rows, edges), BF16), shape((10 * edges, channels), F32),
    ]
    kept = []
    for tick in range(segments - 1):
        out, *residuals = call(
            functools.partial(forward_kernel, tick, sz, slabs, neighbours),
            [*around_all[tick], radial_rate, *weights],
            [whole, shape((coefs, rows, channels), F32), *edge_shapes],
            "forward",
        )
        kept.append(residuals)
        ways = (1, 0) if tick % 2 else (0, -1)
        around_all.append([hop(out, 1, by) for by in ways])
        if tick == 0:
            weights = stage_more(2, weights, around_all[1][0])
    final = segments - 1
    slab_sums = shape((per_slab, channels), F32)
    parts = call(
        functools.partial(turn_kernel, final, sz, slabs, neighbours),
        [*around_all[final], radial_rate, *weights, read_weight.reshape(1, channels)],
        [whole, whole],
        "turn",
        scratch=[pltpu.VMEM(v.shape, v.dtype) for v in edge_shapes],
    )
    for tick in reversed(range(segments - 1)):
        ways = (1, 0) if tick % 2 else (0, -1)
        up = [hop(part, -1, -by) for part, by in zip(parts, ways)]
        pooled, *residuals = kept[tick]
        parts = call(
            functools.partial(backward_kernel, tick, sz),
            [*up, pooled, *around_all[tick], *residuals, *weights],
            [whole, whole] if tick else [slab_sums] * 4,
            "backward",
        )
    here, theirs, straight, cross = parts
    theirs = within(theirs, lambda i: i + 1 - 2 * (i % 2))
    straight = within(straight, lambda i: i - 2 if i % 2 else i + 2)
    cross = within(cross, lambda i: i + 1 if i % 2 else i - 1)
    (both,) = call(join_kernel, [here, theirs, straight, cross], [shape((rows, channels), F32)], "join")
    copies = [both] + [
        lax.ppermute(both, "segment", [(s, (s + stop) % segments) for s in range(segments)])
        for stop in range(1, segments)
    ]
    energies, gradients = call(
        close_kernel, copies, [shape((batches, per_slab), F32), shape((3, batches, per_slab), F32)], "close"
    )
    return energies, gradients.transpose(1, 0, 2)


def solution(mesh):
    in_specs = (
        P(None, "space", None, None),
        P(None, "space"),
        P(),
        P(None, None, "space"),
        P(None, "space", None),
        P("segment", None),
        P("segment", None, None),
        P("segment", None, None, None),
        P("segment", None, None, None),
        P(),
        P(None, "space"),
    )
    out_specs = (P(None, "space"), P(None, None, "space"))
    return jax.shard_map(
        on_device, mesh=mesh, in_specs=in_specs, out_specs=out_specs, check_vma=False
    )
```

```python
import functools

import jax
import jax.numpy as jnp
from jax import lax
from jax.experimental import pallas as pl
from jax.experimental.pallas import tpu as pltpu
from jax.sharding import PartitionSpec as P

SLAB_DEPTH = 2.0
F32 = jnp.float32
BF16 = jnp.bfloat16
VMEM_LIMIT = 16 * 1024 * 1024

MID, LOW, SOURCES = 32, 64, 96
BASE = 256


def split(value):
    high = value.astype(BF16)
    low = (value - high.astype(F32)).astype(BF16)
    return high, low


def split3(value):
    high = value.astype(BF16)
    rest = value - high.astype(F32)
    mid = rest.astype(BF16)
    return high, mid, (rest - mid.astype(F32)).astype(BF16)


def encode(value):
    high, mid, low = split3(value)
    return high.astype(F32) + pltpu.roll(mid.astype(F32), MID, 1) + pltpu.roll(low.astype(F32), LOW, 1)


def decode(value):
    lanes = value.shape[1]
    whole = value + pltpu.roll(value, lanes - MID, 1) + pltpu.roll(value, lanes - LOW, 1)
    lane = lax.broadcasted_iota(jnp.int32, value.shape, 1)
    return jnp.where(lane < 4, whole, 0.0)


def dot(a, b):
    return lax.dot_general(a, b, (((1,), (0,)), ((), ())), preferred_element_type=F32)


def dot_t(a, b):
    return lax.dot_general(a, b, (((1,), (1,)), ((), ())), preferred_element_type=F32)


def fine_dot(value, weights, product):
    rows = value.shape[0]
    stacked = jnp.concatenate(split(value), axis=0)
    outs = []
    for weight in weights:
        out = product(stacked, weight)
        outs.append(out[:rows] + out[rows:])
    return outs


def silu_parts(value):
    gate = 1.0 / (1.0 + jnp.exp(-value))
    return gate, value * gate


class Sizes:
    def __init__(self, zero_shape, one_shape, two_shape, channels):
        self.c = channels
        self.zero = zero_shape[-1] // channels
        self.one = one_shape[-1] // channels
        self.two = two_shape[-1] // channels
        self.coefs = self.zero + 2 * (self.one + self.two)
        self.starts = (self.zero, self.zero + 2 * self.one)
        self.counts = (self.one, self.two)

    def cols(self, first, count=1):
        return slice(first * self.c, (first + count) * self.c)


def picked_group(refs, hot, first, count):
    blocks = [jnp.concatenate([ref[k] for ref in refs], axis=0) for k in range(first, first + count)]
    return dot(hot, jnp.concatenate(blocks, axis=1))


def own_rows(refs, k):
    low, high = (ref[k].astype(F32) for ref in refs)
    slab = low.shape[0] // 2
    return jnp.concatenate([low[slab:], high[:slab]], axis=0)


def forward(refs, edge_refs, zero_ref, one_ref, two_ref, sz, rows, last):
    hot_ref, _, _, geo_ref, turned_ref, scaled_ref = edge_refs
    hot = hot_ref[...]
    edges = hot.shape[0]
    factor = (edges // rows) ** (-0.5)
    radial = geo_ref[:edges, :]

    def scaled(first, count):
        group = picked_group(refs, hot, first, count)
        blocks = [(group[:, sz.cols(n)] * radial).astype(BF16) for n in range(count)]
        for n, block in enumerate(blocks):
            scaled_ref[first + n] = block
        return jnp.concatenate(blocks, axis=1)

    pooled = [None] * sz.coefs
    ones = turned_ref[4 * rows : 5 * rows, :].astype(BF16)
    zin = dot(ones, scaled(0, sz.zero))
    kept = 1 if last else sz.zero
    (zout,) = fine_dot(zin, [zero_ref[:, sz.cols(0, kept)]], dot)
    for k in range(kept):
        pooled[k] = zout[:, sz.cols(k)] * factor
    for order in range(2):
        first, count = sz.starts[order], sz.counts[order]
        weight_ref = (one_ref, two_ref)[order]
        turns = jnp.concatenate(split(turned_ref[2 * order * rows : (2 * order + 2) * rows, :]), axis=0)
        out = dot(turns, scaled(first, 2 * count))
        by_cos = out[:rows] + out[2 * rows : 3 * rows]
        by_sin = out[rows : 2 * rows] + out[3 * rows :]
        half = count * sz.c
        both = jnp.concatenate(
            [by_cos[:, :half] - by_sin[:, half:], by_sin[:, :half] + by_cos[:, half:]], axis=0
        )
        a, b = fine_dot(both, [weight_ref[0], weight_ref[1]], dot)
        out_re = (a[:rows] - b[rows:]) * factor
        out_im = (b[:rows] + a[rows:]) * factor
        for k in range(count):
            pooled[first + k] = out_re[:, sz.cols(k)]
            pooled[first + count + k] = out_im[:, sz.cols(k)]
    return pooled


def signal_of(pooled, sz):
    total = pooled[0]
    for k in range(sz.zero, sz.coefs):
        total = total + pooled[k] * pooled[k]
    return total


def backward(upstream, pooled, edge_refs, rate_ref, zero_ref, one_ref, two_ref, sz, rows, last, outs):
    _, hot_t_ref, net_ref, geo_ref, turned_ref, scaled_ref = edge_refs
    edges = hot_t_ref.shape[1]
    slab = rows // 2
    factor = (edges // rows) ** (-0.5)
    signal = signal_of(pooled, sz)
    gate, _ = silu_parts(signal)
    slope = gate * (1.0 - gate)
    d_signal = upstream[0] * (gate + signal * slope)
    if not last:
        inner = upstream[1] * pooled[1]
        for k in range(2, sz.coefs):
            inner = inner + upstream[k] * pooled[k]
        d_signal = d_signal + inner * slope
    d_pooled = [d_signal * factor]
    for k in range(1, sz.coefs):
        if last:
            d_pooled.append(2.0 * factor * d_signal * pooled[k] if k >= sz.zero else None)
        else:
            term = gate * upstream[k]
            if k >= sz.zero:
                term = term + 2.0 * d_signal * pooled[k]
            d_pooled.append(term * factor)

    rate = rate_ref[...]

    def spread(block):
        return jnp.concatenate([block] * (edges // rows), axis=0)

    def geo(which):
        return geo_ref[which * edges : (which + 1) * edges, :]

    def source_rows(first, count):
        return jnp.concatenate([scaled_ref[k] for k in range(first, first + count)], axis=1)

    def scatter(first, blocks):
        back = dot(hot_t_ref[...], jnp.concatenate([block.astype(BF16) for block in blocks], axis=1))
        for n in range(len(blocks)):
            k = first + n
            part = back[:, sz.cols(n)]
            if not last or k == 0:
                part = part + around(upstream[k], slab)
            outs[0][k] = part[:rows].astype(BF16)
            outs[1][k] = part[rows:].astype(BF16)

    own_row = lax.broadcasted_iota(jnp.int32, (rows, edges), 0)
    own_edge = lax.rem(lax.broadcasted_iota(jnp.int32, (rows, edges), 1), rows) == own_row

    def per_edge(products, which, groups):
        value = products[which * rows : (which + 1) * rows]
        value = value + products[(groups + which) * rows : (groups + which + 1) * rows]
        return jnp.sum(jnp.where(own_edge, value, 0.0), axis=0, keepdims=True)

    def by_rate(value):
        return jnp.concatenate([value[:, sz.cols(n)] * rate for n in range(value.shape[1] // sz.c)], axis=1)

    kept = 1 if last else sz.zero
    (dz,) = fine_dot(jnp.concatenate(d_pooled[:kept], axis=1), [zero_ref[:, sz.cols(0, kept)]], dot_t)
    products = dot_t(jnp.concatenate(split(by_rate(dz)), axis=0), source_rows(0, sz.zero))
    d_len = per_edge(products, 0, 1)
    if outs is not None:
        radial = geo(0)
        scatter(0, [spread(dz[:, sz.cols(k)]) * radial for k in range(sz.zero)])
    c1, s1 = (turned_ref[5 * rows + n : 5 * rows + n + 1, :] for n in range(2))
    turned = []
    for order in range(2):
        first, count = sz.starts[order], sz.counts[order]
        weight_ref = (one_ref, two_ref)[order]
        both = jnp.concatenate(
            [
                jnp.concatenate(d_pooled[first : first + count], axis=1),
                jnp.concatenate(d_pooled[first + count : first + 2 * count], axis=1),
            ],
            axis=0,
        )
        a, b = fine_dot(both, [weight_ref[0], weight_ref[1]], dot_t)
        d_re = a[:rows] + b[rows:]
        d_im = a[rows:] - b[:rows]
        straight = jnp.concatenate([d_re, d_im], axis=1)
        crossed = jnp.concatenate([d_im, -d_re], axis=1)
        four = jnp.concatenate([straight, crossed, by_rate(straight), by_rate(crossed)], axis=0)
        products = dot_t(jnp.concatenate(split(four), axis=0), source_rows(first, 2 * count))
        q_cos, q_sin, r_cos, r_sin = (per_edge(products, n, 4) for n in range(4))
        cos, sin = (c1, s1) if order == 0 else (c1 * c1 - s1 * s1, 2.0 * c1 * s1)
        d_len = d_len + cos * r_cos + sin * r_sin
        turned.append((q_cos, q_sin))
        if outs is not None:
            cos_r, sin_r = geo(1 + 2 * order), geo(2 + 2 * order)
            blocks_re, blocks_im = [], []
            for k in range(count):
                g_re, g_im = spread(d_re[:, sz.cols(k)]), spread(d_im[:, sz.cols(k)])
                blocks_re.append(cos_r * g_re + sin_r * g_im)
                blocks_im.append(cos_r * g_im - sin_r * g_re)
            scatter(first, blocks_re + blocks_im)

    d_len = -d_len
    (dc1, ds1), (dc2, ds2) = turned
    ux, uy, uz, inv_planar = (turned_ref[5 * rows + n : 5 * rows + n + 1, :] for n in range(2, 6))
    dc1 = dc1 + 2.0 * (c1 * dc2 + s1 * ds2)
    ds1 = ds1 + 2.0 * (c1 * ds2 - s1 * dc2)
    along = c1 * dc1 + s1 * ds1
    dx = (dc1 - along * c1) * inv_planar + d_len * ux
    dy = (ds1 - along * s1) * inv_planar + d_len * uy
    change = jnp.where(own_row == 0, dx, jnp.where(own_row == 1, dy, jnp.where(own_row == 2, d_len * uz, 0.0)))
    moved = sum(dot(part, net_ref[...]) for part in split3(change))
    lanes = moved.shape[1]
    moved = jnp.transpose(jnp.concatenate([moved, jnp.zeros((lanes - rows, lanes), F32)], axis=0))
    return moved[: 2 * rows]


def around(own, slab):
    edge = jnp.zeros((slab, own.shape[1]), F32)
    return jnp.concatenate([edge, own, edge], axis=0)


def place_of(pair, pairs, segment):
    if segment == 0:
        return pair
    return 2 * pair if pair < pairs // 2 else 2 * (pairs - 1 - pair) + 1


def first_slab(slabs):
    slab_now = lax.axis_index("space")
    segment = lax.axis_index("segment")
    chip = slab_now // 2
    folded = jnp.where(lax.rem(chip, 2) == 0, chip // 2, slabs // 2 - 1 - chip // 2)
    pair = jnp.where(segment == 0, chip, folded)
    return lax.rem(2 * pair + lax.rem(segment, 2) - 1 + slabs, slabs), lax.rem(slab_now, 2)


def send_back(moved, outs, sz):
    rows = moved.shape[0] // 2
    coded = encode(moved).astype(BF16)
    outs[0][sz.coefs] = coded[:rows]
    outs[1][sz.coefs] = coded[rows:]


def share(moved, outs):
    slab = moved.shape[0] // 4
    left, low, high, right = (moved[n * slab : (n + 1) * slab] for n in range(4))
    even = lax.rem(lax.axis_index("space"), 2) == 0
    outs[0][...] = jnp.where(even, low, high)
    outs[1][...] = jnp.where(even, high, low)
    outs[2][...] = jnp.where(even, right, left)
    outs[3][...] = jnp.where(even, left, right)


def join_kernel(here_ref, theirs_ref, straight_ref, cross_ref, both_ref):
    slab = here_ref.shape[0]
    even = lax.rem(lax.axis_index("space"), 2) == 0
    here = here_ref[...] + straight_ref[...]
    there = theirs_ref[...] + cross_ref[...]
    both_ref[:slab, :] = jnp.where(even, here, there)
    both_ref[slab:, :] = jnp.where(even, there, here)


def close_kernel(*refs):
    *sums_refs, energies_ref, places_ref = refs
    slab = energies_ref.shape[1]
    for n, ref in enumerate(sums_refs):

        @pl.when(lax.axis_index("segment") == n)
        def _(ref=ref):
            sums = ref[...]
            rows, c = sums.shape
            turned = jnp.transpose(jnp.concatenate([sums, jnp.zeros((c - rows, c), F32)], axis=0))
            for b in range(2):
                energies_ref[b : b + 1, :] = turned[3:4, b * slab : (b + 1) * slab]
                for n in range(3):
                    places_ref[n, b : b + 1, :] = turned[n : n + 1, b * slab : (b + 1) * slab]


def pack_kernel(
    node_hbm, places_hbm, species_hbm, sources_hbm, grad_hbm, table_hbm, mine_ref, other_ref,
    states, places, species, sources, grads, table, sems
):
    @pl.when(lax.axis_index("segment") == 0)
    def _():
        pack(
            (node_hbm, places_hbm, species_hbm, sources_hbm, grad_hbm, table_hbm), mine_ref, other_ref,
            states, places, species, sources, grads, table, sems,
        )


def pack(given, mine_ref, other_ref, states, places, species, sources, grads, table, sems):
    batch = lax.rem(lax.axis_index("space"), 2)
    copies = []
    for n, (source, target) in enumerate(zip(given, (states, places, species, sources, grads, table))):
        copies.append(pltpu.make_async_copy(source, target, sems.at[n]))
        copies[-1].start()
    for copy in copies:
        copy.wait()
    coefs, per_slab, c = states.shape[1:]
    lane = lax.broadcasted_iota(jnp.int32, (per_slab, c), 1)
    eye = (
        lax.broadcasted_iota(jnp.int32, (per_slab, per_slab), 0)
        == lax.broadcasted_iota(jnp.int32, (per_slab, per_slab), 1)
    )

    def column(row):
        return jnp.sum(jnp.where(eye, jnp.broadcast_to(row, (per_slab, per_slab)), 0.0), axis=1, keepdims=True)

    both = []
    for b in range(2):
        names = column(species[b : b + 1, :].astype(F32)).astype(jnp.int32)
        kinds = table.shape[0]
        hot = (names == lax.broadcasted_iota(jnp.int32, (per_slab, kinds), 1)).astype(BF16)
        first = (states[b, 0].astype(F32) + dot(hot, table[...])).astype(BF16)
        extra = jnp.zeros((per_slab, c), F32)
        for n in range(3):
            extra = jnp.where(lane == n, column(places[n, b : b + 1, :]), extra)
        extra = encode(jnp.where(lane == 3, column(grads[b : b + 1, :]), extra))
        for j in range(sources.shape[2]):
            index = sources[b, :, j : j + 1]
            extra = jnp.where(lane == SOURCES + j, (index // BASE).astype(F32), extra)
            extra = jnp.where(lane == SOURCES + 8 + j, (index % BASE).astype(F32), extra)
        both.append((first, extra.astype(BF16)))
    for ref, chosen in ((mine_ref, batch), (other_ref, 1 - batch)):
        ref[pl.ds(0, coefs)] = states[chosen]
        ref[0] = jnp.where(chosen == 0, both[0][0].astype(F32), both[1][0].astype(F32)).astype(BF16)
        ref[coefs] = jnp.where(chosen == 0, both[0][1].astype(F32), both[1][1].astype(F32)).astype(BF16)


def open_kernel(mine_ref, partner_ref, straight_ref, cross_ref, low_ref, high_ref):
    @pl.when(lax.axis_index("segment") == 0)
    def _():
        even = lax.rem(lax.axis_index("space"), 2) == 0

        def choose(a, b):
            return jnp.where(even, a, b)

        for k in range(low_ref.shape[0]):
            mine, partner = mine_ref[k].astype(F32), partner_ref[k].astype(F32)
            straight, cross = straight_ref[k].astype(F32), cross_ref[k].astype(F32)
            low_ref[k] = jnp.concatenate([choose(cross, straight), choose(mine, partner)], axis=0).astype(BF16)
            high_ref[k] = jnp.concatenate([choose(partner, mine), choose(straight, cross)], axis=0).astype(BF16)


def edges_of(refs, coefs, slabs, neighbours, rate_ref, edge_refs):
    hot_ref, hot_t_ref, net_ref, geo_ref, turned_ref, _ = edge_refs
    start, _ = first_slab(slabs)
    extra = jnp.concatenate([ref[coefs].astype(F32) for ref in refs], axis=0)
    window, c = extra.shape
    rows = window // 2
    per_slab = rows // 2
    edges = rows * neighbours
    numbers = decode(extra)
    own_extra = extra[per_slab : per_slab + rows]
    low = pltpu.roll(own_extra, c - 8, 1)
    index = own_extra.astype(jnp.int32) * BASE + low.astype(jnp.int32)
    place = lax.rem(index // per_slab - start + slabs, slabs) * per_slab + index % per_slab
    columns = lax.broadcasted_iota(jnp.int32, (rows, c), 1)
    hot = jnp.concatenate(
        [
            (place[:, SOURCES + j : SOURCES + j + 1] == columns).astype(F32)
            for j in range(neighbours)
        ],
        axis=0,
    )
    lane = lax.broadcasted_iota(jnp.int32, (edges, c), 1)
    atom = lax.rem(lax.broadcasted_iota(jnp.int32, (edges, c), 0), rows)
    net_ref[...] = (hot - (lane == atom + per_slab).astype(F32)).astype(BF16)
    hot_t_ref[...] = jnp.transpose(hot).astype(BF16)[:window]
    hot = hot.astype(BF16)[:, :window]
    hot_ref[...] = hot
    lift = lax.broadcasted_iota(jnp.int32, (window, c), 0) // per_slab - 1
    offset = []
    for n in range(3):
        column = jnp.broadcast_to(numbers[:, n : n + 1], (window, c))
        if n == 2:
            column = column + SLAB_DEPTH * lift.astype(F32)
        there = sum(dot(hot, part) for part in split3(column))
        offset.append(there - jnp.concatenate([column[per_slab : per_slab + rows]] * neighbours, axis=0))
    flat = offset[0] * offset[0] + offset[1] * offset[1] + 1.0
    length = jnp.sqrt(flat + offset[2] * offset[2])
    planar = jnp.sqrt(flat)
    c1, s1 = offset[0] / planar, offset[1] / planar
    c2, s2 = c1 * c1 - s1 * s1, 2.0 * c1 * s1
    radial = jnp.exp(-rate_ref[...] * length)
    for n, value in enumerate((radial, c1 * radial, s1 * radial, c2 * radial, s2 * radial)):
        geo_ref[n * edges : (n + 1) * edges, :] = value
    packed = jnp.where(lax.rem(lane, rows) == atom, 1.0, 0.0)
    for n, value in enumerate((c1, s1, c2, s2)):
        packed = jnp.where(lane // rows == n, packed * value, packed)
    singles = (c1, s1, offset[0] / length, offset[1] / length, offset[2] / length, 1.0 / planar)
    for n, value in enumerate(singles):
        packed = jnp.where(lane == 5 * rows + n, value, packed)
    turned_ref[...] = jnp.transpose(packed)
    return numbers[per_slab : per_slab + rows]


def stage_kernel(zero_hbm, one_hbm, two_hbm, zero_ref, one_ref, two_ref, sems):
    pairs = [(zero_hbm, zero_ref)]
    for source, target in ((one_hbm, one_ref), (two_hbm, two_ref)):
        pairs += [(source.at[n], target.at[n]) for n in range(2)]
    copies = [pltpu.make_async_copy(source, target, sems.at[n]) for n, (source, target) in enumerate(pairs)]
    for copy in copies:
        copy.start()
    for copy in copies:
        copy.wait()


def forward_kernel(
    tick, sz, slabs, neighbours, low_ref, high_ref, rate_ref, zero_ref, one_ref, two_ref,
    out_ref, pooled_ref, *edge_refs
):
    @pl.when(lax.axis_index("segment") == tick)
    def _():
        rows = low_ref.shape[1]
        refs = (low_ref, high_ref)
        edges_of(refs, sz.coefs, slabs, neighbours, rate_ref, edge_refs)
        pooled = forward(refs, edge_refs, zero_ref, one_ref, two_ref, sz, rows, False)
        signal = signal_of(pooled, sz)
        gate, lifted = silu_parts(signal)
        for k in range(sz.coefs):
            pooled_ref[k] = pooled[k]
            added = lifted if k == 0 else gate * pooled[k]
            out_ref[k] = (own_rows(refs, k) + added).astype(BF16)
        out_ref[sz.coefs] = own_rows(refs, sz.coefs).astype(BF16)


def turn_kernel(
    tick, sz, slabs, neighbours, low_ref, high_ref, rate_ref, zero_ref, one_ref, two_ref, read_ref,
    back_low_ref, back_high_ref, *edge_refs
):
    @pl.when(lax.axis_index("segment") == tick)
    def _():
        rows = low_ref.shape[1]
        refs = (low_ref, high_ref)
        outs = (back_low_ref, back_high_ref)
        own = edges_of(refs, sz.coefs, slabs, neighbours, rate_ref, edge_refs)
        pooled = forward(refs, edge_refs, zero_ref, one_ref, two_ref, sz, rows, True)
        signal = signal_of(pooled, sz)
        _, lifted = silu_parts(signal)
        updated = own_rows(refs, 0) + lifted
        gate, active = silu_parts(updated)
        read = read_ref[...]
        energy = jnp.sum(read * active, axis=1, keepdims=True)
        lane = lax.broadcasted_iota(jnp.int32, (rows, sz.c), 1)
        energy = around(jnp.where(lane == 3, energy, 0.0), rows // 2)
        upstream = [own[:, 3:4] * read * (gate + updated * gate * (1.0 - gate))]
        moved = backward(upstream, pooled, edge_refs, rate_ref, zero_ref, one_ref, two_ref, sz, rows, True, outs)
        send_back(moved + energy, outs, sz)


def backward_kernel(tick, sz, up_low_ref, up_high_ref, rate_ref, pooled_ref, *more):
    edge_refs = more[:6]
    zero_ref, one_ref, two_ref, *outs = more[6:]

    @pl.when(lax.axis_index("segment") == tick)
    def _():
        rows = up_low_ref.shape[1]
        upstream = [up_low_ref[k].astype(F32) + up_high_ref[k].astype(F32) for k in range(sz.coefs)]
        pooled = [pooled_ref[k] for k in range(sz.coefs)]
        moved = backward(
            upstream, pooled, edge_refs, rate_ref, zero_ref, one_ref, two_ref, sz, rows, False, outs if tick else None
        )
        carried = decode(up_low_ref[sz.coefs].astype(F32)) + decode(up_high_ref[sz.coefs].astype(F32))
        moved = moved + around(carried, rows // 2)
        if tick:
            send_back(moved, outs, sz)
        else:
            share(moved, outs)


def call(body, operands, shapes, name, spaces=None, scratch=()):
    spaces = spaces or [pltpu.VMEM] * len(operands)
    operands = [pltpu.with_memory_space_constraint(value, space) for value, space in zip(operands, spaces)]
    return pl.pallas_call(
        body,
        out_shape=shapes,
        in_specs=[pl.BlockSpec(memory_space=space) for space in spaces],
        out_specs=[pl.BlockSpec(memory_space=pltpu.VMEM) for _ in shapes],
        scratch_shapes=list(scratch),
        compiler_params=pltpu.CompilerParams(vmem_limit_bytes=VMEM_LIMIT),
        name=name,
    )(*operands)


def on_device(
    node_states,
    species,
    species_table,
    places,
    sources,
    radial_rate,
    zero_weight,
    one_weight,
    two_weight,
    read_weight,
    energy_grad,
):
    segments = lax.axis_size("segment")
    slabs = lax.axis_size("space")
    batches, per_slab = species.shape
    coefs, channels = node_states.shape[2:]
    neighbours = sources.shape[2]
    rows = batches * per_slab
    edges = rows * neighbours
    sz = Sizes(zero_weight.shape, one_weight.shape, two_weight.shape, channels)
    axes = ("segment", "space")
    shape = jax.ShapeDtypeStruct

    pairs = slabs // 2

    def within(value, target):
        ways = [(s * slabs + i, s * slabs + target(i) % slabs) for s in range(segments) for i in range(slabs)]
        return lax.ppermute(value, axes, ways)

    def hop(value, step, by):
        ways = []
        for start in range(segments):
            stop = (start + step) % segments
            for q in range(pairs):
                a, b = place_of(q, pairs, start), place_of((q + by) % pairs, pairs, stop)
                ways += [(start * slabs + 2 * a + c, stop * slabs + 2 * b + c) for c in range(2)]
        return lax.ppermute(value, axes, ways)

    raw = [
        node_states.transpose(0, 2, 1, 3), places.transpose(1, 0, 2), species, sources, energy_grad, species_table,
    ]
    packed = shape((coefs + 1, per_slab, channels), BF16)
    mine, other = call(
        pack_kernel, raw, [packed, packed], "pack", [pltpu.HBM] * len(raw),
        [pltpu.VMEM(v.shape, v.dtype) for v in raw] + [pltpu.SemaphoreType.DMA((len(raw),))],
    )
    partner = within(other, lambda i: i + 1 - 2 * (i % 2))
    straight = within(mine, lambda i: i + 2 if i % 2 else i - 2)
    cross = within(other, lambda i: i + 1 if i % 2 else i - 1)
    stored = [zero_weight[0], one_weight[0], two_weight[0]]
    spaces = [pltpu.HBM] * 3
    on_chip = [pltpu.VMEM(w.shape, w.dtype) for w in stored]
    sems = [pltpu.SemaphoreType.DMA((5,))]
    weights = call(stage_kernel, stored, on_chip, "stage", spaces, sems)
    whole = shape((coefs + 1, rows, channels), BF16)
    around_all = [call(open_kernel, [mine, partner, straight, cross], [whole, whole], "open")]
    edge_shapes = [
        shape((edges, 2 * rows), BF16), shape((2 * rows, edges), BF16), shape((edges, channels), BF16),
        shape((5 * edges, channels), F32), shape((channels, edges), F32), shape((coefs, edges, channels), BF16),
    ]
    kept = []
    for tick in range(segments - 1):
        out, *residuals = call(
            functools.partial(forward_kernel, tick, sz, slabs, neighbours),
            [*around_all[tick], radial_rate, *weights],
            [whole, shape((coefs, rows, channels), F32), *edge_shapes],
            "forward",
        )
        kept.append(residuals)
        ways = (1, 0) if tick % 2 else (0, -1)
        around_all.append([hop(out, 1, by) for by in ways])
    final = segments - 1
    slab_sums = shape((per_slab, channels), F32)
    parts = call(
        functools.partial(turn_kernel, final, sz, slabs, neighbours),
        [*around_all[final], radial_rate, *weights, read_weight.reshape(1, channels)],
        [whole, whole],
        "turn",
        scratch=[pltpu.VMEM(v.shape, v.dtype) for v in edge_shapes],
    )
    for tick in reversed(range(segments - 1)):
        ways = (1, 0) if tick % 2 else (0, -1)
        up = [hop(part, -1, -by) for part, by in zip(parts, ways)]
        pooled, *residuals = kept[tick]
        parts = call(
            functools.partial(backward_kernel, tick, sz),
            [*up, radial_rate, pooled, *residuals, *weights],
            [whole, whole] if tick else [slab_sums] * 4,
            "backward",
        )
    here, theirs, straight, cross = parts
    theirs = within(theirs, lambda i: i + 1 - 2 * (i % 2))
    straight = within(straight, lambda i: i - 2 if i % 2 else i + 2)
    cross = within(cross, lambda i: i + 1 if i % 2 else i - 1)
    (both,) = call(join_kernel, [here, theirs, straight, cross], [shape((rows, channels), F32)], "join")
    copies = [both] + [
        lax.ppermute(both, "segment", [(s, (s + stop) % segments) for s in range(segments)])
        for stop in range(1, segments)
    ]
    energies, gradients = call(
        close_kernel, copies, [shape((batches, per_slab), F32), shape((3, batches, per_slab), F32)], "close"
    )
    return energies, gradients.transpose(1, 0, 2)


def solution(mesh):
    in_specs = (
        P(None, "space", None, None),
        P(None, "space"),
        P(),
        P(None, None, "space"),
        P(None, "space", None),
        P("segment", None),
        P("segment", None, None),
        P("segment", None, None, None),
        P("segment", None, None, None),
        P(),
        P(None, "space"),
    )
    out_specs = (P(None, "space"), P(None, None, "space"))
    return jax.shard_map(
        on_device, mesh=mesh, in_specs=in_specs, out_specs=out_specs, check_vma=False
    )
```

```python
import functools

import jax
import jax.numpy as jnp
from jax import lax
from jax.experimental import pallas as pl
from jax.experimental.pallas import tpu as pltpu
from jax.sharding import PartitionSpec as P

SLAB_DEPTH = 2.0
F32 = jnp.float32
BF16 = jnp.bfloat16
VMEM_LIMIT = 16 * 1024 * 1024

MID, LOW, SOURCES = 32, 64, 96
BASE = 256


def split(value):
    high = value.astype(BF16)
    low = (value - high.astype(F32)).astype(BF16)
    return high, low


def split3(value):
    high = value.astype(BF16)
    rest = value - high.astype(F32)
    mid = rest.astype(BF16)
    return high, mid, (rest - mid.astype(F32)).astype(BF16)


def encode(value):
    high, mid, low = split3(value)
    return high.astype(F32) + pltpu.roll(mid.astype(F32), MID, 1) + pltpu.roll(low.astype(F32), LOW, 1)


def decode(value):
    lanes = value.shape[1]
    whole = value + pltpu.roll(value, lanes - MID, 1) + pltpu.roll(value, lanes - LOW, 1)
    lane = lax.broadcasted_iota(jnp.int32, value.shape, 1)
    return jnp.where(lane < 4, whole, 0.0)


def dot(a, b):
    return lax.dot_general(a, b, (((1,), (0,)), ((), ())), preferred_element_type=F32)


def dot_t(a, b):
    return lax.dot_general(a, b, (((1,), (1,)), ((), ())), preferred_element_type=F32)


def fine_dot(value, weights, product):
    rows = value.shape[0]
    stacked = jnp.concatenate(split(value), axis=0)
    outs = []
    for weight in weights:
        out = product(stacked, weight)
        outs.append(out[:rows] + out[rows:])
    return outs


def silu_parts(value):
    gate = 1.0 / (1.0 + jnp.exp(-value))
    return gate, value * gate


class Sizes:
    def __init__(self, zero_shape, one_shape, two_shape, channels):
        self.c = channels
        self.zero = zero_shape[-1] // channels
        self.one = one_shape[-1] // channels
        self.two = two_shape[-1] // channels
        self.coefs = self.zero + 2 * (self.one + self.two)
        self.starts = (self.zero, self.zero + 2 * self.one)
        self.counts = (self.one, self.two)

    def cols(self, first, count=1):
        return slice(first * self.c, (first + count) * self.c)


def picked_group(refs, hot, first, count):
    blocks = [jnp.concatenate([ref[k] for ref in refs], axis=0) for k in range(first, first + count)]
    return dot(hot, jnp.concatenate(blocks, axis=1))


def own_rows(refs, k):
    low, high = (ref[k].astype(F32) for ref in refs)
    slab = low.shape[0] // 2
    return jnp.concatenate([low[slab:], high[:slab]], axis=0)


def pool(value, rows):
    total = value[:rows]
    for start in range(rows, value.shape[0], rows):
        total = total + value[start : start + rows]
    return total


def geo_at(geo_ref, which, edges):
    return geo_ref[which * edges : (which + 1) * edges, :]


def forward(refs, hot_ref, geo_ref, faded_ref, zero_ref, one_ref, two_ref, sz, rows, last):
    hot = hot_ref[...]
    edges = hot.shape[0]
    factor = (edges // rows) ** (-0.5)
    radial = geo_at(geo_ref, 0, edges)

    def scaled(block, k):
        faded = block * radial
        faded_ref[k] = faded
        return faded.astype(BF16).astype(F32)

    pooled = [None] * sz.coefs
    group = picked_group(refs, hot, 0, sz.zero)
    zin = jnp.concatenate(
        [pool(scaled(group[:, sz.cols(k)], k), rows) for k in range(sz.zero)], axis=1
    )
    kept = 1 if last else sz.zero
    (zout,) = fine_dot(zin, [zero_ref[:, sz.cols(0, kept)]], dot)
    for k in range(kept):
        pooled[k] = zout[:, sz.cols(k)] * factor
    for order in range(2):
        first, count = sz.starts[order], sz.counts[order]
        weight_ref = (one_ref, two_ref)[order]
        cos = geo_at(geo_ref, 1 + 2 * order, edges)
        sin = geo_at(geo_ref, 2 + 2 * order, edges)
        group = picked_group(refs, hot, first, 2 * count)
        res, ims = [], []
        for k in range(count):
            re = scaled(group[:, sz.cols(k)], first + k)
            im = scaled(group[:, sz.cols(count + k)], first + count + k)
            res.append(pool(cos * re - sin * im, rows))
            ims.append(pool(sin * re + cos * im, rows))
        both = jnp.concatenate(
            [jnp.concatenate(res, axis=1), jnp.concatenate(ims, axis=1)], axis=0
        )
        a, b = fine_dot(both, [weight_ref[0], weight_ref[1]], dot)
        out_re = (a[:rows] - b[rows:]) * factor
        out_im = (b[:rows] + a[rows:]) * factor
        for k in range(count):
            pooled[first + k] = out_re[:, sz.cols(k)]
            pooled[first + count + k] = out_im[:, sz.cols(k)]
    return pooled


def signal_of(pooled, sz):
    total = pooled[0]
    for k in range(sz.zero, sz.coefs):
        total = total + pooled[k] * pooled[k]
    return total


def backward(
    upstream, pooled, hot_t_ref, geo_ref, faded_ref, zero_ref, one_ref, two_ref, sz, rows, last, outs
):
    hot_t = hot_t_ref[...]
    edges = hot_t.shape[1]
    slab = rows // 2
    factor = (edges // rows) ** (-0.5)
    signal = signal_of(pooled, sz)
    gate, _ = silu_parts(signal)
    slope = gate * (1.0 - gate)
    d_signal = upstream[0] * (gate + signal * slope)
    if not last:
        inner = upstream[1] * pooled[1]
        for k in range(2, sz.coefs):
            inner = inner + upstream[k] * pooled[k]
        d_signal = d_signal + inner * slope
    d_pooled = [d_signal * factor]
    for k in range(1, sz.coefs):
        if last:
            d_pooled.append(2.0 * factor * d_signal * pooled[k] if k >= sz.zero else None)
        else:
            term = gate * upstream[k]
            if k >= sz.zero:
                term = term + 2.0 * d_signal * pooled[k]
            d_pooled.append(term * factor)

    radial = geo_at(geo_ref, 0, edges)
    kept = 1 if last else sz.zero
    (dz,) = fine_dot(jnp.concatenate(d_pooled[:kept], axis=1), [zero_ref[:, sz.cols(0, kept)]], dot_t)

    def spread(block):
        return jnp.concatenate([block] * (edges // rows), axis=0)

    def scatter(first, blocks):
        if outs is None:
            return
        back = dot(hot_t, jnp.concatenate([block.astype(BF16) for block in blocks], axis=1))
        for n in range(len(blocks)):
            k = first + n
            part = back[:, sz.cols(n)]
            if not last or k == 0:
                part = part + around(upstream[k], slab)
            outs[0][k] = part[:rows].astype(BF16)
            outs[1][k] = part[rows:].astype(BF16)

    q_len = jnp.zeros((edges, sz.c), F32)
    blocks = []
    for k in range(sz.zero):
        grad = spread(dz[:, sz.cols(k)])
        q_len = q_len + grad * faded_ref[k]
        if outs is not None:
            blocks.append(grad * radial)
    scatter(0, blocks)
    q_turn = []
    for order in range(2):
        first, count = sz.starts[order], sz.counts[order]
        weight_ref = (one_ref, two_ref)[order]
        cos = geo_at(geo_ref, 1 + 2 * order, edges)
        sin = geo_at(geo_ref, 2 + 2 * order, edges)
        both = jnp.concatenate(
            [
                jnp.concatenate(d_pooled[first : first + count], axis=1),
                jnp.concatenate(d_pooled[first + count : first + 2 * count], axis=1),
            ],
            axis=0,
        )
        a, b = fine_dot(both, [weight_ref[0], weight_ref[1]], dot_t)
        d_re = a[:rows] + b[rows:]
        d_im = a[rows:] - b[:rows]
        q_cos = jnp.zeros((edges, sz.c), F32)
        q_sin = jnp.zeros((edges, sz.c), F32)
        cos_r = cos * radial
        sin_r = sin * radial
        blocks_re, blocks_im = [], []
        for k in range(count):
            re = faded_ref[first + k]
            im = faded_ref[first + count + k]
            g_re = spread(d_re[:, sz.cols(k)])
            g_im = spread(d_im[:, sz.cols(k)])
            q_cos = q_cos + (re * g_re + im * g_im)
            q_sin = q_sin + (re * g_im - im * g_re)
            if outs is not None:
                blocks_re.append(cos_r * g_re + sin_r * g_im)
                blocks_im.append(cos_r * g_im - sin_r * g_re)
        scatter(first, blocks_re + blocks_im)
        q_len = q_len + cos * q_cos + sin * q_sin
        q_turn.append((q_cos, q_sin))

    rate = geo_at(geo_ref, 9, edges)

    def total(value):
        return jnp.sum(value, axis=1, keepdims=True)

    d_len = -total(q_len * rate)
    (dc1, ds1), (dc2, ds2) = [(total(a), total(b)) for a, b in q_turn]
    c1, s1 = geo_at(geo_ref, 1, edges), geo_at(geo_ref, 2, edges)
    ux, uy, uz = (geo_at(geo_ref, 5 + n, edges) for n in range(3))
    inv_planar = geo_at(geo_ref, 8, edges)
    dc1 = dc1 + 2.0 * (c1 * dc2 + s1 * ds2)
    ds1 = ds1 + 2.0 * (c1 * ds2 - s1 * dc2)
    along = c1 * dc1 + s1 * ds1
    dx = (dc1 - along * c1) * inv_planar + d_len * ux
    dy = (ds1 - along * s1) * inv_planar + d_len * uy
    dz_ = d_len * uz
    lane = lax.broadcasted_iota(jnp.int32, (edges, sz.c), 1)
    change = jnp.where(lane == 0, dx, jnp.where(lane == 1, dy, jnp.where(lane == 2, dz_, 0.0)))
    moved = sum(dot(hot_t, part) for part in split3(change))
    return moved - around(pool(change, rows), slab)


def around(own, slab):
    edge = jnp.zeros((slab, own.shape[1]), F32)
    return jnp.concatenate([edge, own, edge], axis=0)


def place_of(pair, pairs, segment):
    if segment == 0:
        return pair
    return 2 * pair if pair < pairs // 2 else 2 * (pairs - 1 - pair) + 1


def first_slab(slabs):
    slab_now = lax.axis_index("space")
    segment = lax.axis_index("segment")
    chip = slab_now // 2
    folded = jnp.where(lax.rem(chip, 2) == 0, chip // 2, slabs // 2 - 1 - chip // 2)
    pair = jnp.where(segment == 0, chip, folded)
    return lax.rem(2 * pair + lax.rem(segment, 2) - 1 + slabs, slabs), lax.rem(slab_now, 2)


def send_back(moved, outs, sz):
    rows = moved.shape[0] // 2
    coded = encode(moved).astype(BF16)
    outs[0][sz.coefs] = coded[:rows]
    outs[1][sz.coefs] = coded[rows:]


def share(moved, outs):
    slab = moved.shape[0] // 4
    left, low, high, right = (moved[n * slab : (n + 1) * slab] for n in range(4))
    even = lax.rem(lax.axis_index("space"), 2) == 0
    outs[0][...] = jnp.where(even, low, high)
    outs[1][...] = jnp.where(even, high, low)
    outs[2][...] = jnp.where(even, right, left)
    outs[3][...] = jnp.where(even, left, right)


def join_kernel(here_ref, theirs_ref, straight_ref, cross_ref, both_ref):
    slab = here_ref.shape[0]
    even = lax.rem(lax.axis_index("space"), 2) == 0
    here = here_ref[...] + straight_ref[...]
    there = theirs_ref[...] + cross_ref[...]
    both_ref[:slab, :] = jnp.where(even, here, there)
    both_ref[slab:, :] = jnp.where(even, there, here)


def close_kernel(*refs):
    *sums_refs, energies_ref, places_ref = refs
    slab = energies_ref.shape[1]
    for n, ref in enumerate(sums_refs):

        @pl.when(lax.axis_index("segment") == n)
        def _(ref=ref):
            sums = ref[...]
            rows, c = sums.shape
            turned = jnp.transpose(jnp.concatenate([sums, jnp.zeros((c - rows, c), F32)], axis=0))
            for b in range(2):
                energies_ref[b : b + 1, :] = turned[3:4, b * slab : (b + 1) * slab]
                for n in range(3):
                    places_ref[n, b : b + 1, :] = turned[n : n + 1, b * slab : (b + 1) * slab]


def pack_kernel(
    node_hbm, places_hbm, species_hbm, sources_hbm, grad_hbm, table_hbm, mine_ref, other_ref,
    states, places, species, sources, grads, table, sems
):
    @pl.when(lax.axis_index("segment") == 0)
    def _():
        pack(
            (node_hbm, places_hbm, species_hbm, sources_hbm, grad_hbm, table_hbm), mine_ref, other_ref,
            states, places, species, sources, grads, table, sems,
        )


def pack(given, mine_ref, other_ref, states, places, species, sources, grads, table, sems):
    batch = lax.rem(lax.axis_index("space"), 2)
    copies = []
    for n, (source, target) in enumerate(zip(given, (states, places, species, sources, grads, table))):
        copies.append(pltpu.make_async_copy(source, target, sems.at[n]))
        copies[-1].start()
    for copy in copies:
        copy.wait()
    coefs, per_slab, c = states.shape[1:]
    lane = lax.broadcasted_iota(jnp.int32, (per_slab, c), 1)
    eye = (
        lax.broadcasted_iota(jnp.int32, (per_slab, per_slab), 0)
        == lax.broadcasted_iota(jnp.int32, (per_slab, per_slab), 1)
    )

    def column(row):
        return jnp.sum(jnp.where(eye, jnp.broadcast_to(row, (per_slab, per_slab)), 0.0), axis=1, keepdims=True)

    both = []
    for b in range(2):
        names = column(species[b : b + 1, :].astype(F32)).astype(jnp.int32)
        kinds = table.shape[0]
        hot = (names == lax.broadcasted_iota(jnp.int32, (per_slab, kinds), 1)).astype(BF16)
        first = (states[b, 0].astype(F32) + dot(hot, table[...])).astype(BF16)
        extra = jnp.zeros((per_slab, c), F32)
        for n in range(3):
            extra = jnp.where(lane == n, column(places[n, b : b + 1, :]), extra)
        extra = encode(jnp.where(lane == 3, column(grads[b : b + 1, :]), extra))
        for j in range(sources.shape[2]):
            index = sources[b, :, j : j + 1]
            extra = jnp.where(lane == SOURCES + j, (index // BASE).astype(F32), extra)
            extra = jnp.where(lane == SOURCES + 8 + j, (index % BASE).astype(F32), extra)
        both.append((first, extra.astype(BF16)))
    for ref, chosen in ((mine_ref, batch), (other_ref, 1 - batch)):
        ref[pl.ds(0, coefs)] = states[chosen]
        ref[0] = jnp.where(chosen == 0, both[0][0].astype(F32), both[1][0].astype(F32)).astype(BF16)
        ref[coefs] = jnp.where(chosen == 0, both[0][1].astype(F32), both[1][1].astype(F32)).astype(BF16)


def open_kernel(mine_ref, partner_ref, straight_ref, cross_ref, low_ref, high_ref):
    @pl.when(lax.axis_index("segment") == 0)
    def _():
        even = lax.rem(lax.axis_index("space"), 2) == 0

        def choose(a, b):
            return jnp.where(even, a, b)

        for k in range(low_ref.shape[0]):
            mine, partner = mine_ref[k].astype(F32), partner_ref[k].astype(F32)
            straight, cross = straight_ref[k].astype(F32), cross_ref[k].astype(F32)
            low_ref[k] = jnp.concatenate([choose(cross, straight), choose(mine, partner)], axis=0).astype(BF16)
            high_ref[k] = jnp.concatenate([choose(partner, mine), choose(straight, cross)], axis=0).astype(BF16)


def edges_of(refs, coefs, slabs, neighbours, rate_ref, hot_ref, hot_t_ref, geo_ref):
    start, _ = first_slab(slabs)
    extra = jnp.concatenate([ref[coefs].astype(F32) for ref in refs], axis=0)
    window, c = extra.shape
    rows = window // 2
    per_slab = rows // 2
    edges = rows * neighbours
    numbers = decode(extra)
    own_extra = extra[per_slab : per_slab + rows]
    low = pltpu.roll(own_extra, c - 8, 1)
    index = own_extra.astype(jnp.int32) * BASE + low.astype(jnp.int32)
    place = lax.rem(index // per_slab - start + slabs, slabs) * per_slab + index % per_slab
    columns = lax.broadcasted_iota(jnp.int32, (rows, c), 1)
    hot = jnp.concatenate(
        [
            (place[:, SOURCES + j : SOURCES + j + 1] == columns).astype(F32)
            for j in range(neighbours)
        ],
        axis=0,
    )
    hot_t_ref[...] = jnp.transpose(hot).astype(BF16)[:window]
    hot = hot.astype(BF16)[:, :window]
    hot_ref[...] = hot
    lift = lax.broadcasted_iota(jnp.int32, (window, c), 0) // per_slab - 1
    offset = []
    for n in range(3):
        column = jnp.broadcast_to(numbers[:, n : n + 1], (window, c))
        if n == 2:
            column = column + SLAB_DEPTH * lift.astype(F32)
        there = sum(dot(hot, part) for part in split3(column))
        offset.append(there - jnp.concatenate([column[per_slab : per_slab + rows]] * neighbours, axis=0))
    flat = offset[0] * offset[0] + offset[1] * offset[1] + 1.0
    length = jnp.sqrt(flat + offset[2] * offset[2])
    planar = jnp.sqrt(flat)
    c1, s1 = offset[0] / planar, offset[1] / planar
    rate = jnp.broadcast_to(rate_ref[...], (edges, c))
    values = [
        jnp.exp(-rate * length),
        c1,
        s1,
        c1 * c1 - s1 * s1,
        2.0 * c1 * s1,
        offset[0] / length,
        offset[1] / length,
        offset[2] / length,
        1.0 / planar,
        rate,
    ]
    for n, value in enumerate(values):
        geo_ref[n * edges : (n + 1) * edges, :] = value
    return numbers[per_slab : per_slab + rows]


def stage_kernel(zero_hbm, one_hbm, two_hbm, zero_ref, one_ref, two_ref, sems):
    pairs = [(zero_hbm, zero_ref)]
    for source, target in ((one_hbm, one_ref), (two_hbm, two_ref)):
        pairs += [(source.at[n], target.at[n]) for n in range(2)]
    copies = [pltpu.make_async_copy(source, target, sems.at[n]) for n, (source, target) in enumerate(pairs)]
    for copy in copies:
        copy.start()
    for copy in copies:
        copy.wait()


def forward_kernel(
    tick, sz, slabs, neighbours, low_ref, high_ref, rate_ref, zero_ref, one_ref, two_ref,
    out_ref, pooled_ref, hot_t_ref, geo_ref, faded_ref, hot_ref
):
    @pl.when(lax.axis_index("segment") == tick)
    def _():
        rows = low_ref.shape[1]
        refs = (low_ref, high_ref)
        edges_of(refs, sz.coefs, slabs, neighbours, rate_ref, hot_ref, hot_t_ref, geo_ref)
        pooled = forward(refs, hot_ref, geo_ref, faded_ref, zero_ref, one_ref, two_ref, sz, rows, False)
        signal = signal_of(pooled, sz)
        gate, lifted = silu_parts(signal)
        for k in range(sz.coefs):
            pooled_ref[k] = pooled[k]
            added = lifted if k == 0 else gate * pooled[k]
            out_ref[k] = (own_rows(refs, k) + added).astype(BF16)
        out_ref[sz.coefs] = own_rows(refs, sz.coefs).astype(BF16)


def turn_kernel(
    tick, sz, slabs, neighbours, low_ref, high_ref, rate_ref, zero_ref, one_ref, two_ref, read_ref,
    back_low_ref, back_high_ref, hot_ref, hot_t_ref, geo_ref, faded_ref
):
    @pl.when(lax.axis_index("segment") == tick)
    def _():
        rows = low_ref.shape[1]
        refs = (low_ref, high_ref)
        outs = (back_low_ref, back_high_ref)
        own = edges_of(refs, sz.coefs, slabs, neighbours, rate_ref, hot_ref, hot_t_ref, geo_ref)
        pooled = forward(refs, hot_ref, geo_ref, faded_ref, zero_ref, one_ref, two_ref, sz, rows, True)
        signal = signal_of(pooled, sz)
        _, lifted = silu_parts(signal)
        updated = own_rows(refs, 0) + lifted
        gate, active = silu_parts(updated)
        read = read_ref[...]
        energy = jnp.sum(read * active, axis=1, keepdims=True)
        lane = lax.broadcasted_iota(jnp.int32, (rows, sz.c), 1)
        energy = around(jnp.where(lane == 3, energy, 0.0), rows // 2)
        upstream = [own[:, 3:4] * read * (gate + updated * gate * (1.0 - gate))]
        moved = backward(
            upstream, pooled, hot_t_ref, geo_ref, faded_ref, zero_ref, one_ref, two_ref, sz, rows, True, outs
        )
        send_back(moved + energy, outs, sz)


def backward_kernel(
    tick, sz, up_low_ref, up_high_ref, pooled_ref, hot_t_ref, geo_ref, faded_ref, zero_ref, one_ref, two_ref, *outs
):
    @pl.when(lax.axis_index("segment") == tick)
    def _():
        rows = up_low_ref.shape[1]
        upstream = [up_low_ref[k].astype(F32) + up_high_ref[k].astype(F32) for k in range(sz.coefs)]
        pooled = [pooled_ref[k] for k in range(sz.coefs)]
        moved = backward(
            upstream, pooled, hot_t_ref, geo_ref, faded_ref, zero_ref, one_ref, two_ref, sz, rows, False,
            outs if tick else None,
        )
        carried = decode(up_low_ref[sz.coefs].astype(F32)) + decode(up_high_ref[sz.coefs].astype(F32))
        moved = moved + around(carried, rows // 2)
        if tick:
            send_back(moved, outs, sz)
        else:
            share(moved, outs)


def call(body, operands, shapes, name, spaces=None, scratch=()):
    spaces = spaces or [pltpu.VMEM] * len(operands)
    operands = [pltpu.with_memory_space_constraint(value, space) for value, space in zip(operands, spaces)]
    return pl.pallas_call(
        body,
        out_shape=shapes,
        in_specs=[pl.BlockSpec(memory_space=space) for space in spaces],
        out_specs=[pl.BlockSpec(memory_space=pltpu.VMEM) for _ in shapes],
        scratch_shapes=list(scratch),
        compiler_params=pltpu.CompilerParams(vmem_limit_bytes=VMEM_LIMIT),
        name=name,
    )(*operands)


def on_device(
    node_states,
    species,
    species_table,
    places,
    sources,
    radial_rate,
    zero_weight,
    one_weight,
    two_weight,
    read_weight,
    energy_grad,
):
    segments = lax.axis_size("segment")
    slabs = lax.axis_size("space")
    batches, per_slab = species.shape
    coefs, channels = node_states.shape[2:]
    neighbours = sources.shape[2]
    rows = batches * per_slab
    edges = rows * neighbours
    sz = Sizes(zero_weight.shape, one_weight.shape, two_weight.shape, channels)
    axes = ("segment", "space")
    shape = jax.ShapeDtypeStruct

    pairs = slabs // 2

    def within(value, target):
        ways = [(s * slabs + i, s * slabs + target(i) % slabs) for s in range(segments) for i in range(slabs)]
        return lax.ppermute(value, axes, ways)

    def hop(value, step, by):
        ways = []
        for start in range(segments):
            stop = (start + step) % segments
            for q in range(pairs):
                a, b = place_of(q, pairs, start), place_of((q + by) % pairs, pairs, stop)
                ways += [(start * slabs + 2 * a + c, stop * slabs + 2 * b + c) for c in range(2)]
        return lax.ppermute(value, axes, ways)

    raw = [
        node_states.transpose(0, 2, 1, 3), places.transpose(1, 0, 2), species, sources, energy_grad, species_table,
    ]
    packed = shape((coefs + 1, per_slab, channels), BF16)
    mine, other = call(
        pack_kernel, raw, [packed, packed], "pack", [pltpu.HBM] * len(raw),
        [pltpu.VMEM(v.shape, v.dtype) for v in raw] + [pltpu.SemaphoreType.DMA((len(raw),))],
    )
    partner = within(other, lambda i: i + 1 - 2 * (i % 2))
    straight = within(mine, lambda i: i + 2 if i % 2 else i - 2)
    cross = within(other, lambda i: i + 1 if i % 2 else i - 1)
    stored = [zero_weight[0], one_weight[0], two_weight[0]]
    spaces = [pltpu.HBM] * 3
    on_chip = [pltpu.VMEM(w.shape, w.dtype) for w in stored]
    sems = [pltpu.SemaphoreType.DMA((5,))]
    weights = call(stage_kernel, stored, on_chip, "stage", spaces, sems)
    whole = shape((coefs + 1, rows, channels), BF16)
    around_all = [call(open_kernel, [mine, partner, straight, cross], [whole, whole], "open")]
    kept_shapes = [
        shape((2 * rows, edges), BF16), shape((10 * edges, channels), F32), shape((coefs, edges, channels), F32),
    ]
    hot = [pltpu.VMEM((edges, 2 * rows), BF16)]
    kept = []
    for tick in range(segments - 1):
        out, *residuals = call(
            functools.partial(forward_kernel, tick, sz, slabs, neighbours),
            [*around_all[tick], radial_rate, *weights],
            [whole, shape((coefs, rows, channels), F32), *kept_shapes],
            "forward",
            scratch=hot,
        )
        kept.append(residuals)
        ways = (1, 0) if tick % 2 else (0, -1)
        around_all.append([hop(out, 1, by) for by in ways])
    final = segments - 1
    slab_sums = shape((per_slab, channels), F32)
    parts = call(
        functools.partial(turn_kernel, final, sz, slabs, neighbours),
        [*around_all[final], radial_rate, *weights, read_weight.reshape(1, channels)],
        [whole, whole],
        "turn",
        scratch=hot + [pltpu.VMEM(v.shape, v.dtype) for v in kept_shapes],
    )
    for tick in reversed(range(segments - 1)):
        ways = (1, 0) if tick % 2 else (0, -1)
        up = [hop(part, -1, -by) for part, by in zip(parts, ways)]
        pooled, *residuals = kept[tick]
        parts = call(
            functools.partial(backward_kernel, tick, sz),
            [*up, pooled, *residuals, *weights],
            [whole, whole] if tick else [slab_sums] * 4,
            "backward",
        )
    here, theirs, straight, cross = parts
    theirs = within(theirs, lambda i: i + 1 - 2 * (i % 2))
    straight = within(straight, lambda i: i - 2 if i % 2 else i + 2)
    cross = within(cross, lambda i: i + 1 if i % 2 else i - 1)
    (both,) = call(join_kernel, [here, theirs, straight, cross], [shape((rows, channels), F32)], "join")
    copies = [both] + [
        lax.ppermute(both, "segment", [(s, (s + stop) % segments) for s in range(segments)])
        for stop in range(1, segments)
    ]
    energies, gradients = call(
        close_kernel, copies, [shape((batches, per_slab), F32), shape((3, batches, per_slab), F32)], "close"
    )
    return energies, gradients.transpose(1, 0, 2)


def solution(mesh):
    in_specs = (
        P(None, "space", None, None),
        P(None, "space"),
        P(),
        P(None, None, "space"),
        P(None, "space", None),
        P("segment", None),
        P("segment", None, None),
        P("segment", None, None, None),
        P("segment", None, None, None),
        P(),
        P(None, "space"),
    )
    out_specs = (P(None, "space"), P(None, None, "space"))
    return jax.shard_map(
        on_device, mesh=mesh, in_specs=in_specs, out_specs=out_specs, check_vma=False
    )
```

```python
import functools

import jax
import jax.numpy as jnp
from jax import lax
from jax.experimental import pallas as pl
from jax.experimental.pallas import tpu as pltpu
from jax.sharding import PartitionSpec as P

SLAB_DEPTH = 2.0
F32 = jnp.float32
BF16 = jnp.bfloat16
VMEM_LIMIT = 16 * 1024 * 1024

MID, LOW, SOURCES = 32, 64, 96
BASE = 256


def split(value):
    high = value.astype(BF16)
    low = (value - high.astype(F32)).astype(BF16)
    return high, low


def split3(value):
    high = value.astype(BF16)
    rest = value - high.astype(F32)
    mid = rest.astype(BF16)
    return high, mid, (rest - mid.astype(F32)).astype(BF16)


def encode(value):
    high, mid, low = split3(value)
    return high.astype(F32) + pltpu.roll(mid.astype(F32), MID, 1) + pltpu.roll(low.astype(F32), LOW, 1)


def decode(value):
    lanes = value.shape[1]
    whole = value + pltpu.roll(value, lanes - MID, 1) + pltpu.roll(value, lanes - LOW, 1)
    lane = lax.broadcasted_iota(jnp.int32, value.shape, 1)
    return jnp.where(lane < 4, whole, 0.0)


def dot(a, b):
    return lax.dot_general(a, b, (((1,), (0,)), ((), ())), preferred_element_type=F32)


def dot_t(a, b):
    return lax.dot_general(a, b, (((1,), (1,)), ((), ())), preferred_element_type=F32)


def fine_dot(value, weights, product):
    rows = value.shape[0]
    stacked = jnp.concatenate(split(value), axis=0)
    outs = []
    for weight in weights:
        out = product(stacked, weight)
        outs.append(out[:rows] + out[rows:])
    return outs


def silu_parts(value):
    gate = 1.0 / (1.0 + jnp.exp(-value))
    return gate, value * gate


class Sizes:
    def __init__(self, zero_shape, one_shape, two_shape, channels):
        self.c = channels
        self.zero = zero_shape[-1] // channels
        self.one = one_shape[-1] // channels
        self.two = two_shape[-1] // channels
        self.coefs = self.zero + 2 * (self.one + self.two)
        self.starts = (self.zero, self.zero + 2 * self.one)
        self.counts = (self.one, self.two)

    def cols(self, first, count=1):
        return slice(first * self.c, (first + count) * self.c)


def picked_group(refs, hot, first, count):
    blocks = [jnp.concatenate([ref[k] for ref in refs], axis=0) for k in range(first, first + count)]
    return dot(hot, jnp.concatenate(blocks, axis=1))


def own_rows(refs, k):
    low, high = (ref[k].astype(F32) for ref in refs)
    slab = low.shape[0] // 2
    return jnp.concatenate([low[slab:], high[:slab]], axis=0)


def pool(value, rows):
    total = value[:rows]
    for start in range(rows, value.shape[0], rows):
        total = total + value[start : start + rows]
    return total


def geo_at(geo_ref, which, edges):
    return geo_ref[which * edges : (which + 1) * edges, :]


def forward(refs, hot_ref, geo_ref, faded_ref, zero_ref, one_ref, two_ref, sz, rows, last):
    hot = hot_ref[...]
    edges = hot.shape[0]
    factor = (edges // rows) ** (-0.5)
    radial = geo_at(geo_ref, 0, edges)

    def scaled(block, k):
        faded = block * radial
        faded_ref[k] = faded
        return faded.astype(BF16).astype(F32)

    pooled = [None] * sz.coefs
    group = picked_group(refs, hot, 0, sz.zero)
    zin = jnp.concatenate(
        [pool(scaled(group[:, sz.cols(k)], k), rows) for k in range(sz.zero)], axis=1
    )
    kept = 1 if last else sz.zero
    (zout,) = fine_dot(zin, [zero_ref[:, sz.cols(0, kept)]], dot)
    for k in range(kept):
        pooled[k] = zout[:, sz.cols(k)] * factor
    for order in range(2):
        first, count = sz.starts[order], sz.counts[order]
        weight_ref = (one_ref, two_ref)[order]
        cos = geo_at(geo_ref, 1 + 2 * order, edges)
        sin = geo_at(geo_ref, 2 + 2 * order, edges)
        group = picked_group(refs, hot, first, 2 * count)
        res, ims = [], []
        for k in range(count):
            re = scaled(group[:, sz.cols(k)], first + k)
            im = scaled(group[:, sz.cols(count + k)], first + count + k)
            res.append(pool(cos * re - sin * im, rows))
            ims.append(pool(sin * re + cos * im, rows))
        both = jnp.concatenate(
            [jnp.concatenate(res, axis=1), jnp.concatenate(ims, axis=1)], axis=0
        )
        a, b = fine_dot(both, [weight_ref[0], weight_ref[1]], dot)
        out_re = (a[:rows] - b[rows:]) * factor
        out_im = (b[:rows] + a[rows:]) * factor
        for k in range(count):
            pooled[first + k] = out_re[:, sz.cols(k)]
            pooled[first + count + k] = out_im[:, sz.cols(k)]
    return pooled


def signal_of(pooled, sz):
    total = pooled[0]
    for k in range(sz.zero, sz.coefs):
        total = total + pooled[k] * pooled[k]
    return total


def backward(
    upstream, pooled, hot_t_ref, geo_ref, faded_ref, zero_ref, one_ref, two_ref, sz, rows, last, outs
):
    hot_t = hot_t_ref[...]
    edges = hot_t.shape[1]
    slab = rows // 2
    factor = (edges // rows) ** (-0.5)
    signal = signal_of(pooled, sz)
    gate, _ = silu_parts(signal)
    slope = gate * (1.0 - gate)
    d_signal = upstream[0] * (gate + signal * slope)
    if not last:
        inner = upstream[1] * pooled[1]
        for k in range(2, sz.coefs):
            inner = inner + upstream[k] * pooled[k]
        d_signal = d_signal + inner * slope
    d_pooled = [d_signal * factor]
    for k in range(1, sz.coefs):
        if last:
            d_pooled.append(2.0 * factor * d_signal * pooled[k] if k >= sz.zero else None)
        else:
            term = gate * upstream[k]
            if k >= sz.zero:
                term = term + 2.0 * d_signal * pooled[k]
            d_pooled.append(term * factor)

    radial = geo_at(geo_ref, 0, edges)
    kept = 1 if last else sz.zero
    (dz,) = fine_dot(jnp.concatenate(d_pooled[:kept], axis=1), [zero_ref[:, sz.cols(0, kept)]], dot_t)

    def spread(block):
        return jnp.concatenate([block] * (edges // rows), axis=0)

    def scatter(first, blocks):
        if outs is None:
            return
        back = dot(hot_t, jnp.concatenate([block.astype(BF16) for block in blocks], axis=1))
        for n in range(len(blocks)):
            k = first + n
            part = back[:, sz.cols(n)]
            if not last or k == 0:
                part = part + around(upstream[k], slab)
            outs[0][k] = part[:rows].astype(BF16)
            outs[1][k] = part[rows:].astype(BF16)

    q_len = jnp.zeros((edges, sz.c), F32)
    blocks = []
    for k in range(sz.zero):
        grad = spread(dz[:, sz.cols(k)])
        q_len = q_len + grad * faded_ref[k]
        if outs is not None:
            blocks.append(grad * radial)
    scatter(0, blocks)
    q_turn = []
    for order in range(2):
        first, count = sz.starts[order], sz.counts[order]
        weight_ref = (one_ref, two_ref)[order]
        cos = geo_at(geo_ref, 1 + 2 * order, edges)
        sin = geo_at(geo_ref, 2 + 2 * order, edges)
        both = jnp.concatenate(
            [
                jnp.concatenate(d_pooled[first : first + count], axis=1),
                jnp.concatenate(d_pooled[first + count : first + 2 * count], axis=1),
            ],
            axis=0,
        )
        a, b = fine_dot(both, [weight_ref[0], weight_ref[1]], dot_t)
        d_re = a[:rows] + b[rows:]
        d_im = a[rows:] - b[:rows]
        q_cos = jnp.zeros((edges, sz.c), F32)
        q_sin = jnp.zeros((edges, sz.c), F32)
        cos_r = cos * radial
        sin_r = sin * radial
        blocks_re, blocks_im = [], []
        for k in range(count):
            re = faded_ref[first + k]
            im = faded_ref[first + count + k]
            g_re = spread(d_re[:, sz.cols(k)])
            g_im = spread(d_im[:, sz.cols(k)])
            q_cos = q_cos + (re * g_re + im * g_im)
            q_sin = q_sin + (re * g_im - im * g_re)
            if outs is not None:
                blocks_re.append(cos_r * g_re + sin_r * g_im)
                blocks_im.append(cos_r * g_im - sin_r * g_re)
        scatter(first, blocks_re + blocks_im)
        q_len = q_len + cos * q_cos + sin * q_sin
        q_turn.append((q_cos, q_sin))

    rate = geo_at(geo_ref, 9, edges)

    def total(value):
        return jnp.sum(value, axis=1, keepdims=True)

    d_len = -total(q_len * rate)
    (dc1, ds1), (dc2, ds2) = [(total(a), total(b)) for a, b in q_turn]
    c1, s1 = geo_at(geo_ref, 1, edges), geo_at(geo_ref, 2, edges)
    ux, uy, uz = (geo_at(geo_ref, 5 + n, edges) for n in range(3))
    inv_planar = geo_at(geo_ref, 8, edges)
    dc1 = dc1 + 2.0 * (c1 * dc2 + s1 * ds2)
    ds1 = ds1 + 2.0 * (c1 * ds2 - s1 * dc2)
    along = c1 * dc1 + s1 * ds1
    dx = (dc1 - along * c1) * inv_planar + d_len * ux
    dy = (ds1 - along * s1) * inv_planar + d_len * uy
    dz_ = d_len * uz
    lane = lax.broadcasted_iota(jnp.int32, (edges, sz.c), 1)
    change = jnp.where(lane == 0, dx, jnp.where(lane == 1, dy, jnp.where(lane == 2, dz_, 0.0)))
    moved = sum(dot(hot_t, part) for part in split3(change))
    return moved - around(pool(change, rows), slab)


def around(own, slab):
    edge = jnp.zeros((slab, own.shape[1]), F32)
    return jnp.concatenate([edge, own, edge], axis=0)


def place_of(pair, pairs, segment):
    if segment == 0:
        return pair
    return 2 * pair if pair < pairs // 2 else 2 * (pairs - 1 - pair) + 1


def first_slab(slabs):
    slab_now = lax.axis_index("space")
    segment = lax.axis_index("segment")
    chip = slab_now // 2
    folded = jnp.where(lax.rem(chip, 2) == 0, chip // 2, slabs // 2 - 1 - chip // 2)
    pair = jnp.where(segment == 0, chip, folded)
    return lax.rem(2 * pair + lax.rem(segment, 2) - 1 + slabs, slabs), lax.rem(slab_now, 2)


def send_back(moved, outs, sz):
    rows = moved.shape[0] // 2
    coded = encode(moved).astype(BF16)
    outs[0][sz.coefs] = coded[:rows]
    outs[1][sz.coefs] = coded[rows:]


def share(moved, outs):
    slab = moved.shape[0] // 4
    left, low, high, right = (moved[n * slab : (n + 1) * slab] for n in range(4))
    even = lax.rem(lax.axis_index("space"), 2) == 0
    outs[0][...] = jnp.where(even, low, high)
    outs[1][...] = jnp.where(even, high, low)
    outs[2][...] = jnp.where(even, right, left)
    outs[3][...] = jnp.where(even, left, right)


def join_kernel(here_ref, theirs_ref, straight_ref, cross_ref, both_ref):
    slab = here_ref.shape[0]
    even = lax.rem(lax.axis_index("space"), 2) == 0
    here = here_ref[...] + straight_ref[...]
    there = theirs_ref[...] + cross_ref[...]
    both_ref[:slab, :] = jnp.where(even, here, there)
    both_ref[slab:, :] = jnp.where(even, there, here)


def close_kernel(*refs):
    *sums_refs, energies_ref, places_ref = refs
    slab = energies_ref.shape[1]
    for n, ref in enumerate(sums_refs):

        @pl.when(lax.axis_index("segment") == n)
        def _(ref=ref):
            sums = ref[...]
            rows, c = sums.shape
            turned = jnp.transpose(jnp.concatenate([sums, jnp.zeros((c - rows, c), F32)], axis=0))
            for b in range(2):
                energies_ref[b : b + 1, :] = turned[3:4, b * slab : (b + 1) * slab]
                for n in range(3):
                    places_ref[n, b : b + 1, :] = turned[n : n + 1, b * slab : (b + 1) * slab]


def pack_kernel(
    node_hbm, places_hbm, species_hbm, sources_hbm, grad_hbm, table_hbm, mine_ref, other_ref,
    states, places, species, sources, grads, table, sems
):
    @pl.when(lax.axis_index("segment") == 0)
    def _():
        pack(
            (node_hbm, places_hbm, species_hbm, sources_hbm, grad_hbm, table_hbm), mine_ref, other_ref,
            states, places, species, sources, grads, table, sems,
        )


def pack(given, mine_ref, other_ref, states, places, species, sources, grads, table, sems):
    batch = lax.rem(lax.axis_index("space"), 2)
    copies = []
    for n, (source, target) in enumerate(zip(given, (states, places, species, sources, grads, table))):
        copies.append(pltpu.make_async_copy(source, target, sems.at[n]))
        copies[-1].start()
    for copy in copies:
        copy.wait()
    coefs, per_slab, c = states.shape[1:]
    lane = lax.broadcasted_iota(jnp.int32, (per_slab, c), 1)
    eye = (
        lax.broadcasted_iota(jnp.int32, (per_slab, per_slab), 0)
        == lax.broadcasted_iota(jnp.int32, (per_slab, per_slab), 1)
    )

    def column(row):
        return jnp.sum(jnp.where(eye, jnp.broadcast_to(row, (per_slab, per_slab)), 0.0), axis=1, keepdims=True)

    both = []
    for b in range(2):
        names = column(species[b : b + 1, :].astype(F32)).astype(jnp.int32)
        kinds = table.shape[0]
        hot = (names == lax.broadcasted_iota(jnp.int32, (per_slab, kinds), 1)).astype(BF16)
        first = (states[b, 0].astype(F32) + dot(hot, table[...])).astype(BF16)
        extra = jnp.zeros((per_slab, c), F32)
        for n in range(3):
            extra = jnp.where(lane == n, column(places[n, b : b + 1, :]), extra)
        extra = encode(jnp.where(lane == 3, column(grads[b : b + 1, :]), extra))
        for j in range(sources.shape[2]):
            index = sources[b, :, j : j + 1]
            extra = jnp.where(lane == SOURCES + j, (index // BASE).astype(F32), extra)
            extra = jnp.where(lane == SOURCES + 8 + j, (index % BASE).astype(F32), extra)
        both.append((first, extra.astype(BF16)))
    for ref, chosen in ((mine_ref, batch), (other_ref, 1 - batch)):
        ref[pl.ds(0, coefs)] = states[chosen]
        ref[0] = jnp.where(chosen == 0, both[0][0].astype(F32), both[1][0].astype(F32)).astype(BF16)
        ref[coefs] = jnp.where(chosen == 0, both[0][1].astype(F32), both[1][1].astype(F32)).astype(BF16)


def open_kernel(mine_ref, partner_ref, straight_ref, cross_ref, low_ref, high_ref):
    @pl.when(lax.axis_index("segment") == 0)
    def _():
        even = lax.rem(lax.axis_index("space"), 2) == 0

        def choose(a, b):
            return jnp.where(even, a, b)

        for k in range(low_ref.shape[0]):
            mine, partner = mine_ref[k].astype(F32), partner_ref[k].astype(F32)
            straight, cross = straight_ref[k].astype(F32), cross_ref[k].astype(F32)
            low_ref[k] = jnp.concatenate([choose(cross, straight), choose(mine, partner)], axis=0).astype(BF16)
            high_ref[k] = jnp.concatenate([choose(partner, mine), choose(straight, cross)], axis=0).astype(BF16)


def edges_of(refs, coefs, slabs, neighbours, rate_ref, hot_ref, hot_t_ref, geo_ref):
    start, _ = first_slab(slabs)
    extra = jnp.concatenate([ref[coefs].astype(F32) for ref in refs], axis=0)
    window, c = extra.shape
    rows = window // 2
    per_slab = rows // 2
    edges = rows * neighbours
    numbers = decode(extra)
    own_extra = extra[per_slab : per_slab + rows]
    low = pltpu.roll(own_extra, c - 8, 1)
    index = own_extra.astype(jnp.int32) * BASE + low.astype(jnp.int32)
    place = lax.rem(index // per_slab - start + slabs, slabs) * per_slab + index % per_slab
    columns = lax.broadcasted_iota(jnp.int32, (rows, c), 1)
    hot = jnp.concatenate(
        [
            (place[:, SOURCES + j : SOURCES + j + 1] == columns).astype(F32)
            for j in range(neighbours)
        ],
        axis=0,
    )
    hot_t_ref[...] = jnp.transpose(hot).astype(BF16)[:window]
    hot = hot.astype(BF16)[:, :window]
    hot_ref[...] = hot
    lift = lax.broadcasted_iota(jnp.int32, (window, c), 0) // per_slab - 1
    offset = []
    for n in range(3):
        column = jnp.broadcast_to(numbers[:, n : n + 1], (window, c))
        if n == 2:
            column = column + SLAB_DEPTH * lift.astype(F32)
        there = sum(dot(hot, part) for part in split3(column))
        offset.append(there - jnp.concatenate([column[per_slab : per_slab + rows]] * neighbours, axis=0))
    flat = offset[0] * offset[0] + offset[1] * offset[1] + 1.0
    length = jnp.sqrt(flat + offset[2] * offset[2])
    planar = jnp.sqrt(flat)
    c1, s1 = offset[0] / planar, offset[1] / planar
    rate = jnp.broadcast_to(rate_ref[...], (edges, c))
    values = [
        jnp.exp(-rate * length),
        c1,
        s1,
        c1 * c1 - s1 * s1,
        2.0 * c1 * s1,
        offset[0] / length,
        offset[1] / length,
        offset[2] / length,
        1.0 / planar,
        rate,
    ]
    for n, value in enumerate(values):
        geo_ref[n * edges : (n + 1) * edges, :] = value
    return numbers[per_slab : per_slab + rows]


def stage_kernel(zero_hbm, one_hbm, two_hbm, zero_ref, one_ref, two_ref, sems):
    pairs = [(zero_hbm, zero_ref)]
    for source, target in ((one_hbm, one_ref), (two_hbm, two_ref)):
        pairs += [(source.at[n], target.at[n]) for n in range(2)]
    copies = [pltpu.make_async_copy(source, target, sems.at[n]) for n, (source, target) in enumerate(pairs)]
    for copy in copies:
        copy.start()
    for copy in copies:
        copy.wait()


def forward_kernel(
    tick, sz, slabs, neighbours, low_ref, high_ref, rate_ref, zero_ref, one_ref, two_ref,
    out_ref, pooled_ref, hot_t_ref, geo_ref, faded_ref, hot_ref
):
    @pl.when(lax.axis_index("segment") == tick)
    def _():
        rows = low_ref.shape[1]
        refs = (low_ref, high_ref)
        edges_of(refs, sz.coefs, slabs, neighbours, rate_ref, hot_ref, hot_t_ref, geo_ref)
        pooled = forward(refs, hot_ref, geo_ref, faded_ref, zero_ref, one_ref, two_ref, sz, rows, False)
        signal = signal_of(pooled, sz)
        gate, lifted = silu_parts(signal)
        for k in range(sz.coefs):
            pooled_ref[k] = pooled[k]
            added = lifted if k == 0 else gate * pooled[k]
            out_ref[k] = (own_rows(refs, k) + added).astype(BF16)
        out_ref[sz.coefs] = own_rows(refs, sz.coefs).astype(BF16)


def turn_kernel(
    tick, sz, slabs, neighbours, low_ref, high_ref, rate_ref, zero_ref, one_ref, two_ref, read_ref,
    back_low_ref, back_high_ref, hot_ref, hot_t_ref, geo_ref, faded_ref
):
    @pl.when(lax.axis_index("segment") == tick)
    def _():
        rows = low_ref.shape[1]
        refs = (low_ref, high_ref)
        outs = (back_low_ref, back_high_ref)
        own = edges_of(refs, sz.coefs, slabs, neighbours, rate_ref, hot_ref, hot_t_ref, geo_ref)
        pooled = forward(refs, hot_ref, geo_ref, faded_ref, zero_ref, one_ref, two_ref, sz, rows, True)
        signal = signal_of(pooled, sz)
        _, lifted = silu_parts(signal)
        updated = own_rows(refs, 0) + lifted
        gate, active = silu_parts(updated)
        read = read_ref[...]
        energy = jnp.sum(read * active, axis=1, keepdims=True)
        lane = lax.broadcasted_iota(jnp.int32, (rows, sz.c), 1)
        energy = around(jnp.where(lane == 3, energy, 0.0), rows // 2)
        upstream = [own[:, 3:4] * read * (gate + updated * gate * (1.0 - gate))]
        moved = backward(
            upstream, pooled, hot_t_ref, geo_ref, faded_ref, zero_ref, one_ref, two_ref, sz, rows, True, outs
        )
        send_back(moved + energy, outs, sz)


def backward_kernel(
    tick, sz, up_low_ref, up_high_ref, pooled_ref, hot_t_ref, geo_ref, faded_ref, zero_ref, one_ref, two_ref, *outs
):
    @pl.when(lax.axis_index("segment") == tick)
    def _():
        rows = up_low_ref.shape[1]
        upstream = [up_low_ref[k].astype(F32) + up_high_ref[k].astype(F32) for k in range(sz.coefs)]
        pooled = [pooled_ref[k] for k in range(sz.coefs)]
        moved = backward(
            upstream, pooled, hot_t_ref, geo_ref, faded_ref, zero_ref, one_ref, two_ref, sz, rows, False,
            outs if tick else None,
        )
        carried = decode(up_low_ref[sz.coefs].astype(F32)) + decode(up_high_ref[sz.coefs].astype(F32))
        moved = moved + around(carried, rows // 2)
        if tick:
            send_back(moved, outs, sz)
        else:
            share(moved, outs)


def call(body, operands, shapes, name, spaces=None, scratch=()):
    spaces = spaces or [pltpu.VMEM] * len(operands)
    operands = [pltpu.with_memory_space_constraint(value, space) for value, space in zip(operands, spaces)]
    return pl.pallas_call(
        body,
        out_shape=shapes,
        in_specs=[pl.BlockSpec(memory_space=space) for space in spaces],
        out_specs=[pl.BlockSpec(memory_space=pltpu.VMEM) for _ in shapes],
        scratch_shapes=list(scratch),
        compiler_params=pltpu.CompilerParams(vmem_limit_bytes=VMEM_LIMIT),
        name=name,
    )(*operands)


def on_device(
    node_states,
    species,
    species_table,
    places,
    sources,
    radial_rate,
    zero_weight,
    one_weight,
    two_weight,
    read_weight,
    energy_grad,
):
    segments = lax.axis_size("segment")
    slabs = lax.axis_size("space")
    batches, per_slab = species.shape
    coefs, channels = node_states.shape[2:]
    neighbours = sources.shape[2]
    rows = batches * per_slab
    edges = rows * neighbours
    sz = Sizes(zero_weight.shape, one_weight.shape, two_weight.shape, channels)
    axes = ("segment", "space")
    shape = jax.ShapeDtypeStruct

    pairs = slabs // 2

    def within(value, target):
        ways = [(s * slabs + i, s * slabs + target(i) % slabs) for s in range(segments) for i in range(slabs)]
        return lax.ppermute(value, axes, ways)

    def hop(value, start, stop, by):
        ways = [(place_of(q, pairs, start), place_of((q + by) % pairs, pairs, stop)) for q in range(pairs)]
        ways = [(start * slabs + 2 * a + c, stop * slabs + 2 * b + c) for a, b in ways for c in range(2)]
        ways += [(b, a) for a, b in ways]
        moving = {a for a, _ in ways}
        ways += [(i, i + 1 - 2 * (i % 2)) for i in range(segments * slabs) if i not in moving]
        return lax.ppermute(value, axes, ways)

    raw = [
        node_states.transpose(0, 2, 1, 3), places.transpose(1, 0, 2), species, sources, energy_grad, species_table,
    ]
    packed = shape((coefs + 1, per_slab, channels), BF16)
    mine, other = call(
        pack_kernel, raw, [packed, packed], "pack", [pltpu.HBM] * len(raw),
        [pltpu.VMEM(v.shape, v.dtype) for v in raw] + [pltpu.SemaphoreType.DMA((len(raw),))],
    )
    partner = within(other, lambda i: i + 1 - 2 * (i % 2))
    straight = within(mine, lambda i: i + 2 if i % 2 else i - 2)
    cross = within(other, lambda i: i + 1 if i % 2 else i - 1)
    stored = [zero_weight[0], one_weight[0], two_weight[0]]
    spaces = [pltpu.HBM] * 3
    on_chip = [pltpu.VMEM(w.shape, w.dtype) for w in stored]
    sems = [pltpu.SemaphoreType.DMA((5,))]
    weights = call(stage_kernel, stored, on_chip, "stage", spaces, sems)
    whole = shape((coefs + 1, rows, channels), BF16)
    around_all = [call(open_kernel, [mine, partner, straight, cross], [whole, whole], "open")]
    kept_shapes = [
        shape((2 * rows, edges), BF16), shape((10 * edges, channels), F32), shape((coefs, edges, channels), F32),
    ]
    hot = [pltpu.VMEM((edges, 2 * rows), BF16)]
    kept = []
    for tick in range(segments - 1):
        out, *residuals = call(
            functools.partial(forward_kernel, tick, sz, slabs, neighbours),
            [*around_all[tick], radial_rate, *weights],
            [whole, shape((coefs, rows, channels), F32), *kept_shapes],
            "forward",
            scratch=hot,
        )
        kept.append(residuals)
        ways = (1, 0) if tick % 2 else (0, -1)
        around_all.append([hop(out, tick, tick + 1, by) for by in ways])
    final = segments - 1
    slab_sums = shape((per_slab, channels), F32)
    parts = call(
        functools.partial(turn_kernel, final, sz, slabs, neighbours),
        [*around_all[final], radial_rate, *weights, read_weight.reshape(1, channels)],
        [whole, whole],
        "turn",
        scratch=hot + [pltpu.VMEM(v.shape, v.dtype) for v in kept_shapes],
    )
    for tick in reversed(range(segments - 1)):
        ways = (1, 0) if tick % 2 else (0, -1)
        up = [hop(part, tick + 1, tick, -by) for part, by in zip(parts, ways)]
        pooled, *residuals = kept[tick]
        parts = call(
            functools.partial(backward_kernel, tick, sz),
            [*up, pooled, *residuals, *weights],
            [whole, whole] if tick else [slab_sums] * 4,
            "backward",
        )
    here, theirs, straight, cross = parts
    theirs = within(theirs, lambda i: i + 1 - 2 * (i % 2))
    straight = within(straight, lambda i: i - 2 if i % 2 else i + 2)
    cross = within(cross, lambda i: i + 1 if i % 2 else i - 1)
    (both,) = call(join_kernel, [here, theirs, straight, cross], [shape((rows, channels), F32)], "join")
    copies = [both] + [
        lax.ppermute(both, "segment", [(s, (s + stop) % segments) for s in range(segments)])
        for stop in range(1, segments)
    ]
    energies, gradients = call(
        close_kernel, copies, [shape((batches, per_slab), F32), shape((3, batches, per_slab), F32)], "close"
    )
    return energies, gradients.transpose(1, 0, 2)


def solution(mesh):
    in_specs = (
        P(None, "space", None, None),
        P(None, "space"),
        P(),
        P(None, None, "space"),
        P(None, "space", None),
        P("segment", None),
        P("segment", None, None),
        P("segment", None, None, None),
        P("segment", None, None, None),
        P(),
        P(None, "space"),
    )
    out_specs = (P(None, "space"), P(None, None, "space"))
    return jax.shard_map(
        on_device, mesh=mesh, in_specs=in_specs, out_specs=out_specs, check_vma=False
    )
```

```python
import functools

import jax
import jax.numpy as jnp
from jax import lax
from jax.experimental import pallas as pl
from jax.experimental.pallas import tpu as pltpu
from jax.sharding import PartitionSpec as P

SLAB_DEPTH = 2.0
F32 = jnp.float32
BF16 = jnp.bfloat16
VMEM_LIMIT = 16 * 1024 * 1024

MID, LOW, SOURCES = 32, 64, 96
BASE = 256


def split(value):
    high = value.astype(BF16)
    low = (value - high.astype(F32)).astype(BF16)
    return high, low


def split3(value):
    high = value.astype(BF16)
    rest = value - high.astype(F32)
    mid = rest.astype(BF16)
    return high, mid, (rest - mid.astype(F32)).astype(BF16)


def encode(value):
    high, mid, low = split3(value)
    return high.astype(F32) + pltpu.roll(mid.astype(F32), MID, 1) + pltpu.roll(low.astype(F32), LOW, 1)


def decode(value):
    lanes = value.shape[1]
    whole = value + pltpu.roll(value, lanes - MID, 1) + pltpu.roll(value, lanes - LOW, 1)
    lane = lax.broadcasted_iota(jnp.int32, value.shape, 1)
    return jnp.where(lane < 4, whole, 0.0)


def dot(a, b):
    return lax.dot_general(a, b, (((1,), (0,)), ((), ())), preferred_element_type=F32)


def dot_t(a, b):
    return lax.dot_general(a, b, (((1,), (1,)), ((), ())), preferred_element_type=F32)


def fine_dot(value, weights, product):
    rows = value.shape[0]
    stacked = jnp.concatenate(split(value), axis=0)
    outs = []
    for weight in weights:
        out = product(stacked, weight)
        outs.append(out[:rows] + out[rows:])
    return outs


def silu_parts(value):
    gate = 1.0 / (1.0 + jnp.exp(-value))
    return gate, value * gate


class Sizes:
    def __init__(self, zero_shape, one_shape, two_shape, channels):
        self.c = channels
        self.zero = zero_shape[-1] // channels
        self.one = one_shape[-1] // channels
        self.two = two_shape[-1] // channels
        self.coefs = self.zero + 2 * (self.one + self.two)
        self.starts = (self.zero, self.zero + 2 * self.one)
        self.counts = (self.one, self.two)

    def cols(self, first, count=1):
        return slice(first * self.c, (first + count) * self.c)


def picked_group(refs, hot, first, count):
    blocks = [jnp.concatenate([ref[k] for ref in refs], axis=0) for k in range(first, first + count)]
    return dot(hot, jnp.concatenate(blocks, axis=1))


def own_rows(refs, k):
    low, high = (ref[k].astype(F32) for ref in refs)
    slab = low.shape[0] // 2
    return jnp.concatenate([low[slab:], high[:slab]], axis=0)


def pool(value, rows):
    total = value[:rows]
    for start in range(rows, value.shape[0], rows):
        total = total + value[start : start + rows]
    return total


def geo_at(geo_ref, which, edges):
    return geo_ref[which * edges : (which + 1) * edges, :]


def forward(refs, hot_ref, geo_ref, faded_ref, zero_ref, one_ref, two_ref, sz, rows, last):
    hot = hot_ref[...]
    edges = hot.shape[0]
    factor = (edges // rows) ** (-0.5)
    radial = geo_at(geo_ref, 0, edges)

    def scaled(block, k):
        faded = block * radial
        faded_ref[k] = faded
        return faded.astype(BF16).astype(F32)

    pooled = [None] * sz.coefs
    group = picked_group(refs, hot, 0, sz.zero)
    zin = jnp.concatenate(
        [pool(scaled(group[:, sz.cols(k)], k), rows) for k in range(sz.zero)], axis=1
    )
    kept = 1 if last else sz.zero
    (zout,) = fine_dot(zin, [zero_ref[:, sz.cols(0, kept)]], dot)
    for k in range(kept):
        pooled[k] = zout[:, sz.cols(k)] * factor
    for order in range(2):
        first, count = sz.starts[order], sz.counts[order]
        weight_ref = (one_ref, two_ref)[order]
        cos = geo_at(geo_ref, 1 + 2 * order, edges)
        sin = geo_at(geo_ref, 2 + 2 * order, edges)
        group = picked_group(refs, hot, first, 2 * count)
        res, ims = [], []
        for k in range(count):
            re = scaled(group[:, sz.cols(k)], first + k)
            im = scaled(group[:, sz.cols(count + k)], first + count + k)
            res.append(pool(cos * re - sin * im, rows))
            ims.append(pool(sin * re + cos * im, rows))
        both = jnp.concatenate(
            [jnp.concatenate(res, axis=1), jnp.concatenate(ims, axis=1)], axis=0
        )
        a, b = fine_dot(both, [weight_ref[0], weight_ref[1]], dot)
        out_re = (a[:rows] - b[rows:]) * factor
        out_im = (b[:rows] + a[rows:]) * factor
        for k in range(count):
            pooled[first + k] = out_re[:, sz.cols(k)]
            pooled[first + count + k] = out_im[:, sz.cols(k)]
    return pooled


def signal_of(pooled, sz):
    total = pooled[0]
    for k in range(sz.zero, sz.coefs):
        total = total + pooled[k] * pooled[k]
    return total


def backward(
    upstream, pooled, hot_t_ref, geo_ref, faded_ref, zero_ref, one_ref, two_ref, sz, rows, last, outs
):
    hot_t = hot_t_ref[...]
    edges = hot_t.shape[1]
    slab = rows // 2
    factor = (edges // rows) ** (-0.5)
    signal = signal_of(pooled, sz)
    gate, _ = silu_parts(signal)
    slope = gate * (1.0 - gate)
    d_signal = upstream[0] * (gate + signal * slope)
    if not last:
        inner = upstream[1] * pooled[1]
        for k in range(2, sz.coefs):
            inner = inner + upstream[k] * pooled[k]
        d_signal = d_signal + inner * slope
    d_pooled = [d_signal * factor]
    for k in range(1, sz.coefs):
        if last:
            d_pooled.append(2.0 * factor * d_signal * pooled[k] if k >= sz.zero else None)
        else:
            term = gate * upstream[k]
            if k >= sz.zero:
                term = term + 2.0 * d_signal * pooled[k]
            d_pooled.append(term * factor)

    radial = geo_at(geo_ref, 0, edges)
    kept = 1 if last else sz.zero
    (dz,) = fine_dot(jnp.concatenate(d_pooled[:kept], axis=1), [zero_ref[:, sz.cols(0, kept)]], dot_t)

    def spread(block):
        return jnp.concatenate([block] * (edges // rows), axis=0)

    def scatter(first, blocks):
        if outs is None:
            return
        back = dot(hot_t, jnp.concatenate([block.astype(BF16) for block in blocks], axis=1))
        for n in range(len(blocks)):
            k = first + n
            part = back[:, sz.cols(n)]
            if not last or k == 0:
                part = part + around(upstream[k], slab)
            outs[0][k] = part[:rows].astype(BF16)
            outs[1][k] = part[rows:].astype(BF16)

    q_len = jnp.zeros((edges, sz.c), F32)
    blocks = []
    for k in range(sz.zero):
        grad = spread(dz[:, sz.cols(k)])
        q_len = q_len + grad * faded_ref[k]
        if outs is not None:
            blocks.append(grad * radial)
    scatter(0, blocks)
    q_turn = []
    for order in range(2):
        first, count = sz.starts[order], sz.counts[order]
        weight_ref = (one_ref, two_ref)[order]
        cos = geo_at(geo_ref, 1 + 2 * order, edges)
        sin = geo_at(geo_ref, 2 + 2 * order, edges)
        both = jnp.concatenate(
            [
                jnp.concatenate(d_pooled[first : first + count], axis=1),
                jnp.concatenate(d_pooled[first + count : first + 2 * count], axis=1),
            ],
            axis=0,
        )
        a, b = fine_dot(both, [weight_ref[0], weight_ref[1]], dot_t)
        d_re = a[:rows] + b[rows:]
        d_im = a[rows:] - b[:rows]
        q_cos = jnp.zeros((edges, sz.c), F32)
        q_sin = jnp.zeros((edges, sz.c), F32)
        cos_r = cos * radial
        sin_r = sin * radial
        blocks_re, blocks_im = [], []
        for k in range(count):
            re = faded_ref[first + k]
            im = faded_ref[first + count + k]
            g_re = spread(d_re[:, sz.cols(k)])
            g_im = spread(d_im[:, sz.cols(k)])
            q_cos = q_cos + (re * g_re + im * g_im)
            q_sin = q_sin + (re * g_im - im * g_re)
            if outs is not None:
                blocks_re.append(cos_r * g_re + sin_r * g_im)
                blocks_im.append(cos_r * g_im - sin_r * g_re)
        scatter(first, blocks_re + blocks_im)
        q_len = q_len + cos * q_cos + sin * q_sin
        q_turn.append((q_cos, q_sin))

    rate = geo_at(geo_ref, 9, edges)

    def total(value):
        return jnp.sum(value, axis=1, keepdims=True)

    d_len = -total(q_len * rate)
    (dc1, ds1), (dc2, ds2) = [(total(a), total(b)) for a, b in q_turn]
    c1, s1 = geo_at(geo_ref, 1, edges), geo_at(geo_ref, 2, edges)
    ux, uy, uz = (geo_at(geo_ref, 5 + n, edges) for n in range(3))
    inv_planar = geo_at(geo_ref, 8, edges)
    dc1 = dc1 + 2.0 * (c1 * dc2 + s1 * ds2)
    ds1 = ds1 + 2.0 * (c1 * ds2 - s1 * dc2)
    along = c1 * dc1 + s1 * ds1
    dx = (dc1 - along * c1) * inv_planar + d_len * ux
    dy = (ds1 - along * s1) * inv_planar + d_len * uy
    dz_ = d_len * uz
    lane = lax.broadcasted_iota(jnp.int32, (edges, sz.c), 1)
    change = jnp.where(lane == 0, dx, jnp.where(lane == 1, dy, jnp.where(lane == 2, dz_, 0.0)))
    moved = sum(dot(hot_t, part) for part in split3(change))
    return moved - around(pool(change, rows), slab)


def around(own, slab):
    edge = jnp.zeros((slab, own.shape[1]), F32)
    return jnp.concatenate([edge, own, edge], axis=0)


def place_of(pair, pairs, segment):
    if segment == 0:
        return pair
    return 2 * pair if pair < pairs // 2 else 2 * (pairs - 1 - pair) + 1


def first_slab(slabs):
    slab_now = lax.axis_index("space")
    segment = lax.axis_index("segment")
    chip = slab_now // 2
    folded = jnp.where(lax.rem(chip, 2) == 0, chip // 2, slabs // 2 - 1 - chip // 2)
    pair = jnp.where(segment == 0, chip, folded)
    return lax.rem(2 * pair + lax.rem(segment, 2) - 1 + slabs, slabs), lax.rem(slab_now, 2)


def send_back(moved, outs, sz):
    rows = moved.shape[0] // 2
    coded = encode(moved).astype(BF16)
    outs[0][sz.coefs] = coded[:rows]
    outs[1][sz.coefs] = coded[rows:]


def share(moved, outs):
    slab = moved.shape[0] // 4
    left, low, high, right = (moved[n * slab : (n + 1) * slab] for n in range(4))
    even = lax.rem(lax.axis_index("space"), 2) == 0
    outs[0][...] = jnp.where(even, low, high)
    outs[1][...] = jnp.where(even, high, low)
    outs[2][...] = jnp.where(even, right, left)
    outs[3][...] = jnp.where(even, left, right)


def join_kernel(here_ref, theirs_ref, straight_ref, cross_ref, both_ref):
    slab = here_ref.shape[0]
    even = lax.rem(lax.axis_index("space"), 2) == 0
    here = here_ref[...] + straight_ref[...]
    there = theirs_ref[...] + cross_ref[...]
    both_ref[:slab, :] = jnp.where(even, here, there)
    both_ref[slab:, :] = jnp.where(even, there, here)


def close_kernel(*refs):
    *sums_refs, energies_ref, places_ref = refs
    slab = energies_ref.shape[1]
    for n, ref in enumerate(sums_refs):

        @pl.when(lax.axis_index("segment") == n)
        def _(ref=ref):
            sums = ref[...]
            rows, c = sums.shape
            turned = jnp.transpose(jnp.concatenate([sums, jnp.zeros((c - rows, c), F32)], axis=0))
            for b in range(2):
                energies_ref[b : b + 1, :] = turned[3:4, b * slab : (b + 1) * slab]
                for n in range(3):
                    places_ref[n, b : b + 1, :] = turned[n : n + 1, b * slab : (b + 1) * slab]


def pack_kernel(
    node_hbm, places_hbm, species_hbm, sources_hbm, grad_hbm, table_hbm, mine_ref, other_ref,
    states, places, species, sources, grads, table, sems
):
    @pl.when(lax.axis_index("segment") == 0)
    def _():
        pack(
            (node_hbm, places_hbm, species_hbm, sources_hbm, grad_hbm, table_hbm), mine_ref, other_ref,
            states, places, species, sources, grads, table, sems,
        )


def pack(given, mine_ref, other_ref, states, places, species, sources, grads, table, sems):
    batch = lax.rem(lax.axis_index("space"), 2)
    copies = []
    for n, (source, target) in enumerate(zip(given, (states, places, species, sources, grads, table))):
        copies.append(pltpu.make_async_copy(source, target, sems.at[n]))
        copies[-1].start()
    for copy in copies:
        copy.wait()
    coefs, per_slab, c = states.shape[1:]
    lane = lax.broadcasted_iota(jnp.int32, (per_slab, c), 1)
    eye = (
        lax.broadcasted_iota(jnp.int32, (per_slab, per_slab), 0)
        == lax.broadcasted_iota(jnp.int32, (per_slab, per_slab), 1)
    )

    def column(row):
        return jnp.sum(jnp.where(eye, jnp.broadcast_to(row, (per_slab, per_slab)), 0.0), axis=1, keepdims=True)

    both = []
    for b in range(2):
        names = column(species[b : b + 1, :].astype(F32)).astype(jnp.int32)
        kinds = table.shape[0]
        hot = (names == lax.broadcasted_iota(jnp.int32, (per_slab, kinds), 1)).astype(BF16)
        first = (states[b, 0].astype(F32) + dot(hot, table[...])).astype(BF16)
        extra = jnp.zeros((per_slab, c), F32)
        for n in range(3):
            extra = jnp.where(lane == n, column(places[n, b : b + 1, :]), extra)
        extra = encode(jnp.where(lane == 3, column(grads[b : b + 1, :]), extra))
        for j in range(sources.shape[2]):
            index = sources[b, :, j : j + 1]
            extra = jnp.where(lane == SOURCES + j, (index // BASE).astype(F32), extra)
            extra = jnp.where(lane == SOURCES + 8 + j, (index % BASE).astype(F32), extra)
        both.append((first, extra.astype(BF16)))
    for ref, chosen in ((mine_ref, batch), (other_ref, 1 - batch)):
        ref[pl.ds(0, coefs)] = states[chosen]
        ref[0] = jnp.where(chosen == 0, both[0][0].astype(F32), both[1][0].astype(F32)).astype(BF16)
        ref[coefs] = jnp.where(chosen == 0, both[0][1].astype(F32), both[1][1].astype(F32)).astype(BF16)


def open_kernel(mine_ref, partner_ref, straight_ref, cross_ref, low_ref, high_ref):
    @pl.when(lax.axis_index("segment") == 0)
    def _():
        even = lax.rem(lax.axis_index("space"), 2) == 0

        def choose(a, b):
            return jnp.where(even, a, b)

        for k in range(low_ref.shape[0]):
            mine, partner = mine_ref[k].astype(F32), partner_ref[k].astype(F32)
            straight, cross = straight_ref[k].astype(F32), cross_ref[k].astype(F32)
            low_ref[k] = jnp.concatenate([choose(cross, straight), choose(mine, partner)], axis=0).astype(BF16)
            high_ref[k] = jnp.concatenate([choose(partner, mine), choose(straight, cross)], axis=0).astype(BF16)


def edges_of(refs, coefs, slabs, neighbours, rate_ref, hot_ref, hot_t_ref, geo_ref):
    start, _ = first_slab(slabs)
    extra = jnp.concatenate([ref[coefs].astype(F32) for ref in refs], axis=0)
    window, c = extra.shape
    rows = window // 2
    per_slab = rows // 2
    edges = rows * neighbours
    numbers = decode(extra)
    own_extra = extra[per_slab : per_slab + rows]
    low = pltpu.roll(own_extra, c - 8, 1)
    index = own_extra.astype(jnp.int32) * BASE + low.astype(jnp.int32)
    place = lax.rem(index // per_slab - start + slabs, slabs) * per_slab + index % per_slab
    columns = lax.broadcasted_iota(jnp.int32, (rows, c), 1)
    hot = jnp.concatenate(
        [
            (place[:, SOURCES + j : SOURCES + j + 1] == columns).astype(F32)
            for j in range(neighbours)
        ],
        axis=0,
    )
    hot_t_ref[...] = jnp.transpose(hot).astype(BF16)[:window]
    hot = hot.astype(BF16)[:, :window]
    hot_ref[...] = hot
    lift = lax.broadcasted_iota(jnp.int32, (window, c), 0) // per_slab - 1
    offset = []
    for n in range(3):
        column = jnp.broadcast_to(numbers[:, n : n + 1], (window, c))
        if n == 2:
            column = column + SLAB_DEPTH * lift.astype(F32)
        there = sum(dot(hot, part) for part in split3(column))
        offset.append(there - jnp.concatenate([column[per_slab : per_slab + rows]] * neighbours, axis=0))
    flat = offset[0] * offset[0] + offset[1] * offset[1] + 1.0
    length = jnp.sqrt(flat + offset[2] * offset[2])
    planar = jnp.sqrt(flat)
    c1, s1 = offset[0] / planar, offset[1] / planar
    rate = jnp.broadcast_to(rate_ref[...], (edges, c))
    values = [
        jnp.exp(-rate * length),
        c1,
        s1,
        c1 * c1 - s1 * s1,
        2.0 * c1 * s1,
        offset[0] / length,
        offset[1] / length,
        offset[2] / length,
        1.0 / planar,
        rate,
    ]
    for n, value in enumerate(values):
        geo_ref[n * edges : (n + 1) * edges, :] = value
    return numbers[per_slab : per_slab + rows]


def stage_kernel(zero_hbm, one_hbm, two_hbm, zero_ref, one_ref, two_ref, sems):
    pairs = [(zero_hbm, zero_ref)]
    for source, target in ((one_hbm, one_ref), (two_hbm, two_ref)):
        pairs += [(source.at[n], target.at[n]) for n in range(2)]
    copies = [pltpu.make_async_copy(source, target, sems.at[n]) for n, (source, target) in enumerate(pairs)]
    for copy in copies:
        copy.start()
    for copy in copies:
        copy.wait()


def forward_kernel(
    tick, sz, slabs, neighbours, low_ref, high_ref, rate_ref, zero_ref, one_ref, two_ref,
    out_ref, pooled_ref, hot_t_ref, geo_ref, faded_ref, hot_ref
):
    @pl.when(lax.axis_index("segment") == tick)
    def _():
        rows = low_ref.shape[1]
        refs = (low_ref, high_ref)
        edges_of(refs, sz.coefs, slabs, neighbours, rate_ref, hot_ref, hot_t_ref, geo_ref)
        pooled = forward(refs, hot_ref, geo_ref, faded_ref, zero_ref, one_ref, two_ref, sz, rows, False)
        signal = signal_of(pooled, sz)
        gate, lifted = silu_parts(signal)
        for k in range(sz.coefs):
            pooled_ref[k] = pooled[k]
            added = lifted if k == 0 else gate * pooled[k]
            out_ref[k] = (own_rows(refs, k) + added).astype(BF16)
        out_ref[sz.coefs] = own_rows(refs, sz.coefs).astype(BF16)


def turn_kernel(
    tick, sz, slabs, neighbours, low_ref, high_ref, rate_ref, zero_ref, one_ref, two_ref, read_ref,
    back_low_ref, back_high_ref, hot_ref, hot_t_ref, geo_ref, faded_ref
):
    @pl.when(lax.axis_index("segment") == tick)
    def _():
        rows = low_ref.shape[1]
        refs = (low_ref, high_ref)
        outs = (back_low_ref, back_high_ref)
        own = edges_of(refs, sz.coefs, slabs, neighbours, rate_ref, hot_ref, hot_t_ref, geo_ref)
        pooled = forward(refs, hot_ref, geo_ref, faded_ref, zero_ref, one_ref, two_ref, sz, rows, True)
        signal = signal_of(pooled, sz)
        _, lifted = silu_parts(signal)
        updated = own_rows(refs, 0) + lifted
        gate, active = silu_parts(updated)
        read = read_ref[...]
        energy = jnp.sum(read * active, axis=1, keepdims=True)
        lane = lax.broadcasted_iota(jnp.int32, (rows, sz.c), 1)
        energy = around(jnp.where(lane == 3, energy, 0.0), rows // 2)
        upstream = [own[:, 3:4] * read * (gate + updated * gate * (1.0 - gate))]
        moved = backward(
            upstream, pooled, hot_t_ref, geo_ref, faded_ref, zero_ref, one_ref, two_ref, sz, rows, True, outs
        )
        send_back(moved + energy, outs, sz)


def backward_kernel(
    tick, sz, up_low_ref, up_high_ref, pooled_ref, hot_t_ref, geo_ref, faded_ref, zero_ref, one_ref, two_ref, *outs
):
    @pl.when(lax.axis_index("segment") == tick)
    def _():
        rows = up_low_ref.shape[1]
        upstream = [up_low_ref[k].astype(F32) + up_high_ref[k].astype(F32) for k in range(sz.coefs)]
        pooled = [pooled_ref[k] for k in range(sz.coefs)]
        moved = backward(
            upstream, pooled, hot_t_ref, geo_ref, faded_ref, zero_ref, one_ref, two_ref, sz, rows, False,
            outs if tick else None,
        )
        carried = decode(up_low_ref[sz.coefs].astype(F32)) + decode(up_high_ref[sz.coefs].astype(F32))
        moved = moved + around(carried, rows // 2)
        if tick:
            send_back(moved, outs, sz)
        else:
            share(moved, outs)


def call(body, operands, shapes, name, spaces=None, scratch=()):
    spaces = spaces or [pltpu.VMEM] * len(operands)
    operands = [pltpu.with_memory_space_constraint(value, space) for value, space in zip(operands, spaces)]
    return pl.pallas_call(
        body,
        out_shape=shapes,
        in_specs=[pl.BlockSpec(memory_space=space) for space in spaces],
        out_specs=[pl.BlockSpec(memory_space=pltpu.VMEM) for _ in shapes],
        scratch_shapes=list(scratch),
        compiler_params=pltpu.CompilerParams(vmem_limit_bytes=VMEM_LIMIT),
        name=name,
    )(*operands)


def on_device(
    node_states,
    species,
    species_table,
    places,
    sources,
    radial_rate,
    zero_weight,
    one_weight,
    two_weight,
    read_weight,
    energy_grad,
):
    segments = lax.axis_size("segment")
    slabs = lax.axis_size("space")
    batches, per_slab = species.shape
    coefs, channels = node_states.shape[2:]
    neighbours = sources.shape[2]
    rows = batches * per_slab
    edges = rows * neighbours
    sz = Sizes(zero_weight.shape, one_weight.shape, two_weight.shape, channels)
    axes = ("segment", "space")
    shape = jax.ShapeDtypeStruct

    pairs = slabs // 2

    def within(value, target):
        ways = [(s * slabs + i, s * slabs + target(i) % slabs) for s in range(segments) for i in range(slabs)]
        return lax.ppermute(value, axes, ways)

    def hop(value, start, stop, by, way):
        ways = [(place_of(q, pairs, start), place_of((q + by) % pairs, pairs, stop)) for q in range(pairs)]
        ways = [(start * slabs + 2 * a + c, stop * slabs + 2 * b + c) for a, b in ways for c in range(2)]
        idle = [s for s in range(segments) if s not in (start, stop)]
        if idle:
            third = idle[way % len(idle)]
            ways += [(stop * slabs + i, third * slabs + i) for i in range(slabs)]
            ways += [(third * slabs + i, start * slabs + i) for i in range(slabs)]
        else:
            ways += [(b, a) for a, b in ways]
        moving = {a for a, _ in ways}
        ways += [(i, i + 1 - 2 * (i % 2)) for i in range(segments * slabs) if i not in moving]
        return lax.ppermute(value, axes, ways)

    raw = [
        node_states.transpose(0, 2, 1, 3), places.transpose(1, 0, 2), species, sources, energy_grad, species_table,
    ]
    packed = shape((coefs + 1, per_slab, channels), BF16)
    mine, other = call(
        pack_kernel, raw, [packed, packed], "pack", [pltpu.HBM] * len(raw),
        [pltpu.VMEM(v.shape, v.dtype) for v in raw] + [pltpu.SemaphoreType.DMA((len(raw),))],
    )
    partner = within(other, lambda i: i + 1 - 2 * (i % 2))
    straight = within(mine, lambda i: i + 2 if i % 2 else i - 2)
    cross = within(other, lambda i: i + 1 if i % 2 else i - 1)
    stored = [zero_weight[0], one_weight[0], two_weight[0]]
    spaces = [pltpu.HBM] * 3
    on_chip = [pltpu.VMEM(w.shape, w.dtype) for w in stored]
    sems = [pltpu.SemaphoreType.DMA((5,))]
    weights = call(stage_kernel, stored, on_chip, "stage", spaces, sems)
    whole = shape((coefs + 1, rows, channels), BF16)
    around_all = [call(open_kernel, [mine, partner, straight, cross], [whole, whole], "open")]
    kept_shapes = [
        shape((2 * rows, edges), BF16), shape((10 * edges, channels), F32), shape((coefs, edges, channels), F32),
    ]
    hot = [pltpu.VMEM((edges, 2 * rows), BF16)]
    kept = []
    for tick in range(segments - 1):
        out, *residuals = call(
            functools.partial(forward_kernel, tick, sz, slabs, neighbours),
            [*around_all[tick], radial_rate, *weights],
            [whole, shape((coefs, rows, channels), F32), *kept_shapes],
            "forward",
            scratch=hot,
        )
        kept.append(residuals)
        ways = (1, 0) if tick % 2 else (0, -1)
        around_all.append([hop(out, tick, tick + 1, by, way) for way, by in enumerate(ways)])
    final = segments - 1
    slab_sums = shape((per_slab, channels), F32)
    parts = call(
        functools.partial(turn_kernel, final, sz, slabs, neighbours),
        [*around_all[final], radial_rate, *weights, read_weight.reshape(1, channels)],
        [whole, whole],
        "turn",
        scratch=hot + [pltpu.VMEM(v.shape, v.dtype) for v in kept_shapes],
    )
    for tick in reversed(range(segments - 1)):
        ways = (1, 0) if tick % 2 else (0, -1)
        up = [hop(part, tick + 1, tick, -by, way) for way, (part, by) in enumerate(zip(parts, ways))]
        pooled, *residuals = kept[tick]
        parts = call(
            functools.partial(backward_kernel, tick, sz),
            [*up, pooled, *residuals, *weights],
            [whole, whole] if tick else [slab_sums] * 4,
            "backward",
        )
    here, theirs, straight, cross = parts
    theirs = within(theirs, lambda i: i + 1 - 2 * (i % 2))
    straight = within(straight, lambda i: i - 2 if i % 2 else i + 2)
    cross = within(cross, lambda i: i + 1 if i % 2 else i - 1)
    (both,) = call(join_kernel, [here, theirs, straight, cross], [shape((rows, channels), F32)], "join")
    copies = [both] + [
        lax.ppermute(both, "segment", [(s, (s + stop) % segments) for s in range(segments)])
        for stop in range(1, segments)
    ]
    energies, gradients = call(
        close_kernel, copies, [shape((batches, per_slab), F32), shape((3, batches, per_slab), F32)], "close"
    )
    return energies, gradients.transpose(1, 0, 2)


def solution(mesh):
    in_specs = (
        P(None, "space", None, None),
        P(None, "space"),
        P(),
        P(None, None, "space"),
        P(None, "space", None),
        P("segment", None),
        P("segment", None, None),
        P("segment", None, None, None),
        P("segment", None, None, None),
        P(),
        P(None, "space"),
    )
    out_specs = (P(None, "space"), P(None, None, "space"))
    return jax.shard_map(
        on_device, mesh=mesh, in_specs=in_specs, out_specs=out_specs, check_vma=False
    )
```

```python
import functools

import jax
import jax.numpy as jnp
from jax import lax
from jax.experimental import pallas as pl
from jax.experimental.pallas import tpu as pltpu
from jax.sharding import PartitionSpec as P

SLAB_DEPTH = 2.0
F32 = jnp.float32
BF16 = jnp.bfloat16
VMEM_LIMIT = 16 * 1024 * 1024

MID, LOW, SOURCES = 32, 64, 96
BASE = 256


def split(value):
    high = value.astype(BF16)
    low = (value - high.astype(F32)).astype(BF16)
    return high, low


def split3(value):
    high = value.astype(BF16)
    rest = value - high.astype(F32)
    mid = rest.astype(BF16)
    return high, mid, (rest - mid.astype(F32)).astype(BF16)


def encode(value):
    high, mid, low = split3(value)
    return high.astype(F32) + pltpu.roll(mid.astype(F32), MID, 1) + pltpu.roll(low.astype(F32), LOW, 1)


def decode(value):
    lanes = value.shape[1]
    whole = value + pltpu.roll(value, lanes - MID, 1) + pltpu.roll(value, lanes - LOW, 1)
    lane = lax.broadcasted_iota(jnp.int32, value.shape, 1)
    return jnp.where(lane < 4, whole, 0.0)


def dot(a, b):
    return lax.dot_general(a, b, (((1,), (0,)), ((), ())), preferred_element_type=F32)


def dot_t(a, b):
    return lax.dot_general(a, b, (((1,), (1,)), ((), ())), preferred_element_type=F32)


def fine_dot(value, weights, product):
    rows = value.shape[0]
    stacked = jnp.concatenate(split(value), axis=0)
    outs = []
    for weight in weights:
        out = product(stacked, weight)
        outs.append(out[:rows] + out[rows:])
    return outs


def silu_parts(value):
    gate = 1.0 / (1.0 + jnp.exp(-value))
    return gate, value * gate


class Sizes:
    def __init__(self, zero_shape, one_shape, two_shape, channels):
        self.c = channels
        self.zero = zero_shape[-1] // channels
        self.one = one_shape[-1] // channels
        self.two = two_shape[-1] // channels
        self.coefs = self.zero + 2 * (self.one + self.two)
        self.starts = (self.zero, self.zero + 2 * self.one)
        self.counts = (self.one, self.two)

    def cols(self, first, count=1):
        return slice(first * self.c, (first + count) * self.c)


def picked_group(refs, hot, first, count):
    blocks = [jnp.concatenate([ref[k] for ref in refs], axis=0) for k in range(first, first + count)]
    return dot(hot, jnp.concatenate(blocks, axis=1))


def own_rows(refs, k):
    low, high = (ref[k].astype(F32) for ref in refs)
    slab = low.shape[0] // 2
    return jnp.concatenate([low[slab:], high[:slab]], axis=0)


def pool(value, rows):
    total = value[:rows]
    for start in range(rows, value.shape[0], rows):
        total = total + value[start : start + rows]
    return total


def geo_at(geo_ref, which, edges):
    return geo_ref[which * edges : (which + 1) * edges, :]


def forward(refs, hot_ref, geo_ref, faded_ref, zero_ref, one_ref, two_ref, sz, rows, last):
    hot = hot_ref[...]
    edges = hot.shape[0]
    factor = (edges // rows) ** (-0.5)
    radial = geo_at(geo_ref, 0, edges)

    def scaled(block, k):
        faded = block * radial
        faded_ref[k] = faded
        return faded.astype(BF16).astype(F32)

    pooled = [None] * sz.coefs
    group = picked_group(refs, hot, 0, sz.zero)
    zin = jnp.concatenate(
        [pool(scaled(group[:, sz.cols(k)], k), rows) for k in range(sz.zero)], axis=1
    )
    kept = 1 if last else sz.zero
    (zout,) = fine_dot(zin, [zero_ref[:, sz.cols(0, kept)]], dot)
    for k in range(kept):
        pooled[k] = zout[:, sz.cols(k)] * factor
    for order in range(2):
        first, count = sz.starts[order], sz.counts[order]
        weight_ref = (one_ref, two_ref)[order]
        cos = geo_at(geo_ref, 1 + 2 * order, edges)
        sin = geo_at(geo_ref, 2 + 2 * order, edges)
        group = picked_group(refs, hot, first, 2 * count)
        res, ims = [], []
        for k in range(count):
            re = scaled(group[:, sz.cols(k)], first + k)
            im = scaled(group[:, sz.cols(count + k)], first + count + k)
            res.append(pool(cos * re - sin * im, rows))
            ims.append(pool(sin * re + cos * im, rows))
        both = jnp.concatenate(
            [jnp.concatenate(res, axis=1), jnp.concatenate(ims, axis=1)], axis=0
        )
        a, b = fine_dot(both, [weight_ref[0], weight_ref[1]], dot)
        out_re = (a[:rows] - b[rows:]) * factor
        out_im = (b[:rows] + a[rows:]) * factor
        for k in range(count):
            pooled[first + k] = out_re[:, sz.cols(k)]
            pooled[first + count + k] = out_im[:, sz.cols(k)]
    return pooled


def signal_of(pooled, sz):
    total = pooled[0]
    for k in range(sz.zero, sz.coefs):
        total = total + pooled[k] * pooled[k]
    return total


def backward(
    upstream, pooled, hot_t_ref, geo_ref, faded_ref, zero_ref, one_ref, two_ref, sz, rows, last, outs
):
    hot_t = hot_t_ref[...]
    edges = hot_t.shape[1]
    slab = rows // 2
    factor = (edges // rows) ** (-0.5)
    signal = signal_of(pooled, sz)
    gate, _ = silu_parts(signal)
    slope = gate * (1.0 - gate)
    d_signal = upstream[0] * (gate + signal * slope)
    if not last:
        inner = upstream[1] * pooled[1]
        for k in range(2, sz.coefs):
            inner = inner + upstream[k] * pooled[k]
        d_signal = d_signal + inner * slope
    d_pooled = [d_signal * factor]
    for k in range(1, sz.coefs):
        if last:
            d_pooled.append(2.0 * factor * d_signal * pooled[k] if k >= sz.zero else None)
        else:
            term = gate * upstream[k]
            if k >= sz.zero:
                term = term + 2.0 * d_signal * pooled[k]
            d_pooled.append(term * factor)

    radial = geo_at(geo_ref, 0, edges)
    kept = 1 if last else sz.zero
    (dz,) = fine_dot(jnp.concatenate(d_pooled[:kept], axis=1), [zero_ref[:, sz.cols(0, kept)]], dot_t)

    def spread(block):
        return jnp.concatenate([block] * (edges // rows), axis=0)

    def scatter(first, blocks):
        if outs is None:
            return
        back = dot(hot_t, jnp.concatenate([block.astype(BF16) for block in blocks], axis=1))
        for n in range(len(blocks)):
            k = first + n
            part = back[:, sz.cols(n)]
            if not last or k == 0:
                part = part + around(upstream[k], slab)
            outs[0][k] = part[:rows].astype(BF16)
            outs[1][k] = part[rows:].astype(BF16)

    q_len = jnp.zeros((edges, sz.c), F32)
    blocks = []
    for k in range(sz.zero):
        grad = spread(dz[:, sz.cols(k)])
        q_len = q_len + grad * faded_ref[k]
        if outs is not None:
            blocks.append(grad * radial)
    scatter(0, blocks)
    q_turn = []
    for order in range(2):
        first, count = sz.starts[order], sz.counts[order]
        weight_ref = (one_ref, two_ref)[order]
        cos = geo_at(geo_ref, 1 + 2 * order, edges)
        sin = geo_at(geo_ref, 2 + 2 * order, edges)
        both = jnp.concatenate(
            [
                jnp.concatenate(d_pooled[first : first + count], axis=1),
                jnp.concatenate(d_pooled[first + count : first + 2 * count], axis=1),
            ],
            axis=0,
        )
        a, b = fine_dot(both, [weight_ref[0], weight_ref[1]], dot_t)
        d_re = a[:rows] + b[rows:]
        d_im = a[rows:] - b[:rows]
        q_cos = jnp.zeros((edges, sz.c), F32)
        q_sin = jnp.zeros((edges, sz.c), F32)
        cos_r = cos * radial
        sin_r = sin * radial
        blocks_re, blocks_im = [], []
        for k in range(count):
            re = faded_ref[first + k]
            im = faded_ref[first + count + k]
            g_re = spread(d_re[:, sz.cols(k)])
            g_im = spread(d_im[:, sz.cols(k)])
            q_cos = q_cos + (re * g_re + im * g_im)
            q_sin = q_sin + (re * g_im - im * g_re)
            if outs is not None:
                blocks_re.append(cos_r * g_re + sin_r * g_im)
                blocks_im.append(cos_r * g_im - sin_r * g_re)
        scatter(first, blocks_re + blocks_im)
        q_len = q_len + cos * q_cos + sin * q_sin
        q_turn.append((q_cos, q_sin))

    rate = geo_at(geo_ref, 9, edges)

    def total(value):
        return jnp.sum(value, axis=1, keepdims=True)

    d_len = -total(q_len * rate)
    (dc1, ds1), (dc2, ds2) = [(total(a), total(b)) for a, b in q_turn]
    c1, s1 = geo_at(geo_ref, 1, edges), geo_at(geo_ref, 2, edges)
    ux, uy, uz = (geo_at(geo_ref, 5 + n, edges) for n in range(3))
    inv_planar = geo_at(geo_ref, 8, edges)
    dc1 = dc1 + 2.0 * (c1 * dc2 + s1 * ds2)
    ds1 = ds1 + 2.0 * (c1 * ds2 - s1 * dc2)
    along = c1 * dc1 + s1 * ds1
    dx = (dc1 - along * c1) * inv_planar + d_len * ux
    dy = (ds1 - along * s1) * inv_planar + d_len * uy
    dz_ = d_len * uz
    lane = lax.broadcasted_iota(jnp.int32, (edges, sz.c), 1)
    change = jnp.where(lane == 0, dx, jnp.where(lane == 1, dy, jnp.where(lane == 2, dz_, 0.0)))
    moved = sum(dot(hot_t, part) for part in split3(change))
    return moved - around(pool(change, rows), slab)


def around(own, slab):
    edge = jnp.zeros((slab, own.shape[1]), F32)
    return jnp.concatenate([edge, own, edge], axis=0)


def place_of(pair, pairs, segment):
    if segment == 0:
        return pair
    return 2 * pair if pair < pairs // 2 else 2 * (pairs - 1 - pair) + 1


def first_slab(slabs):
    slab_now = lax.axis_index("space")
    segment = lax.axis_index("segment")
    chip = slab_now // 2
    folded = jnp.where(lax.rem(chip, 2) == 0, chip // 2, slabs // 2 - 1 - chip // 2)
    pair = jnp.where(segment == 0, chip, folded)
    return lax.rem(2 * pair + lax.rem(segment, 2) - 1 + slabs, slabs), lax.rem(slab_now, 2)


def send_back(moved, outs, sz):
    rows = moved.shape[0] // 2
    coded = encode(moved).astype(BF16)
    outs[0][sz.coefs] = coded[:rows]
    outs[1][sz.coefs] = coded[rows:]


def share(moved, outs):
    slab = moved.shape[0] // 4
    left, low, high, right = (moved[n * slab : (n + 1) * slab] for n in range(4))
    even = lax.rem(lax.axis_index("space"), 2) == 0
    outs[0][...] = jnp.where(even, low, high)
    outs[1][...] = jnp.where(even, high, low)
    outs[2][...] = jnp.where(even, right, left)
    outs[3][...] = jnp.where(even, left, right)


def join_kernel(here_ref, theirs_ref, straight_ref, cross_ref, both_ref):
    slab = here_ref.shape[0]
    even = lax.rem(lax.axis_index("space"), 2) == 0
    here = here_ref[...] + straight_ref[...]
    there = theirs_ref[...] + cross_ref[...]
    both_ref[:slab, :] = jnp.where(even, here, there)
    both_ref[slab:, :] = jnp.where(even, there, here)


def close_kernel(*refs):
    *sums_refs, energies_ref, places_ref = refs
    slab = energies_ref.shape[1]
    for n, ref in enumerate(sums_refs):

        @pl.when(lax.axis_index("segment") == n)
        def _(ref=ref):
            sums = ref[...]
            rows, c = sums.shape
            turned = jnp.transpose(jnp.concatenate([sums, jnp.zeros((c - rows, c), F32)], axis=0))
            for b in range(2):
                energies_ref[b : b + 1, :] = turned[3:4, b * slab : (b + 1) * slab]
                for n in range(3):
                    places_ref[n, b : b + 1, :] = turned[n : n + 1, b * slab : (b + 1) * slab]


def pack_kernel(
    node_hbm, places_hbm, species_hbm, sources_hbm, grad_hbm, table_hbm, mine_ref, other_ref,
    states, places, species, sources, grads, table, sems
):
    @pl.when(lax.axis_index("segment") == 0)
    def _():
        pack(
            (node_hbm, places_hbm, species_hbm, sources_hbm, grad_hbm, table_hbm), mine_ref, other_ref,
            states, places, species, sources, grads, table, sems,
        )


def pack(given, mine_ref, other_ref, states, places, species, sources, grads, table, sems):
    batch = lax.rem(lax.axis_index("space"), 2)
    copies = []
    for n, (source, target) in enumerate(zip(given, (states, places, species, sources, grads, table))):
        copies.append(pltpu.make_async_copy(source, target, sems.at[n]))
        copies[-1].start()
    for copy in copies:
        copy.wait()
    coefs, per_slab, c = states.shape[1:]
    lane = lax.broadcasted_iota(jnp.int32, (per_slab, c), 1)
    eye = (
        lax.broadcasted_iota(jnp.int32, (per_slab, per_slab), 0)
        == lax.broadcasted_iota(jnp.int32, (per_slab, per_slab), 1)
    )

    def column(row):
        return jnp.sum(jnp.where(eye, jnp.broadcast_to(row, (per_slab, per_slab)), 0.0), axis=1, keepdims=True)

    both = []
    for b in range(2):
        names = column(species[b : b + 1, :].astype(F32)).astype(jnp.int32)
        kinds = table.shape[0]
        hot = (names == lax.broadcasted_iota(jnp.int32, (per_slab, kinds), 1)).astype(BF16)
        first = (states[b, 0].astype(F32) + dot(hot, table[...])).astype(BF16)
        extra = jnp.zeros((per_slab, c), F32)
        for n in range(3):
            extra = jnp.where(lane == n, column(places[n, b : b + 1, :]), extra)
        extra = encode(jnp.where(lane == 3, column(grads[b : b + 1, :]), extra))
        for j in range(sources.shape[2]):
            index = sources[b, :, j : j + 1]
            extra = jnp.where(lane == SOURCES + j, (index // BASE).astype(F32), extra)
            extra = jnp.where(lane == SOURCES + 8 + j, (index % BASE).astype(F32), extra)
        both.append((first, extra.astype(BF16)))
    for ref, chosen in ((mine_ref, batch), (other_ref, 1 - batch)):
        ref[pl.ds(0, coefs)] = states[chosen]
        ref[0] = jnp.where(chosen == 0, both[0][0].astype(F32), both[1][0].astype(F32)).astype(BF16)
        ref[coefs] = jnp.where(chosen == 0, both[0][1].astype(F32), both[1][1].astype(F32)).astype(BF16)


def open_kernel(mine_ref, partner_ref, straight_ref, cross_ref, low_ref, high_ref):
    @pl.when(lax.axis_index("segment") == 0)
    def _():
        even = lax.rem(lax.axis_index("space"), 2) == 0

        def choose(a, b):
            return jnp.where(even, a, b)

        for k in range(low_ref.shape[0]):
            mine, partner = mine_ref[k].astype(F32), partner_ref[k].astype(F32)
            straight, cross = straight_ref[k].astype(F32), cross_ref[k].astype(F32)
            low_ref[k] = jnp.concatenate([choose(cross, straight), choose(mine, partner)], axis=0).astype(BF16)
            high_ref[k] = jnp.concatenate([choose(partner, mine), choose(straight, cross)], axis=0).astype(BF16)


def edges_of(refs, coefs, slabs, neighbours, rate_ref, hot_ref, hot_t_ref, geo_ref):
    start, _ = first_slab(slabs)
    extra = jnp.concatenate([ref[coefs].astype(F32) for ref in refs], axis=0)
    window, c = extra.shape
    rows = window // 2
    per_slab = rows // 2
    edges = rows * neighbours
    numbers = decode(extra)
    own_extra = extra[per_slab : per_slab + rows]
    low = pltpu.roll(own_extra, c - 8, 1)
    index = own_extra.astype(jnp.int32) * BASE + low.astype(jnp.int32)
    place = lax.rem(index // per_slab - start + slabs, slabs) * per_slab + index % per_slab
    columns = lax.broadcasted_iota(jnp.int32, (rows, c), 1)
    hot = jnp.concatenate(
        [
            (place[:, SOURCES + j : SOURCES + j + 1] == columns).astype(F32)
            for j in range(neighbours)
        ],
        axis=0,
    )
    hot_t_ref[...] = jnp.transpose(hot).astype(BF16)[:window]
    hot = hot.astype(BF16)[:, :window]
    hot_ref[...] = hot
    lift = lax.broadcasted_iota(jnp.int32, (window, c), 0) // per_slab - 1
    offset = []
    for n in range(3):
        column = jnp.broadcast_to(numbers[:, n : n + 1], (window, c))
        if n == 2:
            column = column + SLAB_DEPTH * lift.astype(F32)
        there = sum(dot(hot, part) for part in split3(column))
        offset.append(there - jnp.concatenate([column[per_slab : per_slab + rows]] * neighbours, axis=0))
    flat = offset[0] * offset[0] + offset[1] * offset[1] + 1.0
    length = jnp.sqrt(flat + offset[2] * offset[2])
    planar = jnp.sqrt(flat)
    c1, s1 = offset[0] / planar, offset[1] / planar
    rate = jnp.broadcast_to(rate_ref[...], (edges, c))
    values = [
        jnp.exp(-rate * length),
        c1,
        s1,
        c1 * c1 - s1 * s1,
        2.0 * c1 * s1,
        offset[0] / length,
        offset[1] / length,
        offset[2] / length,
        1.0 / planar,
        rate,
    ]
    for n, value in enumerate(values):
        geo_ref[n * edges : (n + 1) * edges, :] = value
    return numbers[per_slab : per_slab + rows]


def stage_kernel(zero_hbm, one_hbm, two_hbm, zero_ref, one_ref, two_ref, sems):
    pairs = [(zero_hbm, zero_ref)]
    for source, target in ((one_hbm, one_ref), (two_hbm, two_ref)):
        pairs += [(source.at[n], target.at[n]) for n in range(2)]
    copies = [pltpu.make_async_copy(source, target, sems.at[n]) for n, (source, target) in enumerate(pairs)]
    for copy in copies:
        copy.start()
    for copy in copies:
        copy.wait()


def forward_kernel(
    tick, sz, slabs, neighbours, low_ref, high_ref, rate_ref, zero_ref, one_ref, two_ref,
    out_ref, pooled_ref, hot_t_ref, geo_ref, faded_ref, hot_ref
):
    @pl.when(lax.axis_index("segment") == tick)
    def _():
        rows = low_ref.shape[1]
        refs = (low_ref, high_ref)
        edges_of(refs, sz.coefs, slabs, neighbours, rate_ref, hot_ref, hot_t_ref, geo_ref)
        pooled = forward(refs, hot_ref, geo_ref, faded_ref, zero_ref, one_ref, two_ref, sz, rows, False)
        signal = signal_of(pooled, sz)
        gate, lifted = silu_parts(signal)
        for k in range(sz.coefs):
            pooled_ref[k] = pooled[k]
            added = lifted if k == 0 else gate * pooled[k]
            out_ref[k] = (own_rows(refs, k) + added).astype(BF16)
        out_ref[sz.coefs] = own_rows(refs, sz.coefs).astype(BF16)


def turn_kernel(
    tick, sz, slabs, neighbours, low_ref, high_ref, rate_ref, zero_ref, one_ref, two_ref, read_ref,
    back_low_ref, back_high_ref, hot_ref, hot_t_ref, geo_ref, faded_ref
):
    @pl.when(lax.axis_index("segment") == tick)
    def _():
        rows = low_ref.shape[1]
        refs = (low_ref, high_ref)
        outs = (back_low_ref, back_high_ref)
        own = edges_of(refs, sz.coefs, slabs, neighbours, rate_ref, hot_ref, hot_t_ref, geo_ref)
        pooled = forward(refs, hot_ref, geo_ref, faded_ref, zero_ref, one_ref, two_ref, sz, rows, True)
        signal = signal_of(pooled, sz)
        _, lifted = silu_parts(signal)
        updated = own_rows(refs, 0) + lifted
        gate, active = silu_parts(updated)
        read = read_ref[...]
        energy = jnp.sum(read * active, axis=1, keepdims=True)
        lane = lax.broadcasted_iota(jnp.int32, (rows, sz.c), 1)
        energy = around(jnp.where(lane == 3, energy, 0.0), rows // 2)
        upstream = [own[:, 3:4] * read * (gate + updated * gate * (1.0 - gate))]
        moved = backward(
            upstream, pooled, hot_t_ref, geo_ref, faded_ref, zero_ref, one_ref, two_ref, sz, rows, True, outs
        )
        send_back(moved + energy, outs, sz)


def backward_kernel(
    tick, sz, up_low_ref, up_high_ref, pooled_ref, hot_t_ref, geo_ref, faded_ref, zero_ref, one_ref, two_ref, *outs
):
    @pl.when(lax.axis_index("segment") == tick)
    def _():
        rows = up_low_ref.shape[1]
        upstream = [up_low_ref[k].astype(F32) + up_high_ref[k].astype(F32) for k in range(sz.coefs)]
        pooled = [pooled_ref[k] for k in range(sz.coefs)]
        moved = backward(
            upstream, pooled, hot_t_ref, geo_ref, faded_ref, zero_ref, one_ref, two_ref, sz, rows, False,
            outs if tick else None,
        )
        carried = decode(up_low_ref[sz.coefs].astype(F32)) + decode(up_high_ref[sz.coefs].astype(F32))
        moved = moved + around(carried, rows // 2)
        if tick:
            send_back(moved, outs, sz)
        else:
            share(moved, outs)


def call(body, operands, shapes, name, spaces=None, scratch=()):
    spaces = spaces or [pltpu.VMEM] * len(operands)
    operands = [pltpu.with_memory_space_constraint(value, space) for value, space in zip(operands, spaces)]
    return pl.pallas_call(
        body,
        out_shape=shapes,
        in_specs=[pl.BlockSpec(memory_space=space) for space in spaces],
        out_specs=[pl.BlockSpec(memory_space=pltpu.VMEM) for _ in shapes],
        scratch_shapes=list(scratch),
        compiler_params=pltpu.CompilerParams(vmem_limit_bytes=VMEM_LIMIT),
        name=name,
    )(*operands)


def on_device(
    node_states,
    species,
    species_table,
    places,
    sources,
    radial_rate,
    zero_weight,
    one_weight,
    two_weight,
    read_weight,
    energy_grad,
):
    segments = lax.axis_size("segment")
    slabs = lax.axis_size("space")
    batches, per_slab = species.shape
    coefs, channels = node_states.shape[2:]
    neighbours = sources.shape[2]
    rows = batches * per_slab
    edges = rows * neighbours
    sz = Sizes(zero_weight.shape, one_weight.shape, two_weight.shape, channels)
    axes = ("segment", "space")
    shape = jax.ShapeDtypeStruct

    pairs = slabs // 2

    def within(value, target):
        ways = [(s * slabs + i, s * slabs + target(i) % slabs) for s in range(segments) for i in range(slabs)]
        return lax.ppermute(value, axes, ways)

    def hop(value, start, stop, by, way):
        ways = [(place_of(q, pairs, start), place_of((q + by) % pairs, pairs, stop)) for q in range(pairs)]
        ways = [(start * slabs + 2 * a + c, stop * slabs + 2 * b + c) for a, b in ways for c in range(2)]
        idle = [s for s in range(segments) if s not in (start, stop)]
        if idle:
            third = idle[way % len(idle)]
            ways += [(stop * slabs + i, third * slabs + i) for i in range(slabs)]
            ways += [(third * slabs + i, start * slabs + i) for i in range(slabs)]
        else:
            ways += [(b, a) for a, b in ways]
        moving = {a for a, _ in ways}
        ways += [(i, i + 1 - 2 * (i % 2)) for i in range(segments * slabs) if i not in moving]
        return lax.ppermute(value, axes, ways)

    raw = [
        node_states.transpose(0, 2, 1, 3), places.transpose(1, 0, 2), species, sources, energy_grad, species_table,
    ]
    packed = shape((coefs + 1, per_slab, channels), BF16)
    mine, other = call(
        pack_kernel, raw, [packed, packed], "pack", [pltpu.HBM] * len(raw),
        [pltpu.VMEM(v.shape, v.dtype) for v in raw] + [pltpu.SemaphoreType.DMA((len(raw),))],
    )
    partner = within(other, lambda i: i + 1 - 2 * (i % 2))
    straight = within(mine, lambda i: i + 2 if i % 2 else i - 2)
    cross = within(other, lambda i: i + 1 if i % 2 else i - 1)
    stored = [zero_weight[0], one_weight[0], two_weight[0]]
    spaces = [pltpu.HBM] * 3
    on_chip = [pltpu.VMEM(w.shape, w.dtype) for w in stored]
    sems = [pltpu.SemaphoreType.DMA((5,))]
    weights = call(stage_kernel, stored, on_chip, "stage", spaces, sems)
    whole = shape((coefs + 1, rows, channels), BF16)
    around_all = [call(open_kernel, [mine, partner, straight, cross], [whole, whole], "open")]
    kept_shapes = [
        shape((2 * rows, edges), BF16), shape((10 * edges, channels), F32), shape((coefs, edges, channels), F32),
    ]
    hot = [pltpu.VMEM((edges, 2 * rows), BF16)]
    kept = []
    for tick in range(segments - 1):
        out, *residuals = call(
            functools.partial(forward_kernel, tick, sz, slabs, neighbours),
            [*around_all[tick], radial_rate, *weights],
            [whole, shape((coefs, rows, channels), F32), *kept_shapes],
            "forward",
            scratch=hot,
        )
        kept.append(residuals)
        ways = (1, 0) if tick % 2 else (0, -1)
        around_all.append([hop(out, tick, tick + 1, by, way) for way, by in enumerate(ways)])
    final = segments - 1
    slab_sums = shape((per_slab, channels), F32)
    parts = call(
        functools.partial(turn_kernel, final, sz, slabs, neighbours),
        [*around_all[final], radial_rate, *weights, read_weight.reshape(1, channels)],
        [whole, whole],
        "turn",
        scratch=hot + [pltpu.VMEM(v.shape, v.dtype) for v in kept_shapes],
    )
    for tick in reversed(range(segments - 1)):
        ways = (1, 0) if tick % 2 else (0, -1)
        up = [hop(part, tick + 1, tick, -by, way) for way, (part, by) in enumerate(zip(parts, ways))]
        pooled, *residuals = kept[tick]
        parts = call(
            functools.partial(backward_kernel, tick, sz),
            [*up, pooled, *residuals, *weights],
            [whole, whole] if tick else [slab_sums] * 4,
            "backward",
        )
    here, theirs, straight, cross = parts
    theirs = within(theirs, lambda i: i + 1 - 2 * (i % 2))
    straight = within(straight, lambda i: i - 2 if i % 2 else i + 2)
    cross = within(cross, lambda i: i + 1 if i % 2 else i - 1)
    (both,) = call(join_kernel, [here, theirs, straight, cross], [shape((rows, channels), F32)], "join")

    def across(section, i, stop):
        if section in (0, stop):
            return stop - section, i
        return section, i + 1 - 2 * (i % 2)

    copies = [both] + [
        lax.ppermute(
            both,
            axes,
            [
                (s * slabs + i, t * slabs + j)
                for s in range(segments)
                for i in range(slabs)
                for t, j in [across(s, i, stop)]
            ],
        )
        for stop in range(1, segments)
    ]
    energies, gradients = call(
        close_kernel, copies, [shape((batches, per_slab), F32), shape((3, batches, per_slab), F32)], "close"
    )
    return energies, gradients.transpose(1, 0, 2)


def solution(mesh):
    in_specs = (
        P(None, "space", None, None),
        P(None, "space"),
        P(),
        P(None, None, "space"),
        P(None, "space", None),
        P("segment", None),
        P("segment", None, None),
        P("segment", None, None, None),
        P("segment", None, None, None),
        P(),
        P(None, "space"),
    )
    out_specs = (P(None, "space"), P(None, None, "space"))
    return jax.shard_map(
        on_device, mesh=mesh, in_specs=in_specs, out_specs=out_specs, check_vma=False
    )
```

```python
import functools

import jax
import jax.numpy as jnp
from jax import lax
from jax.experimental import pallas as pl
from jax.experimental.pallas import tpu as pltpu
from jax.sharding import PartitionSpec as P

SLAB_DEPTH = 2.0
F32 = jnp.float32
BF16 = jnp.bfloat16
VMEM_LIMIT = 16 * 1024 * 1024

MID, LOW, SOURCES = 32, 64, 96
BASE = 256


def split(value):
    high = value.astype(BF16)
    low = (value - high.astype(F32)).astype(BF16)
    return high, low


def split3(value):
    high = value.astype(BF16)
    rest = value - high.astype(F32)
    mid = rest.astype(BF16)
    return high, mid, (rest - mid.astype(F32)).astype(BF16)


def encode(value):
    high, mid, low = split3(value)
    return high.astype(F32) + pltpu.roll(mid.astype(F32), MID, 1) + pltpu.roll(low.astype(F32), LOW, 1)


def decode(value):
    lanes = value.shape[1]
    whole = value + pltpu.roll(value, lanes - MID, 1) + pltpu.roll(value, lanes - LOW, 1)
    lane = lax.broadcasted_iota(jnp.int32, value.shape, 1)
    return jnp.where(lane < 4, whole, 0.0)


def dot(a, b):
    return lax.dot_general(a, b, (((1,), (0,)), ((), ())), preferred_element_type=F32)


def dot_t(a, b):
    return lax.dot_general(a, b, (((1,), (1,)), ((), ())), preferred_element_type=F32)


def fine_dot(value, weights, product):
    rows = value.shape[0]
    stacked = jnp.concatenate(split(value), axis=0)
    outs = []
    for weight in weights:
        out = product(stacked, weight)
        outs.append(out[:rows] + out[rows:])
    return outs


def silu_parts(value):
    gate = 1.0 / (1.0 + jnp.exp(-value))
    return gate, value * gate


class Sizes:
    def __init__(self, zero_shape, one_shape, two_shape, channels):
        self.c = channels
        self.zero = zero_shape[-1] // channels
        self.one = one_shape[-1] // channels
        self.two = two_shape[-1] // channels
        self.coefs = self.zero + 2 * (self.one + self.two)
        self.starts = (self.zero, self.zero + 2 * self.one)
        self.counts = (self.one, self.two)

    def cols(self, first, count=1):
        return slice(first * self.c, (first + count) * self.c)


def picked_group(refs, hot, first, count):
    blocks = [jnp.concatenate([ref[k] for ref in refs], axis=0) for k in range(first, first + count)]
    return dot(hot, jnp.concatenate(blocks, axis=1))


def own_rows(refs, k):
    low, high = (ref[k].astype(F32) for ref in refs)
    slab = low.shape[0] // 2
    return jnp.concatenate([low[slab:], high[:slab]], axis=0)


def pool(value, rows):
    total = value[:rows]
    for start in range(rows, value.shape[0], rows):
        total = total + value[start : start + rows]
    return total


def geo_at(geo_ref, which, edges):
    return geo_ref[which * edges : (which + 1) * edges, :]


def forward(refs, hot_ref, geo_ref, faded_ref, zero_ref, one_ref, two_ref, sz, rows, last):
    hot = hot_ref[...]
    edges = hot.shape[0]
    factor = (edges // rows) ** (-0.5)
    radial = geo_at(geo_ref, 0, edges)

    def scaled(block, k):
        faded = block * radial
        faded_ref[k] = faded
        return faded.astype(BF16).astype(F32)

    pooled = [None] * sz.coefs
    group = picked_group(refs, hot, 0, sz.zero)
    zin = jnp.concatenate(
        [pool(scaled(group[:, sz.cols(k)], k), rows) for k in range(sz.zero)], axis=1
    )
    kept = 1 if last else sz.zero
    (zout,) = fine_dot(zin, [zero_ref[:, sz.cols(0, kept)]], dot)
    for k in range(kept):
        pooled[k] = zout[:, sz.cols(k)] * factor
    for order in range(2):
        first, count = sz.starts[order], sz.counts[order]
        weight_ref = (one_ref, two_ref)[order]
        cos = geo_at(geo_ref, 1 + 2 * order, edges)
        sin = geo_at(geo_ref, 2 + 2 * order, edges)
        group = picked_group(refs, hot, first, 2 * count)
        res, ims = [], []
        for k in range(count):
            re = scaled(group[:, sz.cols(k)], first + k)
            im = scaled(group[:, sz.cols(count + k)], first + count + k)
            res.append(pool(cos * re - sin * im, rows))
            ims.append(pool(sin * re + cos * im, rows))
        both = jnp.concatenate(
            [jnp.concatenate(res, axis=1), jnp.concatenate(ims, axis=1)], axis=0
        )
        a, b = fine_dot(both, [weight_ref[0], weight_ref[1]], dot)
        out_re = (a[:rows] - b[rows:]) * factor
        out_im = (b[:rows] + a[rows:]) * factor
        for k in range(count):
            pooled[first + k] = out_re[:, sz.cols(k)]
            pooled[first + count + k] = out_im[:, sz.cols(k)]
    return pooled


def signal_of(pooled, sz):
    total = pooled[0]
    for k in range(sz.zero, sz.coefs):
        total = total + pooled[k] * pooled[k]
    return total


def backward(
    upstream, pooled, hot_t_ref, geo_ref, faded_ref, zero_ref, one_ref, two_ref, sz, rows, last, outs
):
    hot_t = hot_t_ref[...]
    edges = hot_t.shape[1]
    slab = rows // 2
    factor = (edges // rows) ** (-0.5)
    signal = signal_of(pooled, sz)
    gate, _ = silu_parts(signal)
    slope = gate * (1.0 - gate)
    d_signal = upstream[0] * (gate + signal * slope)
    if not last:
        inner = upstream[1] * pooled[1]
        for k in range(2, sz.coefs):
            inner = inner + upstream[k] * pooled[k]
        d_signal = d_signal + inner * slope
    d_pooled = [d_signal * factor]
    for k in range(1, sz.coefs):
        if last:
            d_pooled.append(2.0 * factor * d_signal * pooled[k] if k >= sz.zero else None)
        else:
            term = gate * upstream[k]
            if k >= sz.zero:
                term = term + 2.0 * d_signal * pooled[k]
            d_pooled.append(term * factor)

    radial = geo_at(geo_ref, 0, edges)
    kept = 1 if last else sz.zero
    (dz,) = fine_dot(jnp.concatenate(d_pooled[:kept], axis=1), [zero_ref[:, sz.cols(0, kept)]], dot_t)

    def spread(block):
        return jnp.concatenate([block] * (edges // rows), axis=0)

    def scatter(first, blocks):
        if outs is None:
            return
        back = dot(hot_t, jnp.concatenate([block.astype(BF16) for block in blocks], axis=1))
        for n in range(len(blocks)):
            k = first + n
            part = back[:, sz.cols(n)]
            if not last or k == 0:
                part = part + around(upstream[k], slab)
            outs[0][k] = part[:rows].astype(BF16)
            outs[1][k] = part[rows:].astype(BF16)

    q_len = jnp.zeros((edges, sz.c), F32)
    blocks = []
    for k in range(sz.zero):
        grad = spread(dz[:, sz.cols(k)])
        q_len = q_len + grad * faded_ref[k]
        if outs is not None:
            blocks.append(grad * radial)
    scatter(0, blocks)
    q_turn = []
    for order in range(2):
        first, count = sz.starts[order], sz.counts[order]
        weight_ref = (one_ref, two_ref)[order]
        cos = geo_at(geo_ref, 1 + 2 * order, edges)
        sin = geo_at(geo_ref, 2 + 2 * order, edges)
        both = jnp.concatenate(
            [
                jnp.concatenate(d_pooled[first : first + count], axis=1),
                jnp.concatenate(d_pooled[first + count : first + 2 * count], axis=1),
            ],
            axis=0,
        )
        a, b = fine_dot(both, [weight_ref[0], weight_ref[1]], dot_t)
        d_re = a[:rows] + b[rows:]
        d_im = a[rows:] - b[:rows]
        q_cos = jnp.zeros((edges, sz.c), F32)
        q_sin = jnp.zeros((edges, sz.c), F32)
        cos_r = cos * radial
        sin_r = sin * radial
        blocks_re, blocks_im = [], []
        for k in range(count):
            re = faded_ref[first + k]
            im = faded_ref[first + count + k]
            g_re = spread(d_re[:, sz.cols(k)])
            g_im = spread(d_im[:, sz.cols(k)])
            q_cos = q_cos + (re * g_re + im * g_im)
            q_sin = q_sin + (re * g_im - im * g_re)
            if outs is not None:
                blocks_re.append(cos_r * g_re + sin_r * g_im)
                blocks_im.append(cos_r * g_im - sin_r * g_re)
        scatter(first, blocks_re + blocks_im)
        q_len = q_len + cos * q_cos + sin * q_sin
        q_turn.append((q_cos, q_sin))

    rate = geo_at(geo_ref, 9, edges)

    def total(value):
        return jnp.sum(value, axis=1, keepdims=True)

    d_len = -total(q_len * rate)
    (dc1, ds1), (dc2, ds2) = [(total(a), total(b)) for a, b in q_turn]
    c1, s1 = geo_at(geo_ref, 1, edges), geo_at(geo_ref, 2, edges)
    ux, uy, uz = (geo_at(geo_ref, 5 + n, edges) for n in range(3))
    inv_planar = geo_at(geo_ref, 8, edges)
    dc1 = dc1 + 2.0 * (c1 * dc2 + s1 * ds2)
    ds1 = ds1 + 2.0 * (c1 * ds2 - s1 * dc2)
    along = c1 * dc1 + s1 * ds1
    dx = (dc1 - along * c1) * inv_planar + d_len * ux
    dy = (ds1 - along * s1) * inv_planar + d_len * uy
    dz_ = d_len * uz
    lane = lax.broadcasted_iota(jnp.int32, (edges, sz.c), 1)
    change = jnp.where(lane == 0, dx, jnp.where(lane == 1, dy, jnp.where(lane == 2, dz_, 0.0)))
    moved = sum(dot(hot_t, part) for part in split3(change))
    return moved - around(pool(change, rows), slab)


def around(own, slab):
    edge = jnp.zeros((slab, own.shape[1]), F32)
    return jnp.concatenate([edge, own, edge], axis=0)


def place_of(pair, pairs, segment):
    if segment == 0:
        return pair
    return 2 * pair if pair < pairs // 2 else 2 * (pairs - 1 - pair) + 1


def first_slab(slabs):
    slab_now = lax.axis_index("space")
    segment = lax.axis_index("segment")
    chip = slab_now // 2
    folded = jnp.where(lax.rem(chip, 2) == 0, chip // 2, slabs // 2 - 1 - chip // 2)
    pair = jnp.where(segment == 0, chip, folded)
    return lax.rem(2 * pair + lax.rem(segment, 2) - 1 + slabs, slabs), lax.rem(slab_now, 2)


def send_back(moved, outs, sz):
    rows = moved.shape[0] // 2
    coded = encode(moved).astype(BF16)
    outs[0][sz.coefs] = coded[:rows]
    outs[1][sz.coefs] = coded[rows:]


def share(moved, outs):
    slab = moved.shape[0] // 4
    left, low, high, right = (moved[n * slab : (n + 1) * slab] for n in range(4))
    even = lax.rem(lax.axis_index("space"), 2) == 0
    outs[0][...] = jnp.where(even, low, high)
    outs[1][...] = jnp.where(even, high, low)
    outs[2][...] = jnp.where(even, right, left)
    outs[3][...] = jnp.where(even, left, right)


def join_kernel(here_ref, theirs_ref, straight_ref, cross_ref, both_ref):
    slab = here_ref.shape[0]
    even = lax.rem(lax.axis_index("space"), 2) == 0
    here = here_ref[...] + straight_ref[...]
    there = theirs_ref[...] + cross_ref[...]
    both_ref[:slab, :] = jnp.where(even, here, there)
    both_ref[slab:, :] = jnp.where(even, there, here)


def close_kernel(*refs):
    *sums_refs, energies_ref, places_ref = refs
    slab = energies_ref.shape[1]
    for n, ref in enumerate(sums_refs):

        @pl.when(lax.axis_index("segment") == n)
        def _(ref=ref):
            sums = ref[...]
            rows, c = sums.shape
            turned = jnp.transpose(jnp.concatenate([sums, jnp.zeros((c - rows, c), F32)], axis=0))
            for b in range(2):
                energies_ref[b : b + 1, :] = turned[3:4, b * slab : (b + 1) * slab]
                for n in range(3):
                    places_ref[n, b : b + 1, :] = turned[n : n + 1, b * slab : (b + 1) * slab]


def pack_kernel(
    node_hbm, places_hbm, species_hbm, sources_hbm, grad_hbm, table_hbm, mine_ref, other_ref,
    states, places, species, sources, grads, table, sems
):
    @pl.when(lax.axis_index("segment") == 0)
    def _():
        pack(
            (node_hbm, places_hbm, species_hbm, sources_hbm, grad_hbm, table_hbm), mine_ref, other_ref,
            states, places, species, sources, grads, table, sems,
        )


def pack(given, mine_ref, other_ref, states, places, species, sources, grads, table, sems):
    batch = lax.rem(lax.axis_index("space"), 2)
    copies = []
    for n, (source, target) in enumerate(zip(given, (states, places, species, sources, grads, table))):
        copies.append(pltpu.make_async_copy(source, target, sems.at[n]))
        copies[-1].start()
    for copy in copies:
        copy.wait()
    coefs, per_slab, c = states.shape[1:]
    lane = lax.broadcasted_iota(jnp.int32, (per_slab, c), 1)
    eye = (
        lax.broadcasted_iota(jnp.int32, (per_slab, per_slab), 0)
        == lax.broadcasted_iota(jnp.int32, (per_slab, per_slab), 1)
    )

    def column(row):
        return jnp.sum(jnp.where(eye, jnp.broadcast_to(row, (per_slab, per_slab)), 0.0), axis=1, keepdims=True)

    both = []
    for b in range(2):
        names = column(species[b : b + 1, :].astype(F32)).astype(jnp.int32)
        kinds = table.shape[0]
        hot = (names == lax.broadcasted_iota(jnp.int32, (per_slab, kinds), 1)).astype(BF16)
        first = (states[b, 0].astype(F32) + dot(hot, table[...])).astype(BF16)
        extra = jnp.zeros((per_slab, c), F32)
        for n in range(3):
            extra = jnp.where(lane == n, column(places[n, b : b + 1, :]), extra)
        extra = encode(jnp.where(lane == 3, column(grads[b : b + 1, :]), extra))
        for j in range(sources.shape[2]):
            index = sources[b, :, j : j + 1]
            extra = jnp.where(lane == SOURCES + j, (index // BASE).astype(F32), extra)
            extra = jnp.where(lane == SOURCES + 8 + j, (index % BASE).astype(F32), extra)
        both.append((first, extra.astype(BF16)))
    for ref, chosen in ((mine_ref, batch), (other_ref, 1 - batch)):
        ref[pl.ds(0, coefs)] = states[chosen]
        ref[0] = jnp.where(chosen == 0, both[0][0].astype(F32), both[1][0].astype(F32)).astype(BF16)
        ref[coefs] = jnp.where(chosen == 0, both[0][1].astype(F32), both[1][1].astype(F32)).astype(BF16)


def open_kernel(mine_ref, partner_ref, straight_ref, cross_ref, low_ref, high_ref):
    @pl.when(lax.axis_index("segment") == 0)
    def _():
        even = lax.rem(lax.axis_index("space"), 2) == 0

        def choose(a, b):
            return jnp.where(even, a, b)

        for k in range(low_ref.shape[0]):
            mine, partner = mine_ref[k].astype(F32), partner_ref[k].astype(F32)
            straight, cross = straight_ref[k].astype(F32), cross_ref[k].astype(F32)
            low_ref[k] = jnp.concatenate([choose(cross, straight), choose(mine, partner)], axis=0).astype(BF16)
            high_ref[k] = jnp.concatenate([choose(partner, mine), choose(straight, cross)], axis=0).astype(BF16)


def edges_of(refs, coefs, slabs, neighbours, rate_ref, hot_ref, hot_t_ref, geo_ref):
    start, _ = first_slab(slabs)
    extra = jnp.concatenate([ref[coefs].astype(F32) for ref in refs], axis=0)
    window, c = extra.shape
    rows = window // 2
    per_slab = rows // 2
    edges = rows * neighbours
    numbers = decode(extra)
    own_extra = extra[per_slab : per_slab + rows]
    low = pltpu.roll(own_extra, c - 8, 1)
    index = own_extra.astype(jnp.int32) * BASE + low.astype(jnp.int32)
    place = lax.rem(index // per_slab - start + slabs, slabs) * per_slab + index % per_slab
    columns = lax.broadcasted_iota(jnp.int32, (rows, c), 1)
    hot = jnp.concatenate(
        [
            (place[:, SOURCES + j : SOURCES + j + 1] == columns).astype(F32)
            for j in range(neighbours)
        ],
        axis=0,
    )
    hot_t_ref[...] = jnp.transpose(hot).astype(BF16)[:window]
    hot = hot.astype(BF16)[:, :window]
    hot_ref[...] = hot
    lift = lax.broadcasted_iota(jnp.int32, (window, c), 0) // per_slab - 1
    offset = []
    for n in range(3):
        column = jnp.broadcast_to(numbers[:, n : n + 1], (window, c))
        if n == 2:
            column = column + SLAB_DEPTH * lift.astype(F32)
        there = sum(dot(hot, part) for part in split3(column))
        offset.append(there - jnp.concatenate([column[per_slab : per_slab + rows]] * neighbours, axis=0))
    flat = offset[0] * offset[0] + offset[1] * offset[1] + 1.0
    length = jnp.sqrt(flat + offset[2] * offset[2])
    planar = jnp.sqrt(flat)
    c1, s1 = offset[0] / planar, offset[1] / planar
    rate = jnp.broadcast_to(rate_ref[...], (edges, c))
    values = [
        jnp.exp(-rate * length),
        c1,
        s1,
        c1 * c1 - s1 * s1,
        2.0 * c1 * s1,
        offset[0] / length,
        offset[1] / length,
        offset[2] / length,
        1.0 / planar,
        rate,
    ]
    for n, value in enumerate(values):
        geo_ref[n * edges : (n + 1) * edges, :] = value
    return numbers[per_slab : per_slab + rows]


def stage_kernel(late, zero_hbm, one_hbm, two_hbm, *more):
    zero_ref, one_ref, two_ref, sems = more[-4:]
    waits = (lax.axis_index("segment") == 0) & (lax.rem(lax.axis_index("space"), 2) == 0)

    @pl.when(waits == late)
    def _():
        pairs = [(zero_hbm, zero_ref)]
        for source, target in ((one_hbm, one_ref), (two_hbm, two_ref)):
            pairs += [(source.at[n], target.at[n]) for n in range(2)]
        copies = [pltpu.make_async_copy(source, target, sems.at[n]) for n, (source, target) in enumerate(pairs)]
        for copy in copies:
            copy.start()
        for copy in copies:
            copy.wait()


def forward_kernel(
    tick, sz, slabs, neighbours, low_ref, high_ref, rate_ref, zero_ref, one_ref, two_ref,
    out_ref, pooled_ref, hot_t_ref, geo_ref, faded_ref, hot_ref
):
    @pl.when(lax.axis_index("segment") == tick)
    def _():
        rows = low_ref.shape[1]
        refs = (low_ref, high_ref)
        edges_of(refs, sz.coefs, slabs, neighbours, rate_ref, hot_ref, hot_t_ref, geo_ref)
        pooled = forward(refs, hot_ref, geo_ref, faded_ref, zero_ref, one_ref, two_ref, sz, rows, False)
        signal = signal_of(pooled, sz)
        gate, lifted = silu_parts(signal)
        for k in range(sz.coefs):
            pooled_ref[k] = pooled[k]
            added = lifted if k == 0 else gate * pooled[k]
            out_ref[k] = (own_rows(refs, k) + added).astype(BF16)
        out_ref[sz.coefs] = own_rows(refs, sz.coefs).astype(BF16)


def turn_kernel(
    tick, sz, slabs, neighbours, low_ref, high_ref, rate_ref, zero_ref, one_ref, two_ref, read_ref,
    back_low_ref, back_high_ref, hot_ref, hot_t_ref, geo_ref, faded_ref
):
    @pl.when(lax.axis_index("segment") == tick)
    def _():
        rows = low_ref.shape[1]
        refs = (low_ref, high_ref)
        outs = (back_low_ref, back_high_ref)
        own = edges_of(refs, sz.coefs, slabs, neighbours, rate_ref, hot_ref, hot_t_ref, geo_ref)
        pooled = forward(refs, hot_ref, geo_ref, faded_ref, zero_ref, one_ref, two_ref, sz, rows, True)
        signal = signal_of(pooled, sz)
        _, lifted = silu_parts(signal)
        updated = own_rows(refs, 0) + lifted
        gate, active = silu_parts(updated)
        read = read_ref[...]
        energy = jnp.sum(read * active, axis=1, keepdims=True)
        lane = lax.broadcasted_iota(jnp.int32, (rows, sz.c), 1)
        energy = around(jnp.where(lane == 3, energy, 0.0), rows // 2)
        upstream = [own[:, 3:4] * read * (gate + updated * gate * (1.0 - gate))]
        moved = backward(
            upstream, pooled, hot_t_ref, geo_ref, faded_ref, zero_ref, one_ref, two_ref, sz, rows, True, outs
        )
        send_back(moved + energy, outs, sz)


def backward_kernel(
    tick, sz, up_low_ref, up_high_ref, pooled_ref, hot_t_ref, geo_ref, faded_ref, zero_ref, one_ref, two_ref, *outs
):
    @pl.when(lax.axis_index("segment") == tick)
    def _():
        rows = up_low_ref.shape[1]
        upstream = [up_low_ref[k].astype(F32) + up_high_ref[k].astype(F32) for k in range(sz.coefs)]
        pooled = [pooled_ref[k] for k in range(sz.coefs)]
        moved = backward(
            upstream, pooled, hot_t_ref, geo_ref, faded_ref, zero_ref, one_ref, two_ref, sz, rows, False,
            outs if tick else None,
        )
        carried = decode(up_low_ref[sz.coefs].astype(F32)) + decode(up_high_ref[sz.coefs].astype(F32))
        moved = moved + around(carried, rows // 2)
        if tick:
            send_back(moved, outs, sz)
        else:
            share(moved, outs)


def call(body, operands, shapes, name, spaces=None, scratch=(), aliases=None):
    spaces = spaces or [pltpu.VMEM] * len(operands)
    operands = [pltpu.with_memory_space_constraint(value, space) for value, space in zip(operands, spaces)]
    return pl.pallas_call(
        body,
        out_shape=shapes,
        in_specs=[pl.BlockSpec(memory_space=space) for space in spaces],
        out_specs=[pl.BlockSpec(memory_space=pltpu.VMEM) for _ in shapes],
        scratch_shapes=list(scratch),
        input_output_aliases=aliases or {},
        compiler_params=pltpu.CompilerParams(vmem_limit_bytes=VMEM_LIMIT),
        name=name,
    )(*operands)


def on_device(
    node_states,
    species,
    species_table,
    places,
    sources,
    radial_rate,
    zero_weight,
    one_weight,
    two_weight,
    read_weight,
    energy_grad,
):
    segments = lax.axis_size("segment")
    slabs = lax.axis_size("space")
    batches, per_slab = species.shape
    coefs, channels = node_states.shape[2:]
    neighbours = sources.shape[2]
    rows = batches * per_slab
    edges = rows * neighbours
    sz = Sizes(zero_weight.shape, one_weight.shape, two_weight.shape, channels)
    axes = ("segment", "space")
    shape = jax.ShapeDtypeStruct

    pairs = slabs // 2

    def within(value, target):
        ways = [(s * slabs + i, s * slabs + target(i) % slabs) for s in range(segments) for i in range(slabs)]
        return lax.ppermute(value, axes, ways)

    def hop(value, start, stop, by, way):
        ways = [(place_of(q, pairs, start), place_of((q + by) % pairs, pairs, stop)) for q in range(pairs)]
        ways = [(start * slabs + 2 * a + c, stop * slabs + 2 * b + c) for a, b in ways for c in range(2)]
        idle = [s for s in range(segments) if s not in (start, stop)]
        if idle:
            third = idle[way % len(idle)]
            ways += [(stop * slabs + i, third * slabs + i) for i in range(slabs)]
            ways += [(third * slabs + i, start * slabs + i) for i in range(slabs)]
        else:
            ways += [(b, a) for a, b in ways]
        moving = {a for a, _ in ways}
        ways += [(i, i + 1 - 2 * (i % 2)) for i in range(segments * slabs) if i not in moving]
        return lax.ppermute(value, axes, ways)

    raw = [
        node_states.transpose(0, 2, 1, 3), places.transpose(1, 0, 2), species, sources, energy_grad, species_table,
    ]
    packed = shape((coefs + 1, per_slab, channels), BF16)
    mine, other = call(
        pack_kernel, raw, [packed, packed], "pack", [pltpu.HBM] * len(raw),
        [pltpu.VMEM(v.shape, v.dtype) for v in raw] + [pltpu.SemaphoreType.DMA((len(raw),))],
    )
    partner = within(other, lambda i: i + 1 - 2 * (i % 2))
    straight = within(mine, lambda i: i + 2 if i % 2 else i - 2)
    cross = within(other, lambda i: i + 1 if i % 2 else i - 1)
    stored = [zero_weight[0], one_weight[0], two_weight[0]]
    spaces = [pltpu.HBM] * 3
    on_chip = [pltpu.VMEM(w.shape, w.dtype) for w in stored]
    sems = [pltpu.SemaphoreType.DMA((5,))]
    weights = call(functools.partial(stage_kernel, False), stored, on_chip, "stage", spaces, sems)
    whole = shape((coefs + 1, rows, channels), BF16)
    around_all = [call(open_kernel, [mine, partner, straight, cross], [whole, whole], "open")]
    weights = call(
        functools.partial(stage_kernel, True), [*stored, *weights, around_all[0][0]], on_chip, "stage",
        spaces + [pltpu.VMEM] * 4, sems, {3: 0, 4: 1, 5: 2},
    )
    kept_shapes = [
        shape((2 * rows, edges), BF16), shape((10 * edges, channels), F32), shape((coefs, edges, channels), F32),
    ]
    hot = [pltpu.VMEM((edges, 2 * rows), BF16)]
    kept = []
    for tick in range(segments - 1):
        out, *residuals = call(
            functools.partial(forward_kernel, tick, sz, slabs, neighbours),
            [*around_all[tick], radial_rate, *weights],
            [whole, shape((coefs, rows, channels), F32), *kept_shapes],
            "forward",
            scratch=hot,
        )
        kept.append(residuals)
        ways = (1, 0) if tick % 2 else (0, -1)
        around_all.append([hop(out, tick, tick + 1, by, way) for way, by in enumerate(ways)])
    final = segments - 1
    slab_sums = shape((per_slab, channels), F32)
    parts = call(
        functools.partial(turn_kernel, final, sz, slabs, neighbours),
        [*around_all[final], radial_rate, *weights, read_weight.reshape(1, channels)],
        [whole, whole],
        "turn",
        scratch=hot + [pltpu.VMEM(v.shape, v.dtype) for v in kept_shapes],
    )
    for tick in reversed(range(segments - 1)):
        ways = (1, 0) if tick % 2 else (0, -1)
        up = [hop(part, tick + 1, tick, -by, way) for way, (part, by) in enumerate(zip(parts, ways))]
        pooled, *residuals = kept[tick]
        parts = call(
            functools.partial(backward_kernel, tick, sz),
            [*up, pooled, *residuals, *weights],
            [whole, whole] if tick else [slab_sums] * 4,
            "backward",
        )
    here, theirs, straight, cross = parts
    theirs = within(theirs, lambda i: i + 1 - 2 * (i % 2))
    straight = within(straight, lambda i: i - 2 if i % 2 else i + 2)
    cross = within(cross, lambda i: i + 1 if i % 2 else i - 1)
    (both,) = call(join_kernel, [here, theirs, straight, cross], [shape((rows, channels), F32)], "join")

    def across(section, i, stop):
        if section in (0, stop):
            return stop - section, i
        return section, i + 1 - 2 * (i % 2)

    copies = [both] + [
        lax.ppermute(
            both,
            axes,
            [
                (s * slabs + i, t * slabs + j)
                for s in range(segments)
                for i in range(slabs)
                for t, j in [across(s, i, stop)]
            ],
        )
        for stop in range(1, segments)
    ]
    energies, gradients = call(
        close_kernel, copies, [shape((batches, per_slab), F32), shape((3, batches, per_slab), F32)], "close"
    )
    return energies, gradients.transpose(1, 0, 2)


def solution(mesh):
    in_specs = (
        P(None, "space", None, None),
        P(None, "space"),
        P(),
        P(None, None, "space"),
        P(None, "space", None),
        P("segment", None),
        P("segment", None, None),
        P("segment", None, None, None),
        P("segment", None, None, None),
        P(),
        P(None, "space"),
    )
    out_specs = (P(None, "space"), P(None, None, "space"))
    return jax.shard_map(
        on_device, mesh=mesh, in_specs=in_specs, out_specs=out_specs, check_vma=False
    )
```

```python
import functools

import jax
import jax.numpy as jnp
from jax import lax
from jax.experimental import pallas as pl
from jax.experimental.pallas import tpu as pltpu
from jax.sharding import PartitionSpec as P

SLAB_DEPTH = 2.0
F32 = jnp.float32
BF16 = jnp.bfloat16
VMEM_LIMIT = 16 * 1024 * 1024

MID, LOW, SOURCES = 32, 64, 96
BASE = 256


def split(value):
    high = value.astype(BF16)
    low = (value - high.astype(F32)).astype(BF16)
    return high, low


def split3(value):
    high = value.astype(BF16)
    rest = value - high.astype(F32)
    mid = rest.astype(BF16)
    return high, mid, (rest - mid.astype(F32)).astype(BF16)


def encode(value):
    high, mid, low = split3(value)
    return high.astype(F32) + pltpu.roll(mid.astype(F32), MID, 1) + pltpu.roll(low.astype(F32), LOW, 1)


def decode(value):
    lanes = value.shape[1]
    whole = value + pltpu.roll(value, lanes - MID, 1) + pltpu.roll(value, lanes - LOW, 1)
    lane = lax.broadcasted_iota(jnp.int32, value.shape, 1)
    return jnp.where(lane < 4, whole, 0.0)


def dot(a, b):
    return lax.dot_general(a, b, (((1,), (0,)), ((), ())), preferred_element_type=F32)


def fine_dot(value, weights):
    rows = value.shape[0]
    stacked = jnp.concatenate(split(value), axis=0)
    outs = []
    for weight in weights:
        out = dot(stacked, weight)
        outs.append(out[:rows] + out[rows:])
    return outs


def silu_parts(value):
    gate = 1.0 / (1.0 + jnp.exp(-value))
    return gate, value * gate


class Sizes:
    def __init__(self, zero_shape, one_shape, two_shape, channels):
        self.c = channels
        self.zero = zero_shape[-1] // channels
        self.one = one_shape[-1] // channels
        self.two = two_shape[-1] // channels
        self.coefs = self.zero + 2 * (self.one + self.two)
        self.starts = (self.zero, self.zero + 2 * self.one)
        self.counts = (self.one, self.two)

    def cols(self, first, count=1):
        return slice(first * self.c, (first + count) * self.c)


def picked_group(refs, hot, first, count):
    blocks = [jnp.concatenate([ref[k] for ref in refs], axis=0) for k in range(first, first + count)]
    return dot(hot, jnp.concatenate(blocks, axis=1))


def own_rows(refs, k):
    low, high = (ref[k].astype(F32) for ref in refs)
    slab = low.shape[0] // 2
    return jnp.concatenate([low[slab:], high[:slab]], axis=0)


def pool(value, rows):
    total = value[:rows]
    for start in range(rows, value.shape[0], rows):
        total = total + value[start : start + rows]
    return total


def geo_at(geo_ref, which, edges):
    return geo_ref[which * edges : (which + 1) * edges, :]


def forward(refs, hot_ref, geo_ref, faded_ref, zero_ref, one_ref, two_ref, sz, rows, last):
    hot = hot_ref[...]
    edges = hot.shape[0]
    factor = (edges // rows) ** (-0.5)
    radial = geo_at(geo_ref, 0, edges)

    def scaled(block, k):
        faded = block * radial
        faded_ref[k] = faded
        return faded.astype(BF16).astype(F32)

    pooled = [None] * sz.coefs
    group = picked_group(refs, hot, 0, sz.zero)
    zin = jnp.concatenate(
        [pool(scaled(group[:, sz.cols(k)], k), rows) for k in range(sz.zero)], axis=1
    )
    kept = 1 if last else sz.zero
    (zout,) = fine_dot(zin, [zero_ref[:, sz.cols(0, kept)]])
    for k in range(kept):
        pooled[k] = zout[:, sz.cols(k)] * factor
    for order in range(2):
        first, count = sz.starts[order], sz.counts[order]
        weight_ref = (one_ref, two_ref)[order]
        cos = geo_at(geo_ref, 1 + 2 * order, edges)
        sin = geo_at(geo_ref, 2 + 2 * order, edges)
        group = picked_group(refs, hot, first, 2 * count)
        res, ims = [], []
        for k in range(count):
            re = scaled(group[:, sz.cols(k)], first + k)
            im = scaled(group[:, sz.cols(count + k)], first + count + k)
            res.append(pool(cos * re - sin * im, rows))
            ims.append(pool(sin * re + cos * im, rows))
        both = jnp.concatenate(
            [jnp.concatenate(res, axis=1), jnp.concatenate(ims, axis=1)], axis=0
        )
        a, b = fine_dot(both, [weight_ref[0], weight_ref[1]])
        out_re = (a[:rows] - b[rows:]) * factor
        out_im = (b[:rows] + a[rows:]) * factor
        for k in range(count):
            pooled[first + k] = out_re[:, sz.cols(k)]
            pooled[first + count + k] = out_im[:, sz.cols(k)]
    return pooled


def signal_of(pooled, sz):
    total = pooled[0]
    for k in range(sz.zero, sz.coefs):
        total = total + pooled[k] * pooled[k]
    return total


def backward(
    upstream, pooled, hot_t_ref, geo_ref, faded_ref, zero_ref, one_ref, two_ref, sz, rows, last, outs
):
    hot_t = hot_t_ref[...]
    edges = hot_t.shape[1]
    slab = rows // 2
    factor = (edges // rows) ** (-0.5)
    signal = signal_of(pooled, sz)
    gate, _ = silu_parts(signal)
    slope = gate * (1.0 - gate)
    d_signal = upstream[0] * (gate + signal * slope)
    if not last:
        inner = upstream[1] * pooled[1]
        for k in range(2, sz.coefs):
            inner = inner + upstream[k] * pooled[k]
        d_signal = d_signal + inner * slope
    d_pooled = [d_signal * factor]
    for k in range(1, sz.coefs):
        if last:
            d_pooled.append(2.0 * factor * d_signal * pooled[k] if k >= sz.zero else None)
        else:
            term = gate * upstream[k]
            if k >= sz.zero:
                term = term + 2.0 * d_signal * pooled[k]
            d_pooled.append(term * factor)

    radial = geo_at(geo_ref, 0, edges)
    kept = 1 if last else sz.zero
    (dz,) = fine_dot(jnp.concatenate(d_pooled[:kept], axis=1), [zero_ref[sz.cols(0, kept), :]])

    def spread(block):
        return jnp.concatenate([block] * (edges // rows), axis=0)

    def scatter(first, blocks):
        if outs is None:
            return
        back = dot(hot_t, jnp.concatenate([block.astype(BF16) for block in blocks], axis=1))
        for n in range(len(blocks)):
            k = first + n
            part = back[:, sz.cols(n)]
            if not last or k == 0:
                part = part + around(upstream[k], slab)
            outs[0][k] = part[:rows].astype(BF16)
            outs[1][k] = part[rows:].astype(BF16)

    q_len = jnp.zeros((edges, sz.c), F32)
    blocks = []
    for k in range(sz.zero):
        grad = spread(dz[:, sz.cols(k)])
        q_len = q_len + grad * faded_ref[k]
        if outs is not None:
            blocks.append(grad * radial)
    scatter(0, blocks)
    q_turn = []
    for order in range(2):
        first, count = sz.starts[order], sz.counts[order]
        weight_ref = (one_ref, two_ref)[order]
        cos = geo_at(geo_ref, 1 + 2 * order, edges)
        sin = geo_at(geo_ref, 2 + 2 * order, edges)
        both = jnp.concatenate(
            [
                jnp.concatenate(d_pooled[first : first + count], axis=1),
                jnp.concatenate(d_pooled[first + count : first + 2 * count], axis=1),
            ],
            axis=0,
        )
        a, b = fine_dot(both, [weight_ref[0], weight_ref[1]])
        d_re = a[:rows] + b[rows:]
        d_im = a[rows:] - b[:rows]
        q_cos = jnp.zeros((edges, sz.c), F32)
        q_sin = jnp.zeros((edges, sz.c), F32)
        cos_r = cos * radial
        sin_r = sin * radial
        blocks_re, blocks_im = [], []
        for k in range(count):
            re = faded_ref[first + k]
            im = faded_ref[first + count + k]
            g_re = spread(d_re[:, sz.cols(k)])
            g_im = spread(d_im[:, sz.cols(k)])
            q_cos = q_cos + (re * g_re + im * g_im)
            q_sin = q_sin + (re * g_im - im * g_re)
            if outs is not None:
                blocks_re.append(cos_r * g_re + sin_r * g_im)
                blocks_im.append(cos_r * g_im - sin_r * g_re)
        scatter(first, blocks_re + blocks_im)
        q_len = q_len + cos * q_cos + sin * q_sin
        q_turn.append((q_cos, q_sin))

    rate = geo_at(geo_ref, 9, edges)

    def total(value):
        return jnp.sum(value, axis=1, keepdims=True)

    d_len = -total(q_len * rate)
    (dc1, ds1), (dc2, ds2) = [(total(a), total(b)) for a, b in q_turn]
    c1, s1 = geo_at(geo_ref, 1, edges), geo_at(geo_ref, 2, edges)
    ux, uy, uz = (geo_at(geo_ref, 5 + n, edges) for n in range(3))
    inv_planar = geo_at(geo_ref, 8, edges)
    dc1 = dc1 + 2.0 * (c1 * dc2 + s1 * ds2)
    ds1 = ds1 + 2.0 * (c1 * ds2 - s1 * dc2)
    along = c1 * dc1 + s1 * ds1
    dx = (dc1 - along * c1) * inv_planar + d_len * ux
    dy = (ds1 - along * s1) * inv_planar + d_len * uy
    dz_ = d_len * uz
    lane = lax.broadcasted_iota(jnp.int32, (edges, sz.c), 1)
    change = jnp.where(lane == 0, dx, jnp.where(lane == 1, dy, jnp.where(lane == 2, dz_, 0.0)))
    moved = sum(dot(hot_t, part) for part in split3(change))
    return moved - around(pool(change, rows), slab)


def around(own, slab):
    edge = jnp.zeros((slab, own.shape[1]), F32)
    return jnp.concatenate([edge, own, edge], axis=0)


def place_of(pair, pairs, segment):
    if segment == 0:
        return pair
    return 2 * pair if pair < pairs // 2 else 2 * (pairs - 1 - pair) + 1


def first_slab(slabs):
    slab_now = lax.axis_index("space")
    segment = lax.axis_index("segment")
    chip = slab_now // 2
    folded = jnp.where(lax.rem(chip, 2) == 0, chip // 2, slabs // 2 - 1 - chip // 2)
    pair = jnp.where(segment == 0, chip, folded)
    return lax.rem(2 * pair + lax.rem(segment, 2) - 1 + slabs, slabs), lax.rem(slab_now, 2)


def send_back(moved, outs, sz):
    rows = moved.shape[0] // 2
    coded = encode(moved).astype(BF16)
    outs[0][sz.coefs] = coded[:rows]
    outs[1][sz.coefs] = coded[rows:]


def share(moved, outs):
    slab = moved.shape[0] // 4
    left, low, high, right = (moved[n * slab : (n + 1) * slab] for n in range(4))
    even = lax.rem(lax.axis_index("space"), 2) == 0
    outs[0][...] = jnp.where(even, low, high)
    outs[1][...] = jnp.where(even, high, low)
    outs[2][...] = jnp.where(even, right, left)
    outs[3][...] = jnp.where(even, left, right)


def join_kernel(here_ref, theirs_ref, straight_ref, cross_ref, both_ref):
    slab = here_ref.shape[0]
    even = lax.rem(lax.axis_index("space"), 2) == 0
    here = here_ref[...] + straight_ref[...]
    there = theirs_ref[...] + cross_ref[...]
    both_ref[:slab, :] = jnp.where(even, here, there)
    both_ref[slab:, :] = jnp.where(even, there, here)


def close_kernel(*refs):
    *sums_refs, energies_ref, places_ref = refs
    slab = energies_ref.shape[1]
    for n, ref in enumerate(sums_refs):

        @pl.when(lax.axis_index("segment") == n)
        def _(ref=ref):
            sums = ref[...]
            rows, c = sums.shape
            turned = jnp.transpose(jnp.concatenate([sums, jnp.zeros((c - rows, c), F32)], axis=0))
            for b in range(2):
                energies_ref[b : b + 1, :] = turned[3:4, b * slab : (b + 1) * slab]
                for n in range(3):
                    places_ref[n, b : b + 1, :] = turned[n : n + 1, b * slab : (b + 1) * slab]


def pack_kernel(
    node_hbm, places_hbm, species_hbm, sources_hbm, grad_hbm, table_hbm, mine_ref, other_ref,
    states, places, species, sources, grads, table, sems
):
    @pl.when(lax.axis_index("segment") == 0)
    def _():
        pack(
            (node_hbm, places_hbm, species_hbm, sources_hbm, grad_hbm, table_hbm), mine_ref, other_ref,
            states, places, species, sources, grads, table, sems,
        )


def pack(given, mine_ref, other_ref, states, places, species, sources, grads, table, sems):
    batch = lax.rem(lax.axis_index("space"), 2)
    copies = []
    for n, (source, target) in enumerate(zip(given, (states, places, species, sources, grads, table))):
        copies.append(pltpu.make_async_copy(source, target, sems.at[n]))
        copies[-1].start()
    for copy in copies:
        copy.wait()
    coefs, per_slab, c = states.shape[1:]
    lane = lax.broadcasted_iota(jnp.int32, (per_slab, c), 1)
    eye = (
        lax.broadcasted_iota(jnp.int32, (per_slab, per_slab), 0)
        == lax.broadcasted_iota(jnp.int32, (per_slab, per_slab), 1)
    )

    def column(row):
        return jnp.sum(jnp.where(eye, jnp.broadcast_to(row, (per_slab, per_slab)), 0.0), axis=1, keepdims=True)

    both = []
    for b in range(2):
        names = column(species[b : b + 1, :].astype(F32)).astype(jnp.int32)
        kinds = table.shape[0]
        hot = (names == lax.broadcasted_iota(jnp.int32, (per_slab, kinds), 1)).astype(BF16)
        first = (states[b, 0].astype(F32) + dot(hot, table[...])).astype(BF16)
        extra = jnp.zeros((per_slab, c), F32)
        for n in range(3):
            extra = jnp.where(lane == n, column(places[n, b : b + 1, :]), extra)
        extra = encode(jnp.where(lane == 3, column(grads[b : b + 1, :]), extra))
        for j in range(sources.shape[2]):
            index = sources[b, :, j : j + 1]
            extra = jnp.where(lane == SOURCES + j, (index // BASE).astype(F32), extra)
            extra = jnp.where(lane == SOURCES + 8 + j, (index % BASE).astype(F32), extra)
        both.append((first, extra.astype(BF16)))
    for ref, chosen in ((mine_ref, batch), (other_ref, 1 - batch)):
        ref[pl.ds(0, coefs)] = states[chosen]
        ref[0] = jnp.where(chosen == 0, both[0][0].astype(F32), both[1][0].astype(F32)).astype(BF16)
        ref[coefs] = jnp.where(chosen == 0, both[0][1].astype(F32), both[1][1].astype(F32)).astype(BF16)


def open_kernel(mine_ref, partner_ref, straight_ref, cross_ref, low_ref, high_ref):
    @pl.when(lax.axis_index("segment") == 0)
    def _():
        even = lax.rem(lax.axis_index("space"), 2) == 0

        def choose(a, b):
            return jnp.where(even, a, b)

        for k in range(low_ref.shape[0]):
            mine, partner = mine_ref[k].astype(F32), partner_ref[k].astype(F32)
            straight, cross = straight_ref[k].astype(F32), cross_ref[k].astype(F32)
            low_ref[k] = jnp.concatenate([choose(cross, straight), choose(mine, partner)], axis=0).astype(BF16)
            high_ref[k] = jnp.concatenate([choose(partner, mine), choose(straight, cross)], axis=0).astype(BF16)


def edges_of(refs, coefs, slabs, neighbours, rate_ref, hot_ref, hot_t_ref, geo_ref):
    start, _ = first_slab(slabs)
    extra = jnp.concatenate([ref[coefs].astype(F32) for ref in refs], axis=0)
    window, c = extra.shape
    rows = window // 2
    per_slab = rows // 2
    edges = rows * neighbours
    numbers = decode(extra)
    own_extra = extra[per_slab : per_slab + rows]
    low = pltpu.roll(own_extra, c - 8, 1)
    index = own_extra.astype(jnp.int32) * BASE + low.astype(jnp.int32)
    place = lax.rem(index // per_slab - start + slabs, slabs) * per_slab + index % per_slab
    columns = lax.broadcasted_iota(jnp.int32, (rows, c), 1)
    hot = jnp.concatenate(
        [
            (place[:, SOURCES + j : SOURCES + j + 1] == columns).astype(F32)
            for j in range(neighbours)
        ],
        axis=0,
    )
    hot_t_ref[...] = jnp.transpose(hot).astype(BF16)[:window]
    hot = hot.astype(BF16)[:, :window]
    hot_ref[...] = hot
    lift = lax.broadcasted_iota(jnp.int32, (window, c), 0) // per_slab - 1
    offset = []
    for n in range(3):
        column = jnp.broadcast_to(numbers[:, n : n + 1], (window, c))
        if n == 2:
            column = column + SLAB_DEPTH * lift.astype(F32)
        there = sum(dot(hot, part) for part in split3(column))
        offset.append(there - jnp.concatenate([column[per_slab : per_slab + rows]] * neighbours, axis=0))
    flat = offset[0] * offset[0] + offset[1] * offset[1] + 1.0
    length = jnp.sqrt(flat + offset[2] * offset[2])
    planar = jnp.sqrt(flat)
    c1, s1 = offset[0] / planar, offset[1] / planar
    rate = jnp.broadcast_to(rate_ref[...], (edges, c))
    values = [
        jnp.exp(-rate * length),
        c1,
        s1,
        c1 * c1 - s1 * s1,
        2.0 * c1 * s1,
        offset[0] / length,
        offset[1] / length,
        offset[2] / length,
        1.0 / planar,
        rate,
    ]
    for n, value in enumerate(values):
        geo_ref[n * edges : (n + 1) * edges, :] = value
    return numbers[per_slab : per_slab + rows]


def bring(pairs, sems):
    copies = [pltpu.make_async_copy(source, target, sems.at[n]) for n, (source, target) in enumerate(pairs)]
    for copy in copies:
        copy.start()
    for copy in copies:
        copy.wait()


def stage_kernel(late, zero_hbm, one_hbm, two_hbm, *more):
    zero_ref, one_ref, two_ref, *vectors, sems = more[4:] if late else more[2:]
    waits = (lax.axis_index("segment") == 0) & (lax.rem(lax.axis_index("space"), 2) == 0)
    if not late:
        bring(list(zip(more[:2], vectors)), sems)

    @pl.when(waits == late)
    def _():
        pairs = [(zero_hbm, zero_ref)]
        for source, target in ((one_hbm, one_ref), (two_hbm, two_ref)):
            pairs += [(source.at[n], target.at[n]) for n in range(2)]
        bring(pairs, sems)


def flip_kernel(zero_ref, one_ref, two_ref, _, zero_t_ref, one_t_ref, two_t_ref):
    zero_t_ref[...] = jnp.transpose(zero_ref[...])
    for n in range(2):
        one_t_ref[n] = jnp.transpose(one_ref[n])
        two_t_ref[n] = jnp.transpose(two_ref[n])


def forward_kernel(
    tick, sz, slabs, neighbours, low_ref, high_ref, rate_ref, zero_ref, one_ref, two_ref,
    out_ref, pooled_ref, hot_t_ref, geo_ref, faded_ref, hot_ref
):
    @pl.when(lax.axis_index("segment") == tick)
    def _():
        rows = low_ref.shape[1]
        refs = (low_ref, high_ref)
        edges_of(refs, sz.coefs, slabs, neighbours, rate_ref, hot_ref, hot_t_ref, geo_ref)
        pooled = forward(refs, hot_ref, geo_ref, faded_ref, zero_ref, one_ref, two_ref, sz, rows, False)
        signal = signal_of(pooled, sz)
        gate, lifted = silu_parts(signal)
        for k in range(sz.coefs):
            pooled_ref[k] = pooled[k]
            added = lifted if k == 0 else gate * pooled[k]
            out_ref[k] = (own_rows(refs, k) + added).astype(BF16)
        out_ref[sz.coefs] = own_rows(refs, sz.coefs).astype(BF16)


def turn_kernel(
    tick, sz, slabs, neighbours, low_ref, high_ref, rate_ref, zero_ref, one_ref, two_ref,
    zero_t_ref, one_t_ref, two_t_ref, read_ref,
    back_low_ref, back_high_ref, hot_ref, hot_t_ref, geo_ref, faded_ref
):
    @pl.when(lax.axis_index("segment") == tick)
    def _():
        rows = low_ref.shape[1]
        refs = (low_ref, high_ref)
        outs = (back_low_ref, back_high_ref)
        own = edges_of(refs, sz.coefs, slabs, neighbours, rate_ref, hot_ref, hot_t_ref, geo_ref)
        pooled = forward(refs, hot_ref, geo_ref, faded_ref, zero_ref, one_ref, two_ref, sz, rows, True)
        signal = signal_of(pooled, sz)
        _, lifted = silu_parts(signal)
        updated = own_rows(refs, 0) + lifted
        gate, active = silu_parts(updated)
        read = read_ref[...]
        energy = jnp.sum(read * active, axis=1, keepdims=True)
        lane = lax.broadcasted_iota(jnp.int32, (rows, sz.c), 1)
        energy = around(jnp.where(lane == 3, energy, 0.0), rows // 2)
        upstream = [own[:, 3:4] * read * (gate + updated * gate * (1.0 - gate))]
        moved = backward(
            upstream, pooled, hot_t_ref, geo_ref, faded_ref, zero_t_ref, one_t_ref, two_t_ref, sz, rows, True, outs
        )
        send_back(moved + energy, outs, sz)


def backward_kernel(
    tick, sz, up_low_ref, up_high_ref, pooled_ref, hot_t_ref, geo_ref, faded_ref, zero_ref, one_ref, two_ref, *outs
):
    @pl.when(lax.axis_index("segment") == tick)
    def _():
        rows = up_low_ref.shape[1]
        upstream = [up_low_ref[k].astype(F32) + up_high_ref[k].astype(F32) for k in range(sz.coefs)]
        pooled = [pooled_ref[k] for k in range(sz.coefs)]
        moved = backward(
            upstream, pooled, hot_t_ref, geo_ref, faded_ref, zero_ref, one_ref, two_ref, sz, rows, False,
            outs if tick else None,
        )
        carried = decode(up_low_ref[sz.coefs].astype(F32)) + decode(up_high_ref[sz.coefs].astype(F32))
        moved = moved + around(carried, rows // 2)
        if tick:
            send_back(moved, outs, sz)
        else:
            share(moved, outs)


def call(body, operands, shapes, name, spaces=None, scratch=(), aliases=None):
    spaces = spaces or [pltpu.VMEM] * len(operands)
    operands = [pltpu.with_memory_space_constraint(value, space) for value, space in zip(operands, spaces)]
    return pl.pallas_call(
        body,
        out_shape=shapes,
        in_specs=[pl.BlockSpec(memory_space=space) for space in spaces],
        out_specs=[pl.BlockSpec(memory_space=pltpu.VMEM) for _ in shapes],
        scratch_shapes=list(scratch),
        input_output_aliases=aliases or {},
        compiler_params=pltpu.CompilerParams(vmem_limit_bytes=VMEM_LIMIT),
        name=name,
    )(*operands)


def on_device(
    node_states,
    species,
    species_table,
    places,
    sources,
    radial_rate,
    zero_weight,
    one_weight,
    two_weight,
    read_weight,
    energy_grad,
):
    segments = lax.axis_size("segment")
    slabs = lax.axis_size("space")
    batches, per_slab = species.shape
    coefs, channels = node_states.shape[2:]
    neighbours = sources.shape[2]
    rows = batches * per_slab
    edges = rows * neighbours
    sz = Sizes(zero_weight.shape, one_weight.shape, two_weight.shape, channels)
    axes = ("segment", "space")
    shape = jax.ShapeDtypeStruct

    pairs = slabs // 2

    def within(value, target):
        ways = [(s * slabs + i, s * slabs + target(i) % slabs) for s in range(segments) for i in range(slabs)]
        return lax.ppermute(value, axes, ways)

    def hop(value, start, stop, by, way):
        ways = [(place_of(q, pairs, start), place_of((q + by) % pairs, pairs, stop)) for q in range(pairs)]
        ways = [(start * slabs + 2 * a + c, stop * slabs + 2 * b + c) for a, b in ways for c in range(2)]
        idle = [s for s in range(segments) if s not in (start, stop)]
        if idle:
            third = idle[way % len(idle)]
            ways += [(stop * slabs + i, third * slabs + i) for i in range(slabs)]
            ways += [(third * slabs + i, start * slabs + i) for i in range(slabs)]
        else:
            ways += [(b, a) for a, b in ways]
        moving = {a for a, _ in ways}
        ways += [(i, i + 1 - 2 * (i % 2)) for i in range(segments * slabs) if i not in moving]
        return lax.ppermute(value, axes, ways)

    raw = [
        node_states.transpose(0, 2, 1, 3), places.transpose(1, 0, 2), species, sources, energy_grad, species_table,
    ]
    packed = shape((coefs + 1, per_slab, channels), BF16)
    mine, other = call(
        pack_kernel, raw, [packed, packed], "pack", [pltpu.HBM] * len(raw),
        [pltpu.VMEM(v.shape, v.dtype) for v in raw] + [pltpu.SemaphoreType.DMA((len(raw),))],
    )
    partner = within(other, lambda i: i + 1 - 2 * (i % 2))
    straight = within(mine, lambda i: i + 2 if i % 2 else i - 2)
    cross = within(other, lambda i: i + 1 if i % 2 else i - 1)
    stored = [zero_weight[0], one_weight[0], two_weight[0]]
    spaces = [pltpu.HBM] * 3
    on_chip = [pltpu.VMEM(w.shape, w.dtype) for w in stored]
    sems = [pltpu.SemaphoreType.DMA((5,))]
    vectors = [radial_rate, read_weight.reshape(1, channels)]
    *weights, rate, read = call(
        functools.partial(stage_kernel, False), stored + vectors,
        on_chip + [pltpu.VMEM(v.shape, v.dtype) for v in vectors], "stage", [pltpu.HBM] * 5, sems,
    )
    whole = shape((coefs + 1, rows, channels), BF16)
    around_all = [call(open_kernel, [mine, partner, straight, cross], [whole, whole], "open")]
    weights = call(
        functools.partial(stage_kernel, True), [*stored, *weights, around_all[0][0]], on_chip, "stage",
        spaces + [pltpu.VMEM] * 4, sems, {3: 0, 4: 1, 5: 2},
    )
    kept_shapes = [
        shape((2 * rows, edges), BF16), shape((10 * edges, channels), F32), shape((coefs, edges, channels), F32),
    ]
    hot = [pltpu.VMEM((edges, 2 * rows), BF16)]
    kept = []
    for tick in range(segments - 1):
        out, *residuals = call(
            functools.partial(forward_kernel, tick, sz, slabs, neighbours),
            [*around_all[tick], rate, *weights],
            [whole, shape((coefs, rows, channels), F32), *kept_shapes],
            "forward",
            scratch=hot,
        )
        kept.append(residuals)
        if tick == 0:
            flipped = call(flip_kernel, [*weights, out], on_chip, "flip")
        ways = (1, 0) if tick % 2 else (0, -1)
        around_all.append([hop(out, tick, tick + 1, by, way) for way, by in enumerate(ways)])
    final = segments - 1
    slab_sums = shape((per_slab, channels), F32)
    parts = call(
        functools.partial(turn_kernel, final, sz, slabs, neighbours),
        [*around_all[final], rate, *weights, *flipped, read],
        [whole, whole],
        "turn",
        scratch=hot + [pltpu.VMEM(v.shape, v.dtype) for v in kept_shapes],
    )
    for tick in reversed(range(segments - 1)):
        ways = (1, 0) if tick % 2 else (0, -1)
        up = [hop(part, tick + 1, tick, -by, way) for way, (part, by) in enumerate(zip(parts, ways))]
        pooled, *residuals = kept[tick]
        parts = call(
            functools.partial(backward_kernel, tick, sz),
            [*up, pooled, *residuals, *flipped],
            [whole, whole] if tick else [slab_sums] * 4,
            "backward",
        )
    here, theirs, straight, cross = parts
    theirs = within(theirs, lambda i: i + 1 - 2 * (i % 2))
    straight = within(straight, lambda i: i - 2 if i % 2 else i + 2)
    cross = within(cross, lambda i: i + 1 if i % 2 else i - 1)
    (both,) = call(join_kernel, [here, theirs, straight, cross], [shape((rows, channels), F32)], "join")

    def across(section, i, stop):
        if section in (0, stop):
            return stop - section, i
        return section, i + 1 - 2 * (i % 2)

    copies = [both] + [
        lax.ppermute(
            both,
            axes,
            [
                (s * slabs + i, t * slabs + j)
                for s in range(segments)
                for i in range(slabs)
                for t, j in [across(s, i, stop)]
            ],
        )
        for stop in range(1, segments)
    ]
    energies, gradients = call(
        close_kernel, copies, [shape((batches, per_slab), F32), shape((3, batches, per_slab), F32)], "close"
    )
    return energies, gradients.transpose(1, 0, 2)


def solution(mesh):
    in_specs = (
        P(None, "space", None, None),
        P(None, "space"),
        P(),
        P(None, None, "space"),
        P(None, "space", None),
        P("segment", None),
        P("segment", None, None),
        P("segment", None, None, None),
        P("segment", None, None, None),
        P(),
        P(None, "space"),
    )
    out_specs = (P(None, "space"), P(None, None, "space"))
    return jax.shard_map(
        on_device, mesh=mesh, in_specs=in_specs, out_specs=out_specs, check_vma=False
    )
```

```python
import functools

import jax
import jax.numpy as jnp
from jax import lax
from jax.experimental import pallas as pl
from jax.experimental.pallas import tpu as pltpu
from jax.sharding import PartitionSpec as P

SLAB_DEPTH = 2.0
F32 = jnp.float32
BF16 = jnp.bfloat16
VMEM_LIMIT = 16 * 1024 * 1024

MID, LOW, SOURCES = 32, 64, 96
BASE = 256


def split(value):
    high = value.astype(BF16)
    low = (value - high.astype(F32)).astype(BF16)
    return high, low


def split3(value):
    high = value.astype(BF16)
    rest = value - high.astype(F32)
    mid = rest.astype(BF16)
    return high, mid, (rest - mid.astype(F32)).astype(BF16)


def encode(value):
    high, mid, low = split3(value)
    return high.astype(F32) + pltpu.roll(mid.astype(F32), MID, 1) + pltpu.roll(low.astype(F32), LOW, 1)


def decode(value):
    lanes = value.shape[1]
    whole = value + pltpu.roll(value, lanes - MID, 1) + pltpu.roll(value, lanes - LOW, 1)
    lane = lax.broadcasted_iota(jnp.int32, value.shape, 1)
    return jnp.where(lane < 4, whole, 0.0)


def dot(a, b):
    return lax.dot_general(a, b, (((1,), (0,)), ((), ())), preferred_element_type=F32)


def fine_dot(value, weights):
    rows = value.shape[0]
    stacked = jnp.concatenate(split(value), axis=0)
    outs = []
    for weight in weights:
        out = dot(stacked, weight)
        outs.append(out[:rows] + out[rows:])
    return outs


def silu_parts(value):
    gate = 1.0 / (1.0 + jnp.exp(-value))
    return gate, value * gate


class Sizes:
    def __init__(self, zero_shape, one_shape, two_shape, channels):
        self.c = channels
        self.zero = zero_shape[-1] // channels
        self.one = one_shape[-1] // channels
        self.two = two_shape[-1] // channels
        self.coefs = self.zero + 2 * (self.one + self.two)
        self.starts = (self.zero, self.zero + 2 * self.one)
        self.counts = (self.one, self.two)

    def cols(self, first, count=1):
        return slice(first * self.c, (first + count) * self.c)


def picked_group(refs, hot, first, count):
    blocks = [jnp.concatenate([ref[k] for ref in refs], axis=0) for k in range(first, first + count)]
    return dot(hot, jnp.concatenate(blocks, axis=1))


def own_rows(refs, k):
    low, high = (ref[k].astype(F32) for ref in refs)
    slab = low.shape[0] // 2
    return jnp.concatenate([low[slab:], high[:slab]], axis=0)


def pool(value, rows):
    total = value[:rows]
    for start in range(rows, value.shape[0], rows):
        total = total + value[start : start + rows]
    return total


def geo_at(geo_ref, which, edges):
    return geo_ref[which * edges : (which + 1) * edges, :]


def forward(refs, hot_ref, geo_ref, faded_ref, zero_ref, one_ref, two_ref, sz, rows, last):
    hot = hot_ref[...]
    edges = hot.shape[0]
    factor = (edges // rows) ** (-0.5)
    radial = geo_at(geo_ref, 0, edges)

    def scaled(block, k):
        faded = block * radial
        faded_ref[k] = faded
        return faded.astype(BF16).astype(F32)

    pooled = [None] * sz.coefs
    group = picked_group(refs, hot, 0, sz.zero)
    zin = jnp.concatenate(
        [pool(scaled(group[:, sz.cols(k)], k), rows) for k in range(sz.zero)], axis=1
    )
    kept = 1 if last else sz.zero
    (zout,) = fine_dot(zin, [zero_ref[:, sz.cols(0, kept)]])
    for k in range(kept):
        pooled[k] = zout[:, sz.cols(k)] * factor
    for order in range(2):
        first, count = sz.starts[order], sz.counts[order]
        weight_ref = (one_ref, two_ref)[order]
        cos = geo_at(geo_ref, 1 + 2 * order, edges)
        sin = geo_at(geo_ref, 2 + 2 * order, edges)
        group = picked_group(refs, hot, first, 2 * count)
        res, ims = [], []
        for k in range(count):
            re = scaled(group[:, sz.cols(k)], first + k)
            im = scaled(group[:, sz.cols(count + k)], first + count + k)
            res.append(pool(cos * re - sin * im, rows))
            ims.append(pool(sin * re + cos * im, rows))
        both = jnp.concatenate(
            [jnp.concatenate(res, axis=1), jnp.concatenate(ims, axis=1)], axis=0
        )
        a, b = fine_dot(both, [weight_ref[0], weight_ref[1]])
        out_re = (a[:rows] - b[rows:]) * factor
        out_im = (b[:rows] + a[rows:]) * factor
        for k in range(count):
            pooled[first + k] = out_re[:, sz.cols(k)]
            pooled[first + count + k] = out_im[:, sz.cols(k)]
    return pooled


def signal_of(pooled, sz):
    total = pooled[0]
    for k in range(sz.zero, sz.coefs):
        total = total + pooled[k] * pooled[k]
    return total


def backward(
    upstream, pooled, hot_t_ref, geo_ref, faded_ref, zero_ref, one_ref, two_ref, sz, rows, last, outs
):
    hot_t = hot_t_ref[...]
    edges = hot_t.shape[1]
    slab = rows // 2
    factor = (edges // rows) ** (-0.5)
    signal = signal_of(pooled, sz)
    gate, _ = silu_parts(signal)
    slope = gate * (1.0 - gate)
    d_signal = upstream[0] * (gate + signal * slope)
    if not last:
        inner = upstream[1] * pooled[1]
        for k in range(2, sz.coefs):
            inner = inner + upstream[k] * pooled[k]
        d_signal = d_signal + inner * slope
    d_pooled = [d_signal * factor]
    for k in range(1, sz.coefs):
        if last:
            d_pooled.append(2.0 * factor * d_signal * pooled[k] if k >= sz.zero else None)
        else:
            term = gate * upstream[k]
            if k >= sz.zero:
                term = term + 2.0 * d_signal * pooled[k]
            d_pooled.append(term * factor)

    radial = geo_at(geo_ref, 0, edges)
    kept = 1 if last else sz.zero
    (dz,) = fine_dot(jnp.concatenate(d_pooled[:kept], axis=1), [zero_ref[sz.cols(0, kept), :]])

    def spread(block):
        return jnp.concatenate([block] * (edges // rows), axis=0)

    def scatter(first, blocks):
        if outs is None:
            return
        back = dot(hot_t, jnp.concatenate([block.astype(BF16) for block in blocks], axis=1))
        for n in range(len(blocks)):
            k = first + n
            part = back[:, sz.cols(n)]
            if not last or k == 0:
                part = part + around(upstream[k], slab)
            outs[0][k] = part[:rows].astype(BF16)
            outs[1][k] = part[rows:].astype(BF16)

    q_len = jnp.zeros((edges, sz.c), F32)
    blocks = []
    for k in range(sz.zero):
        grad = spread(dz[:, sz.cols(k)])
        q_len = q_len + grad * faded_ref[k]
        if outs is not None:
            blocks.append(grad * radial)
    scatter(0, blocks)
    q_turn = []
    for order in range(2):
        first, count = sz.starts[order], sz.counts[order]
        weight_ref = (one_ref, two_ref)[order]
        cos = geo_at(geo_ref, 1 + 2 * order, edges)
        sin = geo_at(geo_ref, 2 + 2 * order, edges)
        both = jnp.concatenate(
            [
                jnp.concatenate(d_pooled[first : first + count], axis=1),
                jnp.concatenate(d_pooled[first + count : first + 2 * count], axis=1),
            ],
            axis=0,
        )
        a, b = fine_dot(both, [weight_ref[0], weight_ref[1]])
        d_re = a[:rows] + b[rows:]
        d_im = a[rows:] - b[:rows]
        q_cos = jnp.zeros((edges, sz.c), F32)
        q_sin = jnp.zeros((edges, sz.c), F32)
        cos_r = cos * radial
        sin_r = sin * radial
        blocks_re, blocks_im = [], []
        for k in range(count):
            re = faded_ref[first + k]
            im = faded_ref[first + count + k]
            g_re = spread(d_re[:, sz.cols(k)])
            g_im = spread(d_im[:, sz.cols(k)])
            q_cos = q_cos + (re * g_re + im * g_im)
            q_sin = q_sin + (re * g_im - im * g_re)
            if outs is not None:
                blocks_re.append(cos_r * g_re + sin_r * g_im)
                blocks_im.append(cos_r * g_im - sin_r * g_re)
        scatter(first, blocks_re + blocks_im)
        q_len = q_len + cos * q_cos + sin * q_sin
        q_turn.append((q_cos, q_sin))

    rate = geo_at(geo_ref, 9, edges)

    def total(value):
        return jnp.sum(value, axis=1, keepdims=True)

    d_len = -total(q_len * rate)
    (dc1, ds1), (dc2, ds2) = [(total(a), total(b)) for a, b in q_turn]
    c1, s1 = geo_at(geo_ref, 1, edges), geo_at(geo_ref, 2, edges)
    ux, uy, uz = (geo_at(geo_ref, 5 + n, edges) for n in range(3))
    inv_planar = geo_at(geo_ref, 8, edges)
    dc1 = dc1 + 2.0 * (c1 * dc2 + s1 * ds2)
    ds1 = ds1 + 2.0 * (c1 * ds2 - s1 * dc2)
    along = c1 * dc1 + s1 * ds1
    dx = (dc1 - along * c1) * inv_planar + d_len * ux
    dy = (ds1 - along * s1) * inv_planar + d_len * uy
    dz_ = d_len * uz
    lane = lax.broadcasted_iota(jnp.int32, (edges, sz.c), 1)
    change = jnp.where(lane == 0, dx, jnp.where(lane == 1, dy, jnp.where(lane == 2, dz_, 0.0)))
    moved = sum(dot(hot_t, part) for part in split3(change))
    return moved - around(pool(change, rows), slab)


def around(own, slab):
    edge = jnp.zeros((slab, own.shape[1]), F32)
    return jnp.concatenate([edge, own, edge], axis=0)


def place_of(pair, pairs, segment):
    if segment == 0:
        return pair
    return 2 * pair if pair < pairs // 2 else 2 * (pairs - 1 - pair) + 1


def first_slab(slabs):
    slab_now = lax.axis_index("space")
    segment = lax.axis_index("segment")
    chip = slab_now // 2
    folded = jnp.where(lax.rem(chip, 2) == 0, chip // 2, slabs // 2 - 1 - chip // 2)
    pair = jnp.where(segment == 0, chip, folded)
    return lax.rem(2 * pair + lax.rem(segment, 2) - 1 + slabs, slabs), lax.rem(slab_now, 2)


def send_back(moved, outs, sz):
    rows = moved.shape[0] // 2
    coded = encode(moved).astype(BF16)
    outs[0][sz.coefs] = coded[:rows]
    outs[1][sz.coefs] = coded[rows:]


def share(moved, outs):
    slab = moved.shape[0] // 4
    left, low, high, right = (moved[n * slab : (n + 1) * slab] for n in range(4))
    even = lax.rem(lax.axis_index("space"), 2) == 0
    outs[0][...] = jnp.where(even, low, high)
    outs[1][...] = jnp.where(even, high, low)
    outs[2][...] = jnp.where(even, right, left)
    outs[3][...] = jnp.where(even, left, right)


def join_kernel(here_ref, theirs_ref, straight_ref, cross_ref, both_ref):
    slab = here_ref.shape[0]
    even = lax.rem(lax.axis_index("space"), 2) == 0
    here = here_ref[...] + straight_ref[...]
    there = theirs_ref[...] + cross_ref[...]
    both_ref[:slab, :] = jnp.where(even, here, there)
    both_ref[slab:, :] = jnp.where(even, there, here)


def close_kernel(*refs):
    *sums_refs, energies_ref, places_ref = refs
    slab = energies_ref.shape[1]
    for n, ref in enumerate(sums_refs):

        @pl.when(lax.axis_index("segment") == n)
        def _(ref=ref):
            sums = ref[...]
            rows, c = sums.shape
            turned = jnp.transpose(jnp.concatenate([sums, jnp.zeros((c - rows, c), F32)], axis=0))
            for b in range(2):
                energies_ref[b : b + 1, :] = turned[3:4, b * slab : (b + 1) * slab]
                for n in range(3):
                    places_ref[n, b : b + 1, :] = turned[n : n + 1, b * slab : (b + 1) * slab]


def pack_kernel(
    node_hbm, places_hbm, species_hbm, sources_hbm, grad_hbm, table_hbm, mine_ref, other_ref,
    states, places, species, sources, grads, table, sems
):
    @pl.when(lax.axis_index("segment") == 0)
    def _():
        pack(
            (node_hbm, places_hbm, species_hbm, sources_hbm, grad_hbm, table_hbm), mine_ref, other_ref,
            states, places, species, sources, grads, table, sems,
        )


def pack(given, mine_ref, other_ref, states, places, species, sources, grads, table, sems):
    batch = lax.rem(lax.axis_index("space"), 2)
    copies = []
    for n, (source, target) in enumerate(zip(given, (states, places, species, sources, grads, table))):
        copies.append(pltpu.make_async_copy(source, target, sems.at[n]))
        copies[-1].start()
    for copy in copies:
        copy.wait()
    coefs, per_slab, c = states.shape[1:]
    lane = lax.broadcasted_iota(jnp.int32, (per_slab, c), 1)
    eye = (
        lax.broadcasted_iota(jnp.int32, (per_slab, per_slab), 0)
        == lax.broadcasted_iota(jnp.int32, (per_slab, per_slab), 1)
    )

    def column(row):
        return jnp.sum(jnp.where(eye, jnp.broadcast_to(row, (per_slab, per_slab)), 0.0), axis=1, keepdims=True)

    both = []
    for b in range(2):
        names = column(species[b : b + 1, :].astype(F32)).astype(jnp.int32)
        kinds = table.shape[0]
        hot = (names == lax.broadcasted_iota(jnp.int32, (per_slab, kinds), 1)).astype(BF16)
        first = (states[b, 0].astype(F32) + dot(hot, table[...])).astype(BF16)
        extra = jnp.zeros((per_slab, c), F32)
        for n in range(3):
            extra = jnp.where(lane == n, column(places[n, b : b + 1, :]), extra)
        extra = encode(jnp.where(lane == 3, column(grads[b : b + 1, :]), extra))
        for j in range(sources.shape[2]):
            index = sources[b, :, j : j + 1]
            extra = jnp.where(lane == SOURCES + j, (index // BASE).astype(F32), extra)
            extra = jnp.where(lane == SOURCES + 8 + j, (index % BASE).astype(F32), extra)
        both.append((first, extra.astype(BF16)))
    for ref, chosen in ((mine_ref, batch), (other_ref, 1 - batch)):
        ref[pl.ds(0, coefs)] = states[chosen]
        ref[0] = jnp.where(chosen == 0, both[0][0].astype(F32), both[1][0].astype(F32)).astype(BF16)
        ref[coefs] = jnp.where(chosen == 0, both[0][1].astype(F32), both[1][1].astype(F32)).astype(BF16)


def open_kernel(mine_ref, partner_ref, straight_ref, cross_ref, low_ref, high_ref):
    @pl.when(lax.axis_index("segment") == 0)
    def _():
        even = lax.rem(lax.axis_index("space"), 2) == 0

        def choose(a, b):
            return jnp.where(even, a, b)

        for k in range(low_ref.shape[0]):
            mine, partner = mine_ref[k].astype(F32), partner_ref[k].astype(F32)
            straight, cross = straight_ref[k].astype(F32), cross_ref[k].astype(F32)
            low_ref[k] = jnp.concatenate([choose(cross, straight), choose(mine, partner)], axis=0).astype(BF16)
            high_ref[k] = jnp.concatenate([choose(partner, mine), choose(straight, cross)], axis=0).astype(BF16)


def edges_of(refs, coefs, slabs, neighbours, rate_ref, hot_ref, hot_t_ref, geo_ref):
    start, _ = first_slab(slabs)
    extra = jnp.concatenate([ref[coefs].astype(F32) for ref in refs], axis=0)
    window, c = extra.shape
    rows = window // 2
    per_slab = rows // 2
    edges = rows * neighbours
    numbers = decode(extra)
    own_extra = extra[per_slab : per_slab + rows]
    low = pltpu.roll(own_extra, c - 8, 1)
    index = own_extra.astype(jnp.int32) * BASE + low.astype(jnp.int32)
    place = lax.rem(index // per_slab - start + slabs, slabs) * per_slab + index % per_slab
    columns = lax.broadcasted_iota(jnp.int32, (rows, c), 1)
    hot = jnp.concatenate(
        [
            (place[:, SOURCES + j : SOURCES + j + 1] == columns).astype(F32)
            for j in range(neighbours)
        ],
        axis=0,
    )
    hot_t_ref[...] = jnp.transpose(hot).astype(BF16)[:window]
    hot = hot.astype(BF16)[:, :window]
    hot_ref[...] = hot
    lift = lax.broadcasted_iota(jnp.int32, (window, c), 0) // per_slab - 1
    offset = []
    for n in range(3):
        column = jnp.broadcast_to(numbers[:, n : n + 1], (window, c))
        if n == 2:
            column = column + SLAB_DEPTH * lift.astype(F32)
        there = sum(dot(hot, part) for part in split3(column))
        offset.append(there - jnp.concatenate([column[per_slab : per_slab + rows]] * neighbours, axis=0))
    flat = offset[0] * offset[0] + offset[1] * offset[1] + 1.0
    length = jnp.sqrt(flat + offset[2] * offset[2])
    planar = jnp.sqrt(flat)
    c1, s1 = offset[0] / planar, offset[1] / planar
    rate = jnp.broadcast_to(rate_ref[...], (edges, c))
    values = [
        jnp.exp(-rate * length),
        c1,
        s1,
        c1 * c1 - s1 * s1,
        2.0 * c1 * s1,
        offset[0] / length,
        offset[1] / length,
        offset[2] / length,
        1.0 / planar,
        rate,
    ]
    for n, value in enumerate(values):
        geo_ref[n * edges : (n + 1) * edges, :] = value
    return numbers[per_slab : per_slab + rows]


def bring(pairs, sems):
    copies = [pltpu.make_async_copy(source, target, sems.at[n]) for n, (source, target) in enumerate(pairs)]
    for copy in copies:
        copy.start()
    for copy in copies:
        copy.wait()


def stage_kernel(late, zero_hbm, one_hbm, two_hbm, *more):
    zero_ref, one_ref, two_ref, *vectors, sems = more[4:] if late else more[2:]
    waits = (lax.axis_index("segment") == 0) & (lax.rem(lax.axis_index("space"), 2) == 0)
    if not late:
        bring(list(zip(more[:2], vectors)), sems)

    @pl.when(waits == late)
    def _():
        whole = [(zero_hbm, zero_ref)]
        for source, target in ((one_hbm, one_ref), (two_hbm, two_ref)):
            whole += [(source.at[n], target.at[n]) for n in range(2)]
        pairs = []
        for source, target in whole:
            half = source.shape[0] // 2
            pairs += [(source.at[pl.ds(n * half, half)], target.at[pl.ds(n * half, half)]) for n in range(2)]
        bring(pairs, sems)


def flip_kernel(zero_ref, one_ref, two_ref, _, zero_t_ref, one_t_ref, two_t_ref):
    zero_t_ref[...] = jnp.transpose(zero_ref[...])
    for n in range(2):
        one_t_ref[n] = jnp.transpose(one_ref[n])
        two_t_ref[n] = jnp.transpose(two_ref[n])


def forward_kernel(
    tick, sz, slabs, neighbours, low_ref, high_ref, rate_ref, zero_ref, one_ref, two_ref,
    out_ref, pooled_ref, hot_t_ref, geo_ref, faded_ref, hot_ref
):
    @pl.when(lax.axis_index("segment") == tick)
    def _():
        rows = low_ref.shape[1]
        refs = (low_ref, high_ref)
        edges_of(refs, sz.coefs, slabs, neighbours, rate_ref, hot_ref, hot_t_ref, geo_ref)
        pooled = forward(refs, hot_ref, geo_ref, faded_ref, zero_ref, one_ref, two_ref, sz, rows, False)
        signal = signal_of(pooled, sz)
        gate, lifted = silu_parts(signal)
        for k in range(sz.coefs):
            pooled_ref[k] = pooled[k]
            added = lifted if k == 0 else gate * pooled[k]
            out_ref[k] = (own_rows(refs, k) + added).astype(BF16)
        out_ref[sz.coefs] = own_rows(refs, sz.coefs).astype(BF16)


def turn_kernel(
    tick, sz, slabs, neighbours, low_ref, high_ref, rate_ref, zero_ref, one_ref, two_ref,
    zero_t_ref, one_t_ref, two_t_ref, read_ref,
    back_low_ref, back_high_ref, hot_ref, hot_t_ref, geo_ref, faded_ref
):
    @pl.when(lax.axis_index("segment") == tick)
    def _():
        rows = low_ref.shape[1]
        refs = (low_ref, high_ref)
        outs = (back_low_ref, back_high_ref)
        own = edges_of(refs, sz.coefs, slabs, neighbours, rate_ref, hot_ref, hot_t_ref, geo_ref)
        pooled = forward(refs, hot_ref, geo_ref, faded_ref, zero_ref, one_ref, two_ref, sz, rows, True)
        signal = signal_of(pooled, sz)
        _, lifted = silu_parts(signal)
        updated = own_rows(refs, 0) + lifted
        gate, active = silu_parts(updated)
        read = read_ref[...]
        energy = jnp.sum(read * active, axis=1, keepdims=True)
        lane = lax.broadcasted_iota(jnp.int32, (rows, sz.c), 1)
        energy = around(jnp.where(lane == 3, energy, 0.0), rows // 2)
        upstream = [own[:, 3:4] * read * (gate + updated * gate * (1.0 - gate))]
        moved = backward(
            upstream, pooled, hot_t_ref, geo_ref, faded_ref, zero_t_ref, one_t_ref, two_t_ref, sz, rows, True, outs
        )
        send_back(moved + energy, outs, sz)


def backward_kernel(
    tick, sz, up_low_ref, up_high_ref, pooled_ref, hot_t_ref, geo_ref, faded_ref, zero_ref, one_ref, two_ref, *outs
):
    @pl.when(lax.axis_index("segment") == tick)
    def _():
        rows = up_low_ref.shape[1]
        upstream = [up_low_ref[k].astype(F32) + up_high_ref[k].astype(F32) for k in range(sz.coefs)]
        pooled = [pooled_ref[k] for k in range(sz.coefs)]
        moved = backward(
            upstream, pooled, hot_t_ref, geo_ref, faded_ref, zero_ref, one_ref, two_ref, sz, rows, False,
            outs if tick else None,
        )
        carried = decode(up_low_ref[sz.coefs].astype(F32)) + decode(up_high_ref[sz.coefs].astype(F32))
        moved = moved + around(carried, rows // 2)
        if tick:
            send_back(moved, outs, sz)
        else:
            share(moved, outs)


def call(body, operands, shapes, name, spaces=None, scratch=(), aliases=None):
    spaces = spaces or [pltpu.VMEM] * len(operands)
    operands = [pltpu.with_memory_space_constraint(value, space) for value, space in zip(operands, spaces)]
    return pl.pallas_call(
        body,
        out_shape=shapes,
        in_specs=[pl.BlockSpec(memory_space=space) for space in spaces],
        out_specs=[pl.BlockSpec(memory_space=pltpu.VMEM) for _ in shapes],
        scratch_shapes=list(scratch),
        input_output_aliases=aliases or {},
        compiler_params=pltpu.CompilerParams(vmem_limit_bytes=VMEM_LIMIT),
        name=name,
    )(*operands)


def on_device(
    node_states,
    species,
    species_table,
    places,
    sources,
    radial_rate,
    zero_weight,
    one_weight,
    two_weight,
    read_weight,
    energy_grad,
):
    segments = lax.axis_size("segment")
    slabs = lax.axis_size("space")
    batches, per_slab = species.shape
    coefs, channels = node_states.shape[2:]
    neighbours = sources.shape[2]
    rows = batches * per_slab
    edges = rows * neighbours
    sz = Sizes(zero_weight.shape, one_weight.shape, two_weight.shape, channels)
    axes = ("segment", "space")
    shape = jax.ShapeDtypeStruct

    pairs = slabs // 2

    def swapped(i):
        return i + 1 - 2 * (i % 2)

    def within(value, target):
        ways = [(i, target(i) % slabs) for i in range(slabs)]
        ways += [(s * slabs + i, s * slabs + swapped(i)) for s in range(1, segments) for i in range(slabs)]
        return lax.ppermute(value, axes, ways)

    def hop(value, start, stop, by, way):
        ways = [(place_of(q, pairs, start), place_of((q + by) % pairs, pairs, stop)) for q in range(pairs)]
        ways = [(start * slabs + 2 * a + c, stop * slabs + 2 * b + c) for a, b in ways for c in range(2)]
        idle = [s for s in range(segments) if s not in (start, stop)]
        if idle:
            third = idle[way % len(idle)]
            ways += [(stop * slabs + i, third * slabs + i) for i in range(slabs)]
            ways += [(third * slabs + i, start * slabs + i) for i in range(slabs)]
        else:
            ways += [(b, a) for a, b in ways]
        moving = {a for a, _ in ways}
        ways += [(i, swapped(i)) for i in range(segments * slabs) if i not in moving]
        return lax.ppermute(value, axes, ways)

    raw = [
        node_states.transpose(0, 2, 1, 3), places.transpose(1, 0, 2), species, sources, energy_grad, species_table,
    ]
    packed = shape((coefs + 1, per_slab, channels), BF16)
    mine, other = call(
        pack_kernel, raw, [packed, packed], "pack", [pltpu.HBM] * len(raw),
        [pltpu.VMEM(v.shape, v.dtype) for v in raw] + [pltpu.SemaphoreType.DMA((len(raw),))],
    )
    partner = within(other, swapped)
    straight = within(mine, lambda i: i + 2 if i % 2 else i - 2)
    cross = within(other, lambda i: i + 1 if i % 2 else i - 1)
    stored = [zero_weight[0], one_weight[0], two_weight[0]]
    spaces = [pltpu.HBM] * 3
    on_chip = [pltpu.VMEM(w.shape, w.dtype) for w in stored]
    sems = [pltpu.SemaphoreType.DMA((10,))]
    vectors = [radial_rate, read_weight.reshape(1, channels)]
    *weights, rate, read = call(
        functools.partial(stage_kernel, False), stored + vectors,
        on_chip + [pltpu.VMEM(v.shape, v.dtype) for v in vectors], "stage", [pltpu.HBM] * 5, sems,
    )
    whole = shape((coefs + 1, rows, channels), BF16)
    around_all = [call(open_kernel, [mine, partner, straight, cross], [whole, whole], "open")]
    weights = call(
        functools.partial(stage_kernel, True), [*stored, *weights, around_all[0][0]], on_chip, "stage",
        spaces + [pltpu.VMEM] * 4, sems, {3: 0, 4: 1, 5: 2},
    )
    kept_shapes = [
        shape((2 * rows, edges), BF16), shape((10 * edges, channels), F32), shape((coefs, edges, channels), F32),
    ]
    hot = [pltpu.VMEM((edges, 2 * rows), BF16)]
    kept = []
    for tick in range(segments - 1):
        out, *residuals = call(
            functools.partial(forward_kernel, tick, sz, slabs, neighbours),
            [*around_all[tick], rate, *weights],
            [whole, shape((coefs, rows, channels), F32), *kept_shapes],
            "forward",
            scratch=hot,
        )
        kept.append(residuals)
        if tick == 0:
            flipped = call(flip_kernel, [*weights, out], on_chip, "flip")
        ways = (1, 0) if tick % 2 else (0, -1)
        around_all.append([hop(out, tick, tick + 1, by, way) for way, by in enumerate(ways)])
    final = segments - 1
    slab_sums = shape((per_slab, channels), F32)
    parts = call(
        functools.partial(turn_kernel, final, sz, slabs, neighbours),
        [*around_all[final], rate, *weights, *flipped, read],
        [whole, whole],
        "turn",
        scratch=hot + [pltpu.VMEM(v.shape, v.dtype) for v in kept_shapes],
    )
    for tick in reversed(range(segments - 1)):
        ways = (1, 0) if tick % 2 else (0, -1)
        up = [hop(part, tick + 1, tick, -by, way) for way, (part, by) in enumerate(zip(parts, ways))]
        pooled, *residuals = kept[tick]
        parts = call(
            functools.partial(backward_kernel, tick, sz),
            [*up, pooled, *residuals, *flipped],
            [whole, whole] if tick else [slab_sums] * 4,
            "backward",
        )
    here, theirs, straight, cross = parts
    theirs = within(theirs, swapped)
    straight = within(straight, lambda i: i - 2 if i % 2 else i + 2)
    cross = within(cross, lambda i: i + 1 if i % 2 else i - 1)
    (both,) = call(join_kernel, [here, theirs, straight, cross], [shape((rows, channels), F32)], "join")

    def across(section, i, stop):
        if section in (0, stop):
            return stop - section, i
        return section, swapped(i)

    copies = [both] + [
        lax.ppermute(
            both,
            axes,
            [
                (s * slabs + i, t * slabs + j)
                for s in range(segments)
                for i in range(slabs)
                for t, j in [across(s, i, stop)]
            ],
        )
        for stop in range(1, segments)
    ]
    energies, gradients = call(
        close_kernel, copies, [shape((batches, per_slab), F32), shape((3, batches, per_slab), F32)], "close"
    )
    return energies, gradients.transpose(1, 0, 2)


def solution(mesh):
    in_specs = (
        P(None, "space", None, None),
        P(None, "space"),
        P(),
        P(None, None, "space"),
        P(None, "space", None),
        P("segment", None),
        P("segment", None, None),
        P("segment", None, None, None),
        P("segment", None, None, None),
        P(),
        P(None, "space"),
    )
    out_specs = (P(None, "space"), P(None, None, "space"))
    return jax.shard_map(
        on_device, mesh=mesh, in_specs=in_specs, out_specs=out_specs, check_vma=False
    )
```

```python
import functools

import jax
import jax.numpy as jnp
from jax import lax
from jax.experimental import pallas as pl
from jax.experimental.pallas import tpu as pltpu
from jax.sharding import PartitionSpec as P

SLAB_DEPTH = 2.0
F32 = jnp.float32
BF16 = jnp.bfloat16
VMEM_LIMIT = 16 * 1024 * 1024

MID, LOW, SOURCES = 32, 64, 96
BASE = 256


def split(value):
    high = value.astype(BF16)
    low = (value - high.astype(F32)).astype(BF16)
    return high, low


def split3(value):
    high = value.astype(BF16)
    rest = value - high.astype(F32)
    mid = rest.astype(BF16)
    return high, mid, (rest - mid.astype(F32)).astype(BF16)


def encode(value):
    high, mid, low = split3(value)
    return high.astype(F32) + pltpu.roll(mid.astype(F32), MID, 1) + pltpu.roll(low.astype(F32), LOW, 1)


def decode(value):
    lanes = value.shape[1]
    whole = value + pltpu.roll(value, lanes - MID, 1) + pltpu.roll(value, lanes - LOW, 1)
    lane = lax.broadcasted_iota(jnp.int32, value.shape, 1)
    return jnp.where(lane < 4, whole, 0.0)


def dot(a, b):
    return lax.dot_general(a, b, (((1,), (0,)), ((), ())), preferred_element_type=F32)


def fine_dot(value, weights):
    rows = value.shape[0]
    stacked = jnp.concatenate(split(value), axis=0)
    outs = []
    for weight in weights:
        out = dot(stacked, weight)
        outs.append(out[:rows] + out[rows:])
    return outs


def silu_parts(value):
    gate = 1.0 / (1.0 + jnp.exp(-value))
    return gate, value * gate


class Sizes:
    def __init__(self, zero_shape, one_shape, two_shape, channels):
        self.c = channels
        self.zero = zero_shape[-1] // channels
        self.one = one_shape[-1] // channels
        self.two = two_shape[-1] // channels
        self.coefs = self.zero + 2 * (self.one + self.two)
        self.starts = (self.zero, self.zero + 2 * self.one)
        self.counts = (self.one, self.two)

    def cols(self, first, count=1):
        return slice(first * self.c, (first + count) * self.c)


def picked_group(refs, hot, first, count):
    blocks = [jnp.concatenate([ref[k] for ref in refs], axis=0) for k in range(first, first + count)]
    return dot(hot, jnp.concatenate(blocks, axis=1))


def own_rows(refs, k):
    low, high = (ref[k].astype(F32) for ref in refs)
    slab = low.shape[0] // 2
    return jnp.concatenate([low[slab:], high[:slab]], axis=0)


def pool(value, rows):
    total = value[:rows]
    for start in range(rows, value.shape[0], rows):
        total = total + value[start : start + rows]
    return total


def geo_at(geo_ref, which, edges):
    return geo_ref[which * edges : (which + 1) * edges, :]


def forward(refs, hot_ref, geo_ref, faded_ref, zero_ref, one_ref, two_ref, sz, rows, last):
    hot = hot_ref[...]
    edges = hot.shape[0]
    factor = (edges // rows) ** (-0.5)
    radial = geo_at(geo_ref, 0, edges)

    def scaled(block, k):
        faded = block * radial
        faded_ref[k] = faded
        return faded.astype(BF16).astype(F32)

    pooled = [None] * sz.coefs
    group = picked_group(refs, hot, 0, sz.zero)
    zin = jnp.concatenate(
        [pool(scaled(group[:, sz.cols(k)], k), rows) for k in range(sz.zero)], axis=1
    )
    kept = 1 if last else sz.zero
    (zout,) = fine_dot(zin, [zero_ref[:, sz.cols(0, kept)]])
    for k in range(kept):
        pooled[k] = zout[:, sz.cols(k)] * factor
    for order in range(2):
        first, count = sz.starts[order], sz.counts[order]
        weight_ref = (one_ref, two_ref)[order]
        cos = geo_at(geo_ref, 1 + 2 * order, edges)
        sin = geo_at(geo_ref, 2 + 2 * order, edges)
        group = picked_group(refs, hot, first, 2 * count)
        res, ims = [], []
        for k in range(count):
            re = scaled(group[:, sz.cols(k)], first + k)
            im = scaled(group[:, sz.cols(count + k)], first + count + k)
            res.append(pool(cos * re - sin * im, rows))
            ims.append(pool(sin * re + cos * im, rows))
        both = jnp.concatenate(
            [jnp.concatenate(res, axis=1), jnp.concatenate(ims, axis=1)], axis=0
        )
        a, b = fine_dot(both, [weight_ref[0], weight_ref[1]])
        out_re = (a[:rows] - b[rows:]) * factor
        out_im = (b[:rows] + a[rows:]) * factor
        for k in range(count):
            pooled[first + k] = out_re[:, sz.cols(k)]
            pooled[first + count + k] = out_im[:, sz.cols(k)]
    return pooled


def signal_of(pooled, sz):
    total = pooled[0]
    for k in range(sz.zero, sz.coefs):
        total = total + pooled[k] * pooled[k]
    return total


def backward(
    upstream, pooled, hot_t_ref, geo_ref, faded_ref, zero_ref, one_ref, two_ref, sz, rows, last, outs
):
    hot_t = hot_t_ref[...]
    edges = hot_t.shape[1]
    slab = rows // 2
    factor = (edges // rows) ** (-0.5)
    signal = signal_of(pooled, sz)
    gate, _ = silu_parts(signal)
    slope = gate * (1.0 - gate)
    d_signal = upstream[0] * (gate + signal * slope)
    if not last:
        inner = upstream[1] * pooled[1]
        for k in range(2, sz.coefs):
            inner = inner + upstream[k] * pooled[k]
        d_signal = d_signal + inner * slope
    d_pooled = [d_signal * factor]
    for k in range(1, sz.coefs):
        if last:
            d_pooled.append(2.0 * factor * d_signal * pooled[k] if k >= sz.zero else None)
        else:
            term = gate * upstream[k]
            if k >= sz.zero:
                term = term + 2.0 * d_signal * pooled[k]
            d_pooled.append(term * factor)

    radial = geo_at(geo_ref, 0, edges)
    kept = 1 if last else sz.zero
    (dz,) = fine_dot(jnp.concatenate(d_pooled[:kept], axis=1), [zero_ref[sz.cols(0, kept), :]])

    def spread(block):
        return jnp.concatenate([block] * (edges // rows), axis=0)

    def scatter(first, blocks):
        if outs is None:
            return
        back = dot(hot_t, jnp.concatenate([block.astype(BF16) for block in blocks], axis=1))
        for n in range(len(blocks)):
            k = first + n
            part = back[:, sz.cols(n)]
            if not last or k == 0:
                part = part + around(upstream[k], slab)
            outs[0][k] = part[:rows].astype(BF16)
            outs[1][k] = part[rows:].astype(BF16)

    q_len = jnp.zeros((edges, sz.c), F32)
    blocks = []
    for k in range(sz.zero):
        grad = spread(dz[:, sz.cols(k)])
        q_len = q_len + grad * faded_ref[k]
        if outs is not None:
            blocks.append(grad * radial)
    scatter(0, blocks)
    q_turn = []
    for order in range(2):
        first, count = sz.starts[order], sz.counts[order]
        weight_ref = (one_ref, two_ref)[order]
        cos = geo_at(geo_ref, 1 + 2 * order, edges)
        sin = geo_at(geo_ref, 2 + 2 * order, edges)
        both = jnp.concatenate(
            [
                jnp.concatenate(d_pooled[first : first + count], axis=1),
                jnp.concatenate(d_pooled[first + count : first + 2 * count], axis=1),
            ],
            axis=0,
        )
        a, b = fine_dot(both, [weight_ref[0], weight_ref[1]])
        d_re = a[:rows] + b[rows:]
        d_im = a[rows:] - b[:rows]
        q_cos = jnp.zeros((edges, sz.c), F32)
        q_sin = jnp.zeros((edges, sz.c), F32)
        cos_r = cos * radial
        sin_r = sin * radial
        blocks_re, blocks_im = [], []
        for k in range(count):
            re = faded_ref[first + k]
            im = faded_ref[first + count + k]
            g_re = spread(d_re[:, sz.cols(k)])
            g_im = spread(d_im[:, sz.cols(k)])
            q_cos = q_cos + (re * g_re + im * g_im)
            q_sin = q_sin + (re * g_im - im * g_re)
            if outs is not None:
                blocks_re.append(cos_r * g_re + sin_r * g_im)
                blocks_im.append(cos_r * g_im - sin_r * g_re)
        scatter(first, blocks_re + blocks_im)
        q_len = q_len + cos * q_cos + sin * q_sin
        q_turn.append((q_cos, q_sin))

    rate = geo_at(geo_ref, 9, edges)

    def total(value):
        return jnp.sum(value, axis=1, keepdims=True)

    d_len = -total(q_len * rate)
    (dc1, ds1), (dc2, ds2) = [(total(a), total(b)) for a, b in q_turn]
    c1, s1 = geo_at(geo_ref, 1, edges), geo_at(geo_ref, 2, edges)
    ux, uy, uz = (geo_at(geo_ref, 5 + n, edges) for n in range(3))
    inv_planar = geo_at(geo_ref, 8, edges)
    dc1 = dc1 + 2.0 * (c1 * dc2 + s1 * ds2)
    ds1 = ds1 + 2.0 * (c1 * ds2 - s1 * dc2)
    along = c1 * dc1 + s1 * ds1
    dx = (dc1 - along * c1) * inv_planar + d_len * ux
    dy = (ds1 - along * s1) * inv_planar + d_len * uy
    dz_ = d_len * uz
    lane = lax.broadcasted_iota(jnp.int32, (edges, sz.c), 1)
    change = jnp.where(lane == 0, dx, jnp.where(lane == 1, dy, jnp.where(lane == 2, dz_, 0.0)))
    moved = sum(dot(hot_t, part) for part in split3(change))
    return moved - around(pool(change, rows), slab)


def around(own, slab):
    edge = jnp.zeros((slab, own.shape[1]), F32)
    return jnp.concatenate([edge, own, edge], axis=0)


def place_of(pair, pairs, segment):
    if segment == 0:
        return pair
    return 2 * pair if pair < pairs // 2 else 2 * (pairs - 1 - pair) + 1


def first_slab(slabs):
    slab_now = lax.axis_index("space")
    segment = lax.axis_index("segment")
    chip = slab_now // 2
    folded = jnp.where(lax.rem(chip, 2) == 0, chip // 2, slabs // 2 - 1 - chip // 2)
    pair = jnp.where(segment == 0, chip, folded)
    return lax.rem(2 * pair + lax.rem(segment, 2) - 1 + slabs, slabs), lax.rem(slab_now, 2)


def send_back(moved, outs, sz):
    rows = moved.shape[0] // 2
    coded = encode(moved).astype(BF16)
    outs[0][sz.coefs] = coded[:rows]
    outs[1][sz.coefs] = coded[rows:]


def share(moved, outs):
    slab = moved.shape[0] // 4
    left, low, high, right = (moved[n * slab : (n + 1) * slab] for n in range(4))
    even = lax.rem(lax.axis_index("space"), 2) == 0
    outs[0][...] = jnp.where(even, low, high)
    outs[1][...] = jnp.where(even, high, low)
    outs[2][...] = jnp.where(even, right, left)
    outs[3][...] = jnp.where(even, left, right)


def join_kernel(here_ref, theirs_ref, straight_ref, cross_ref, both_ref):
    slab = here_ref.shape[0]
    even = lax.rem(lax.axis_index("space"), 2) == 0
    here = here_ref[...] + straight_ref[...]
    there = theirs_ref[...] + cross_ref[...]
    both_ref[:slab, :] = jnp.where(even, here, there)
    both_ref[slab:, :] = jnp.where(even, there, here)


def close_kernel(*refs):
    *sums_refs, energies_ref, places_ref = refs
    slab = energies_ref.shape[1]
    for n, ref in enumerate(sums_refs):

        @pl.when(lax.axis_index("segment") == n)
        def _(ref=ref):
            sums = ref[...]
            rows, c = sums.shape
            turned = jnp.transpose(jnp.concatenate([sums, jnp.zeros((c - rows, c), F32)], axis=0))
            for b in range(2):
                energies_ref[b : b + 1, :] = turned[3:4, b * slab : (b + 1) * slab]
                for n in range(3):
                    places_ref[n, b : b + 1, :] = turned[n : n + 1, b * slab : (b + 1) * slab]


def pack_kernel(
    node_hbm, places_hbm, species_hbm, sources_hbm, grad_hbm, table_hbm, mine_ref, other_ref,
    states, places, species, sources, grads, table, sems
):
    @pl.when(lax.axis_index("segment") == 0)
    def _():
        pack(
            (node_hbm, places_hbm, species_hbm, sources_hbm, grad_hbm, table_hbm), mine_ref, other_ref,
            states, places, species, sources, grads, table, sems,
        )


def pack(given, mine_ref, other_ref, states, places, species, sources, grads, table, sems):
    batch = lax.rem(lax.axis_index("space"), 2)
    copies = []
    for n, (source, target) in enumerate(zip(given, (states, places, species, sources, grads, table))):
        copies.append(pltpu.make_async_copy(source, target, sems.at[n]))
        copies[-1].start()
    for copy in copies:
        copy.wait()
    coefs, per_slab, c = states.shape[1:]
    lane = lax.broadcasted_iota(jnp.int32, (per_slab, c), 1)
    eye = (
        lax.broadcasted_iota(jnp.int32, (per_slab, per_slab), 0)
        == lax.broadcasted_iota(jnp.int32, (per_slab, per_slab), 1)
    )

    def column(row):
        return jnp.sum(jnp.where(eye, jnp.broadcast_to(row, (per_slab, per_slab)), 0.0), axis=1, keepdims=True)

    both = []
    for b in range(2):
        names = column(species[b : b + 1, :].astype(F32)).astype(jnp.int32)
        kinds = table.shape[0]
        hot = (names == lax.broadcasted_iota(jnp.int32, (per_slab, kinds), 1)).astype(BF16)
        first = (states[b, 0].astype(F32) + dot(hot, table[...])).astype(BF16)
        extra = jnp.zeros((per_slab, c), F32)
        for n in range(3):
            extra = jnp.where(lane == n, column(places[n, b : b + 1, :]), extra)
        extra = encode(jnp.where(lane == 3, column(grads[b : b + 1, :]), extra))
        for j in range(sources.shape[2]):
            index = sources[b, :, j : j + 1]
            extra = jnp.where(lane == SOURCES + j, (index // BASE).astype(F32), extra)
            extra = jnp.where(lane == SOURCES + 8 + j, (index % BASE).astype(F32), extra)
        both.append((first, extra.astype(BF16)))
    for ref, chosen in ((mine_ref, batch), (other_ref, 1 - batch)):
        ref[pl.ds(0, coefs)] = states[chosen]
        ref[0] = jnp.where(chosen == 0, both[0][0].astype(F32), both[1][0].astype(F32)).astype(BF16)
        ref[coefs] = jnp.where(chosen == 0, both[0][1].astype(F32), both[1][1].astype(F32)).astype(BF16)


def open_kernel(mine_ref, partner_ref, straight_ref, cross_ref, low_ref, high_ref):
    @pl.when(lax.axis_index("segment") == 0)
    def _():
        even = lax.rem(lax.axis_index("space"), 2) == 0

        def choose(a, b):
            return jnp.where(even, a, b)

        for k in range(low_ref.shape[0]):
            mine, partner = mine_ref[k].astype(F32), partner_ref[k].astype(F32)
            straight, cross = straight_ref[k].astype(F32), cross_ref[k].astype(F32)
            low_ref[k] = jnp.concatenate([choose(cross, straight), choose(mine, partner)], axis=0).astype(BF16)
            high_ref[k] = jnp.concatenate([choose(partner, mine), choose(straight, cross)], axis=0).astype(BF16)


def edges_of(refs, coefs, slabs, neighbours, rate_ref, hot_ref, hot_t_ref, geo_ref):
    start, _ = first_slab(slabs)
    extra = jnp.concatenate([ref[coefs].astype(F32) for ref in refs], axis=0)
    window, c = extra.shape
    rows = window // 2
    per_slab = rows // 2
    edges = rows * neighbours
    numbers = decode(extra)
    own_extra = extra[per_slab : per_slab + rows]
    low = pltpu.roll(own_extra, c - 8, 1)
    index = own_extra.astype(jnp.int32) * BASE + low.astype(jnp.int32)
    place = lax.rem(index // per_slab - start + slabs, slabs) * per_slab + index % per_slab
    columns = lax.broadcasted_iota(jnp.int32, (rows, c), 1)
    hot = jnp.concatenate(
        [
            (place[:, SOURCES + j : SOURCES + j + 1] == columns).astype(F32)
            for j in range(neighbours)
        ],
        axis=0,
    )
    hot_t_ref[...] = jnp.transpose(hot).astype(BF16)[:window]
    hot = hot.astype(BF16)[:, :window]
    hot_ref[...] = hot
    lift = lax.broadcasted_iota(jnp.int32, (window, c), 0) // per_slab - 1
    offset = []
    for n in range(3):
        column = jnp.broadcast_to(numbers[:, n : n + 1], (window, c))
        if n == 2:
            column = column + SLAB_DEPTH * lift.astype(F32)
        there = sum(dot(hot, part) for part in split3(column))
        offset.append(there - jnp.concatenate([column[per_slab : per_slab + rows]] * neighbours, axis=0))
    flat = offset[0] * offset[0] + offset[1] * offset[1] + 1.0
    length = jnp.sqrt(flat + offset[2] * offset[2])
    planar = jnp.sqrt(flat)
    c1, s1 = offset[0] / planar, offset[1] / planar
    rate = jnp.broadcast_to(rate_ref[...], (edges, c))
    values = [
        jnp.exp(-rate * length),
        c1,
        s1,
        c1 * c1 - s1 * s1,
        2.0 * c1 * s1,
        offset[0] / length,
        offset[1] / length,
        offset[2] / length,
        1.0 / planar,
        rate,
    ]
    for n, value in enumerate(values):
        geo_ref[n * edges : (n + 1) * edges, :] = value
    return numbers[per_slab : per_slab + rows]


def bring(pairs, sems):
    copies = [pltpu.make_async_copy(source, target, sems.at[n]) for n, (source, target) in enumerate(pairs)]
    for copy in copies:
        copy.start()
    for copy in copies:
        copy.wait()


def stage_kernel(late, zero_hbm, one_hbm, two_hbm, *more):
    zero_ref, one_ref, two_ref, *vectors, sems = more[4:] if late else more[2:]
    waits = (lax.axis_index("segment") == 0) & (lax.rem(lax.axis_index("space"), 2) == 0)

    def halves(whole):
        pairs = []
        for source, target in whole:
            half = source.shape[0] // 2
            pairs += [(source.at[pl.ds(n * half, half)], target.at[pl.ds(n * half, half)]) for n in range(2)]
        return pairs

    ones = halves([(one_hbm.at[n], one_ref.at[n]) for n in range(2)])
    if late:
        pl.when(waits)(lambda: bring(ones, sems))
        return
    rest = halves([(zero_hbm, zero_ref)] + [(two_hbm.at[n], two_ref.at[n]) for n in range(2)])
    rest += list(zip(more[:2], vectors))
    pl.when(waits)(lambda: bring(rest, sems))
    pl.when(jnp.logical_not(waits))(lambda: bring(rest + ones, sems))


def flip_kernel(zero_ref, one_ref, two_ref, _, zero_t_ref, one_t_ref, two_t_ref):
    zero_t_ref[...] = jnp.transpose(zero_ref[...])
    for n in range(2):
        one_t_ref[n] = jnp.transpose(one_ref[n])
        two_t_ref[n] = jnp.transpose(two_ref[n])


def forward_kernel(
    tick, sz, slabs, neighbours, low_ref, high_ref, rate_ref, zero_ref, one_ref, two_ref,
    out_ref, pooled_ref, hot_t_ref, geo_ref, faded_ref, hot_ref
):
    @pl.when(lax.axis_index("segment") == tick)
    def _():
        rows = low_ref.shape[1]
        refs = (low_ref, high_ref)
        edges_of(refs, sz.coefs, slabs, neighbours, rate_ref, hot_ref, hot_t_ref, geo_ref)
        pooled = forward(refs, hot_ref, geo_ref, faded_ref, zero_ref, one_ref, two_ref, sz, rows, False)
        signal = signal_of(pooled, sz)
        gate, lifted = silu_parts(signal)
        for k in range(sz.coefs):
            pooled_ref[k] = pooled[k]
            added = lifted if k == 0 else gate * pooled[k]
            out_ref[k] = (own_rows(refs, k) + added).astype(BF16)
        out_ref[sz.coefs] = own_rows(refs, sz.coefs).astype(BF16)


def turn_kernel(
    tick, sz, slabs, neighbours, low_ref, high_ref, rate_ref, zero_ref, one_ref, two_ref,
    zero_t_ref, one_t_ref, two_t_ref, read_ref,
    back_low_ref, back_high_ref, hot_ref, hot_t_ref, geo_ref, faded_ref
):
    @pl.when(lax.axis_index("segment") == tick)
    def _():
        rows = low_ref.shape[1]
        refs = (low_ref, high_ref)
        outs = (back_low_ref, back_high_ref)
        own = edges_of(refs, sz.coefs, slabs, neighbours, rate_ref, hot_ref, hot_t_ref, geo_ref)
        pooled = forward(refs, hot_ref, geo_ref, faded_ref, zero_ref, one_ref, two_ref, sz, rows, True)
        signal = signal_of(pooled, sz)
        _, lifted = silu_parts(signal)
        updated = own_rows(refs, 0) + lifted
        gate, active = silu_parts(updated)
        read = read_ref[...]
        energy = jnp.sum(read * active, axis=1, keepdims=True)
        lane = lax.broadcasted_iota(jnp.int32, (rows, sz.c), 1)
        energy = around(jnp.where(lane == 3, energy, 0.0), rows // 2)
        upstream = [own[:, 3:4] * read * (gate + updated * gate * (1.0 - gate))]
        moved = backward(
            upstream, pooled, hot_t_ref, geo_ref, faded_ref, zero_t_ref, one_t_ref, two_t_ref, sz, rows, True, outs
        )
        send_back(moved + energy, outs, sz)


def backward_kernel(
    tick, sz, up_low_ref, up_high_ref, pooled_ref, hot_t_ref, geo_ref, faded_ref, zero_ref, one_ref, two_ref, *outs
):
    @pl.when(lax.axis_index("segment") == tick)
    def _():
        rows = up_low_ref.shape[1]
        upstream = [up_low_ref[k].astype(F32) + up_high_ref[k].astype(F32) for k in range(sz.coefs)]
        pooled = [pooled_ref[k] for k in range(sz.coefs)]
        moved = backward(
            upstream, pooled, hot_t_ref, geo_ref, faded_ref, zero_ref, one_ref, two_ref, sz, rows, False,
            outs if tick else None,
        )
        carried = decode(up_low_ref[sz.coefs].astype(F32)) + decode(up_high_ref[sz.coefs].astype(F32))
        moved = moved + around(carried, rows // 2)
        if tick:
            send_back(moved, outs, sz)
        else:
            share(moved, outs)


def call(body, operands, shapes, name, spaces=None, scratch=(), aliases=None):
    spaces = spaces or [pltpu.VMEM] * len(operands)
    operands = [pltpu.with_memory_space_constraint(value, space) for value, space in zip(operands, spaces)]
    return pl.pallas_call(
        body,
        out_shape=shapes,
        in_specs=[pl.BlockSpec(memory_space=space) for space in spaces],
        out_specs=[pl.BlockSpec(memory_space=pltpu.VMEM) for _ in shapes],
        scratch_shapes=list(scratch),
        input_output_aliases=aliases or {},
        compiler_params=pltpu.CompilerParams(vmem_limit_bytes=VMEM_LIMIT),
        name=name,
    )(*operands)


def on_device(
    node_states,
    species,
    species_table,
    places,
    sources,
    radial_rate,
    zero_weight,
    one_weight,
    two_weight,
    read_weight,
    energy_grad,
):
    segments = lax.axis_size("segment")
    slabs = lax.axis_size("space")
    batches, per_slab = species.shape
    coefs, channels = node_states.shape[2:]
    neighbours = sources.shape[2]
    rows = batches * per_slab
    edges = rows * neighbours
    sz = Sizes(zero_weight.shape, one_weight.shape, two_weight.shape, channels)
    axes = ("segment", "space")
    shape = jax.ShapeDtypeStruct

    pairs = slabs // 2

    def swapped(i):
        return i + 1 - 2 * (i % 2)

    def within(value, target):
        ways = [(i, target(i) % slabs) for i in range(slabs)]
        ways += [(s * slabs + i, s * slabs + swapped(i)) for s in range(1, segments) for i in range(slabs)]
        return lax.ppermute(value, axes, ways)

    def hop(value, start, stop, by, way):
        ways = [(place_of(q, pairs, start), place_of((q + by) % pairs, pairs, stop)) for q in range(pairs)]
        ways = [(start * slabs + 2 * a + c, stop * slabs + 2 * b + c) for a, b in ways for c in range(2)]
        idle = [s for s in range(segments) if s not in (start, stop)]
        if idle:
            third = idle[way % len(idle)]
            ways += [(stop * slabs + i, third * slabs + i) for i in range(slabs)]
            ways += [(third * slabs + i, start * slabs + i) for i in range(slabs)]
        else:
            ways += [(b, a) for a, b in ways]
        moving = {a for a, _ in ways}
        ways += [(i, swapped(i)) for i in range(segments * slabs) if i not in moving]
        return lax.ppermute(value, axes, ways)

    raw = [
        node_states.transpose(0, 2, 1, 3), places.transpose(1, 0, 2), species, sources, energy_grad, species_table,
    ]
    packed = shape((coefs + 1, per_slab, channels), BF16)
    mine, other = call(
        pack_kernel, raw, [packed, packed], "pack", [pltpu.HBM] * len(raw),
        [pltpu.VMEM(v.shape, v.dtype) for v in raw] + [pltpu.SemaphoreType.DMA((len(raw),))],
    )
    partner = within(other, swapped)
    straight = within(mine, lambda i: i + 2 if i % 2 else i - 2)
    cross = within(other, lambda i: i + 1 if i % 2 else i - 1)
    stored = [zero_weight[0], one_weight[0], two_weight[0]]
    spaces = [pltpu.HBM] * 3
    on_chip = [pltpu.VMEM(w.shape, w.dtype) for w in stored]
    sems = [pltpu.SemaphoreType.DMA((12,))]
    vectors = [radial_rate, read_weight.reshape(1, channels)]
    *weights, rate, read = call(
        functools.partial(stage_kernel, False), stored + vectors,
        on_chip + [pltpu.VMEM(v.shape, v.dtype) for v in vectors], "stage", [pltpu.HBM] * 5, sems,
    )
    whole = shape((coefs + 1, rows, channels), BF16)
    around_all = [call(open_kernel, [mine, partner, straight, cross], [whole, whole], "open")]
    weights = call(
        functools.partial(stage_kernel, True), [*stored, *weights, around_all[0][0]], on_chip, "stage",
        spaces + [pltpu.VMEM] * 4, sems, {3: 0, 4: 1, 5: 2},
    )
    kept_shapes = [
        shape((2 * rows, edges), BF16), shape((10 * edges, channels), F32), shape((coefs, edges, channels), F32),
    ]
    hot = [pltpu.VMEM((edges, 2 * rows), BF16)]
    kept = []
    for tick in range(segments - 1):
        out, *residuals = call(
            functools.partial(forward_kernel, tick, sz, slabs, neighbours),
            [*around_all[tick], rate, *weights],
            [whole, shape((coefs, rows, channels), F32), *kept_shapes],
            "forward",
            scratch=hot,
        )
        kept.append(residuals)
        if tick == 0:
            flipped = call(flip_kernel, [*weights, out], on_chip, "flip")
        ways = (1, 0) if tick % 2 else (0, -1)
        around_all.append([hop(out, tick, tick + 1, by, way) for way, by in enumerate(ways)])
    final = segments - 1
    slab_sums = shape((per_slab, channels), F32)
    parts = call(
        functools.partial(turn_kernel, final, sz, slabs, neighbours),
        [*around_all[final], rate, *weights, *flipped, read],
        [whole, whole],
        "turn",
        scratch=hot + [pltpu.VMEM(v.shape, v.dtype) for v in kept_shapes],
    )
    for tick in reversed(range(segments - 1)):
        ways = (1, 0) if tick % 2 else (0, -1)
        up = [hop(part, tick + 1, tick, -by, way) for way, (part, by) in enumerate(zip(parts, ways))]
        pooled, *residuals = kept[tick]
        parts = call(
            functools.partial(backward_kernel, tick, sz),
            [*up, pooled, *residuals, *flipped],
            [whole, whole] if tick else [slab_sums] * 4,
            "backward",
        )
    here, theirs, straight, cross = parts
    theirs = within(theirs, swapped)
    straight = within(straight, lambda i: i - 2 if i % 2 else i + 2)
    cross = within(cross, lambda i: i + 1 if i % 2 else i - 1)
    (both,) = call(join_kernel, [here, theirs, straight, cross], [shape((rows, channels), F32)], "join")

    def across(section, i, stop):
        if stop == segments - 1 and stop > 1:
            ring = {0: stop, stop: stop - 1, stop - 1: 0}
            if section in ring:
                return ring[section], i
        elif section in (0, stop):
            return stop - section, i
        return section, swapped(i)

    copies = [both] + [
        lax.ppermute(
            both,
            axes,
            [
                (s * slabs + i, t * slabs + j)
                for s in range(segments)
                for i in range(slabs)
                for t, j in [across(s, i, stop)]
            ],
        )
        for stop in range(1, segments)
    ]
    energies, gradients = call(
        close_kernel, copies, [shape((batches, per_slab), F32), shape((3, batches, per_slab), F32)], "close"
    )
    return energies, gradients.transpose(1, 0, 2)


def solution(mesh):
    in_specs = (
        P(None, "space", None, None),
        P(None, "space"),
        P(),
        P(None, None, "space"),
        P(None, "space", None),
        P("segment", None),
        P("segment", None, None),
        P("segment", None, None, None),
        P("segment", None, None, None),
        P(),
        P(None, "space"),
    )
    out_specs = (P(None, "space"), P(None, None, "space"))
    return jax.shard_map(
        on_device, mesh=mesh, in_specs=in_specs, out_specs=out_specs, check_vma=False
    )
```

```python
import functools

import jax
import jax.numpy as jnp
from jax import lax
from jax.experimental import pallas as pl
from jax.experimental.pallas import tpu as pltpu
from jax.sharding import PartitionSpec as P

SLAB_DEPTH = 2.0
F32 = jnp.float32
BF16 = jnp.bfloat16
VMEM_LIMIT = 16 * 1024 * 1024

MID, LOW, SOURCES = 32, 64, 96
BASE = 256


def split(value):
    high = value.astype(BF16)
    low = (value - high.astype(F32)).astype(BF16)
    return high, low


def split3(value):
    high = value.astype(BF16)
    rest = value - high.astype(F32)
    mid = rest.astype(BF16)
    return high, mid, (rest - mid.astype(F32)).astype(BF16)


def encode(value):
    high, mid, low = split3(value)
    return high.astype(F32) + pltpu.roll(mid.astype(F32), MID, 1) + pltpu.roll(low.astype(F32), LOW, 1)


def decode(value):
    lanes = value.shape[1]
    whole = value + pltpu.roll(value, lanes - MID, 1) + pltpu.roll(value, lanes - LOW, 1)
    lane = lax.broadcasted_iota(jnp.int32, value.shape, 1)
    return jnp.where(lane < 4, whole, 0.0)


def dot(a, b):
    return lax.dot_general(a, b, (((1,), (0,)), ((), ())), preferred_element_type=F32)


def fine_dot(value, weights):
    rows = value.shape[0]
    stacked = jnp.concatenate(split(value), axis=0)
    outs = []
    for weight in weights:
        out = dot(stacked, weight)
        outs.append(out[:rows] + out[rows:])
    return outs


def silu_parts(value):
    gate = 1.0 / (1.0 + jnp.exp(-value))
    return gate, value * gate


class Sizes:
    def __init__(self, zero_shape, one_shape, two_shape, channels):
        self.c = channels
        self.zero = zero_shape[-1] // channels
        self.one = one_shape[-1] // channels
        self.two = two_shape[-1] // channels
        self.coefs = self.zero + 2 * (self.one + self.two)
        self.starts = (self.zero, self.zero + 2 * self.one)
        self.counts = (self.one, self.two)

    def cols(self, first, count=1):
        return slice(first * self.c, (first + count) * self.c)


def picked_group(refs, hot, first, count):
    blocks = [jnp.concatenate([ref[k] for ref in refs], axis=0) for k in range(first, first + count)]
    return dot(hot, jnp.concatenate(blocks, axis=1))


def own_rows(refs, k):
    low, high = (ref[k].astype(F32) for ref in refs)
    slab = low.shape[0] // 2
    return jnp.concatenate([low[slab:], high[:slab]], axis=0)


def pool(value, rows):
    total = value[:rows]
    for start in range(rows, value.shape[0], rows):
        total = total + value[start : start + rows]
    return total


def geo_at(geo_ref, which, edges):
    return geo_ref[which * edges : (which + 1) * edges, :]


def forward(refs, hot_ref, geo_ref, faded_ref, zero_ref, one_ref, two_ref, sz, rows, last):
    hot = hot_ref[...]
    edges = hot.shape[0]
    factor = (edges // rows) ** (-0.5)
    radial = geo_at(geo_ref, 0, edges)

    def scaled(block, k):
        faded = block * radial
        faded_ref[k] = faded
        return faded.astype(BF16).astype(F32)

    pooled = [None] * sz.coefs
    group = picked_group(refs, hot, 0, sz.zero)
    zin = jnp.concatenate(
        [pool(scaled(group[:, sz.cols(k)], k), rows) for k in range(sz.zero)], axis=1
    )
    kept = 1 if last else sz.zero
    (zout,) = fine_dot(zin, [zero_ref[:, sz.cols(0, kept)]])
    for k in range(kept):
        pooled[k] = zout[:, sz.cols(k)] * factor
    for order in range(2):
        first, count = sz.starts[order], sz.counts[order]
        weight_ref = (one_ref, two_ref)[order]
        cos = geo_at(geo_ref, 1 + 2 * order, edges)
        sin = geo_at(geo_ref, 2 + 2 * order, edges)
        group = picked_group(refs, hot, first, 2 * count)
        res, ims = [], []
        for k in range(count):
            re = scaled(group[:, sz.cols(k)], first + k)
            im = scaled(group[:, sz.cols(count + k)], first + count + k)
            res.append(pool(cos * re - sin * im, rows))
            ims.append(pool(sin * re + cos * im, rows))
        both = jnp.concatenate(
            [jnp.concatenate(res, axis=1), jnp.concatenate(ims, axis=1)], axis=0
        )
        a, b = fine_dot(both, [weight_ref[0], weight_ref[1]])
        out_re = (a[:rows] - b[rows:]) * factor
        out_im = (b[:rows] + a[rows:]) * factor
        for k in range(count):
            pooled[first + k] = out_re[:, sz.cols(k)]
            pooled[first + count + k] = out_im[:, sz.cols(k)]
    return pooled


def signal_of(pooled, sz):
    total = pooled[0]
    for k in range(sz.zero, sz.coefs):
        total = total + pooled[k] * pooled[k]
    return total


def backward(
    upstream, pooled, hot_t_ref, geo_ref, faded_ref, zero_ref, one_ref, two_ref, sz, rows, last, outs
):
    hot_t = hot_t_ref[...]
    edges = hot_t.shape[1]
    slab = rows // 2
    factor = (edges // rows) ** (-0.5)
    signal = signal_of(pooled, sz)
    gate, _ = silu_parts(signal)
    slope = gate * (1.0 - gate)
    d_signal = upstream[0] * (gate + signal * slope)
    if not last:
        inner = upstream[1] * pooled[1]
        for k in range(2, sz.coefs):
            inner = inner + upstream[k] * pooled[k]
        d_signal = d_signal + inner * slope
    d_pooled = [d_signal * factor]
    for k in range(1, sz.coefs):
        if last:
            d_pooled.append(2.0 * factor * d_signal * pooled[k] if k >= sz.zero else None)
        else:
            term = gate * upstream[k]
            if k >= sz.zero:
                term = term + 2.0 * d_signal * pooled[k]
            d_pooled.append(term * factor)

    radial = geo_at(geo_ref, 0, edges)
    kept = 1 if last else sz.zero
    (dz,) = fine_dot(jnp.concatenate(d_pooled[:kept], axis=1), [zero_ref[sz.cols(0, kept), :]])

    def spread(block):
        return jnp.concatenate([block] * (edges // rows), axis=0)

    def scatter(first, blocks):
        if outs is None:
            return
        back = dot(hot_t, jnp.concatenate([block.astype(BF16) for block in blocks], axis=1))
        for n in range(len(blocks)):
            k = first + n
            part = back[:, sz.cols(n)]
            if not last or k == 0:
                part = part + around(upstream[k], slab)
            outs[0][k] = part[:rows].astype(BF16)
            outs[1][k] = part[rows:].astype(BF16)

    q_len = jnp.zeros((edges, sz.c), F32)
    blocks = []
    for k in range(sz.zero):
        grad = spread(dz[:, sz.cols(k)])
        q_len = q_len + grad * faded_ref[k]
        if outs is not None:
            blocks.append(grad * radial)
    scatter(0, blocks)
    q_turn = []
    for order in range(2):
        first, count = sz.starts[order], sz.counts[order]
        weight_ref = (one_ref, two_ref)[order]
        cos = geo_at(geo_ref, 1 + 2 * order, edges)
        sin = geo_at(geo_ref, 2 + 2 * order, edges)
        both = jnp.concatenate(
            [
                jnp.concatenate(d_pooled[first : first + count], axis=1),
                jnp.concatenate(d_pooled[first + count : first + 2 * count], axis=1),
            ],
            axis=0,
        )
        a, b = fine_dot(both, [weight_ref[0], weight_ref[1]])
        d_re = a[:rows] + b[rows:]
        d_im = a[rows:] - b[:rows]
        q_cos = jnp.zeros((edges, sz.c), F32)
        q_sin = jnp.zeros((edges, sz.c), F32)
        cos_r = cos * radial
        sin_r = sin * radial
        blocks_re, blocks_im = [], []
        for k in range(count):
            re = faded_ref[first + k]
            im = faded_ref[first + count + k]
            g_re = spread(d_re[:, sz.cols(k)])
            g_im = spread(d_im[:, sz.cols(k)])
            q_cos = q_cos + (re * g_re + im * g_im)
            q_sin = q_sin + (re * g_im - im * g_re)
            if outs is not None:
                blocks_re.append(cos_r * g_re + sin_r * g_im)
                blocks_im.append(cos_r * g_im - sin_r * g_re)
        scatter(first, blocks_re + blocks_im)
        q_len = q_len + cos * q_cos + sin * q_sin
        q_turn.append((q_cos, q_sin))

    rate = geo_at(geo_ref, 9, edges)

    def total(value):
        return jnp.sum(value, axis=1, keepdims=True)

    d_len = -total(q_len * rate)
    (dc1, ds1), (dc2, ds2) = [(total(a), total(b)) for a, b in q_turn]
    c1, s1 = geo_at(geo_ref, 1, edges), geo_at(geo_ref, 2, edges)
    ux, uy, uz = (geo_at(geo_ref, 5 + n, edges) for n in range(3))
    inv_planar = geo_at(geo_ref, 8, edges)
    dc1 = dc1 + 2.0 * (c1 * dc2 + s1 * ds2)
    ds1 = ds1 + 2.0 * (c1 * ds2 - s1 * dc2)
    along = c1 * dc1 + s1 * ds1
    dx = (dc1 - along * c1) * inv_planar + d_len * ux
    dy = (ds1 - along * s1) * inv_planar + d_len * uy
    dz_ = d_len * uz
    lane = lax.broadcasted_iota(jnp.int32, (edges, sz.c), 1)
    change = jnp.where(lane == 0, dx, jnp.where(lane == 1, dy, jnp.where(lane == 2, dz_, 0.0)))
    moved = sum(dot(hot_t, part) for part in split3(change))
    return moved - around(pool(change, rows), slab)


def around(own, slab):
    edge = jnp.zeros((slab, own.shape[1]), F32)
    return jnp.concatenate([edge, own, edge], axis=0)


def place_of(pair, pairs, segment):
    if segment == 0:
        return pair
    return 2 * pair if pair < pairs // 2 else 2 * (pairs - 1 - pair) + 1


def first_slab(slabs):
    slab_now = lax.axis_index("space")
    segment = lax.axis_index("segment")
    chip = slab_now // 2
    folded = jnp.where(lax.rem(chip, 2) == 0, chip // 2, slabs // 2 - 1 - chip // 2)
    pair = jnp.where(segment == 0, chip, folded)
    return lax.rem(2 * pair + lax.rem(segment, 2) - 1 + slabs, slabs), lax.rem(slab_now, 2)


def send_back(moved, outs, sz):
    rows = moved.shape[0] // 2
    coded = encode(moved).astype(BF16)
    outs[0][sz.coefs] = coded[:rows]
    outs[1][sz.coefs] = coded[rows:]


def share(moved, outs):
    slab = moved.shape[0] // 4
    left, low, high, right = (moved[n * slab : (n + 1) * slab] for n in range(4))
    even = lax.rem(lax.axis_index("space"), 2) == 0
    outs[0][...] = jnp.where(even, low, high)
    outs[1][...] = jnp.where(even, high, low)
    outs[2][...] = jnp.where(even, right, left)
    outs[3][...] = jnp.where(even, left, right)


def join_kernel(here_ref, theirs_ref, straight_ref, cross_ref, both_ref):
    slab = here_ref.shape[0]
    even = lax.rem(lax.axis_index("space"), 2) == 0
    here = here_ref[...] + straight_ref[...]
    there = theirs_ref[...] + cross_ref[...]
    both_ref[:slab, :] = jnp.where(even, here, there)
    both_ref[slab:, :] = jnp.where(even, there, here)


def close_kernel(*refs):
    *sums_refs, energies_ref, places_ref = refs
    slab = energies_ref.shape[1]
    for n, ref in enumerate(sums_refs):

        @pl.when(lax.axis_index("segment") == n)
        def _(ref=ref):
            sums = ref[...]
            rows, c = sums.shape
            turned = jnp.transpose(jnp.concatenate([sums, jnp.zeros((c - rows, c), F32)], axis=0))
            for b in range(2):
                energies_ref[b : b + 1, :] = turned[3:4, b * slab : (b + 1) * slab]
                for n in range(3):
                    places_ref[n, b : b + 1, :] = turned[n : n + 1, b * slab : (b + 1) * slab]


def pack_kernel(
    node_hbm, places_hbm, species_hbm, sources_hbm, grad_hbm, table_hbm, mine_ref, other_ref,
    states, places, species, sources, grads, table, sems
):
    @pl.when(lax.axis_index("segment") == 0)
    def _():
        pack(
            (node_hbm, places_hbm, species_hbm, sources_hbm, grad_hbm, table_hbm), mine_ref, other_ref,
            states, places, species, sources, grads, table, sems,
        )


def pack(given, mine_ref, other_ref, states, places, species, sources, grads, table, sems):
    batch = lax.rem(lax.axis_index("space"), 2)
    copies = []
    for n, (source, target) in enumerate(zip(given, (states, places, species, sources, grads, table))):
        copies.append(pltpu.make_async_copy(source, target, sems.at[n]))
        copies[-1].start()
    for copy in copies:
        copy.wait()
    coefs, per_slab, c = states.shape[1:]
    lane = lax.broadcasted_iota(jnp.int32, (per_slab, c), 1)
    eye = (
        lax.broadcasted_iota(jnp.int32, (per_slab, per_slab), 0)
        == lax.broadcasted_iota(jnp.int32, (per_slab, per_slab), 1)
    )

    def column(row):
        return jnp.sum(jnp.where(eye, jnp.broadcast_to(row, (per_slab, per_slab)), 0.0), axis=1, keepdims=True)

    both = []
    for b in range(2):
        names = column(species[b : b + 1, :].astype(F32)).astype(jnp.int32)
        kinds = table.shape[0]
        hot = (names == lax.broadcasted_iota(jnp.int32, (per_slab, kinds), 1)).astype(BF16)
        first = (states[b, 0].astype(F32) + dot(hot, table[...])).astype(BF16)
        extra = jnp.zeros((per_slab, c), F32)
        for n in range(3):
            extra = jnp.where(lane == n, column(places[n, b : b + 1, :]), extra)
        extra = encode(jnp.where(lane == 3, column(grads[b : b + 1, :]), extra))
        for j in range(sources.shape[2]):
            index = sources[b, :, j : j + 1]
            extra = jnp.where(lane == SOURCES + j, (index // BASE).astype(F32), extra)
            extra = jnp.where(lane == SOURCES + 8 + j, (index % BASE).astype(F32), extra)
        both.append((first, extra.astype(BF16)))
    for ref, chosen in ((mine_ref, batch), (other_ref, 1 - batch)):
        ref[pl.ds(0, coefs)] = states[chosen]
        ref[0] = jnp.where(chosen == 0, both[0][0].astype(F32), both[1][0].astype(F32)).astype(BF16)
        ref[coefs] = jnp.where(chosen == 0, both[0][1].astype(F32), both[1][1].astype(F32)).astype(BF16)


def open_kernel(mine_ref, partner_ref, straight_ref, cross_ref, low_ref, high_ref):
    @pl.when(lax.axis_index("segment") == 0)
    def _():
        even = lax.rem(lax.axis_index("space"), 2) == 0

        def choose(a, b):
            return jnp.where(even, a, b)

        for k in range(low_ref.shape[0]):
            mine, partner = mine_ref[k].astype(F32), partner_ref[k].astype(F32)
            straight, cross = straight_ref[k].astype(F32), cross_ref[k].astype(F32)
            low_ref[k] = jnp.concatenate([choose(cross, straight), choose(mine, partner)], axis=0).astype(BF16)
            high_ref[k] = jnp.concatenate([choose(partner, mine), choose(straight, cross)], axis=0).astype(BF16)


def edges_of(refs, coefs, slabs, neighbours, rate_ref, hot_ref, hot_t_ref, geo_ref):
    start, _ = first_slab(slabs)
    extra = jnp.concatenate([ref[coefs].astype(F32) for ref in refs], axis=0)
    window, c = extra.shape
    rows = window // 2
    per_slab = rows // 2
    edges = rows * neighbours
    numbers = decode(extra)
    own_extra = extra[per_slab : per_slab + rows]
    low = pltpu.roll(own_extra, c - 8, 1)
    index = own_extra.astype(jnp.int32) * BASE + low.astype(jnp.int32)
    place = lax.rem(index // per_slab - start + slabs, slabs) * per_slab + index % per_slab
    columns = lax.broadcasted_iota(jnp.int32, (rows, c), 1)
    hot = jnp.concatenate(
        [
            (place[:, SOURCES + j : SOURCES + j + 1] == columns).astype(F32)
            for j in range(neighbours)
        ],
        axis=0,
    )
    hot_t_ref[...] = jnp.transpose(hot).astype(BF16)[:window]
    hot = hot.astype(BF16)[:, :window]
    hot_ref[...] = hot
    lift = lax.broadcasted_iota(jnp.int32, (window, c), 0) // per_slab - 1
    offset = []
    for n in range(3):
        column = jnp.broadcast_to(numbers[:, n : n + 1], (window, c))
        if n == 2:
            column = column + SLAB_DEPTH * lift.astype(F32)
        there = sum(dot(hot, part) for part in split3(column))
        offset.append(there - jnp.concatenate([column[per_slab : per_slab + rows]] * neighbours, axis=0))
    flat = offset[0] * offset[0] + offset[1] * offset[1] + 1.0
    length = jnp.sqrt(flat + offset[2] * offset[2])
    planar = jnp.sqrt(flat)
    c1, s1 = offset[0] / planar, offset[1] / planar
    rate = jnp.broadcast_to(rate_ref[...], (edges, c))
    values = [
        jnp.exp(-rate * length),
        c1,
        s1,
        c1 * c1 - s1 * s1,
        2.0 * c1 * s1,
        offset[0] / length,
        offset[1] / length,
        offset[2] / length,
        1.0 / planar,
        rate,
    ]
    for n, value in enumerate(values):
        geo_ref[n * edges : (n + 1) * edges, :] = value
    return numbers[per_slab : per_slab + rows]


def bring(pairs, sems):
    copies = [pltpu.make_async_copy(source, target, sems.at[n]) for n, (source, target) in enumerate(pairs)]
    for copy in copies:
        copy.start()
    for copy in copies:
        copy.wait()


def stage_kernel(late, zero_hbm, one_hbm, two_hbm, *more):
    zero_ref, one_ref, two_ref, *vectors, sems = more[4:] if late else more[2:]
    waits = (lax.axis_index("segment") == 0) & (lax.rem(lax.axis_index("space"), 2) == 0)
    if not late:
        bring(list(zip(more[:2], vectors)), sems)

    @pl.when(waits == late)
    def _():
        whole = [(zero_hbm, zero_ref)]
        for source, target in ((one_hbm, one_ref), (two_hbm, two_ref)):
            whole += [(source.at[n], target.at[n]) for n in range(2)]
        pairs = []
        for source, target in whole:
            half = source.shape[0] // 2
            pairs += [(source.at[pl.ds(n * half, half)], target.at[pl.ds(n * half, half)]) for n in range(2)]
        bring(pairs, sems)


def flip_kernel(zero_ref, one_ref, two_ref, _, zero_t_ref, one_t_ref, two_t_ref):
    zero_t_ref[...] = jnp.transpose(zero_ref[...])
    for n in range(2):
        one_t_ref[n] = jnp.transpose(one_ref[n])
        two_t_ref[n] = jnp.transpose(two_ref[n])


def forward_kernel(
    tick, swap, sz, slabs, neighbours, low_ref, high_ref, rate_ref, zero_ref, one_ref, two_ref,
    out_ref, pooled_ref, hot_t_ref, geo_ref, faded_ref, hot_ref
):
    @pl.when(lax.axis_index("segment") == tick)
    def _():
        rows = low_ref.shape[1]
        refs = (high_ref, low_ref) if swap else (low_ref, high_ref)
        edges_of(refs, sz.coefs, slabs, neighbours, rate_ref, hot_ref, hot_t_ref, geo_ref)
        pooled = forward(refs, hot_ref, geo_ref, faded_ref, zero_ref, one_ref, two_ref, sz, rows, False)
        signal = signal_of(pooled, sz)
        gate, lifted = silu_parts(signal)
        for k in range(sz.coefs):
            pooled_ref[k] = pooled[k]
            added = lifted if k == 0 else gate * pooled[k]
            out_ref[k] = (own_rows(refs, k) + added).astype(BF16)
        out_ref[sz.coefs] = own_rows(refs, sz.coefs).astype(BF16)


def turn_kernel(
    tick, swap, sz, slabs, neighbours, low_ref, high_ref, rate_ref, zero_ref, one_ref, two_ref,
    zero_t_ref, one_t_ref, two_t_ref, read_ref,
    back_low_ref, back_high_ref, hot_ref, hot_t_ref, geo_ref, faded_ref
):
    @pl.when(lax.axis_index("segment") == tick)
    def _():
        rows = low_ref.shape[1]
        refs = (high_ref, low_ref) if swap else (low_ref, high_ref)
        outs = (back_low_ref, back_high_ref)
        own = edges_of(refs, sz.coefs, slabs, neighbours, rate_ref, hot_ref, hot_t_ref, geo_ref)
        pooled = forward(refs, hot_ref, geo_ref, faded_ref, zero_ref, one_ref, two_ref, sz, rows, True)
        signal = signal_of(pooled, sz)
        _, lifted = silu_parts(signal)
        updated = own_rows(refs, 0) + lifted
        gate, active = silu_parts(updated)
        read = read_ref[...]
        energy = jnp.sum(read * active, axis=1, keepdims=True)
        lane = lax.broadcasted_iota(jnp.int32, (rows, sz.c), 1)
        energy = around(jnp.where(lane == 3, energy, 0.0), rows // 2)
        upstream = [own[:, 3:4] * read * (gate + updated * gate * (1.0 - gate))]
        moved = backward(
            upstream, pooled, hot_t_ref, geo_ref, faded_ref, zero_t_ref, one_t_ref, two_t_ref, sz, rows, True, outs
        )
        send_back(moved + energy, outs, sz)


def backward_kernel(
    tick, sz, up_low_ref, up_high_ref, pooled_ref, hot_t_ref, geo_ref, faded_ref, zero_ref, one_ref, two_ref, *outs
):
    @pl.when(lax.axis_index("segment") == tick)
    def _():
        rows = up_low_ref.shape[1]
        upstream = [up_low_ref[k].astype(F32) + up_high_ref[k].astype(F32) for k in range(sz.coefs)]
        pooled = [pooled_ref[k] for k in range(sz.coefs)]
        moved = backward(
            upstream, pooled, hot_t_ref, geo_ref, faded_ref, zero_ref, one_ref, two_ref, sz, rows, False,
            outs if tick else None,
        )
        carried = decode(up_low_ref[sz.coefs].astype(F32)) + decode(up_high_ref[sz.coefs].astype(F32))
        moved = moved + around(carried, rows // 2)
        if tick:
            send_back(moved, outs, sz)
        else:
            share(moved, outs)


def call(body, operands, shapes, name, spaces=None, scratch=(), aliases=None):
    spaces = spaces or [pltpu.VMEM] * len(operands)
    operands = [pltpu.with_memory_space_constraint(value, space) for value, space in zip(operands, spaces)]
    return pl.pallas_call(
        body,
        out_shape=shapes,
        in_specs=[pl.BlockSpec(memory_space=space) for space in spaces],
        out_specs=[pl.BlockSpec(memory_space=pltpu.VMEM) for _ in shapes],
        scratch_shapes=list(scratch),
        input_output_aliases=aliases or {},
        compiler_params=pltpu.CompilerParams(vmem_limit_bytes=VMEM_LIMIT),
        name=name,
    )(*operands)


def on_device(
    node_states,
    species,
    species_table,
    places,
    sources,
    radial_rate,
    zero_weight,
    one_weight,
    two_weight,
    read_weight,
    energy_grad,
):
    segments = lax.axis_size("segment")
    slabs = lax.axis_size("space")
    batches, per_slab = species.shape
    coefs, channels = node_states.shape[2:]
    neighbours = sources.shape[2]
    rows = batches * per_slab
    edges = rows * neighbours
    sz = Sizes(zero_weight.shape, one_weight.shape, two_weight.shape, channels)
    axes = ("segment", "space")
    shape = jax.ShapeDtypeStruct

    pairs = slabs // 2

    def swapped(i):
        return i + 1 - 2 * (i % 2)

    def within(value, target):
        ways = [(i, target(i) % slabs) for i in range(slabs)]
        ways += [(s * slabs + i, s * slabs + swapped(i)) for s in range(1, segments) for i in range(slabs)]
        return lax.ppermute(value, axes, ways)

    def hop(value, start, stop, by, way):
        ways = [(place_of(q, pairs, start), place_of((q + by) % pairs, pairs, stop)) for q in range(pairs)]
        ways = [(start * slabs + 2 * a + c, stop * slabs + 2 * b + c) for a, b in ways for c in range(2)]
        idle = [s for s in range(segments) if s not in (start, stop)]
        if idle:
            third = idle[way % len(idle)]
            ways += [(stop * slabs + i, third * slabs + i) for i in range(slabs)]
            ways += [(third * slabs + i, start * slabs + i) for i in range(slabs)]
        else:
            ways += [(b, a) for a, b in ways]
        moving = {a for a, _ in ways}
        ways += [(i, swapped(i)) for i in range(segments * slabs) if i not in moving]
        return lax.ppermute(value, axes, ways)

    raw = [
        node_states.transpose(0, 2, 1, 3), places.transpose(1, 0, 2), species, sources, energy_grad, species_table,
    ]
    packed = shape((coefs + 1, per_slab, channels), BF16)
    mine, other = call(
        pack_kernel, raw, [packed, packed], "pack", [pltpu.HBM] * len(raw),
        [pltpu.VMEM(v.shape, v.dtype) for v in raw] + [pltpu.SemaphoreType.DMA((len(raw),))],
    )
    partner = within(other, swapped)
    straight = within(mine, lambda i: i + 2 if i % 2 else i - 2)
    cross = within(other, lambda i: i + 1 if i % 2 else i - 1)
    stored = [zero_weight[0], one_weight[0], two_weight[0]]
    spaces = [pltpu.HBM] * 3
    on_chip = [pltpu.VMEM(w.shape, w.dtype) for w in stored]
    sems = [pltpu.SemaphoreType.DMA((10,))]
    vectors = [radial_rate, read_weight.reshape(1, channels)]
    *weights, rate, read = call(
        functools.partial(stage_kernel, False), stored + vectors,
        on_chip + [pltpu.VMEM(v.shape, v.dtype) for v in vectors], "stage", [pltpu.HBM] * 5, sems,
    )
    whole = shape((coefs + 1, rows, channels), BF16)
    around_all = [call(open_kernel, [mine, partner, straight, cross], [whole, whole], "open")]
    weights = call(
        functools.partial(stage_kernel, True), [*stored, *weights, around_all[0][0]], on_chip, "stage",
        spaces + [pltpu.VMEM] * 4, sems, {3: 0, 4: 1, 5: 2},
    )
    kept_shapes = [
        shape((2 * rows, edges), BF16), shape((10 * edges, channels), F32), shape((coefs, edges, channels), F32),
    ]
    hot = [pltpu.VMEM((edges, 2 * rows), BF16)]
    kept, swaps = [], [False]
    for tick in range(segments - 1):
        out, *residuals = call(
            functools.partial(forward_kernel, tick, swaps[tick], sz, slabs, neighbours),
            [*around_all[tick], rate, *weights],
            [whole, shape((coefs, rows, channels), F32), *kept_shapes],
            "forward",
            scratch=hot,
        )
        kept.append(residuals)
        if tick == 0:
            flipped = call(flip_kernel, [*weights, out], on_chip, "flip")
        ways = (1, 0) if tick % 2 else (0, -1)
        sent = [hop(out, tick, tick + 1, by, way) for way, by in enumerate(ways)]
        swaps.append(ways[0] == 0)
        around_all.append(sent[::-1] if swaps[-1] else sent)
    final = segments - 1
    slab_sums = shape((per_slab, channels), F32)
    parts = call(
        functools.partial(turn_kernel, final, swaps[final], sz, slabs, neighbours),
        [*around_all[final], rate, *weights, *flipped, read],
        [whole, whole],
        "turn",
        scratch=hot + [pltpu.VMEM(v.shape, v.dtype) for v in kept_shapes],
    )
    for tick in reversed(range(segments - 1)):
        ways = (1, 0) if tick % 2 else (0, -1)
        up = [hop(part, tick + 1, tick, -by, way) for way, (part, by) in enumerate(zip(parts, ways))]
        pooled, *residuals = kept[tick]
        parts = call(
            functools.partial(backward_kernel, tick, sz),
            [*(up if ways[0] == 0 else up[::-1]), pooled, *residuals, *flipped],
            [whole, whole] if tick else [slab_sums] * 4,
            "backward",
        )
    here, theirs, straight, cross = parts
    theirs = within(theirs, swapped)
    straight = within(straight, lambda i: i - 2 if i % 2 else i + 2)
    cross = within(cross, lambda i: i + 1 if i % 2 else i - 1)
    (both,) = call(join_kernel, [here, theirs, straight, cross], [shape((rows, channels), F32)], "join")

    def across(section, i, stop):
        if section in (0, stop):
            return stop - section, i
        return section, swapped(i)

    copies = [both] + [
        lax.ppermute(
            both,
            axes,
            [
                (s * slabs + i, t * slabs + j)
                for s in range(segments)
                for i in range(slabs)
                for t, j in [across(s, i, stop)]
            ],
        )
        for stop in range(1, segments)
    ]
    energies, gradients = call(
        close_kernel, copies, [shape((batches, per_slab), F32), shape((3, batches, per_slab), F32)], "close"
    )
    return energies, gradients.transpose(1, 0, 2)


def solution(mesh):
    in_specs = (
        P(None, "space", None, None),
        P(None, "space"),
        P(),
        P(None, None, "space"),
        P(None, "space", None),
        P("segment", None),
        P("segment", None, None),
        P("segment", None, None, None),
        P("segment", None, None, None),
        P(),
        P(None, "space"),
    )
    out_specs = (P(None, "space"), P(None, None, "space"))
    return jax.shard_map(
        on_device, mesh=mesh, in_specs=in_specs, out_specs=out_specs, check_vma=False
    )
```
